32 devices in a mesh: narrow: 2 (over core), wide: 16 (over z, y, x).
Axes of the slice: x: 2, y: 2, z: 4, core: 2. Of those that a mesh axis runs over, the one named last changes fastest.
Arguments:
- char_ids: int32 [32, 512, 50], P(('narrow', 'wide')), may hold values from 0 to 261
- word_lengths: int32 [32, 512], P(('narrow', 'wide')), may hold values from 1 to 50, as said below
- type_ids: int32 [32, 512], P(('narrow', 'wide')), may hold values from 0 to 1
- cotangent: bfloat16 [32, 512, 768], P(('narrow', 'wide')), may hold values from -6 to 6
- character_embedding_table: bfloat16 [262, 16], replicated, may hold values from -4 to 4
- conv_weight: bfloat16 [112, 2048], P(None, 'wide'), may hold values from -0.75 to 0.75
- conv_bias: bfloat16 [2048], P('wide'), may hold values from -1.75 to 1.75
- high_weight: bfloat16 [2, 2048, 4096], P(None, None, 'wide'), may hold values from -0.125 to 0.125
- high_bias: bfloat16 [2, 4096], P(None, 'wide'), may hold values from -1.75 to 1.75
- proj_weight: bfloat16 [2048, 768], P('wide'), may hold values from -0.25 to 0.25
- proj_bias: bfloat16 [768], P('wide'), may hold values from -1.75 to 1.75
- pos_table: bfloat16 [512, 768], P(None, 'wide'), may hold values from -3 to 3
- type_table: bfloat16 [2, 768], P(None, 'wide'), may hold values from -3 to 3
- embed_gain: bfloat16 [768], P('wide'), may hold values from 0.5 to 1.5
- embed_shift: bfloat16 [768], P('wide'), may hold values from -1.75 to 1.75
- qkv_weight: bfloat16 [768, 2304], P(None, 'wide'), may hold values from -0.21875 to 0.21875
- attn_bias: bfloat16 [1536], P('wide'), may hold values from -1.75 to 1.75
- out_weight: bfloat16 [768, 768], P('wide'), may hold values from -1.25 to 1.25
- out_bias: bfloat16 [768], P('wide'), may hold values from -1.75 to 1.75
- attn_gain: bfloat16 [768], P('wide'), may hold values from 0.5 to 1.5
- attn_shift: bfloat16 [768], P('wide'), may hold values from -1.75 to 1.75
- up_weight: bfloat16 [768, 3072], P(None, 'wide'), may hold values from -0.21875 to 0.21875
- up_bias: bfloat16 [3072], P('wide'), may hold values from -1.75 to 1.75
- down_weight: bfloat16 [3072, 768], P('wide'), may hold values from -0.109375 to 0.109375
- down_bias: bfloat16 [768], P('wide'), may hold values from -1.75 to 1.75
- ffn_gain: bfloat16 [768], P('wide'), may hold values from 0.5 to 1.5
- ffn_shift: bfloat16 [768], P('wide'), may hold values from -1.75 to 1.75
Outputs:
- hidden_out: bfloat16 [32, 512, 768], P(('narrow', 'wide'))
- grad_char_table: float32 [262, 16], replicated
- grad_conv_weight: float32 [112, 2048], P(None, ('narrow', 'wide'))
- grad_conv_bias: float32 [2048], P(('narrow', 'wide'))
- grad_high_weight: float32 [2, 2048, 4096], P(None, None, ('narrow', 'wide'))
- grad_high_bias: float32 [2, 4096], P(None, ('narrow', 'wide'))
- grad_proj_weight: float32 [2048, 768], P(('narrow', 'wide'))
- grad_proj_bias: float32 [768], P(('narrow', 'wide'))
- grad_pos_table: float32 [512, 768], P(None, ('narrow', 'wide'))
- grad_type_table: float32 [2, 768], P(None, ('narrow', 'wide'))
- grad_embed_gain: float32 [768], P(('narrow', 'wide'))
- grad_embed_shift: float32 [768], P(('narrow', 'wide'))
- grad_qkv_weight: float32 [768, 2304], P(None, ('narrow', 'wide'))
- grad_attn_bias: float32 [1536], P(('narrow', 'wide'))
- grad_out_weight: float32 [768, 768], P(('narrow', 'wide'))
- grad_out_bias: float32 [768], P(('narrow', 'wide'))
- grad_attn_gain: float32 [768], P(('narrow', 'wide'))
- grad_attn_shift: float32 [768], P(('narrow', 'wide'))
- grad_up_weight: float32 [768, 3072], P(None, ('narrow', 'wide'))
- grad_up_bias: float32 [3072], P(('narrow', 'wide'))
- grad_down_weight: float32 [3072, 768], P(('narrow', 'wide'))
- grad_down_bias: float32 [768], P(('narrow', 'wide'))
- grad_ffn_gain: float32 [768], P(('narrow', 'wide'))
- grad_ffn_shift: float32 [768], P(('narrow', 'wide'))
The draws below stay inside these ranges and needn't reach their ends.
Inputs may be any that keep to these rules, and one draw needn't show every extreme that they name: `word_lengths`: every sequence holds at least one word of 50 characters.
All inputs are finite; a program needn't handle non-finite values.
Results may differ from the reference program's by a relative error of at most 0.017.
Values may be sent and summed in bfloat16 or wider, within the bound.
No kernel may reach another device: no remote copies, remote signals or barrier semaphores. Data moves between devices by JAX's collectives and lax.ppermute only.
A program may use at most 384 MiB of HBM per device.

```python
import functools
import math
import jax
import jax.numpy as jnp
from jax import lax

D = 768
HEADS = 12
HEAD_DIM = 64
FF = 3072
FILTERS = 2048
CHAR_DIM = 16
CHAR_VOCAB = 262
CHARS = 50
TAPS = 7
HIGHWAYS = 2
SEQ_LEN = 512
SEQS = 32


def draw_word_lengths(key, part):
    key = jax.random.fold_in(key, 11)
    keys_list = jax.random.split(key, 4)
    shorter = jax.random.randint(keys_list[0], (SEQS, SEQ_LEN), 1, 9)
    longer = jax.random.randint(keys_list[1], (SEQS, SEQ_LEN), 0, CHARS)
    rarely = jax.random.randint(keys_list[2], (SEQS, SEQ_LEN), 0, 6) == 0
    lengths_all = jnp.minimum(shorter + jnp.where(rarely, longer, 0), CHARS)
    longest = jax.random.randint(keys_list[3], (SEQS, 1), 0, SEQ_LEN)
    return jnp.where(jnp.arange(SEQ_LEN)[None, :] == longest, CHARS, lengths_all).astype(jnp.int32)


def plant(array, stream_key, low, top_value):
    longest = array.shape.index(max(array.shape))
    spots = []
    for shift in (0, 1):
        where = [jax.random.randint(jax.random.fold_in(stream_key, axis), (), 0, length) for axis, length in enumerate(array.shape)]
        where[longest] = (where[longest] + shift) % array.shape[longest]
        spots.append(tuple(where))
    return array.at[spots[0]].set(low).at[spots[1]].set(top_value)


def steps_of(own_key, shape, shards, low, top_value):
    def one(dim, blocks):
        steps = jax.random.uniform(jax.random.fold_in(jax.random.fold_in(own_key, 6), dim), (blocks,), jnp.float32, low / len(shards), top_value / len(shards))
        return jnp.repeat(jnp.exp(steps), shape[dim] // blocks).reshape((-1,) + (1,) * (len(shape) - dim - 1))

    gain = one(*shards[0])
    for cut in shards[1:]:
        gain = gain * one(*cut)
    return gain


def noise(stream_key, dims, deviation, most, shards=(), dtype=jnp.bfloat16):
    loudness = steps_of(stream_key, dims, shards, -0.22, 0.18) if shards else 1.0
    drawn = jax.random.normal(stream_key, dims, jnp.float32) * deviation * loudness
    return jnp.minimum(jnp.maximum(drawn, -most), most).astype(dtype)


def setup_inputs(seed: int = 0) -> dict:
    streams_of = jax.random.split(jax.random.key(seed), 28)
    char_ids = plant(jax.random.randint(streams_of[0], (SEQS, SEQ_LEN, CHARS), 0, CHAR_VOCAB), jax.random.fold_in(streams_of[0], 1), 0, CHAR_VOCAB - 1).astype(jnp.int32)
    word_lengths = draw_word_lengths(jax.random.fold_in(streams_of[27], 71), 0)
    type_ids = plant(jax.random.randint(streams_of[2], (SEQS, SEQ_LEN), 0, 2), jax.random.fold_in(streams_of[2], 1), 0, 1).astype(jnp.int32)
    cotangent = noise(streams_of[3], (SEQS, SEQ_LEN, D), 1.0, 6.0, ((0, 32),))
    character_embedding_table = noise(streams_of[4], (CHAR_VOCAB, CHAR_DIM), 1.0, 4.0)
    conv_weight = noise(streams_of[5], (TAPS * CHAR_DIM, FILTERS), 64 ** -0.5, 0.75, ((1, 16),))
    conv_bias = noise(streams_of[6], (FILTERS,), 0.3, 1.75, ((0, 16),))
    high_weight = noise(streams_of[7], (HIGHWAYS, FILTERS, 2 * FILTERS), FILTERS ** -0.5, 0.125, ((2, 16),))
    high_bias = noise(streams_of[8], (HIGHWAYS, 2 * FILTERS), 0.3, 1.75, ((1, 16),))
    proj_weight = noise(streams_of[9], (FILTERS, D), (FILTERS // 4) ** -0.5, 0.25, ((0, 16),))
    proj_bias = noise(streams_of[10], (D,), 0.3, 1.75, ((0, 16),))
    pos_table = noise(streams_of[11], (SEQ_LEN, D), 0.5, 3.0, ((1, 16),))
    type_table = noise(streams_of[12], (2, D), 0.5, 3.0, ((1, 16),))
    embed_gain = jnp.clip(1.0 + 0.1 * jax.random.normal(streams_of[13], (D,), jnp.float32), 0.5, 1.5).astype(jnp.bfloat16)
    embed_shift = noise(streams_of[14], (D,), 0.3, 1.75, ((0, 16),))
    qkv_weight = noise(streams_of[15], (D, 3 * D), D ** -0.5, 0.21875, ((1, 16),))
    attn_bias = noise(streams_of[16], (2 * D,), 0.3, 1.75, ((0, 16),))
    out_weight = noise(streams_of[17], (D, D), (D // 32) ** -0.5, 1.25, ((0, 16),))
    out_bias = noise(streams_of[18], (D,), 0.3, 1.75, ((0, 16),))
    attn_gain = jnp.clip(1.0 + 0.1 * jax.random.normal(streams_of[19], (D,), jnp.float32), 0.5, 1.5).astype(jnp.bfloat16)
    attn_shift = noise(streams_of[20], (D,), 0.3, 1.75, ((0, 16),))
    up_weight = noise(streams_of[21], (D, FF), D ** -0.5, 0.21875, ((1, 16),))
    up_bias = noise(streams_of[22], (FF,), 0.3, 1.75, ((0, 16),))
    down_weight = noise(streams_of[23], (FF, D), FF ** -0.5, 0.109375, ((0, 16),))
    down_bias = noise(streams_of[24], (D,), 0.3, 1.75, ((0, 16),))
    ffn_gain = jnp.clip(1.0 + 0.1 * jax.random.normal(streams_of[25], (D,), jnp.float32), 0.5, 1.5).astype(jnp.bfloat16)
    ffn_shift = noise(streams_of[26], (D,), 0.3, 1.75, ((0, 16),))
    return dict(char_ids=char_ids, word_lengths=word_lengths, type_ids=type_ids, cotangent=cotangent, character_embedding_table=character_embedding_table, conv_weight=conv_weight, conv_bias=conv_bias, high_weight=high_weight, high_bias=high_bias, proj_weight=proj_weight, proj_bias=proj_bias, pos_table=pos_table, type_table=type_table, embed_gain=embed_gain, embed_shift=embed_shift, qkv_weight=qkv_weight, attn_bias=attn_bias, out_weight=out_weight, out_bias=out_bias, attn_gain=attn_gain, attn_shift=attn_shift, up_weight=up_weight, up_bias=up_bias, down_weight=down_weight, down_bias=down_bias, ffn_gain=ffn_gain, ffn_shift=ffn_shift)


@jax.custom_vjp
def low(v):
    return lax.optimization_barrier(v.astype(jnp.bfloat16)).astype(jnp.float32)

@jax.custom_vjp
def low_back(v):
    return v

def low_keep(v):
    return (low(v), None)

def low_pass(kept, grad):
    return (grad,)

def back_keep(v):
    return (v, None)

def back_low(kept, grad):
    return (low(grad),)
low.defvjp(low_keep, low_pass)
low_back.defvjp(back_keep, back_low)
HIGHEST = lax.Precision.HIGHEST
EPSILON = 1e-12

def product(left_rows, right_rows):
    return jnp.dot(left_rows, right_rows, precision=HIGHEST)

def norm_rows(value, norm_gain, norm_shift):
    center = lax.optimization_barrier(jnp.mean(value, axis=-1, keepdims=True))
    offsets = value - center
    spread = lax.optimization_barrier(jnp.mean(offsets * offsets, axis=-1, keepdims=True))
    return offsets * lax.rsqrt(spread + EPSILON) * norm_gain + norm_shift

def filter_widths():
    column = jnp.arange(FILTERS)
    widths = jnp.ones((FILTERS,), jnp.int32)
    for exponent in range(6):
        widths = widths + (column >= FILTERS * 2 ** exponent // 64).astype(jnp.int32)
    return widths

def pool_words(table, matrix, conv_b, inputs):
    char_block, block_size_entry = inputs
    live_mask = (jnp.arange(CHARS)[None, :] < block_size_entry[:, None]).astype(jnp.float32)
    vectors = low_back(jnp.take(table, char_block, axis=0) * live_mask[:, :, None])
    padded = jnp.pad(vectors, ((0, 0), (0, TAPS), (0, 0)))
    windows = jnp.concatenate([padded[:, offset:offset + CHARS, :] for offset in range(TAPS + 1)], axis=2)
    prior_value = low_back(product(windows.reshape(-1, (TAPS + 1) * CHAR_DIM), matrix) + conv_b)
    activated = jax.nn.silu(prior_value).reshape(block_size_entry.shape[0], CHARS, FILTERS)
    return lax.optimization_barrier(jnp.sum(activated * live_mask[:, :, None], axis=1)) / block_size_entry[:, None].astype(jnp.float32)

def embed_words(char_rows, size_rows, type_rows, params):
    table, conv_w, conv_b, high_w, high_b, proj_w, proj_b, pos_t, type_t, norm_gain, norm_shift = params
    usable = jnp.arange(TAPS * CHAR_DIM)[:, None] // CHAR_DIM < filter_widths()[None, :]
    matrix = jnp.concatenate([jnp.where(usable, conv_w, 0.0), jnp.zeros((CHAR_DIM, FILTERS), jnp.float32)], axis=0)
    block_words = math.gcd(SEQ_LEN, 128)
    pooled = lax.map(jax.checkpoint(functools.partial(pool_words, table, matrix, conv_b)), (char_rows.reshape(-1, block_words, CHARS), size_rows.reshape(-1, block_words)))
    highway = pooled.reshape(SEQ_LEN, FILTERS)
    for layer in range(HIGHWAYS):
        mixed = low_back(product(low(highway), high_w[layer]) + high_b[layer])
        gating = jax.nn.sigmoid(mixed[:, FILTERS:])
        highway = gating * highway + (1.0 - gating) * jax.nn.silu(mixed[:, :FILTERS])
    word_vec = low_back(product(low(highway), proj_w) + proj_b)
    type_vec = jnp.where(type_rows[:, None] == 1, type_t[1][None, :], type_t[0][None, :])
    return norm_rows(word_vec + pos_t + type_vec, norm_gain, norm_shift)

def encode(embedded, params):
    qkv_w, attn_b, out_w, out_b, gain_one, shift_one, up_w, up_b, down_w, down_b, gain_two, shift_two = params
    bias_three = jnp.concatenate([attn_b[:D], jnp.zeros((D,), jnp.float32), attn_b[D:]])
    qkv_rows = low(low_back(product(low(embedded), qkv_w) + bias_three))
    sections = qkv_rows.reshape(SEQ_LEN, 3, HEADS, HEAD_DIM).transpose(1, 2, 0, 3)
    scaling = HEAD_DIM ** (-0.5)
    scores = low_back(scaling * jnp.einsum('hqd,hkd->hqk', sections[0], sections[1], precision=HIGHEST))
    attention = low(jax.nn.softmax(scores, axis=-1))
    context = low(low_back(jnp.einsum('hqk,hkd->hqd', attention, sections[2], precision=HIGHEST)))
    merged = context.transpose(1, 0, 2).reshape(SEQ_LEN, D)
    branch = low_back(product(merged, out_w) + out_b)
    first = norm_rows(embedded + branch, gain_one, shift_one)
    inner = low_back(product(low(first), up_w) + up_b)
    activation = low(jax.nn.gelu(inner, approximate=False))
    ffn_out = low_back(product(activation, down_w) + down_b)
    return norm_rows(first + ffn_out, gain_two, shift_two)

def reference(char_ids, word_lengths, type_ids, cotangent, character_embedding_table, conv_weight, conv_bias, high_weight, high_bias, proj_weight, proj_bias, pos_table, type_table, embed_gain, embed_shift, qkv_weight, attn_bias, out_weight, out_bias, attn_gain, attn_shift, up_weight, up_bias, down_weight, down_bias, ffn_gain, ffn_shift):
    embed_params = tuple((value.astype(jnp.float32) for value in (character_embedding_table, conv_weight, conv_bias, high_weight, high_bias, proj_weight, proj_bias, pos_table, type_table, embed_gain, embed_shift)))
    encoder_params = tuple((value.astype(jnp.float32) for value in (qkv_weight, attn_bias, out_weight, out_bias, attn_gain, attn_shift, up_weight, up_bias, down_weight, down_bias, ffn_gain, ffn_shift)))

    def forward(embed_p, encoder_p):

        def one_sequence(inputs):
            return encode(embed_words(inputs[0], inputs[1], inputs[2], embed_p), encoder_p)
        return lax.map(jax.checkpoint(one_sequence), (char_ids, word_lengths, type_ids))
    hidden, pullback = jax.vjp(forward, embed_params, encoder_params)
    embed_grads, encoder_grads = pullback(cotangent.astype(jnp.float32))
    g_table, g_conv, g_conv_b, g_high, g_high_b, g_proj, g_proj_b, g_pos, g_type, g_gain_zero, g_shift_zero = embed_grads
    g_qkv, g_attn_b, g_out, g_out_b, g_gain_one, g_shift_one, g_up, g_up_b, g_down, g_down_b, g_gain_two, g_shift_two = encoder_grads
    return (hidden.astype(jnp.bfloat16), g_table, g_conv, g_conv_b, g_high, g_high_b, g_proj, g_proj_b, g_pos, g_type, g_gain_zero, g_shift_zero, g_qkv, g_attn_b, g_out, g_out_b, g_gain_one, g_shift_one, g_up, g_up_b, g_down, g_down_b, g_gain_two, g_shift_two)
```

```python
from functools import partial

import jax
import jax.numpy as jnp
from jax import lax
from jax.experimental import pallas as pl
from jax.experimental.pallas import tpu as pltpu
from jax.sharding import PartitionSpec as P

HEADS = 12
HEAD_DIM = 64
CHAR_DIM = 16
TAPS = 7
EPSILON = 1e-12

LANES = 128
GROUP = LANES // CHAR_DIM
BLOCK_WORDS = 32
CHUNK_BLOCKS = 16
CHUNK = BLOCK_WORDS * CHUNK_BLOCKS
TABLE_PAD = 384
ROW_TILE = 128
BIAS_LANE = TAPS * CHAR_DIM

F32 = jnp.float32
BF16 = jnp.bfloat16
VMEM = pl.BlockSpec(memory_space=pltpu.VMEM)
SMEM = pl.BlockSpec(memory_space=pltpu.SMEM)
MIB = 1024 * 1024


def dot(left, right):
    return lax.dot_general(left, right, (((1,), (0,)), ((), ())), preferred_element_type=F32)


def dot_nt(left, right):
    return lax.dot_general(left, right, (((1,), (1,)), ((), ())), preferred_element_type=F32)


def dot_tn(left, right):
    return lax.dot_general(left, right, (((0,), (0,)), ((), ())), preferred_element_type=F32)


def column_sum(values):
    return jnp.sum(values.astype(F32), axis=0)


def filter_widths(filter_count):
    column = jnp.arange(filter_count)
    widths = jnp.ones((filter_count,), jnp.int32)
    for exponent in range(6):
        widths = widths + (column >= filter_count * 2**exponent // 64).astype(jnp.int32)
    return widths


def sort_words(char_ids, lengths, groups):
    words, chars = char_ids.shape
    index = jnp.arange(words)
    longer = lengths[None, :] > lengths[:, None]
    tie = (lengths[None, :] == lengths[:, None]) & (index[None, :] < index[:, None])
    rank = jnp.sum((longer | tie).astype(jnp.int32), axis=1)
    perm = (rank[None, :] == index[:, None]).astype(BF16)
    live = jnp.arange(chars)[None, :] < lengths[:, None]
    shifted = jnp.where(live, char_ids + 1, 0)
    packed = jnp.concatenate(
        [shifted >> 4, shifted & 15, lengths[:, None]], axis=1
    ).astype(BF16)
    sorted_packed = dot(perm, packed).astype(jnp.int32)
    ids = (sorted_packed[:, :chars] << 4) + sorted_packed[:, chars : 2 * chars] - 1
    ids = jnp.pad(ids, ((0, 0), (0, GROUP * groups - chars)), constant_values=-1)
    sorted_lengths = sorted_packed[:, 2 * chars]
    tile_count = words // BLOCK_WORDS
    tile_max = jnp.max(sorted_lengths.reshape(tile_count, BLOCK_WORDS), axis=1)
    cum = jnp.cumsum(tile_max)
    total = cum[-1]
    block = jnp.arange(tile_count * chars + CHUNK_BLOCKS)
    tile = jnp.sum((block[:, None] >= cum[None, :]).astype(jnp.int32), axis=1)
    start = jnp.sum(
        jnp.where(tile[:, None] == jnp.arange(tile_count)[None, :], (cum - tile_max)[None, :], 0),
        axis=1,
    )
    valid = block < total
    position = jnp.where(valid, block - start, chars).astype(jnp.int32)
    tile = jnp.where(valid, tile, 0).astype(jnp.int32)
    chunks = (total + CHUNK_BLOCKS - 1) // CHUNK_BLOCKS
    reach = jnp.sum(
        (sorted_lengths[None, :] > GROUP * jnp.arange(groups - 1)[:, None]).astype(jnp.int32), axis=1
    )
    scalars = jnp.concatenate([chunks[None], (reach + ROW_TILE - 1) // ROW_TILE]).astype(jnp.int32)
    return perm, ids, sorted_lengths, scalars, tile, position


def build_windows(chunk, tile_ref, pos_ref, g_ref, len_ref, x_ref):
    lane = lax.broadcasted_iota(jnp.int32, (BLOCK_WORDS, LANES), 1)
    for b in range(CHUNK_BLOCKS):
        block = chunk * CHUNK_BLOCKS + b
        row = pl.multiple_of(tile_ref[block] * BLOCK_WORDS, BLOCK_WORDS)
        position = pos_ref[block]
        group = position >> 3
        offset = (position & 7) * CHAR_DIM
        shift = lax.rem(LANES - offset, LANES)
        here = pltpu.roll(g_ref[group, pl.ds(row, BLOCK_WORDS), :].astype(F32), shift, 1)
        after = pltpu.roll(g_ref[group + 1, pl.ds(row, BLOCK_WORDS), :].astype(F32), shift, 1)
        live = (len_ref[pl.ds(row, BLOCK_WORDS), :] > position).astype(F32)
        value = jnp.where(lane < LANES - offset, here, after)
        value = jnp.where(lane < BIAS_LANE, value, jnp.where(lane == BIAS_LANE, live, 0.0))
        x_ref[b * BLOCK_WORDS : (b + 1) * BLOCK_WORDS, :] = value.astype(BF16)


def conv_forward_kernel(
    scalar_ref, tile_ref, pos_ref, ids_ref, table_ref, w_ref, len_ref, pooled_ref, g_ref, x_ref, pre_ref
):
    groups = g_ref.shape[0]
    filters = w_ref.shape[1]
    part = pre_ref.shape[1]
    g_ref[...] = jnp.zeros_like(g_ref)
    pooled_ref[...] = jnp.zeros_like(pooled_ref)
    identity = lax.broadcasted_iota(jnp.int32, (ROW_TILE, TABLE_PAD), 1)
    for group in range(groups - 1):

        def embed(step, carry, group=group):
            row = pl.multiple_of(step * ROW_TILE, ROW_TILE)
            total = jnp.zeros((ROW_TILE, LANES), F32)
            for k in range(GROUP):
                column = group * GROUP + k
                hot = (ids_ref[pl.ds(row, ROW_TILE), column : column + 1] == identity).astype(F32)
                total = total + dot(hot.astype(BF16), table_ref[k])
            g_ref[group, pl.ds(row, ROW_TILE), :] = total.astype(BF16)
            return carry

        lax.fori_loop(0, scalar_ref[1 + group], embed, 0)

    def step(chunk, carry):
        build_windows(chunk, tile_ref, pos_ref, g_ref, len_ref, x_ref)
        for first in range(0, filters, part):
            half = dot(x_ref[...], w_ref[:, first : first + part])
            pre_ref[...] = half + half * jnp.tanh(half)
            for b in range(CHUNK_BLOCKS):
                row = pl.multiple_of(
                    tile_ref[chunk * CHUNK_BLOCKS + b] * BLOCK_WORDS, BLOCK_WORDS
                )
                pooled_ref[pl.ds(row, BLOCK_WORDS), first : first + part] += pre_ref[
                    b * BLOCK_WORDS : (b + 1) * BLOCK_WORDS, :
                ]
        return carry

    lax.fori_loop(0, scalar_ref[0], step, 0)
    pooled_ref[...] = pooled_ref[...] / len_ref[...].astype(F32)


def conv_forward(prep, table_blocks, half_matrix):
    _, ids, lengths, scalars, tile, position = prep
    words = ids.shape[0]
    groups = ids.shape[1] // GROUP
    filters = half_matrix.shape[1]
    return pl.pallas_call(
        conv_forward_kernel,
        out_shape=(
            jax.ShapeDtypeStruct((words, filters), F32),
            jax.ShapeDtypeStruct((groups, words, LANES), BF16),
        ),
        in_specs=[SMEM, SMEM, SMEM, VMEM, VMEM, VMEM, VMEM],
        out_specs=(VMEM, VMEM),
        scratch_shapes=[pltpu.VMEM((CHUNK, LANES), BF16), pltpu.VMEM((CHUNK, 512), F32)],
        compiler_params=pltpu.CompilerParams(vmem_limit_bytes=32 * MIB),
        name="conv_forward",
    )(scalars, tile, position, ids, table_blocks, half_matrix, lengths[:, None])


def conv_backward_kernel(
    scalar_ref, tile_ref, pos_ref, g_ref, w_ref, len_ref, gp_ref, gg_in_ref, dw_ref, gg_ref, x_ref, d_ref
):
    lane = lax.broadcasted_iota(jnp.int32, (BLOCK_WORDS, LANES), 1)
    dw_ref[...] = jnp.zeros_like(dw_ref)
    gg_ref[...] = gg_in_ref[...]

    def step(chunk, carry):
        build_windows(chunk, tile_ref, pos_ref, g_ref, len_ref, x_ref)
        half = dot(x_ref[...], w_ref[...])
        tanh = jnp.tanh(half)
        slope = (1.0 + tanh) * (1.0 + (half - half * tanh))
        for b in range(CHUNK_BLOCKS):
            rows = slice(b * BLOCK_WORDS, (b + 1) * BLOCK_WORDS)
            row = pl.multiple_of(tile_ref[chunk * CHUNK_BLOCKS + b] * BLOCK_WORDS, BLOCK_WORDS)
            d_ref[rows, :] = (gp_ref[pl.ds(row, BLOCK_WORDS), :] * slope[rows]).astype(BF16)
        dw_ref[...] += dot_tn(x_ref[...], d_ref[...])
        gx = dot_nt(d_ref[...], w_ref[...])
        for b in range(CHUNK_BLOCKS):
            block = chunk * CHUNK_BLOCKS + b
            row = pl.multiple_of(tile_ref[block] * BLOCK_WORDS, BLOCK_WORDS)
            position = pos_ref[block]
            group = position >> 3
            offset = (position & 7) * CHAR_DIM
            value = gx[b * BLOCK_WORDS : (b + 1) * BLOCK_WORDS, :]
            value = pltpu.roll(jnp.where(lane < BIAS_LANE, value, 0.0), offset, 1)
            gg_ref[group, pl.ds(row, BLOCK_WORDS), :] += jnp.where(lane >= offset, value, 0.0)
            gg_ref[group + 1, pl.ds(row, BLOCK_WORDS), :] += jnp.where(lane < offset, value, 0.0)
        return carry

    lax.fori_loop(0, scalar_ref[0], step, 0)


def conv_backward(prep, char_groups, half_matrix, grad_scaled, grad_groups, first, part):
    _, ids, lengths, scalars, tile, position = prep
    filters = half_matrix.shape[1]
    return pl.pallas_call(
        conv_backward_kernel,
        grid=(1,),
        out_shape=(
            jax.ShapeDtypeStruct((LANES, part), F32),
            jax.ShapeDtypeStruct(grad_groups.shape, F32),
        ),
        in_specs=[
            SMEM,
            SMEM,
            SMEM,
            VMEM,
            pl.BlockSpec((LANES, part), lambda i: (0, first // part)),
            VMEM,
            pl.BlockSpec((grad_scaled.shape[0], part), lambda i: (0, first // part)),
            VMEM,
        ],
        out_specs=(VMEM, VMEM),
        scratch_shapes=[pltpu.VMEM((CHUNK, LANES), BF16), pltpu.VMEM((CHUNK, part), BF16)],
        compiler_params=pltpu.CompilerParams(vmem_limit_bytes=32 * MIB),
        name="conv_backward",
    )(scalars, tile, position, char_groups, half_matrix, lengths[:, None], grad_scaled, grad_groups)


def table_kernel(scalar_ref, ids_ref, gg_ref, out_ref):
    groups = gg_ref.shape[0]
    out_ref[...] = jnp.zeros_like(out_ref)
    identity = lax.broadcasted_iota(jnp.int32, (TABLE_PAD, ROW_TILE), 0)
    for group in range(groups - 1):

        def step(index, carry, group=group):
            row = pl.multiple_of(index * ROW_TILE, ROW_TILE)
            grad = (2.0 * gg_ref[group, pl.ds(row, ROW_TILE), :]).astype(BF16)
            for k in range(GROUP):
                column = group * GROUP + k
                hot = (ids_ref[column : column + 1, pl.ds(row, ROW_TILE)] == identity).astype(F32)
                out_ref[k] += dot(hot.astype(BF16), grad)
            return carry

        lax.fori_loop(0, scalar_ref[1 + group], step, 0)


def table_gradient(prep, grad_groups, vocabulary):
    ids, scalars = prep[1], prep[3]
    total = pl.pallas_call(
        table_kernel,
        out_shape=jax.ShapeDtypeStruct((GROUP, TABLE_PAD, LANES), F32),
        in_specs=[SMEM, VMEM, VMEM],
        out_specs=VMEM,
        compiler_params=pltpu.CompilerParams(vmem_limit_bytes=32 * MIB),
        name="table_gradient",
    )(scalars, ids.T, grad_groups)
    parts = [total[k, :vocabulary, k * CHAR_DIM : (k + 1) * CHAR_DIM] for k in range(GROUP)]
    return sum(parts[1:], parts[0])


def table_lanes(table):
    padded = jnp.pad(table, ((0, TABLE_PAD - table.shape[0]), (0, 0)))
    return jnp.stack(
        [
            jnp.pad(padded, ((0, 0), (k * CHAR_DIM, LANES - (k + 1) * CHAR_DIM)))
            for k in range(GROUP)
        ]
    )


def piece_specs(pieces, steps_per_array=2):
    specs = []
    for half in pieces:
        for chunk in half:
            for number, array in enumerate(chunk):

                def index(j, *_, number=number):
                    return (0, jnp.clip(j - number * steps_per_array, 0, steps_per_array - 1), 0, 0)

                specs.append(pl.BlockSpec((2, 1) + array.shape[2:], index))
    return specs


def flat_pieces(pieces):
    return [array for half in pieces for chunk in half for array in chunk]


def highway_forward_kernel(layout, place_ref, select_ref, core_ref, h_ref, bias_ref, *refs):
    halves, chunks, arrays, rows = layout
    pieces = refs[: halves * chunks * arrays]
    next_ref, transform_ref, gating_ref, low_ref = refs[halves * chunks * arrays :]
    step = pl.program_id(0)
    width = next_ref.shape[1]

    @pl.when(step == 0)
    def _():
        low_ref[...] = h_ref[...].astype(BF16)

    block = place_ref[step]
    blocks = bias_ref.shape[0] // 2
    first = select_ref[step]
    own = core_ref[0]
    for array in range(arrays):

        @pl.when(step // 2 == array)
        def _(array=array):
            transform = jnp.broadcast_to(bias_ref[block], transform_ref.shape)
            gate = jnp.broadcast_to(bias_ref[block + blocks], transform_ref.shape)
            for half in range(halves):
                for chunk in range(chunks):
                    ref = pieces[(half * chunks + chunk) * arrays + array]
                    start = (own if half == 0 else 1 - own) * (chunks * rows) + chunk * rows
                    left = low_ref[:, pl.ds(pl.multiple_of(start, rows), rows)]
                    transform = transform + dot(left, ref[first, 0])
                    gate = gate + dot(left, ref[1 - first, 0])
            gating = 1.0 / (1.0 + jnp.exp(-gate))
            activated = transform / (1.0 + jnp.exp(-transform))
            h = h_ref[:, pl.ds(pl.multiple_of(block * width, width), width)]
            transform_ref[...] = transform
            gating_ref[...] = gating
            next_ref[...] = gating * h + (1.0 - gating) * activated


def highway_forward(h, pieces, bias_blocks, place, select, core):
    words, features = h.shape
    width = bias_blocks.shape[2]
    flat = flat_pieces(pieces)
    layout = (len(pieces), len(pieces[0]), len(pieces[0][0]), flat[0].shape[2])
    column = pl.BlockSpec((words, width), lambda j, place, *_: (0, place[j]))
    whole = lambda shape: pl.BlockSpec(shape, lambda j, *_: (0,) * len(shape))
    return pl.pallas_call(
        partial(highway_forward_kernel, layout),
        grid_spec=pltpu.PrefetchScalarGridSpec(
            num_scalar_prefetch=3,
            grid=(features // width,),
            in_specs=[whole(h.shape), whole(bias_blocks.shape)] + piece_specs(pieces),
            out_specs=[column, column, column, whole(h.shape)],
        ),
        out_shape=(
            jax.ShapeDtypeStruct(h.shape, F32),
            jax.ShapeDtypeStruct(h.shape, F32),
            jax.ShapeDtypeStruct(h.shape, F32),
            jax.ShapeDtypeStruct(h.shape, BF16),
        ),
        compiler_params=pltpu.CompilerParams(vmem_limit_bytes=56 * MIB),
        name="highway_forward",
    )(place, select, core, h, bias_blocks, *flat)


def highway_backward_kernel(layout, place_ref, select_ref, core_ref, grad_ref, h_ref, t_ref, g_ref, *refs):
    halves, chunks, arrays, rows = layout
    pieces = refs[: halves * chunks * arrays]
    mixed_ref, sums_ref, out_ref = refs[halves * chunks * arrays :]
    step = pl.program_id(0)
    width = grad_ref.shape[1]

    @pl.when(step == 0)
    def _():
        out_ref[...] = jnp.zeros_like(out_ref)

    own = core_ref[0]
    block = place_ref[step]
    first = select_ref[step]
    grad = grad_ref[...]
    transform = t_ref[...]
    gating = g_ref[...]
    sigmoid = 1.0 / (1.0 + jnp.exp(-transform))
    activated = transform * sigmoid
    low_t = (grad * (1.0 - gating) * (sigmoid + activated * (1.0 - sigmoid))).astype(BF16)
    low_g = (grad * (h_ref[...] - activated) * gating * (1.0 - gating)).astype(BF16)
    mixed_ref[0] = low_t
    mixed_ref[1] = low_g
    sums_ref[0] = jnp.sum(low_t.astype(F32), axis=0, keepdims=True)
    sums_ref[1] = jnp.sum(low_g.astype(F32), axis=0, keepdims=True)
    for array in range(arrays):

        @pl.when(step // 2 == array)
        def _(array=array):
            for half in range(halves):
                for chunk in range(chunks):
                    ref = pieces[(half * chunks + chunk) * arrays + array]
                    start = (own if half == 0 else 1 - own) * (chunks * rows) + chunk * rows
                    columns = pl.ds(pl.multiple_of(start, rows), rows)
                    out_ref[:, columns] += dot_nt(low_t, ref[first, 0]) + dot_nt(
                        low_g, ref[1 - first, 0]
                    )

    out_ref[:, pl.ds(pl.multiple_of(block * width, width), width)] += grad * gating


def highway_backward(grad, h, transform, gating, pieces, place, select, core):
    words, features = h.shape
    flat = flat_pieces(pieces)
    width = flat[0].shape[3]
    layout = (len(pieces), len(pieces[0]), len(pieces[0][0]), flat[0].shape[2])
    column = pl.BlockSpec((words, width), lambda j, place, *_: (0, place[j]))
    return pl.pallas_call(
        partial(highway_backward_kernel, layout),
        grid_spec=pltpu.PrefetchScalarGridSpec(
            num_scalar_prefetch=3,
            grid=(features // width,),
            in_specs=[column] * 4 + piece_specs(pieces),
            out_specs=[
                pl.BlockSpec((2, words, width), lambda j, place, *_: (0, 0, place[j])),
                pl.BlockSpec((2, 1, width), lambda j, place, *_: (0, 0, place[j])),
                pl.BlockSpec(h.shape, lambda j, *_: (0, 0)),
            ],
        ),
        out_shape=(
            jax.ShapeDtypeStruct((2, words, features), BF16),
            jax.ShapeDtypeStruct((2, 1, features), F32),
            jax.ShapeDtypeStruct(h.shape, F32),
        ),
        compiler_params=pltpu.CompilerParams(vmem_limit_bytes=56 * MIB),
        name="highway_backward",
    )(place, select, core, grad, h, transform, gating, *flat)


def weight_kernel(which_ref, left_ref, right_ref, out_ref):
    value = dot(left_ref[...], right_ref[0]).astype(BF16)
    width = out_ref.shape[2]
    out_ref[0] = value[:, :width]
    out_ref[1] = value[:, width:]


def highway_weight_gradient(which, turned, mixed, first, rows, width):
    words, features = mixed.shape[1:]
    return pl.pallas_call(
        weight_kernel,
        grid_spec=pltpu.PrefetchScalarGridSpec(
            num_scalar_prefetch=1,
            grid=(features // (2 * width),),
            in_specs=[
                pl.BlockSpec((rows, words), lambda j, which: (first // rows, 0)),
                pl.BlockSpec((1, words, 2 * width), lambda j, which: (which[0], 0, j)),
            ],
            out_specs=pl.BlockSpec((2, rows, width), lambda j, which: (j, 0, 0)),
        ),
        out_shape=jax.ShapeDtypeStruct((features // width, rows, width), BF16),
        compiler_params=pltpu.CompilerParams(vmem_limit_bytes=32 * MIB),
        name="highway_weight",
    )(which, turned, mixed)


def turn_kernel(value_ref, out_ref):
    out_ref[...] = value_ref[...].T.astype(BF16)


def turn(value):
    rows, columns = value.shape
    return pl.pallas_call(
        turn_kernel,
        grid=(columns // 256,),
        in_specs=[pl.BlockSpec((rows, 256), lambda j: (0, j))],
        out_specs=pl.BlockSpec((256, rows), lambda j: (j, 0)),
        out_shape=jax.ShapeDtypeStruct((columns, rows), BF16),
        compiler_params=pltpu.CompilerParams(vmem_limit_bytes=32 * MIB),
        name="turn",
    )(value)


def place_rows_kernel(splits, place_ref, core_ref, *refs):
    arrays = (len(refs) - len(splits) - 1) // 2
    own_refs, other_refs = refs[:arrays], refs[arrays : 2 * arrays]
    out_refs, whole_ref = refs[2 * arrays : -1], refs[-1]
    step = pl.program_id(0)
    half_rows = own_refs[0].shape[1]
    core = core_ref[0]
    for array in range(arrays):

        @pl.when(step // 4 == array)
        def _(array=array):
            align = lambda start: pl.ds(pl.multiple_of(start, 16), half_rows)
            whole_ref[align(core * half_rows), :] = own_refs[array][0]
            whole_ref[align((1 - core) * half_rows), :] = other_refs[array][0]

    start = 0
    for rows, out_ref in zip(splits, out_refs):
        out_ref[...] = whole_ref[start : start + rows, :]
        start += rows


def place_rows(own, other, place, core, splits):
    half_rows, columns = own[0].shape[1:]

    def index(number):
        return lambda j, *_: (jnp.clip(j - 4 * number, 0, 3), 0, 0)

    specs = [pl.BlockSpec((1, half_rows, columns), index(number)) for number in range(len(own))]
    return pl.pallas_call(
        partial(place_rows_kernel, splits),
        grid_spec=pltpu.PrefetchScalarGridSpec(
            num_scalar_prefetch=2,
            grid=(4 * len(own),),
            in_specs=specs + specs,
            out_specs=[
                pl.BlockSpec((rows, columns), lambda j, place, *_: (place[j], 0)) for rows in splits
            ],
            scratch_shapes=[pltpu.VMEM((2 * half_rows, columns), BF16)],
        ),
        out_shape=[
            jax.ShapeDtypeStruct((4 * len(own) * rows, columns), BF16) for rows in splits
        ],
        compiler_params=pltpu.CompilerParams(vmem_limit_bytes=32 * MIB),
        name="place_rows",
    )(place, core, *own, *other)


X_PAIRS = [(w, w ^ 1) for w in range(16)]
Y_PAIRS = [(w, w ^ 2) for w in range(16)]
Z_RING = [(w, (w + 4) % 16) for w in range(16)]
CORES = [(0, 1), (1, 0)]


def swap_cores(value):
    return lax.ppermute(value, "narrow", CORES)


def along(value, pairs):
    return lax.ppermute(value, "wide", pairs)


def ring_gather(value):
    received = [value]
    for _ in range(3):
        received.append(along(received[-1], Z_RING))
    return received


def gather_ring_first(value, order):
    own = jnp.stack(ring_gather(value))
    if order == "zxy":
        over_x = along(own, X_PAIRS)
        return [own, over_x, along(own, Y_PAIRS), along(over_x, Y_PAIRS)]
    over_y = along(own, Y_PAIRS)
    return [own, along(own, X_PAIRS), over_y, along(over_y, X_PAIRS)]


def gather_ring_last(value):
    over_x = along(value, X_PAIRS)
    return ring_gather(
        jnp.stack([value, over_x, along(value, Y_PAIRS), along(over_x, Y_PAIRS)])
    )


def total_of(terms):
    return sum((term.astype(F32) for term in terms[1:]), terms[0].astype(F32))


def pick(terms, index, axis):
    return [lax.dynamic_index_in_dim(term, index, axis, keepdims=False) for term in terms]


def halve(terms, coordinate, axis, pairs):
    sent = total_of(pick(terms, 1 - coordinate, axis)).astype(BF16)
    return pick(terms, coordinate, axis) + [along(sent, pairs)]


def ring_reduce(terms, z):
    running = []
    for distance in (3, 2, 1):
        sent = total_of(pick(terms, (z + distance) % 4, 0) + running).astype(BF16)
        running = [along(sent, Z_RING)]
    return pick(terms, z, 0) + running


def scatter_sum(keep, send, coords, order):
    z, y, x = coords
    shape = (4, 2, 2) + keep.shape[1:]
    terms = [keep.reshape(shape), swap_cores(send).reshape(shape)]
    if order == "zyx":
        terms = ring_reduce(terms, z)
        terms = halve(terms, y, 0, Y_PAIRS)
        terms = halve(terms, x, 0, X_PAIRS)
    elif order == "yxz":
        terms = halve(terms, y, 1, Y_PAIRS)
        terms = halve(terms, x, 1, X_PAIRS)
        terms = ring_reduce(terms, z)
    else:
        terms = halve(terms, x, 2, X_PAIRS)
        terms = halve(terms, y, 1, Y_PAIRS)
        terms = ring_reduce(terms, z)
    return total_of(terms)


def scatter_vectors(parts, devices):
    packed = [
        jnp.moveaxis(part.reshape(part.shape[:-1] + (devices, -1)), -2, 0).reshape(devices, -1)
        for part in parts
    ]
    total = lax.psum_scatter(
        jnp.concatenate(packed, axis=1), ("narrow", "wide"), scatter_dimension=0, tiled=True
    )[0]
    results, start = [], 0
    for part in parts:
        shape = part.shape[:-1] + (part.shape[-1] // devices,)
        size = part.size // devices
        results.append(total[start : start + size].reshape(shape))
        start += size
    return results


def gather_vectors(parts, wide):
    packed = jnp.concatenate(parts)
    packed = jnp.pad(packed, (0, -packed.shape[0] % 1024))
    whole = lax.all_gather(packed, "wide", axis=0, tiled=False)
    results, start = [], 0
    for part in parts:
        results.append(whole[:, start : start + part.shape[0]].reshape(-1))
        start += part.shape[0]
    return results


class Exchange:
    def __init__(self):
        self.core = lax.axis_index("narrow")
        index = lax.axis_index("wide")
        self.z, self.y, self.x = index // 4, (index // 2) % 2, index % 2

    def half(self, value, rows, offset=0):
        start = self.core * (value.shape[0] // 2) + offset
        return lax.dynamic_slice_in_dim(value, start, rows, 0)

    def highway_pieces(self, weight, chunks):
        rows = weight.shape[0] // (2 * chunks)
        own, other = [], []
        for chunk in range(chunks):
            block = self.half(weight, rows, chunk * rows)
            arrays = gather_ring_first(block, "zxy" if chunk % 2 == 0 else "zyx")
            arrays = [array.reshape((2, 2) + block.shape) for array in arrays]
            own.append(arrays)
            other.append([swap_cores(array) for array in arrays])
        return own, other

    def rows(self, values, order):
        value = jnp.concatenate(values, axis=0)
        splits = [value.shape[0] for value in values]
        half = self.half(value, value.shape[0] // 2)
        arrays = gather_ring_last(half) if order == "xyz" else gather_ring_first(half, order)
        others = [swap_cores(array) for array in arrays]
        step = jnp.arange(16)
        near, slot = (step % 4, step // 4) if order == "xyz" else (step // 4, step % 4)
        place = (
            (self.z - slot) % 4 * 4 + (self.y ^ (near >> 1)) * 2 + (self.x ^ (near & 1))
        ).astype(jnp.int32)
        return place_rows(arrays, others, place, self.core[None].astype(jnp.int32), splits)

    def turned_pos(self, value):
        return value.T.reshape(-1, 768)

    def sum_columns(self, keep, send, order):
        return scatter_sum(keep, send, (self.z, self.y, self.x), order)

    def sum_rows(self, grads, order):
        columns = grads[0].shape[1]
        blocks = [grad.astype(BF16).reshape(2, 16, -1, columns) for grad in grads]
        packed = jnp.concatenate(blocks, axis=2)
        keep = lax.dynamic_index_in_dim(packed, self.core, 0, keepdims=False)
        send = lax.dynamic_index_in_dim(packed, 1 - self.core, 0, keepdims=False)
        total = scatter_sum(keep, send, (self.z, self.y, self.x), order)
        results, start = [], 0
        for block in blocks:
            results.append(total[start : start + block.shape[2]])
            start += block.shape[2]
        return results


class PlainExchange:
    def __init__(self):
        self.core = self.z = self.y = self.x = jnp.zeros((), jnp.int32)

    def highway_pieces(self, weight, chunks):
        whole = lax.all_gather(weight, "wide", axis=1, tiled=True)
        rows = whole.shape[0] // (2 * chunks)
        width = whole.shape[1] // 16
        halves = []
        for half in range(2):
            pieces = []
            for chunk in range(chunks):
                start = (half * chunks + chunk) * rows
                arrays = []
                for near in range(4):
                    slots = []
                    for slot in range(4):
                        block = (-slot % 4) * 4 + near
                        slots.append(
                            whole[start : start + rows, block * width : (block + 1) * width]
                        )
                    arrays.append(jnp.stack(slots).reshape(2, 2, rows, width))
                pieces.append(arrays)
            halves.append(pieces)
        return halves

    def rows(self, values, order):
        return [lax.all_gather(value, "wide", axis=0, tiled=True) for value in values]

    def turned_pos(self, value):
        return value.T

    def sum_columns(self, keep, send, order):
        whole = jnp.concatenate([keep, send], axis=0)
        rows = whole.shape[1]
        whole = jnp.moveaxis(whole, 1, 0).reshape(rows, -1)
        return lax.psum_scatter(
            whole, ("narrow", "wide"), scatter_dimension=1, tiled=True
        ).astype(F32)

    def sum_rows(self, grads, order):
        return [
            lax.psum_scatter(
                grad.astype(BF16), ("narrow", "wide"), scatter_dimension=0, tiled=True
            ).astype(F32)
            for grad in grads
        ]


def norm_rows(value, norm_gain, norm_shift):
    center = jnp.mean(value, axis=-1, keepdims=True)
    offsets = value - center
    spread = jnp.mean(offsets * offsets, axis=-1, keepdims=True)
    return offsets * lax.rsqrt(spread + EPSILON) * norm_gain + norm_shift


def norm_back(value, norm_gain, grad_rows):
    center = jnp.mean(value, axis=-1, keepdims=True)
    offsets = value - center
    spread = jnp.mean(offsets * offsets, axis=-1, keepdims=True)
    scale = lax.rsqrt(spread + EPSILON)
    normal = offsets * scale
    inner = grad_rows * norm_gain
    grad = scale * (
        inner
        - jnp.mean(inner, axis=-1, keepdims=True)
        - normal * jnp.mean(inner * normal, axis=-1, keepdims=True)
    )
    return grad, jnp.sum(grad_rows * normal, axis=0), jnp.sum(grad_rows, axis=0)


def softmax_parts(query, key):
    scores = dot_nt(query, key) * HEAD_DIM ** (-0.5)
    exponent = jnp.exp(scores - jnp.max(scores, axis=-1, keepdims=True))
    return exponent, 1.0 / jnp.sum(exponent, axis=-1, keepdims=True)


def attend_kernel(query_ref, key_ref, value_ref, out_ref):
    for start in range(0, LANES, HEAD_DIM):
        head = slice(start, start + HEAD_DIM)
        exponent, scale = softmax_parts(query_ref[:, head], key_ref[:, head])
        attention = (exponent * scale).astype(BF16)
        out_ref[:, head] = dot(attention, value_ref[:, head]).astype(BF16)


def third(number, words, thirds):
    return pl.BlockSpec((words, LANES), lambda j: (0, number * thirds + j))


def attend(qkv):
    words = qkv.shape[0]
    pairs = qkv.shape[1] // (3 * LANES)
    return pl.pallas_call(
        attend_kernel,
        grid=(pairs,),
        in_specs=[third(number, words, pairs) for number in range(3)],
        out_specs=third(0, words, pairs),
        out_shape=jax.ShapeDtypeStruct((words, pairs * LANES), BF16),
        compiler_params=pltpu.CompilerParams(vmem_limit_bytes=32 * MIB),
        name="attend",
    )(qkv, qkv, qkv)


def attend_back_kernel(
    query_ref, key_ref, value_ref, grad_ref, grad_query_ref, grad_key_ref, grad_value_ref
):
    scaling = HEAD_DIM ** (-0.5)
    for start in range(0, LANES, HEAD_DIM):
        head = slice(start, start + HEAD_DIM)
        query, key = query_ref[:, head], key_ref[:, head]
        grad = grad_ref[:, head]
        exponent, scale = softmax_parts(query, key)
        attention = exponent * scale
        grad_attention = dot_nt(grad, value_ref[:, head])
        inner = jnp.sum(grad_attention * attention, axis=-1, keepdims=True)
        grad_scores = (attention * (grad_attention - inner)).astype(BF16)
        grad_value_ref[:, head] = dot_tn(attention.astype(BF16), grad).astype(BF16)
        grad_query_ref[:, head] = (dot(grad_scores, key) * scaling).astype(BF16)
        grad_key_ref[:, head] = (dot_tn(grad_scores, query) * scaling).astype(BF16)


def attend_back(qkv, grad_context):
    words = qkv.shape[0]
    pairs = qkv.shape[1] // (3 * LANES)
    out = third(0, words, pairs)
    return jnp.concatenate(
        pl.pallas_call(
            attend_back_kernel,
            grid=(pairs,),
            in_specs=[third(number, words, pairs) for number in range(3)] + [out],
            out_specs=(out, out, out),
            out_shape=(jax.ShapeDtypeStruct(grad_context.shape, BF16),) * 3,
            compiler_params=pltpu.CompilerParams(vmem_limit_bytes=32 * MIB),
            name="attend_back",
        )(qkv, qkv, qkv, grad_context),
        axis=1,
    )


def body(
    permutes,
    wide,
    devices,
    char_ids,
    word_lengths,
    type_ids,
    cotangent,
    character_embedding_table,
    conv_weight,
    conv_bias,
    high_weight,
    high_bias,
    proj_weight,
    proj_bias,
    pos_table,
    type_table,
    embed_gain,
    embed_shift,
    qkv_weight,
    attn_bias,
    out_weight,
    out_bias,
    attn_gain,
    attn_shift,
    up_weight,
    up_bias,
    down_weight,
    down_bias,
    ffn_gain,
    ffn_shift,
):
    net = Exchange() if permutes else PlainExchange()
    layers = high_weight.shape[0]
    words, chars = char_ids.shape[1:]
    lengths = word_lengths[0]
    row_chunks = 2

    vectors = gather_vectors(
        [high_bias[layer] for layer in range(layers)]
        + [
            attn_bias,
            type_table[0],
            type_table[1],
            proj_bias,
            embed_gain,
            embed_shift,
            out_bias,
            attn_gain,
            attn_shift,
            up_bias,
            down_bias,
            ffn_gain,
            ffn_shift,
        ],
        wide,
    )
    high_bias_all, attn_bias_all = vectors[:layers], vectors[layers]
    (
        type_zero,
        type_one,
        proj_bias_all,
        gain_zero,
        shift_zero,
        out_bias_all,
        gain_one,
        shift_one,
        up_bias_all,
        down_bias_all,
        gain_two,
        shift_two,
    ) = (value.astype(F32) for value in vectors[layers + 1 :])
    conv_rows = conv_weight.shape[0]
    conv_blocks = lax.all_gather(
        jnp.pad(
            jnp.concatenate([conv_weight, conv_bias[None]], axis=0),
            ((0, LANES - conv_rows - 1), (0, 0)),
        ),
        "wide",
        axis=0,
        tiled=False,
    )
    conv_all = jnp.concatenate([conv_blocks[w] for w in range(wide)], axis=1)
    pieces = [net.highway_pieces(high_weight[layer], row_chunks) for layer in range(layers)]
    turned_pos = net.turned_pos(pos_table)
    proj_all, pos_all = net.rows([proj_weight, turned_pos], "zxy")
    qkv_all, out_all = net.rows([qkv_weight.T, out_weight], "zyx")
    up_all, down_all = net.rows([up_weight.T, down_weight], "xyz")
    model_width = proj_all.shape[1]
    pos_rows = pos_all.reshape(model_width, words).T.astype(F32)

    filters = conv_all.shape[1]
    row = jnp.arange(LANES)[:, None]
    usable = row // CHAR_DIM < filter_widths(filters)[None, :]
    half_matrix = jnp.where(usable | (row >= conv_rows), conv_all * BF16(0.5), BF16(0.0))
    prep = sort_words(char_ids[0], lengths, chars // GROUP + 2)
    perm, sorted_lengths = prep[0], prep[2]
    pooled, char_groups = conv_forward(prep, table_lanes(character_embedding_table), half_matrix)
    features = pooled.shape[1]
    width = 2 * features // 16
    step = jnp.arange(8)
    near, low_slot = step // 2, step % 2
    slot_z = (net.z - low_slot) % 4
    place = ((slot_z & 1) * 4 + (net.y ^ (near >> 1)) * 2 + (net.x ^ (near & 1))).astype(jnp.int32)
    select = (slot_z // 2).astype(jnp.int32)
    core = net.core[None].astype(jnp.int32)
    bias_blocks = [bias.astype(F32).reshape(16, 1, width) for bias in high_bias_all]
    states, lows, transforms, gatings = [pooled], [], [], []
    for layer in range(layers):
        after, transform, gating, low = highway_forward(
            states[-1], pieces[layer], bias_blocks[layer], place, select, core
        )
        states.append(after)
        lows.append(low)
        transforms.append(transform)
        gatings.append(gating)
    turned = [turn(low) for low in lows]
    last = dot_tn(perm, states[-1].astype(BF16)).astype(BF16)
    word_vec = dot(last, proj_all) + proj_bias_all
    type_rows = jnp.where(type_ids[0][:, None] == 1, type_one[None], type_zero[None])
    summed = word_vec + pos_rows + type_rows
    embedded = norm_rows(summed, gain_zero, shift_zero)
    low_embedded = embedded.astype(BF16)

    bias_three = jnp.concatenate(
        [
            attn_bias_all[:model_width],
            jnp.zeros((model_width,), BF16),
            attn_bias_all[model_width:],
        ]
    ).astype(F32)
    qkv = (dot_nt(low_embedded, qkv_all) + bias_three).astype(BF16)
    context = attend(qkv)
    first_in = embedded + (dot(context, out_all) + out_bias_all)
    first = norm_rows(first_in, gain_one, shift_one)
    low_first = first.astype(BF16)
    inner = dot_nt(low_first, up_all) + up_bias_all
    activation = jax.nn.gelu(inner, approximate=False).astype(BF16)
    second_in = first + (dot(activation, down_all) + down_bias_all)
    hidden_out = norm_rows(second_in, gain_two, shift_two).astype(BF16)

    grad_second, grad_ffn_gain, grad_ffn_shift = norm_back(
        second_in, gain_two, cotangent[0].astype(F32)
    )
    grad_ffn = grad_second.astype(BF16)
    grad_down = dot_tn(activation, grad_ffn)
    grad_down_bias = column_sum(grad_ffn)
    _, gelu_pull = jax.vjp(partial(jax.nn.gelu, approximate=False), inner)
    grad_inner = gelu_pull(dot_nt(grad_ffn, down_all))[0].astype(BF16)
    grad_up = dot_tn(grad_inner, low_first)
    grad_up_bias = column_sum(grad_inner)
    sum_up, sum_down = net.sum_rows([grad_up, grad_down], "zyx")
    grad_resid, grad_attn_gain, grad_attn_shift = norm_back(
        first_in, gain_one, grad_second + dot(grad_inner, up_all)
    )
    grad_branch = grad_resid.astype(BF16)
    grad_out = dot_tn(context, grad_branch)
    grad_out_bias = column_sum(grad_branch)
    grad_context = dot_nt(grad_branch, out_all).astype(BF16)
    grad_qkv = attend_back(qkv, grad_context)
    grad_qkv_weight = dot_tn(grad_qkv, low_embedded)
    sum_qkv, sum_out = net.sum_rows([grad_qkv_weight, grad_out], "xyz")
    qkv_sums = column_sum(grad_qkv)
    grad_attn_bias = jnp.concatenate([qkv_sums[:model_width], qkv_sums[2 * model_width :]])

    grad_summed, grad_embed_gain, grad_embed_shift = norm_back(
        summed, gain_zero, grad_resid + dot(grad_qkv, qkv_all)
    )
    type_hot = (type_ids[0] == 1).astype(F32)[:, None]
    grad_type = jnp.stack(
        [jnp.sum((1.0 - type_hot) * grad_summed, axis=0), jnp.sum(type_hot * grad_summed, axis=0)]
    )
    grad_word = grad_summed.astype(BF16)
    grad_proj = dot_tn(last, grad_word)
    grad_proj_bias = column_sum(grad_word)
    (sum_proj,) = net.sum_rows([grad_proj], "yxz")
    (sum_pos,) = net.sum_rows([turn(grad_summed)], "zyx")
    sum_pos = sum_pos.T
    vector_sums = scatter_vectors(
        [
            grad_proj_bias,
            grad_type,
            grad_embed_gain,
            grad_embed_shift,
            grad_attn_bias,
            grad_out_bias,
            grad_attn_gain,
            grad_attn_shift,
            grad_up_bias,
            grad_down_bias,
            grad_ffn_gain,
            grad_ffn_shift,
        ],
        devices,
    )
    (
        sum_proj_bias,
        sum_type,
        sum_embed_gain,
        sum_embed_shift,
        sum_attn_bias,
        sum_out_bias,
        sum_attn_gain,
        sum_attn_shift,
        sum_up_bias,
        sum_down_bias,
        sum_ffn_gain,
        sum_ffn_shift,
    ) = vector_sums

    running = dot_nt(dot(perm, grad_word).astype(BF16), proj_all)
    chunk_rows = features // 4
    keep_half = core
    send_half = 1 - core
    high_sums, bias_sums = [None] * layers, [None] * layers
    for layer in reversed(range(layers)):
        mixed, sums, running = highway_backward(
            running,
            states[layer],
            transforms[layer],
            gatings[layer],
            pieces[layer],
            place,
            select,
            core,
        )
        bias_sums[layer] = sums.reshape(-1)
        parts = []
        for chunk in range(4):
            send, keep = (
                highway_weight_gradient(
                    which, turned[layer], mixed, chunk * chunk_rows, chunk_rows, width // 2
                )
                for which in (send_half, keep_half)
            )
            parts.append(net.sum_columns(keep, send, "yxz" if chunk % 2 == 0 else "xyz"))
        high_sums[layer] = jnp.concatenate(parts, axis=0)
    sum_high = jnp.stack(high_sums)

    grad_scaled = running * (0.5 / sorted_lengths.astype(F32))[:, None]
    grad_groups = jnp.zeros(char_groups.shape, F32)
    matrix_parts = []
    filter_part = 512
    for start in range(0, features, filter_part):
        part, grad_groups = conv_backward(
            prep, char_groups, half_matrix, grad_scaled, grad_groups, start, filter_part
        )
        matrix_parts.append(part)
    grad_matrix = jnp.concatenate(matrix_parts, axis=1)
    grad_table = table_gradient(prep, grad_groups, character_embedding_table.shape[0])
    sum_conv, sum_conv_bias, sum_high_bias = scatter_vectors(
        [
            jnp.where(usable, grad_matrix, 0.0)[:conv_rows],
            grad_matrix[conv_rows],
            jnp.stack(bias_sums),
        ],
        devices,
    )
    sum_table = lax.psum(grad_table, ("narrow", "wide"))
    return (
        hidden_out[None],
        sum_table,
        sum_conv,
        sum_conv_bias,
        sum_high,
        sum_high_bias,
        sum_proj,
        sum_proj_bias,
        sum_pos,
        sum_type,
        sum_embed_gain,
        sum_embed_shift,
        sum_qkv.T,
        sum_attn_bias,
        sum_out,
        sum_out_bias,
        sum_attn_gain,
        sum_attn_shift,
        sum_up.T,
        sum_up_bias,
        sum_down,
        sum_down_bias,
        sum_ffn_gain,
        sum_ffn_shift,
    )


def solution(mesh):
    narrow, wide = mesh.shape["narrow"], mesh.shape["wide"]
    both = ("narrow", "wide")
    placed = (
        P(both, None, None),
        P(both, None),
        P(both, None),
        P(both, None, None),
        P(),
        P(None, "wide"),
        P("wide"),
        P(None, None, "wide"),
        P(None, "wide"),
        P("wide", None),
        P("wide"),
        P(None, "wide"),
        P(None, "wide"),
        P("wide"),
        P("wide"),
        P(None, "wide"),
        P("wide"),
        P("wide", None),
        P("wide"),
        P("wide"),
        P("wide"),
        P(None, "wide"),
        P("wide"),
        P("wide", None),
        P("wide"),
        P("wide"),
        P("wide"),
    )
    return jax.shard_map(
        partial(body, (narrow, wide) == (2, 16), wide, narrow * wide),
        mesh=mesh,
        in_specs=placed,
        out_specs=(
            P(both, None, None),
            P(),
            P(None, both),
            P(both),
            P(None, None, both),
            P(None, both),
            P(both, None),
            P(both),
            P(None, both),
            P(None, both),
            P(both),
            P(both),
            P(None, both),
            P(both),
            P(both, None),
            P(both),
            P(both),
            P(both),
            P(None, both),
            P(both),
            P(both, None),
            P(both),
            P(both),
            P(both),
        ),
        check_vma=False,
    )
```

```python
from functools import partial

import jax
import jax.numpy as jnp
from jax import lax
from jax.experimental import pallas as pl
from jax.experimental.pallas import tpu as pltpu
from jax.sharding import PartitionSpec as P

HEADS = 12
HEAD_DIM = 64
CHAR_DIM = 16
TAPS = 7
EPSILON = 1e-12

LANES = 128
GROUP = LANES // CHAR_DIM
BLOCK_WORDS = 32
CHUNK_BLOCKS = 16
CHUNK = BLOCK_WORDS * CHUNK_BLOCKS
TABLE_PAD = 384
ROW_TILE = 128
BIAS_LANE = TAPS * CHAR_DIM

F32 = jnp.float32
BF16 = jnp.bfloat16
VMEM = pl.BlockSpec(memory_space=pltpu.VMEM)
SMEM = pl.BlockSpec(memory_space=pltpu.SMEM)
MIB = 1024 * 1024


def cost(microseconds):
    return pl.CostEstimate(
        flops=int(microseconds * 1.1e9), bytes_accessed=int(microseconds * 3e6), transcendentals=0
    )


def dot(left, right):
    return lax.dot_general(left, right, (((1,), (0,)), ((), ())), preferred_element_type=F32)


def dot_nt(left, right):
    return lax.dot_general(left, right, (((1,), (1,)), ((), ())), preferred_element_type=F32)


def dot_tn(left, right):
    return lax.dot_general(left, right, (((0,), (0,)), ((), ())), preferred_element_type=F32)


def column_sum(values):
    return jnp.sum(values.astype(F32), axis=0)


def filter_widths(filter_count):
    column = jnp.arange(filter_count)
    widths = jnp.ones((filter_count,), jnp.int32)
    for exponent in range(6):
        widths = widths + (column >= filter_count * 2**exponent // 64).astype(jnp.int32)
    return widths


def sort_words(char_ids, lengths, groups):
    words, chars = char_ids.shape
    index = jnp.arange(words)
    longer = lengths[None, :] > lengths[:, None]
    tie = (lengths[None, :] == lengths[:, None]) & (index[None, :] < index[:, None])
    rank = jnp.sum((longer | tie).astype(jnp.int32), axis=1)
    perm = (rank[None, :] == index[:, None]).astype(BF16)
    live = jnp.arange(chars)[None, :] < lengths[:, None]
    shifted = jnp.where(live, char_ids + 1, 0)
    packed = jnp.concatenate(
        [shifted >> 4, shifted & 15, lengths[:, None]], axis=1
    ).astype(BF16)
    sorted_packed = dot(perm, packed).astype(jnp.int32)
    ids = (sorted_packed[:, :chars] << 4) + sorted_packed[:, chars : 2 * chars] - 1
    ids = jnp.pad(ids, ((0, 0), (0, GROUP * groups - chars)), constant_values=-1)
    sorted_lengths = sorted_packed[:, 2 * chars]
    tile_count = words // BLOCK_WORDS
    tile_max = jnp.max(sorted_lengths.reshape(tile_count, BLOCK_WORDS), axis=1)
    cum = jnp.cumsum(tile_max)
    total = cum[-1]
    block = jnp.arange(tile_count * chars + CHUNK_BLOCKS)
    tile = jnp.sum((block[:, None] >= cum[None, :]).astype(jnp.int32), axis=1)
    start = jnp.sum(
        jnp.where(tile[:, None] == jnp.arange(tile_count)[None, :], (cum - tile_max)[None, :], 0),
        axis=1,
    )
    valid = block < total
    position = jnp.where(valid, block - start, chars).astype(jnp.int32)
    tile = jnp.where(valid, tile, 0).astype(jnp.int32)
    chunks = (total + CHUNK_BLOCKS - 1) // CHUNK_BLOCKS
    reach = jnp.sum(
        (sorted_lengths[None, :] > GROUP * jnp.arange(groups - 1)[:, None]).astype(jnp.int32), axis=1
    )
    scalars = jnp.concatenate([chunks[None], (reach + ROW_TILE - 1) // ROW_TILE]).astype(jnp.int32)
    return perm, ids, sorted_lengths, scalars, tile, position


def build_windows(chunk, tile_ref, pos_ref, g_ref, len_ref, x_ref):
    lane = lax.broadcasted_iota(jnp.int32, (BLOCK_WORDS, LANES), 1)
    for b in range(CHUNK_BLOCKS):
        block = chunk * CHUNK_BLOCKS + b
        row = pl.multiple_of(tile_ref[block] * BLOCK_WORDS, BLOCK_WORDS)
        position = pos_ref[block]
        group = position >> 3
        offset = (position & 7) * CHAR_DIM
        shift = lax.rem(LANES - offset, LANES)
        here = pltpu.roll(g_ref[group, pl.ds(row, BLOCK_WORDS), :].astype(F32), shift, 1)
        after = pltpu.roll(g_ref[group + 1, pl.ds(row, BLOCK_WORDS), :].astype(F32), shift, 1)
        live = (len_ref[pl.ds(row, BLOCK_WORDS), :] > position).astype(F32)
        value = jnp.where(lane < LANES - offset, here, after)
        value = jnp.where(lane < BIAS_LANE, value, jnp.where(lane == BIAS_LANE, live, 0.0))
        x_ref[b * BLOCK_WORDS : (b + 1) * BLOCK_WORDS, :] = value.astype(BF16)


def embed_kernel(scalar_ref, ids_ref, table_ref, g_ref):
    groups = g_ref.shape[0]
    g_ref[...] = jnp.zeros_like(g_ref)
    identity = lax.broadcasted_iota(jnp.int32, (ROW_TILE, TABLE_PAD), 1)
    for group in range(groups - 1):

        def embed(step, carry, group=group):
            row = pl.multiple_of(step * ROW_TILE, ROW_TILE)
            total = jnp.zeros((ROW_TILE, LANES), F32)
            for k in range(GROUP):
                column = group * GROUP + k
                hot = (ids_ref[pl.ds(row, ROW_TILE), column : column + 1] == identity).astype(F32)
                total = total + dot(hot.astype(BF16), table_ref[k])
            g_ref[group, pl.ds(row, ROW_TILE), :] = total.astype(BF16)
            return carry

        lax.fori_loop(0, scalar_ref[1 + group], embed, 0)


def embed_characters(prep, table_blocks):
    _, ids, _, scalars, _, _ = prep
    return pl.pallas_call(
        embed_kernel,
        out_shape=jax.ShapeDtypeStruct((ids.shape[1] // GROUP, ids.shape[0], LANES), BF16),
        in_specs=[SMEM, VMEM, VMEM],
        out_specs=VMEM,
        compiler_params=pltpu.CompilerParams(vmem_limit_bytes=32 * MIB),
        cost_estimate=cost(5),
        name="embed_characters",
    )(scalars, ids, table_blocks)


def conv_forward_kernel(
    scalar_ref, tile_ref, pos_ref, g_ref, w_ref, len_ref, kept_ref, pooled_ref, x_ref, pre_ref
):
    filters = w_ref.shape[1]
    part = pre_ref.shape[1]
    pooled_ref[...] = jnp.zeros_like(pooled_ref)

    def step(chunk, carry):
        build_windows(chunk, tile_ref, pos_ref, g_ref, len_ref, x_ref)
        for first in range(0, filters, part):
            half = dot(x_ref[...], w_ref[:, first : first + part])
            pre_ref[...] = half + half * jnp.tanh(half)
            for b in range(CHUNK_BLOCKS):
                row = pl.multiple_of(
                    tile_ref[chunk * CHUNK_BLOCKS + b] * BLOCK_WORDS, BLOCK_WORDS
                )
                pooled_ref[pl.ds(row, BLOCK_WORDS), first : first + part] += pre_ref[
                    b * BLOCK_WORDS : (b + 1) * BLOCK_WORDS, :
                ]
        return carry

    lax.fori_loop(0, scalar_ref[0], step, 0)
    pooled_ref[...] = pooled_ref[...] / len_ref[...].astype(F32)


def conv_forward(prep, char_groups, half_matrix, pooled, first, part):
    _, ids, lengths, scalars, tile, position = prep
    words = ids.shape[0]
    return pl.pallas_call(
        conv_forward_kernel,
        grid=(1,),
        out_shape=jax.ShapeDtypeStruct((words, half_matrix.shape[1]), F32),
        in_specs=[
            SMEM,
            SMEM,
            SMEM,
            VMEM,
            pl.BlockSpec((LANES, part), lambda i: (0, first // part)),
            VMEM,
            pl.BlockSpec(memory_space=pl.ANY),
        ],
        out_specs=pl.BlockSpec((words, part), lambda i: (0, first // part)),
        scratch_shapes=[pltpu.VMEM((CHUNK, LANES), BF16), pltpu.VMEM((CHUNK, 512), F32)],
        input_output_aliases={6: 0},
        compiler_params=pltpu.CompilerParams(vmem_limit_bytes=32 * MIB),
        cost_estimate=cost(8),
        name="conv_forward",
    )(scalars, tile, position, char_groups, half_matrix, lengths[:, None], pooled)


def conv_backward_kernel(
    scalar_ref, tile_ref, pos_ref, g_ref, w_ref, len_ref, gp_ref, out_ref, gg_ref, x_ref, d_ref, dw_ref
):
    filters = w_ref.shape[1]
    part = 512
    lane = lax.broadcasted_iota(jnp.int32, (BLOCK_WORDS, LANES), 1)
    dw_ref[...] = jnp.zeros_like(dw_ref)
    gg_ref[...] = jnp.zeros_like(gg_ref)

    def step(chunk, carry):
        build_windows(chunk, tile_ref, pos_ref, g_ref, len_ref, x_ref)
        for first in range(0, filters, part):
            columns = slice(first, first + part)
            half = dot(x_ref[...], w_ref[:, columns])
            tanh = jnp.tanh(half)
            slope = (1.0 + tanh) * (1.0 + (half - half * tanh))
            for b in range(CHUNK_BLOCKS):
                rows = slice(b * BLOCK_WORDS, (b + 1) * BLOCK_WORDS)
                row = pl.multiple_of(
                    tile_ref[chunk * CHUNK_BLOCKS + b] * BLOCK_WORDS, BLOCK_WORDS
                )
                d_ref[rows, columns] = (
                    gp_ref[pl.ds(row, BLOCK_WORDS), columns] * slope[rows]
                ).astype(BF16)
            dw_ref[:, columns] += dot_tn(x_ref[...], d_ref[:, columns])
        gx = dot_nt(d_ref[...], w_ref[...])
        for b in range(CHUNK_BLOCKS):
            block = chunk * CHUNK_BLOCKS + b
            row = pl.multiple_of(tile_ref[block] * BLOCK_WORDS, BLOCK_WORDS)
            position = pos_ref[block]
            group = position >> 3
            offset = (position & 7) * CHAR_DIM
            value = gx[b * BLOCK_WORDS : (b + 1) * BLOCK_WORDS, :]
            value = pltpu.roll(jnp.where(lane < BIAS_LANE, value, 0.0), offset, 1)
            gg_ref[group, pl.ds(row, BLOCK_WORDS), :] += jnp.where(lane >= offset, value, 0.0)
            gg_ref[group + 1, pl.ds(row, BLOCK_WORDS), :] += jnp.where(lane < offset, value, 0.0)
        return carry

    lax.fori_loop(0, scalar_ref[0], step, 0)
    out_ref[...] = dw_ref[...].T.astype(BF16)


def conv_backward(prep, char_groups, half_matrix, grad_scaled):
    _, ids, lengths, scalars, tile, position = prep
    filters = half_matrix.shape[1]
    return pl.pallas_call(
        conv_backward_kernel,
        out_shape=(
            jax.ShapeDtypeStruct((filters, LANES), BF16),
            jax.ShapeDtypeStruct(char_groups.shape, F32),
        ),
        in_specs=[SMEM, SMEM, SMEM, VMEM, VMEM, VMEM, VMEM],
        out_specs=(VMEM, VMEM),
        scratch_shapes=[
            pltpu.VMEM((CHUNK, LANES), BF16),
            pltpu.VMEM((CHUNK, filters), BF16),
            pltpu.VMEM((LANES, filters), F32),
        ],
        compiler_params=pltpu.CompilerParams(vmem_limit_bytes=48 * MIB),
        cost_estimate=cost(35),
        name="conv_backward",
    )(scalars, tile, position, char_groups, half_matrix, lengths[:, None], grad_scaled)


def table_kernel(scalar_ref, ids_ref, gg_ref, out_ref):
    groups = gg_ref.shape[0]
    out_ref[...] = jnp.zeros_like(out_ref)
    identity = lax.broadcasted_iota(jnp.int32, (TABLE_PAD, ROW_TILE), 0)
    for group in range(groups - 1):

        def step(index, carry, group=group):
            row = pl.multiple_of(index * ROW_TILE, ROW_TILE)
            grad = (2.0 * gg_ref[group, pl.ds(row, ROW_TILE), :]).astype(BF16)
            for k in range(GROUP):
                column = group * GROUP + k
                hot = (ids_ref[column : column + 1, pl.ds(row, ROW_TILE)] == identity).astype(F32)
                out_ref[k] += dot(hot.astype(BF16), grad)
            return carry

        lax.fori_loop(0, scalar_ref[1 + group], step, 0)


def table_gradient(prep, grad_groups, vocabulary):
    ids, scalars = prep[1], prep[3]
    total = pl.pallas_call(
        table_kernel,
        out_shape=jax.ShapeDtypeStruct((GROUP, TABLE_PAD, LANES), F32),
        in_specs=[SMEM, VMEM, VMEM],
        out_specs=VMEM,
        compiler_params=pltpu.CompilerParams(vmem_limit_bytes=32 * MIB),
        cost_estimate=cost(4),
        name="table_gradient",
    )(scalars, ids.T, grad_groups)
    parts = [total[k, :vocabulary, k * CHAR_DIM : (k + 1) * CHAR_DIM] for k in range(GROUP)]
    return sum(parts[1:], parts[0])


def table_lanes(table):
    padded = jnp.pad(table, ((0, TABLE_PAD - table.shape[0]), (0, 0)))
    return jnp.stack(
        [
            jnp.pad(padded, ((0, 0), (k * CHAR_DIM, LANES - (k + 1) * CHAR_DIM)))
            for k in range(GROUP)
        ]
    )


ANY = pl.BlockSpec(memory_space=pl.ANY)


def flat_pieces(pieces):
    return [array for half in pieces for chunk in half for array in chunk]


def piece_copies(layout, array, slot, first, own, pieces, whole_ref, sems, buffer):
    halves, chunks, arrays, rows = layout
    width = whole_ref.shape[2] // 2
    copies = []
    for half in range(halves):
        for chunk in range(chunks):
            ref = pieces[(half * chunks + chunk) * arrays + array]
            start = (own if half == 0 else 1 - own) * (chunks * rows) + chunk * rows
            start = pl.multiple_of(start, rows)
            for side in range(2):
                copies.append(
                    pltpu.make_async_copy(
                        ref.at[first if side == 0 else 1 - first, slot],
                        whole_ref.at[
                            buffer, pl.ds(start, rows), side * width : (side + 1) * width
                        ],
                        sems.at[buffer, len(copies)],
                    )
                )
    return copies


def fetch_pieces(layout, select_ref, own, pieces, whole_ref, sems):
    step = pl.program_id(0)

    def start(index):
        for array in range(layout[2]):

            @pl.when(index // 2 == array)
            def _(array=array):
                for copy in piece_copies(
                    layout, array, index % 2, select_ref[index], own, pieces, whole_ref, sems, index % 2
                ):
                    copy.start()

    @pl.when(step == 0)
    def _():
        start(0)

    @pl.when(step + 1 < pl.num_programs(0))
    def _():
        start(step + 1)

    buffer = step % 2
    for copy in piece_copies(layout, 0, 0, 0, own, pieces, whole_ref, sems, buffer):
        copy.wait()
    return buffer


def half_tanh(value):
    return 0.5 + 0.5 * jnp.tanh(0.5 * value)


def highway_forward_kernel(layout, place_ref, select_ref, core_ref, h_ref, bias_ref, *refs):
    count = layout[0] * layout[1] * layout[2]
    pieces = refs[:count]
    next_ref, transform_ref, gating_ref, low_ref, whole_ref, sems = refs[count:]
    step = pl.program_id(0)
    width = next_ref.shape[1]

    @pl.when(step == 0)
    def _():
        low_ref[...] = h_ref[...].astype(BF16)

    block = place_ref[step]
    blocks = bias_ref.shape[0] // 2
    buffer = fetch_pieces(layout, select_ref, core_ref[0], pieces, whole_ref, sems)
    mixed = dot(low_ref[...], whole_ref[buffer])
    transform = mixed[:, :width] + bias_ref[block]
    gating = half_tanh(mixed[:, width:] + bias_ref[block + blocks])
    h = h_ref[:, pl.ds(pl.multiple_of(block * width, width), width)]
    activated = transform * half_tanh(transform)
    transform_ref[...] = transform
    gating_ref[...] = gating
    next_ref[...] = activated + gating * (h - activated)


def highway_forward(h, pieces, bias_blocks, place, select, core):
    words, features = h.shape
    width = bias_blocks.shape[2]
    flat = flat_pieces(pieces)
    layout = (len(pieces), len(pieces[0]), len(pieces[0][0]), flat[0].shape[2])
    column = pl.BlockSpec((words, width), lambda j, place, *_: (0, place[j]))
    whole = lambda shape: pl.BlockSpec(shape, lambda j, *_: (0,) * len(shape))
    return pl.pallas_call(
        partial(highway_forward_kernel, layout),
        grid_spec=pltpu.PrefetchScalarGridSpec(
            num_scalar_prefetch=3,
            grid=(features // width,),
            in_specs=[whole(h.shape), whole(bias_blocks.shape)] + [ANY] * len(flat),
            out_specs=[column, column, column, whole(h.shape)],
            scratch_shapes=[
                pltpu.VMEM((2, features, 2 * width), BF16),
                pltpu.SemaphoreType.DMA((2, 2 * layout[0] * layout[1])),
            ],
        ),
        out_shape=(
            jax.ShapeDtypeStruct(h.shape, F32),
            jax.ShapeDtypeStruct(h.shape, F32),
            jax.ShapeDtypeStruct(h.shape, F32),
            jax.ShapeDtypeStruct(h.shape, BF16),
        ),
        compiler_params=pltpu.CompilerParams(vmem_limit_bytes=56 * MIB),
        cost_estimate=cost(19),
        name="highway_forward",
    )(place, select, core, h, bias_blocks, *flat)


def highway_backward_kernel(layout, place_ref, select_ref, core_ref, grad_ref, h_ref, t_ref, g_ref, *refs):
    count = layout[0] * layout[1] * layout[2]
    pieces = refs[:count]
    mixed_ref, sums_ref, out_ref, whole_ref, sems = refs[count:]
    step = pl.program_id(0)
    width = grad_ref.shape[1]
    features = out_ref.shape[1]

    @pl.when(step == 0)
    def _():
        out_ref[...] = jnp.zeros_like(out_ref)

    block = place_ref[step]
    buffer = fetch_pieces(layout, select_ref, core_ref[0], pieces, whole_ref, sems)
    grad = grad_ref[...]
    transform = t_ref[...]
    gating = g_ref[...]
    sigmoid = half_tanh(transform)
    activated = transform * sigmoid
    rest = grad * (1.0 - gating)
    low_t = (rest * (sigmoid + activated * (1.0 - sigmoid))).astype(BF16)
    low_g = (rest * gating * (h_ref[...] - activated)).astype(BF16)
    mixed_ref[0] = low_t
    mixed_ref[1] = low_g
    sums_ref[0] = jnp.sum(low_t.astype(F32), axis=0, keepdims=True)
    sums_ref[1] = jnp.sum(low_g.astype(F32), axis=0, keepdims=True)
    low = jnp.concatenate([low_t, low_g], axis=1)
    for start in range(0, features, 512):
        out_ref[:, start : start + 512] += dot_nt(
            low, whole_ref[buffer, start : start + 512, :]
        )
    out_ref[:, pl.ds(pl.multiple_of(block * width, width), width)] += grad * gating


def highway_backward(grad, h, transform, gating, pieces, place, select, core):
    words, features = h.shape
    flat = flat_pieces(pieces)
    width = flat[0].shape[3]
    layout = (len(pieces), len(pieces[0]), len(pieces[0][0]), flat[0].shape[2])
    column = pl.BlockSpec((words, width), lambda j, place, *_: (0, place[j]))
    return pl.pallas_call(
        partial(highway_backward_kernel, layout),
        grid_spec=pltpu.PrefetchScalarGridSpec(
            num_scalar_prefetch=3,
            grid=(features // width,),
            in_specs=[column] * 4 + [ANY] * len(flat),
            out_specs=[
                pl.BlockSpec((2, words, width), lambda j, place, *_: (0, 0, place[j])),
                pl.BlockSpec((2, 1, width), lambda j, place, *_: (0, 0, place[j])),
                pl.BlockSpec(h.shape, lambda j, *_: (0, 0)),
            ],
            scratch_shapes=[
                pltpu.VMEM((2, features, 2 * width), BF16),
                pltpu.SemaphoreType.DMA((2, 2 * layout[0] * layout[1])),
            ],
        ),
        out_shape=(
            jax.ShapeDtypeStruct((2, words, features), BF16),
            jax.ShapeDtypeStruct((2, 1, features), F32),
            jax.ShapeDtypeStruct(h.shape, F32),
        ),
        compiler_params=pltpu.CompilerParams(vmem_limit_bytes=56 * MIB),
        cost_estimate=cost(21),
        name="highway_backward",
    )(place, select, core, grad, h, transform, gating, *flat)


def weight_kernel(which_ref, left_ref, right_ref, *refs):
    out_ref = refs[-1]
    value = dot(left_ref[...], right_ref[0])
    width = out_ref.shape[2]
    for number in range(out_ref.shape[0]):
        block = value[:, number * width : (number + 1) * width]
        if len(refs) == 2:
            block = block + refs[0][number].astype(F32)
        out_ref[number] = block.astype(BF16)


def highway_weight_gradient(which, turned, mixed, first, rows, width, added=None, part=0):
    words, features = mixed.shape[1:]
    blocks = 8
    out = pl.BlockSpec((blocks, rows, width), lambda j, which: (j, 0, 0))
    return pl.pallas_call(
        weight_kernel,
        grid_spec=pltpu.PrefetchScalarGridSpec(
            num_scalar_prefetch=1,
            grid=(features // (blocks * width),),
            in_specs=[
                pl.BlockSpec((rows, words), lambda j, which: (first // rows, 0)),
                pl.BlockSpec((1, words, blocks * width), lambda j, which: (which[0], 0, j)),
            ]
            + (
                []
                if added is None
                else [pl.BlockSpec((blocks, rows, width), lambda j, which: (j, part, 0))]
            ),
            out_specs=out,
        ),
        out_shape=jax.ShapeDtypeStruct((features // width, rows, width), BF16),
        compiler_params=pltpu.CompilerParams(vmem_limit_bytes=32 * MIB),
        cost_estimate=cost(3),
        name="highway_weight",
    )(which, turned, mixed, *([] if added is None else [added]))


def turn_kernel(value_ref, out_ref):
    out_ref[...] = value_ref[...].T.astype(BF16)


def turn(value):
    rows, columns = value.shape
    return pl.pallas_call(
        turn_kernel,
        grid=(columns // 256,),
        in_specs=[pl.BlockSpec((rows, 256), lambda j: (0, j))],
        out_specs=pl.BlockSpec((256, rows), lambda j: (j, 0)),
        out_shape=jax.ShapeDtypeStruct((columns, rows), BF16),
        compiler_params=pltpu.CompilerParams(vmem_limit_bytes=32 * MIB),
        cost_estimate=cost(1),
        name="turn",
    )(value)


def place_rows_kernel(splits, place_ref, core_ref, *refs):
    arrays = (len(refs) - len(splits) - 1) // 2
    own_refs, other_refs = refs[:arrays], refs[arrays : 2 * arrays]
    out_refs, whole_ref = refs[2 * arrays : -1], refs[-1]
    step = pl.program_id(0)
    half_rows = own_refs[0].shape[1]
    core = core_ref[0]
    for array in range(arrays):

        @pl.when(step // 4 == array)
        def _(array=array):
            align = lambda start: pl.ds(pl.multiple_of(start, 16), half_rows)
            whole_ref[align(core * half_rows), :] = own_refs[array][0]
            whole_ref[align((1 - core) * half_rows), :] = other_refs[array][0]

    start = 0
    for rows, out_ref in zip(splits, out_refs):
        out_ref[...] = whole_ref[start : start + rows, :]
        start += rows


def place_rows(own, other, place, core, splits):
    half_rows, columns = own[0].shape[1:]

    def index(number):
        return lambda j, *_: (jnp.clip(j - 4 * number, 0, 3), 0, 0)

    specs = [pl.BlockSpec((1, half_rows, columns), index(number)) for number in range(len(own))]
    return pl.pallas_call(
        partial(place_rows_kernel, splits),
        grid_spec=pltpu.PrefetchScalarGridSpec(
            num_scalar_prefetch=2,
            grid=(4 * len(own),),
            in_specs=specs + specs,
            out_specs=[
                pl.BlockSpec((rows, columns), lambda j, place, *_: (place[j], 0)) for rows in splits
            ],
            scratch_shapes=[pltpu.VMEM((2 * half_rows, columns), BF16)],
        ),
        out_shape=[
            jax.ShapeDtypeStruct((4 * len(own) * rows, columns), BF16) for rows in splits
        ],
        compiler_params=pltpu.CompilerParams(vmem_limit_bytes=32 * MIB),
        cost_estimate=cost(7),
        name="place_rows",
    )(place, core, *own, *other)


def place_small_kernel(place_ref, *refs):
    inputs, (conv_ref, *row_refs) = refs[:4], refs[4:]
    step = pl.program_id(0)
    for number, ref in enumerate(inputs):

        @pl.when(step // 4 == number)
        def _(ref=ref):
            start = conv_ref.shape[0]
            conv_ref[...] = ref[0, :start, :]
            for row_ref in row_refs:
                row_ref[0] = ref[0, start : start + row_ref.shape[1], :]
                start += row_ref.shape[1]


def place_small(arrays, place, conv_rows, splits):
    rows, columns = arrays[0].shape[1:]

    def index(number):
        return lambda j, *_: (jnp.clip(j - 4 * number, 0, 3), 0, 0)

    return pl.pallas_call(
        place_small_kernel,
        grid_spec=pltpu.PrefetchScalarGridSpec(
            num_scalar_prefetch=1,
            grid=(16,),
            in_specs=[pl.BlockSpec((1, rows, columns), index(number)) for number in range(4)],
            out_specs=[pl.BlockSpec((conv_rows, columns), lambda j, place: (0, place[j]))]
            + [
                pl.BlockSpec((1, count, columns), lambda j, place: (place[j], 0, 0))
                for count in splits
            ],
        ),
        out_shape=[jax.ShapeDtypeStruct((conv_rows, 16 * columns), BF16)]
        + [jax.ShapeDtypeStruct((16, count, columns), BF16) for count in splits],
        compiler_params=pltpu.CompilerParams(vmem_limit_bytes=32 * MIB),
        cost_estimate=cost(2),
        name="place_small",
    )(place, *arrays)


LINKS = {
    "x": [(w, w ^ 1) for w in range(16)],
    "y": [(w, w ^ 2) for w in range(16)],
    "z": [(w, (w + 4) % 16) for w in range(16)],
    "z1": [(w, w ^ 4) for w in range(16)],
    "z2": [(w, w ^ 8) for w in range(16)],
}
CORES = [(0, 1), (1, 0)]


def send(value, link):
    if link == "c":
        return lax.ppermute(value, "narrow", CORES)
    return lax.ppermute(value, "wide", LINKS[link])


def total_of(terms):
    return sum((term.astype(F32) for term in terms[1:]), terms[0].astype(F32))


class Exchange:
    windows = True

    def __init__(self):
        self.core = lax.axis_index("narrow")
        index = lax.axis_index("wide")
        self.z, self.y, self.x = index // 4, (index // 2) % 2, index % 2
        self.state, self.fresh, self.count, self.planned = {}, [], 0, []

    def put(self, key, value):
        self.state[key] = value
        self.fresh.append(key)

    def move(self, key, source, link):
        self.put(key, send(self.state[source], link))

    def plan(self, key, value, link, shape=None):
        self.planned.append((key, value, link, shape))

    def plan_move(self, source, *links):
        for link in links:
            self.plan(source + link, self.state[source], link)

    def plan_ring(self, name, step):
        self.plan(f"{name}r{step}", self.state[f"{name}r{step - 1}" if step > 1 else name], "z")

    def plan_swap(self, *names):
        for name in names:
            self.plan(name + "c", self.state[name], "c")

    def launch(self, values):
        leaves, tree = jax.tree.flatten(values)
        held = lax.optimization_barrier(
            tuple(value for _, value, _, _ in self.planned) + tuple(leaves)
        )
        for (key, _, link, shape), value in zip(self.planned, held):
            value = send(value, link)
            self.put(key, value if shape is None else value.reshape(shape))
        leaves = held[len(self.planned) :]
        self.planned = []
        return jax.tree.unflatten(tree, leaves)

    def window(self, values, hold=()):
        held_keys = [key for key in self.fresh if key in hold]
        self.fresh = [key for key in self.fresh if key not in hold]
        leaves, tree = jax.tree.flatten(values)
        held = lax.optimization_barrier(
            tuple(self.state[key] for key in self.fresh) + tuple(leaves)
        )
        for key, value in zip(self.fresh, held):
            self.state[key] = value
        leaves = held[len(self.fresh) :]
        self.fresh = held_keys
        return jax.tree.unflatten(tree, leaves)

    def swap_chain(self, *names):
        before = None
        for name in names:
            value = self.state[name]
            if before is not None:
                value, self.state[before] = lax.optimization_barrier((value, self.state[before]))
            before = name + "c"
            self.put(before, send(value, "c"))

    def stage(self, values=(), hold=()):
        return self.window(self.launch(values), hold)


    def load(self, name, value, rows=None, offset=0, whole=False):
        if not whole:
            rows = rows or value.shape[0] // 2
            value = lax.dynamic_slice_in_dim(
                value, self.core * (value.shape[0] // 2) + offset, rows, 0
            )
        self.state[name] = value

    def ring(self, name):
        received = [self.state[name]]
        for _ in range(3):
            received.append(send(received[-1], "z"))
        self.put(name + "o", jnp.stack(received))

    def ring_step(self, name, step):
        self.move(f"{name}r{step}", f"{name}r{step - 1}" if step > 1 else name, "z")

    def ring_done(self, name):
        self.state[name + "o"] = jnp.stack(
            [self.state[name]] + [self.state[f"{name}r{step}"] for step in (1, 2, 3)]
        )

    def square(self, name):
        value = self.state[name]
        over_x = send(value, "x")
        self.put(name + "o0", jnp.stack([value, over_x, send(value, "y"), send(over_x, "y")]))

    def turn_ring(self, name, step):
        self.move(f"{name}o{step}", f"{name}o{step - 1}", "z")

    def swap(self, *names):
        for name in names:
            self.move(name + "c", name, "c")

    def near(self, name, suffix=""):
        return [self.state[name + part + suffix] for part in ("o", "ox", "oy", "oxy")]

    def layer(self, name, chunks):
        halves = []
        for suffix in ("", "c"):
            halves.append(
                [
                    [
                        array.reshape((2, 2) + array.shape[1:])
                        for array in self.near(f"{name}{chunk}", suffix)
                    ]
                    for chunk in range(chunks)
                ]
            )
        return halves

    def place(self, ring_last):
        step = jnp.arange(16)
        near, slot = (step % 4, step // 4) if ring_last else (step // 4, step % 4)
        return (
            (self.z - slot) % 4 * 4 + (self.y ^ (near >> 1)) * 2 + (self.x ^ (near & 1))
        ).astype(jnp.int32)

    def rows(self, own, other, splits, ring_last):
        core = self.core[None].astype(jnp.int32)
        return place_rows(own, other, self.place(ring_last), core, splits)


    def split(self, grads):
        blocks = [grad.astype(BF16).reshape(2, 16, -1, grad.shape[1]) for grad in grads]
        return tuple(
            jnp.concatenate(
                [lax.dynamic_index_in_dim(block, which, 0, keepdims=False) for block in blocks],
                axis=1,
            )
            for which in (self.core, 1 - self.core)
        )


class Reduction:
    def __init__(self, net, keep, sent, order):
        shape = (4, 2, 2) + keep.shape[1:]
        self.net, self.order, self.done = net, list(order), 0
        net.count += 1
        self.name = f"sum{net.count}"
        self.terms = [keep.reshape(shape)]
        self.keys, self.running, self.axes = [], None, ["z", "y", "x"]
        self.sent, self.shape = sent, shape

    def all_terms(self):
        return self.terms + [self.net.state[key] for key in self.keys]

    def pick(self, terms, index, axis):
        return [lax.dynamic_index_in_dim(term, index, axis, keepdims=False) for term in terms]

    def keep_only(self, index, axis):
        self.terms = self.pick(self.all_terms(), index, axis)
        self.keys = []

    def step(self, put=None):
        net, link = self.net, self.order[self.done]
        put = put or (lambda key, value, link, shape=None: net.put(
            key, send(value, link) if shape is None else send(value, link).reshape(shape)
        ))
        self.key = key = f"{self.name}_{self.done}"
        self.done += 1
        if link == "c":
            put(key, self.sent, "c", self.shape)
            self.keys.append(key)
        elif link in ("x", "y"):
            axis = self.axes.index(link)
            index = net.x if link == "x" else net.y
            sent = total_of(self.pick(self.all_terms(), 1 - index, axis)).astype(BF16)
            self.keep_only(index, axis)
            self.axes.remove(link)
            put(key, sent, link)
            self.keys.append(key)
        else:
            axis = self.axes.index("z")
            index = (net.z + int(link)) % 4
            terms = self.pick(self.all_terms(), index, axis)
            if self.running is not None:
                terms.append(net.state[self.running])
            put(key, total_of(terms).astype(BF16), "z")
            self.running = key
            if link == "1":
                self.keep_only(net.z, axis)
                self.axes.remove("z")
                self.keys = [key]
        return self

    def result(self):
        assert self.done == len(self.order)
        return total_of(self.all_terms())


class Ring:
    def __init__(self, net, sums):
        self.net, self.sums, self.done, self.running = net, sums, 0, None
        net.count += 1
        self.name = f"ring{net.count}"

    def part(self, distance):
        index = (self.net.z + distance) % 4
        parts = [total_of(item.pick(item.all_terms(), index, 0)) for item in self.sums]
        value = parts[0] if len(parts) == 1 else jnp.concatenate(parts, axis=0)
        if self.running is not None:
            value = value + self.net.state[self.running].astype(F32)
        return value

    def step(self, put=None):
        value = self.part(3 - self.done).astype(BF16)
        self.done += 1
        self.key = key = f"{self.name}_{self.done}"
        if put:
            put(key, value, "z")
        else:
            self.net.put(key, send(value, "z"))
        self.running = key
        return self

    def result(self):
        assert self.done == 3
        return self.part(0)


class Small:
    def __init__(self, net, value):
        self.net, self.value, self.done, self.key = net, value, 0, None
        net.count += 1
        self.name = f"small{net.count}"

    def result(self):
        return self.value if self.key is None else self.value + self.net.state[self.key]

    def step(self, put):
        self.value = self.result()
        self.key = f"{self.name}_{self.done}"
        put(self.key, self.value, ("c", "x", "y", "z1", "z2")[self.done])
        self.done += 1
        return self


class PlainReduction:
    def __init__(self, grads, axis):
        self.grads, self.axis = grads, axis

    def step(self):
        return self

    def result(self):
        return [
            lax.psum_scatter(
                grad.astype(BF16), ("narrow", "wide"), scatter_dimension=self.axis, tiled=True
            ).astype(F32)
            for grad in self.grads
        ]


def norm_rows(value, norm_gain, norm_shift):
    center = jnp.mean(value, axis=-1, keepdims=True)
    offsets = value - center
    spread = jnp.mean(offsets * offsets, axis=-1, keepdims=True)
    return offsets * lax.rsqrt(spread + EPSILON) * norm_gain + norm_shift


def norm_back(value, norm_gain, grad_rows):
    center = jnp.mean(value, axis=-1, keepdims=True)
    offsets = value - center
    spread = jnp.mean(offsets * offsets, axis=-1, keepdims=True)
    scale = lax.rsqrt(spread + EPSILON)
    normal = offsets * scale
    inner = grad_rows * norm_gain
    grad = scale * (
        inner
        - jnp.mean(inner, axis=-1, keepdims=True)
        - normal * jnp.mean(inner * normal, axis=-1, keepdims=True)
    )
    return grad, jnp.sum(grad_rows * normal, axis=0), jnp.sum(grad_rows, axis=0)


def row_copies(slots, own, arrays, array, up_refs, down_refs, up_ref, down_ref, sems, buffer):
    rows = up_refs[0].shape[1]
    copies = []
    for refs, whole_ref in ((up_refs, up_ref), (down_refs, down_ref)):
        for half in range(2):
            ref = refs[half * arrays + array]
            for number, slot in enumerate(slots):
                start = pl.multiple_of((own if half == 0 else 1 - own) * rows, rows)
                copies.append(
                    pltpu.make_async_copy(
                        ref.at[slot],
                        whole_ref.at[buffer, pl.ds(number * 2 * rows + start, rows), :],
                        sems.at[buffer, len(copies)],
                    )
                )
    return copies


def fetch_rows(slot_ref, own, up_refs, down_refs, up_ref, down_ref, sems):
    arrays = len(up_refs) // 2
    step = pl.program_id(0)

    def start(index):
        for array in range(arrays):

            @pl.when(index // 2 == array)
            def _(array=array):
                slots = [slot_ref[index, number] for number in range(2)]
                for copy in row_copies(
                    slots, own, arrays, array, up_refs, down_refs, up_ref, down_ref, sems, index % 2
                ):
                    copy.start()

    @pl.when(step == 0)
    def _():
        start(0)

    @pl.when(step + 1 < pl.num_programs(0))
    def _():
        start(step + 1)

    buffer = step % 2
    for copy in row_copies(
        (0, 0), own, arrays, 0, up_refs, down_refs, up_ref, down_ref, sems, buffer
    ):
        copy.wait()
    return buffer


def normal_share(value, bell):
    t = 1.0 / (1.0 + (0.3275911 * 2**-0.5) * jnp.abs(value))
    series = 1.061405429
    for term in (-1.453152027, 1.421413741, -0.284496736, 0.254829592):
        series = series * t + term
    tail = (0.5 * series) * (t * bell)
    return jnp.where(value < 0.0, tail, 1.0 - tail)


def feed_forward_kernel(
    count, slot_ref, block_ref, core_ref, first_ref, bias_ref, vectors_ref, cotangent_ref, *refs
):
    up_refs, down_refs = refs[:count], refs[count : 2 * count]
    act_ref, slope_ref, hidden_ref, grad_ref, sums_ref, up_ref, down_ref, low_ref, total_ref, sems = refs[
        2 * count :
    ]
    step = pl.program_id(0)

    @pl.when(step == 0)
    def _():
        low_ref[...] = first_ref[...].astype(BF16)
        total_ref[...] = first_ref[...] + vectors_ref[0:1, :]

    buffer = fetch_rows(slot_ref, core_ref[0], up_refs, down_refs, up_ref, down_ref, sems)
    inner = dot_nt(low_ref[...], up_ref[buffer]) + bias_ref[block_ref[step]]
    bell = jnp.exp(-0.5 * inner * inner)
    share = normal_share(inner, bell)
    act = (inner * share).astype(BF16)
    act_ref[0] = act
    slope_ref[0] = (
        share + inner * (bell * (2.0 * jnp.pi) ** -0.5)
    ).astype(BF16)
    total_ref[...] += dot(act, down_ref[buffer])

    @pl.when(step == pl.num_programs(0) - 1)
    def _():
        value = total_ref[...]
        gain, shift = vectors_ref[1:2, :], vectors_ref[2:3, :]
        offsets = value - jnp.mean(value, axis=-1, keepdims=True)
        scale = lax.rsqrt(jnp.mean(offsets * offsets, axis=-1, keepdims=True) + EPSILON)
        normal = offsets * scale
        hidden_ref[...] = (normal * gain + shift).astype(BF16)
        cotangent = cotangent_ref[...].astype(F32)
        pulled = cotangent * gain
        grad = scale * (
            pulled
            - jnp.mean(pulled, axis=-1, keepdims=True)
            - normal * jnp.mean(pulled * normal, axis=-1, keepdims=True)
        )
        grad_ref[...] = grad
        sums_ref[0:1, :] = jnp.sum(cotangent * normal, axis=0, keepdims=True)
        sums_ref[1:2, :] = jnp.sum(cotangent, axis=0, keepdims=True)
        sums_ref[2:3, :] = jnp.sum(grad.astype(BF16).astype(F32), axis=0, keepdims=True)
        sums_ref[3:8, :] = jnp.zeros((5, sums_ref.shape[1]), F32)


def feed_forward(first, pieces, bias_blocks, vectors, cotangent, slots, block, core):
    words, columns = first.shape
    steps, width = bias_blocks.shape[0], bias_blocks.shape[2]
    up, down = pieces
    whole = lambda shape: pl.BlockSpec(shape, lambda j, *_: (0,) * len(shape))
    tile = pl.BlockSpec((1, words, width), lambda j, *_: (j, 0, 0))
    return pl.pallas_call(
        partial(feed_forward_kernel, len(up)),
        grid_spec=pltpu.PrefetchScalarGridSpec(
            num_scalar_prefetch=3,
            grid=(steps,),
            in_specs=[
                whole(first.shape),
                whole(bias_blocks.shape),
                whole(vectors.shape),
                whole(cotangent.shape),
            ]
            + [ANY] * (len(up) + len(down)),
            out_specs=[tile, tile, whole(first.shape), whole(first.shape), whole((8, columns))],
            scratch_shapes=[
                pltpu.VMEM((2, width, columns), BF16),
                pltpu.VMEM((2, width, columns), BF16),
                pltpu.VMEM((words, columns), BF16),
                pltpu.VMEM((words, columns), F32),
                pltpu.SemaphoreType.DMA((2, 8)),
            ],
        ),
        out_shape=(
            jax.ShapeDtypeStruct((steps, words, width), BF16),
            jax.ShapeDtypeStruct((steps, words, width), BF16),
            jax.ShapeDtypeStruct((words, columns), BF16),
            jax.ShapeDtypeStruct((words, columns), F32),
            jax.ShapeDtypeStruct((8, columns), F32),
        ),
        compiler_params=pltpu.CompilerParams(vmem_limit_bytes=48 * MIB),
        cost_estimate=cost(20),
        name="feed_forward",
    )(slots, block, core, first, bias_blocks, vectors, cotangent, *up, *down)


def feed_forward_back_kernel(
    count,
    slot_ref,
    block_ref,
    core_ref,
    grad_ref,
    first_ref,
    act_ref,
    slope_ref,
    value_ref,
    gain_ref,
    *refs,
):
    up_refs, down_refs = refs[:count], refs[count : 2 * count]
    (
        up_keep_ref,
        up_sent_ref,
        down_keep_ref,
        down_sent_ref,
        bias_ref,
        out_ref,
        sums_ref,
        up_ref,
        down_ref,
        low_ref,
        low_first_ref,
        total_ref,
        sems,
    ) = refs[2 * count :]
    step = pl.program_id(0)

    @pl.when(step == 0)
    def _():
        total_ref[...] = grad_ref[...]
        low_ref[...] = grad_ref[...].astype(BF16)
        low_first_ref[...] = first_ref[...].astype(BF16)

    buffer = fetch_rows(slot_ref, core_ref[0], up_refs, down_refs, up_ref, down_ref, sems)
    low = low_ref[...]
    inner = (dot_nt(low, down_ref[buffer]) * slope_ref[0].astype(F32)).astype(BF16)
    bias_ref[0] = jnp.sum(inner.astype(F32), axis=0, keepdims=True)
    grad_down = dot_tn(act_ref[0], low).astype(BF16)
    grad_up = dot_tn(inner, low_first_ref[...]).astype(BF16)
    total_ref[...] += dot(inner, up_ref[buffer])
    rows = up_keep_ref.shape[3]

    def store(value, ref):
        for number in range(4):
            ref[number // 2, 0, number % 2] = value[number * rows : (number + 1) * rows, :]

    @pl.when(step % 2 == 0)
    def _():
        store(grad_up, up_sent_ref)
        store(grad_down, down_sent_ref)

    @pl.when(step % 2 == 1)
    def _():
        store(grad_up, up_keep_ref)
        store(grad_down, down_keep_ref)

    @pl.when(step == pl.num_programs(0) - 1)
    def _():
        value = value_ref[...]
        pulling = total_ref[...]
        offsets = value - jnp.mean(value, axis=-1, keepdims=True)
        scale = lax.rsqrt(jnp.mean(offsets * offsets, axis=-1, keepdims=True) + EPSILON)
        normal = offsets * scale
        pulled = pulling * gain_ref[...]
        grad = scale * (
            pulled
            - jnp.mean(pulled, axis=-1, keepdims=True)
            - normal * jnp.mean(pulled * normal, axis=-1, keepdims=True)
        )
        out_ref[...] = grad
        sums_ref[0:1, :] = jnp.sum(pulling * normal, axis=0, keepdims=True)
        sums_ref[1:2, :] = jnp.sum(pulling, axis=0, keepdims=True)
        sums_ref[2:3, :] = jnp.sum(grad.astype(BF16).astype(F32), axis=0, keepdims=True)
        sums_ref[3:8, :] = jnp.zeros((5, sums_ref.shape[1]), F32)


def feed_forward_back(grad, first, act, slope, value, gain, pieces, slots, block, core):
    words, columns = first.shape
    steps, _, width = act.shape
    up, down = pieces
    rows = width // 4
    whole = lambda shape: pl.BlockSpec(shape, lambda j, *_: (0,) * len(shape))
    tile = pl.BlockSpec((1, words, width), lambda j, *_: (j, 0, 0))
    out = pl.BlockSpec(
        (2, 1, 2, rows, columns), lambda j, slots, block, core: (0, block[j] % (steps // 2), 0, 0, 0)
    )
    part = jax.ShapeDtypeStruct((2, steps // 2, 2, rows, columns), BF16)
    return pl.pallas_call(
        partial(feed_forward_back_kernel, len(up)),
        grid_spec=pltpu.PrefetchScalarGridSpec(
            num_scalar_prefetch=3,
            grid=(steps,),
            in_specs=[
                whole(grad.shape),
                whole(first.shape),
                tile,
                tile,
                whole(value.shape),
                whole(gain.shape),
            ]
            + [ANY] * (len(up) + len(down)),
            out_specs=[
                out,
                out,
                out,
                out,
                pl.BlockSpec((1, 1, width), lambda j, slots, block, core: (block[j], 0, 0)),
                whole(first.shape),
                whole((8, columns)),
            ],
            scratch_shapes=[
                pltpu.VMEM((2, width, columns), BF16),
                pltpu.VMEM((2, width, columns), BF16),
                pltpu.VMEM((words, columns), BF16),
                pltpu.VMEM((words, columns), BF16),
                pltpu.VMEM((words, columns), F32),
                pltpu.SemaphoreType.DMA((2, 8)),
            ],
        ),
        out_shape=(
            part,
            part,
            part,
            part,
            jax.ShapeDtypeStruct((steps, 1, width), F32),
            jax.ShapeDtypeStruct((words, columns), F32),
            jax.ShapeDtypeStruct((8, columns), F32),
        ),
        compiler_params=pltpu.CompilerParams(vmem_limit_bytes=48 * MIB),
        cost_estimate=cost(25),
        name="feed_forward_back",
    )(slots, block, core, grad, first, act, slope, value, gain, *up, *down)


def softmax_parts(query, key):
    scores = dot_nt(query, key)
    scaling = HEAD_DIM ** (-0.5) * 1.4426950408889634
    exponent = jnp.exp2((scores - jnp.max(scores, axis=-1, keepdims=True)) * scaling)
    return exponent, 1.0 / jnp.sum(exponent, axis=-1, keepdims=True)


def attend_kernel(query_ref, key_ref, value_ref, out_ref):
    for start in range(0, LANES, HEAD_DIM):
        head = slice(start, start + HEAD_DIM)
        exponent, scale = softmax_parts(query_ref[:, head], key_ref[:, head])
        attention = (exponent * scale).astype(BF16)
        out_ref[:, head] = dot(attention, value_ref[:, head]).astype(BF16)


def third(number, words, thirds):
    return pl.BlockSpec((words, LANES), lambda j: (0, number * thirds + j))


def attend(qkv):
    words = qkv.shape[0]
    pairs = qkv.shape[1] // (3 * LANES)
    return pl.pallas_call(
        attend_kernel,
        grid=(pairs,),
        in_specs=[third(number, words, pairs) for number in range(3)],
        out_specs=third(0, words, pairs),
        out_shape=jax.ShapeDtypeStruct((words, pairs * LANES), BF16),
        compiler_params=pltpu.CompilerParams(vmem_limit_bytes=32 * MIB),
        cost_estimate=cost(12),
        name="attend",
    )(qkv, qkv, qkv)


def attend_back_kernel(
    query_ref, key_ref, value_ref, grad_ref, grad_query_ref, grad_key_ref, grad_value_ref
):
    scaling = HEAD_DIM ** (-0.5)
    for start in range(0, LANES, HEAD_DIM):
        head = slice(start, start + HEAD_DIM)
        query, key = query_ref[:, head], key_ref[:, head]
        grad = grad_ref[:, head]
        exponent, scale = softmax_parts(query, key)
        attention = exponent * scale
        grad_attention = dot_nt(grad, value_ref[:, head])
        inner = jnp.sum(grad_attention * attention, axis=-1, keepdims=True)
        grad_scores = (attention * (grad_attention - inner)).astype(BF16)
        grad_value_ref[:, head] = dot_tn(attention.astype(BF16), grad).astype(BF16)
        grad_query_ref[:, head] = (dot(grad_scores, key) * scaling).astype(BF16)
        grad_key_ref[:, head] = (dot_tn(grad_scores, query) * scaling).astype(BF16)


def attend_back(qkv, grad_context):
    words = qkv.shape[0]
    pairs = qkv.shape[1] // (3 * LANES)
    out = third(0, words, pairs)
    return jnp.concatenate(
        pl.pallas_call(
            attend_back_kernel,
            grid=(pairs,),
            in_specs=[third(number, words, pairs) for number in range(3)] + [out],
            out_specs=(out, out, out),
            out_shape=(jax.ShapeDtypeStruct(grad_context.shape, BF16),) * 3,
            compiler_params=pltpu.CompilerParams(vmem_limit_bytes=32 * MIB),
            cost_estimate=cost(17),
        name="attend_back",
        )(qkv, qkv, qkv, grad_context),
        axis=1,
    )


def gather_plain(value, axis):
    return lax.all_gather(value, "wide", axis=axis, tiled=True)


def plain_pieces(weight, chunks):
    whole = gather_plain(weight, 1)
    rows = whole.shape[0] // (2 * chunks)
    width = whole.shape[1] // 16
    halves = []
    for half in range(2):
        pieces = []
        for chunk in range(chunks):
            start = (half * chunks + chunk) * rows
            arrays = []
            for near in range(4):
                slots = []
                for slot in range(4):
                    block = (-slot % 4) * 4 + near
                    slots.append(whole[start : start + rows, block * width : (block + 1) * width])
                arrays.append(jnp.stack(slots).reshape(2, 2, rows, width))
            pieces.append(arrays)
        halves.append(pieces)
    return halves


def vector_rows(vectors):
    rows, places, start = [], [], 0
    for vector in vectors:
        count = -(-vector.shape[0] // LANES)
        padded = jnp.pad(vector, (0, count * LANES - vector.shape[0]))
        rows.append(padded.reshape(count, LANES))
        places.append((start, count, vector.shape[0]))
        start += count
    return jnp.pad(jnp.concatenate(rows, axis=0), ((0, -start % 16), (0, 0))), places


def plain_rows(whole):
    rows = whole.shape[0] // 16
    arrays = []
    for half in range(2):
        for near in range(4):
            starts = [((-slot % 4) * 4 + near) * rows + half * rows // 2 for slot in range(4)]
            arrays.append(jnp.stack([whole[start : start + rows // 2] for start in starts]))
    return arrays


def body(
    permutes,
    wide,
    devices,
    char_ids,
    word_lengths,
    type_ids,
    cotangent,
    character_embedding_table,
    conv_weight,
    conv_bias,
    high_weight,
    high_bias,
    proj_weight,
    proj_bias,
    pos_table,
    type_table,
    embed_gain,
    embed_shift,
    qkv_weight,
    attn_bias,
    out_weight,
    out_bias,
    attn_gain,
    attn_shift,
    up_weight,
    up_bias,
    down_weight,
    down_bias,
    ffn_gain,
    ffn_shift,
):
    layers, features = high_weight.shape[:2]
    words, chars = char_ids.shape[1:]
    model_width = proj_weight.shape[1]
    conv_rows = conv_weight.shape[0]
    lengths = word_lengths[0]
    vectors = [high_bias[layer] for layer in range(layers)] + [
        attn_bias,
        type_table[0],
        type_table[1],
        proj_bias,
        embed_gain,
        embed_shift,
        out_bias,
        attn_gain,
        attn_shift,
        up_bias,
        down_bias,
        ffn_gain,
        ffn_shift,
    ]
    conv_block = jnp.pad(
        jnp.concatenate([conv_weight, conv_bias[None]], axis=0),
        ((0, LANES - conv_rows - 1), (0, 0)),
    )
    vector_block, places = vector_rows(vectors)

    if permutes:
        net = Exchange()
        window, launch = net.window, net.launch
        core_index, z, y, x = net.core, net.z, net.y, net.x
        net.load(
            "small",
            jnp.concatenate([conv_block, vector_block, pos_table.T.reshape(-1, LANES)], axis=0),
            whole=True,
        )
        chunk_rows = features // 4
        net.load("L00", high_weight[0], chunk_rows, 0)
        (
            net.state["L00"],
            net.state["small"],
            char_ids,
            lengths,
            high_weight,
            qkv_weight,
            up_weight,
        ) = lax.optimization_barrier(
            (
                net.state["L00"],
                net.state["small"],
                char_ids,
                lengths,
                high_weight,
                qkv_weight,
                up_weight,
            )
        )
        for layer, chunk in ((0, 1), (1, 0), (1, 1)):
            net.load(f"L{layer}{chunk}", high_weight[layer], chunk_rows, chunk * chunk_rows)
        encoder_splits = [
            qkv_weight.shape[1],
            out_weight.shape[0],
            proj_weight.shape[0],
        ]
        net.load(
            "e",
            jnp.concatenate(
                [qkv_weight.T, out_weight, proj_weight],
                axis=0,
            ),
        )
        net.load("up", up_weight.T)
        net.load("down", down_weight)
        net.ring_step("L00", 1)
        net.move("smallx", "small", "x")
        net.move("smally", "small", "y")
    else:
        window = lambda values, hold=(): values
        launch = window
        core_index = z = y = x = jnp.zeros((), jnp.int32)
    prep = sort_words(char_ids[0], lengths, chars // GROUP + 2)
    table_blocks = table_lanes(character_embedding_table)
    prep, table_blocks = window((prep, table_blocks))
    if permutes:
        net.ring_step("L00", 2)
        net.move("smallxy", "smallx", "y")
        net.move("ex", "e", "x")
        net.move("ey", "e", "y")
        window(())
        net.ring_step("L00", 3)
        net.put("smallo0", jnp.stack([net.state["small" + part] for part in ("", "x", "y", "xy")]))
        net.turn_ring("small", 1)
        net.move("exy", "ex", "y")
        window(())
        net.ring_done("L00")
        net.plan_move("L00o", "x", "y")
        net.plan_ring("L01", 1)
        net.plan("smallo2", net.state["smallo1"], "z")
        launch(())
        net.state["eo0"] = jnp.stack([net.state["e" + part] for part in ("", "x", "y", "xy")])
        net.ring_step("L01", 2)
        net.turn_ring("small", 3)
        net.ring_step("L01", 3)
        conv_all, whole_vectors, pos_all = place_small(
            [net.state[f"smallo{step}"] for step in range(4)],
            net.place(True),
            LANES,
            [vector_block.shape[0], pos_table.size // LANES],
        )
        conv_all, whole_vectors, pos_all = window((conv_all, whole_vectors, pos_all))
        net.ring_done("L01")
        net.plan_move("L01o", "x", "y")
        net.plan_ring("L10", 1)
        prep, table_blocks, conv_all, whole_vectors, pos_all = launch(
            (prep, table_blocks, conv_all, whole_vectors, pos_all)
        )
        net.ring_step("L10", 2)
        net.ring_step("L10", 3)
        net.swap_chain("L00o", "L00ox", "L00oy")
    else:
        conv_all = gather_plain(conv_block, 1)
        whole_vectors = lax.all_gather(vector_block, "wide", axis=0, tiled=False)
        pos_all = gather_plain(pos_table.T, 0)
    pos_rows = pos_all.reshape(model_width, words).T.astype(F32)
    whole = [
        whole_vectors[:, start : start + count].reshape(wide, -1)[:, :size].reshape(-1)
        for start, count, size in places
    ]
    filters = conv_all.shape[1]
    row = jnp.arange(LANES)[:, None]
    usable = row // CHAR_DIM < filter_widths(filters)[None, :]
    half_matrix = jnp.where(usable | (row >= conv_rows), conv_all * BF16(0.5), BF16(0.0))
    char_groups = embed_characters(prep, table_blocks)
    pooled = jnp.zeros((words, filters), F32)
    pooled = conv_forward(prep, char_groups, half_matrix, pooled, 0, filters // 2)
    pooled, char_groups, half_matrix, whole, pos_rows = window(
        (pooled, char_groups, half_matrix, whole, pos_rows)
    )
    high_bias_all, attn_bias_all = whole[:layers], whole[layers]
    (
        type_zero,
        type_one,
        proj_bias_all,
        gain_zero,
        shift_zero,
        out_bias_all,
        gain_one,
        shift_one,
        up_bias_all,
        down_bias_all,
        gain_two,
        shift_two,
    ) = (value.astype(F32) for value in whole[layers + 1 :])

    if permutes:
        net.ring_done("L10")
        net.plan("L00oxy", net.state["L00ox"], "y")
        net.plan("L01oxy", net.state["L01oy"], "x")
        net.plan("eo1", net.state["eo0"], "z")
        pooled = launch(pooled)
        net.swap_chain("L01o", "L01ox", "L01oy")
    pooled = conv_forward(prep, char_groups, half_matrix, pooled, filters // 2, filters // 2)
    if permutes:
        pooled = window(pooled)
        net.plan_move("L10o", "x", "y")
        net.plan_ring("L11", 1)
        launch(())
        net.ring_step("L11", 2)
        net.ring_step("L11", 3)
        net.swap_chain("L00oxy", "L01oxy", "eo0")
        pooled = window(pooled)
        net.ring_done("L11")
        net.plan_move("L11o", "x", "y")
        net.plan("eo2", net.state["eo1"], "z")
        pooled = launch(pooled)
        net.swap_chain("L10o", "L10ox", "L10oy")
        pieces = [net.layer("L0", 2)]
    else:
        pieces = [plain_pieces(high_weight[layer], 2) for layer in range(layers)]
    width = 2 * features // 16
    order = jnp.arange(8)
    near, low_slot = order // 2, order % 2
    slot_z = (z - low_slot) % 4
    place = ((slot_z & 1) * 4 + (y ^ (near >> 1)) * 2 + (x ^ (near & 1))).astype(jnp.int32)
    select = (slot_z // 2).astype(jnp.int32)
    core = core_index[None].astype(jnp.int32)
    bias_blocks = [bias.astype(F32).reshape(16, 1, width) for bias in high_bias_all]
    first_layer = highway_forward(pooled, pieces[0], bias_blocks[0], place, select, core)
    first_layer = window(first_layer)

    if permutes:
        net.plan("L10oxy", net.state["L10ox"], "y")
        net.plan("L11oxy", net.state["L11oy"], "x")
        net.plan("eo3", net.state["eo2"], "z")
        first_layer = launch(first_layer)
        net.swap_chain("L11o", "L11ox", "L11oy", "eo1", "eo2")
    turned = [turn(first_layer[3])]
    turned = window(turned)
    if permutes:
        net.plan_swap("L10oxy", "L11oxy", "eo3")
        net.plan_ring("up", 1)
        net.plan_ring("down", 1)
        first_layer = launch(first_layer)
        for step in (2, 3):
            net.ring_step("up", step)
            net.ring_step("down", step)
        pieces.append(net.layer("L1", 2))
        qkv_all, out_all, proj_all = net.rows(
            [net.state[f"eo{step}"] for step in range(4)],
            [net.state[f"eo{step}c"] for step in range(4)],
            encoder_splits,
            True,
        )
    else:
        qkv_all, out_all, proj_all = (
            gather_plain(value, 0) for value in (qkv_weight.T, out_weight, proj_weight)
        )
    second_layer = highway_forward(first_layer[0], pieces[1], bias_blocks[1], place, select, core)
    states = [pooled, first_layer[0], second_layer[0]]
    transforms = [first_layer[1], second_layer[1]]
    gatings = [first_layer[2], second_layer[2]]
    perm, sorted_lengths = prep[0], prep[2]
    last = dot_tn(perm, states[2].astype(BF16)).astype(BF16)
    word_vec = dot(last, proj_all) + proj_bias_all
    type_rows = jnp.where(type_ids[0][:, None] == 1, type_one[None], type_zero[None])
    summed = word_vec + pos_rows + type_rows
    embedded = norm_rows(summed, gain_zero, shift_zero)
    turned.append(turn(second_layer[3]))
    summed, embedded, last, turned = window((summed, embedded, last, turned))

    if permutes:
        net.ring_done("up")
        net.ring_done("down")
        net.plan_move("upo", "x", "y")
        net.plan_move("downo", "x", "y")
        embedded = launch(embedded)
        net.swap_chain("upo", "downo")
    low_embedded = embedded.astype(BF16)
    bias_three = jnp.concatenate(
        [
            attn_bias_all[:model_width],
            jnp.zeros((model_width,), BF16),
            attn_bias_all[model_width:],
        ]
    ).astype(F32)
    qkv = (dot_nt(low_embedded, qkv_all) + bias_three).astype(BF16)
    context = attend(qkv)
    if permutes:
        context = window(context)
        net.plan("upoxy", net.state["upox"], "y")
        net.plan("downoxy", net.state["downoy"], "x")
        context = launch(context)
        net.swap_chain("upox", "upoy", "downox", "downoy")
    first_in = embedded + (dot(context, out_all) + out_bias_all)
    first = norm_rows(first_in, gain_one, shift_one)
    if permutes:
        first_in, first = window((first_in, first))
        net.plan_swap("upoxy", "downoxy")
        first = launch(first)
        feed_pieces = [net.near(name) + net.near(name, "c") for name in ("up", "down")]
    else:
        feed_pieces = [
            plain_rows(gather_plain(value, 0)) for value in (up_weight.T, down_weight)
        ]
    half_of = jnp.where(order % 2 == 0, 1 - core_index, core_index)
    slots = (z - (2 * half_of[:, None] + jnp.arange(2)[None, :])) % 4
    slots = slots.astype(jnp.int32)
    feed_block = (half_of * 4 + (y ^ (near >> 1)) * 2 + (x ^ (near & 1))).astype(jnp.int32)
    feed_rows = up_bias_all.shape[0] // 16
    feed_bias = jnp.moveaxis(up_bias_all.reshape(2, 2, 4, feed_rows), 1, 2).reshape(8, 1, -1)
    act, slope, hidden_out, grad_second, last_sums = feed_forward(
        first,
        feed_pieces,
        feed_bias,
        jnp.stack([down_bias_all, gain_two, shift_two]),
        cotangent[0],
        slots,
        feed_block,
        core,
    )
    grad_ffn_gain, grad_ffn_shift, grad_down_bias = last_sums[0], last_sums[1], last_sums[2]

    def sum_rows(grads, order):
        if permutes:
            return Reduction(net, *net.split(grads), order)
        return PlainReduction(grads, 0)

    def send_layer(layer, mixed, first, rows):
        sent = highway_weight_gradient(1 - core, turned[layer], mixed, first, rows, width // 2)
        key = f"layer{layer}_{first}"
        if permutes:
            net.plan(key, sent, "c")
        return layer, mixed, first, rows, (key if permutes else sent, 0)

    def keep_layer(job, order):
        layer, mixed, first, rows, (key, part) = job
        keep = highway_weight_gradient(
            core,
            turned[layer],
            mixed,
            first,
            rows,
            width // 2,
            net.state[key] if permutes else None,
            part,
        )
        if permutes:
            return Reduction(net, keep, None, order)
        other = key[:, part * rows : (part + 1) * rows]
        whole = jnp.moveaxis(jnp.concatenate([keep, other], axis=0), 1, 0).reshape(rows, -1)
        return PlainReduction([whole], 1)

    def sum_feed(keep, sent, order):
        keep, sent = (value.reshape((16,) + value.shape[3:]) for value in (keep, sent))
        if permutes:
            return Reduction(net, keep, sent, order)
        return sum_rows([jnp.concatenate([keep, sent], axis=0).reshape(-1, model_width)], "")

    def ring_of(*sums):
        return Ring(net, sums) if permutes else sums

    def advance(*sums):
        if permutes:
            for item in sums:
                item.step()

    def ready(*sums):
        if permutes:
            for item in sums:
                item.step(net.plan)

    def held(*sums):
        return tuple(item.key for item in sums) if permutes else ()

    def together(*sums, hold=()):
        if permutes:
            ready(*sums)
            launch(())
            window((), held(*hold))

    up_keep, up_sent, down_keep, down_sent, bias_sums, grad_resid, norm_sums = feed_forward_back(
        grad_second,
        first,
        act,
        slope,
        first_in,
        gain_one[None],
        feed_pieces,
        slots,
        feed_block,
        core,
    )
    grad_up_bias = jnp.moveaxis(bias_sums.reshape(2, 4, 2, feed_rows), 2, 1).reshape(-1)
    grad_attn_gain, grad_attn_shift, grad_out_bias = norm_sums[0], norm_sums[1], norm_sums[2]
    up_keep, up_sent, down_keep, down_sent, grad_resid = window(
        (up_keep, up_sent, down_keep, down_sent, grad_resid)
    )

    sum_up = sum_feed(up_keep, up_sent, "cxy")
    sum_down = sum_feed(down_keep, down_sent, "cyx")
    ready(sum_down, sum_up)
    grad_resid = launch(grad_resid)
    grad_branch = grad_resid.astype(BF16)
    grad_out = dot_tn(context, grad_branch).astype(BF16)
    grad_context = dot_nt(grad_branch, out_all).astype(BF16)
    grad_qkv = attend_back(qkv, grad_context)
    grad_resid, grad_out, grad_qkv = window((grad_resid, grad_out, grad_qkv))

    ready(sum_down, sum_up)
    grad_qkv, grad_resid = launch((grad_qkv, grad_resid))
    grad_qkv_weight = dot_tn(grad_qkv, low_embedded)
    qkv_sums = column_sum(grad_qkv)
    grad_attn_bias = jnp.concatenate([qkv_sums[:model_width], qkv_sums[2 * model_width :]])
    grad_summed, grad_embed_gain, grad_embed_shift = norm_back(
        summed, gain_zero, grad_resid + dot(grad_qkv, qkv_all)
    )
    grad_word = grad_summed.astype(BF16)
    grad_proj_bias = column_sum(grad_word)
    running = dot_nt(dot(perm, grad_word).astype(BF16), proj_all)
    running = window(running)
    ready(sum_down, sum_up)
    running = launch(running)
    mixed_one, sums_one, running = highway_backward(
        running, states[1], transforms[1], gatings[1], pieces[1], place, select, core
    )
    grad_pos = turn(grad_summed)
    if permutes:
        grad_pos = grad_pos.reshape(-1, model_width)
    grad_proj = dot_tn(last, grad_word)
    encoder_grads = [grad_qkv_weight, grad_out, grad_proj]
    type_hot = (type_ids[0] == 1).astype(F32)[:, None]
    vector_grads = [
        grad_proj_bias,
        jnp.sum((1.0 - type_hot) * grad_summed, axis=0),
        jnp.sum(type_hot * grad_summed, axis=0),
        grad_embed_gain,
        grad_embed_shift,
        grad_attn_bias,
        grad_out_bias,
        grad_attn_gain,
        grad_attn_shift,
        grad_up_bias,
        grad_down_bias,
        grad_ffn_gain,
        grad_ffn_shift,
    ]
    if permutes:
        sum_encoder = sum_rows(encoder_grads + [grad_pos], "c321xy")
        mixed_one, running, sum_encoder.terms, sum_encoder.sent = window(
            (mixed_one, running, sum_encoder.terms, sum_encoder.sent)
        )
    else:
        sum_encoder = sum_rows(encoder_grads, "")
        sum_pos = sum_rows([grad_pos], "")

    half_rows, quarter = features // 2, features // 4
    jobs = [send_layer(1, mixed_one, start, half_rows) for start in (0, half_rows)]
    ring_feed = ring_of(sum_up, sum_down)
    ready(sum_encoder, ring_feed)
    running = launch(running)
    mixed_zero, sums_zero, running = highway_backward(
        running, states[0], transforms[0], gatings[0], pieces[0], place, select, core
    )
    mixed_one, mixed_zero, running = window((mixed_one, mixed_zero, running))

    one = [keep_layer(job, order_) for job, order_ in zip(jobs, ("yx", "xy"))]
    jobs = [send_layer(0, mixed_zero, start, half_rows) for start in (0, half_rows)]
    grad_scaled = running * (0.5 / sorted_lengths.astype(F32))[:, None]
    ready(*one, sum_encoder, ring_feed)
    grad_scaled = launch(grad_scaled)
    matrix_turned, grad_groups = conv_backward(prep, char_groups, half_matrix, grad_scaled)
    mixed_zero, matrix_turned, grad_groups = window((mixed_zero, matrix_turned, grad_groups))

    ready(*one, sum_encoder, ring_feed)
    mixed_zero, grad_groups = launch((mixed_zero, grad_groups))
    jobs = [
        (0, mixed_zero, start * quarter, quarter, (jobs[start // 2][-1][0], start % 2))
        for start in range(4)
    ]
    zero = [keep_layer(job, order_) for job, order_ in zip(jobs, ("yx", "yx", "xy", "xy"))]
    first_two = (zero[0], zero[2])
    terms = [item.terms for item in zero] if permutes else ()
    terms, grad_groups = window((terms, grad_groups))
    for item, value in zip(zero, terms):
        item.terms = value

    ready(*first_two, sum_encoder)
    grad_groups = launch(grad_groups)
    grad_table = table_gradient(prep, grad_groups, character_embedding_table.shape[0])
    last_sum, vector_places = vector_rows(
        vector_grads + [sums_zero.reshape(-1), sums_one.reshape(-1), grad_table.reshape(-1)]
    )
    last_sum = window(last_sum)
    last_sum = Small(net, last_sum) if permutes else lax.psum(last_sum, ("narrow", "wide"))

    ring_one = ring_of(*one)
    together(zero[1], zero[3], *first_two, ring_one)
    sum_conv = sum_rows([matrix_turned], "cxy321")
    ring_first = ring_of(*first_two)
    together(zero[1], zero[3], ring_first, ring_one, sum_conv)
    together(ring_first, ring_one, sum_encoder, last_sum, sum_conv)
    together(ring_first, sum_encoder, last_sum, sum_conv)
    ring_last = ring_of(zero[1], zero[3])
    together(ring_last, last_sum, sum_conv)
    together(ring_last, last_sum, sum_conv)
    together(ring_last, last_sum, sum_conv)
    total = last_sum.result() if permutes else last_sum

    device = lax.axis_index("narrow") * wide + lax.axis_index("wide")

    def whole_vector(total, where):
        start, count, size = where
        return total[start : start + count].reshape(-1)[:size]

    def own_part(total, where):
        piece = where[2] // devices
        return lax.dynamic_slice_in_dim(whole_vector(total, where), device * piece, piece, 0)

    results = [own_part(total, where) for where in vector_places[: len(vector_grads)]]
    high_places = vector_places[len(vector_grads) :]
    (
        sum_proj_bias,
        sum_type_zero,
        sum_type_one,
        sum_embed_gain,
        sum_embed_shift,
        sum_attn_bias,
        sum_out_bias,
        sum_attn_gain,
        sum_attn_shift,
        sum_up_bias,
        sum_down_bias,
        sum_ffn_gain,
        sum_ffn_shift,
    ) = results
    sum_high_bias = jnp.stack([own_part(total, where) for where in high_places[:layers]])
    sum_table = whole_vector(total, high_places[layers]).reshape(
        character_embedding_table.shape
    )

    def rows_of(item, sizes):
        total = item.result()
        if not permutes:
            return total
        pieces, start = [], 0
        for size in sizes:
            pieces.append(total[start : start + size])
            start += size
        return pieces

    qkv_rows, sum_out, sum_proj, *rest = rows_of(
        sum_encoder,
        [
            qkv_all.shape[0] // devices,
            out_all.shape[0] // devices,
            proj_all.shape[0] // devices,
            words * model_width // devices // model_width,
        ],
    )
    if permutes:
        pos_rows = rest[0].reshape(-1, words)
    else:
        (pos_rows,) = sum_pos.result()
    if permutes:
        up_rows, down_rows = jnp.split(ring_feed.result(), 2)
    else:
        (up_rows,), (down_rows,) = sum_up.result(), sum_down.result()
    (conv_turned,) = rows_of(sum_conv, [filters // devices])
    own_filters = lax.dynamic_slice_in_dim(
        filter_widths(filters), device * (filters // devices), filters // devices
    )
    taps = jnp.arange(conv_rows)[:, None] // CHAR_DIM
    sum_conv_weight = jnp.where(taps < own_filters[None, :], conv_turned[:, :conv_rows].T, 0.0)

    if permutes:
        first_rows, last_rows = ring_first.result(), ring_last.result()
        parts = [first_rows[:quarter], last_rows[:quarter], first_rows[quarter:], last_rows[quarter:]]
        high_rows = [jnp.concatenate(parts, axis=0), ring_one.result()]
    else:
        high_rows = [
            jnp.concatenate([part for item in sums for part in item.result()], axis=0)
            for sums in (zero, one)
        ]

    return (
        hidden_out[None],
        sum_table,
        sum_conv_weight,
        conv_turned[:, conv_rows],
        jnp.stack(high_rows),
        sum_high_bias,
        sum_proj,
        sum_proj_bias,
        pos_rows.T,
        jnp.stack([sum_type_zero, sum_type_one]),
        sum_embed_gain,
        sum_embed_shift,
        qkv_rows.T,
        sum_attn_bias,
        sum_out,
        sum_out_bias,
        sum_attn_gain,
        sum_attn_shift,
        up_rows.T,
        sum_up_bias,
        down_rows,
        sum_down_bias,
        sum_ffn_gain,
        sum_ffn_shift,
    )


def solution(mesh):
    narrow, wide = mesh.shape["narrow"], mesh.shape["wide"]
    both = ("narrow", "wide")
    placed = (
        P(both, None, None),
        P(both, None),
        P(both, None),
        P(both, None, None),
        P(),
        P(None, "wide"),
        P("wide"),
        P(None, None, "wide"),
        P(None, "wide"),
        P("wide", None),
        P("wide"),
        P(None, "wide"),
        P(None, "wide"),
        P("wide"),
        P("wide"),
        P(None, "wide"),
        P("wide"),
        P("wide", None),
        P("wide"),
        P("wide"),
        P("wide"),
        P(None, "wide"),
        P("wide"),
        P("wide", None),
        P("wide"),
        P("wide"),
        P("wide"),
    )
    return jax.shard_map(
        partial(body, (narrow, wide) == (2, 16), wide, narrow * wide),
        mesh=mesh,
        in_specs=placed,
        out_specs=(
            P(both, None, None),
            P(),
            P(None, both),
            P(both),
            P(None, None, both),
            P(None, both),
            P(both, None),
            P(both),
            P(None, both),
            P(None, both),
            P(both),
            P(both),
            P(None, both),
            P(both),
            P(both, None),
            P(both),
            P(both),
            P(both),
            P(None, both),
            P(both),
            P(both, None),
            P(both),
            P(both),
            P(both),
        ),
        check_vma=False,
    )
```

```python
from functools import partial

import jax
import jax.numpy as jnp
from jax import lax
from jax.experimental import pallas as pl
from jax.experimental.pallas import tpu as pltpu
from jax.sharding import PartitionSpec as P

HEADS = 12
HEAD_DIM = 64
CHAR_DIM = 16
TAPS = 7
EPSILON = 1e-12

LANES = 128
GROUP = LANES // CHAR_DIM
BLOCK_WORDS = 32
CHUNK_BLOCKS = 16
CHUNK = BLOCK_WORDS * CHUNK_BLOCKS
TABLE_PAD = 384
ROW_TILE = 128
BIAS_LANE = TAPS * CHAR_DIM

F32 = jnp.float32
BF16 = jnp.bfloat16
VMEM = pl.BlockSpec(memory_space=pltpu.VMEM)
SMEM = pl.BlockSpec(memory_space=pltpu.SMEM)
MIB = 1024 * 1024


def cost(microseconds):
    return pl.CostEstimate(
        flops=int(microseconds * 1.1e9), bytes_accessed=int(microseconds * 3e6), transcendentals=0
    )


def dot(left, right):
    return lax.dot_general(left, right, (((1,), (0,)), ((), ())), preferred_element_type=F32)


def dot_nt(left, right):
    return lax.dot_general(left, right, (((1,), (1,)), ((), ())), preferred_element_type=F32)


def dot_tn(left, right):
    return lax.dot_general(left, right, (((0,), (0,)), ((), ())), preferred_element_type=F32)


def column_sum(values):
    return jnp.sum(values.astype(F32), axis=0)


def filter_widths(filter_count):
    column = jnp.arange(filter_count)
    widths = jnp.ones((filter_count,), jnp.int32)
    for exponent in range(6):
        widths = widths + (column >= filter_count * 2**exponent // 64).astype(jnp.int32)
    return widths


def sort_words(char_ids, lengths, groups):
    words, chars = char_ids.shape
    index = jnp.arange(words)
    longer = lengths[None, :] > lengths[:, None]
    tie = (lengths[None, :] == lengths[:, None]) & (index[None, :] < index[:, None])
    rank = jnp.sum((longer | tie).astype(jnp.int32), axis=1)
    perm = (rank[None, :] == index[:, None]).astype(BF16)
    live = jnp.arange(chars)[None, :] < lengths[:, None]
    shifted = jnp.where(live, char_ids + 1, 0)
    packed = jnp.concatenate(
        [shifted >> 4, shifted & 15, lengths[:, None]], axis=1
    ).astype(BF16)
    sorted_packed = dot(perm, packed).astype(jnp.int32)
    ids = (sorted_packed[:, :chars] << 4) + sorted_packed[:, chars : 2 * chars] - 1
    ids = jnp.pad(ids, ((0, 0), (0, GROUP * groups - chars)), constant_values=-1)
    sorted_lengths = sorted_packed[:, 2 * chars]
    tile_count = words // BLOCK_WORDS
    tile_max = jnp.max(sorted_lengths.reshape(tile_count, BLOCK_WORDS), axis=1)
    cum = jnp.cumsum(tile_max)
    total = cum[-1]
    block = jnp.arange(tile_count * chars + CHUNK_BLOCKS)
    tile = jnp.sum((block[:, None] >= cum[None, :]).astype(jnp.int32), axis=1)
    start = jnp.sum(
        jnp.where(tile[:, None] == jnp.arange(tile_count)[None, :], (cum - tile_max)[None, :], 0),
        axis=1,
    )
    valid = block < total
    position = jnp.where(valid, block - start, chars).astype(jnp.int32)
    tile = jnp.where(valid, tile, 0).astype(jnp.int32)
    chunks = (total + CHUNK_BLOCKS - 1) // CHUNK_BLOCKS
    reach = jnp.sum(
        (sorted_lengths[None, :] > GROUP * jnp.arange(groups - 1)[:, None]).astype(jnp.int32), axis=1
    )
    scalars = jnp.concatenate([chunks[None], (reach + ROW_TILE - 1) // ROW_TILE]).astype(jnp.int32)
    return perm, ids, sorted_lengths, scalars, tile, position


def build_windows(chunk, tile_ref, pos_ref, g_ref, len_ref, x_ref):
    lane = lax.broadcasted_iota(jnp.int32, (BLOCK_WORDS, LANES), 1)
    for b in range(CHUNK_BLOCKS):
        block = chunk * CHUNK_BLOCKS + b
        row = pl.multiple_of(tile_ref[block] * BLOCK_WORDS, BLOCK_WORDS)
        position = pos_ref[block]
        group = position >> 3
        offset = (position & 7) * CHAR_DIM
        shift = lax.rem(LANES - offset, LANES)
        here = pltpu.roll(g_ref[group, pl.ds(row, BLOCK_WORDS), :].astype(F32), shift, 1)
        after = pltpu.roll(g_ref[group + 1, pl.ds(row, BLOCK_WORDS), :].astype(F32), shift, 1)
        live = (len_ref[pl.ds(row, BLOCK_WORDS), :] > position).astype(F32)
        value = jnp.where(lane < LANES - offset, here, after)
        value = jnp.where(lane < BIAS_LANE, value, jnp.where(lane == BIAS_LANE, live, 0.0))
        x_ref[b * BLOCK_WORDS : (b + 1) * BLOCK_WORDS, :] = value.astype(BF16)


def embed_kernel(scalar_ref, ids_ref, table_ref, g_ref):
    groups = g_ref.shape[0]
    g_ref[...] = jnp.zeros_like(g_ref)
    identity = lax.broadcasted_iota(jnp.int32, (ROW_TILE, TABLE_PAD), 1)
    for group in range(groups - 1):

        def embed(step, carry, group=group):
            row = pl.multiple_of(step * ROW_TILE, ROW_TILE)
            total = jnp.zeros((ROW_TILE, LANES), F32)
            for k in range(GROUP):
                column = group * GROUP + k
                hot = (ids_ref[pl.ds(row, ROW_TILE), column : column + 1] == identity).astype(F32)
                total = total + dot(hot.astype(BF16), table_ref[k])
            g_ref[group, pl.ds(row, ROW_TILE), :] = total.astype(BF16)
            return carry

        lax.fori_loop(0, scalar_ref[1 + group], embed, 0)


def embed_characters(prep, table_blocks):
    _, ids, _, scalars, _, _ = prep
    return pl.pallas_call(
        embed_kernel,
        out_shape=jax.ShapeDtypeStruct((ids.shape[1] // GROUP, ids.shape[0], LANES), BF16),
        in_specs=[SMEM, VMEM, VMEM],
        out_specs=VMEM,
        compiler_params=pltpu.CompilerParams(vmem_limit_bytes=32 * MIB),
        cost_estimate=cost(5),
        name="embed_characters",
    )(scalars, ids, table_blocks)


def conv_forward_kernel(
    scalar_ref, tile_ref, pos_ref, g_ref, w_ref, len_ref, pooled_ref, x_ref, pre_ref
):
    filters = w_ref.shape[1]
    part = pre_ref.shape[1]
    pooled_ref[...] = jnp.zeros_like(pooled_ref)

    def step(chunk, carry):
        build_windows(chunk, tile_ref, pos_ref, g_ref, len_ref, x_ref)
        for first in range(0, filters, part):
            half = dot(x_ref[...], w_ref[:, first : first + part])
            pre_ref[...] = half + half * jnp.tanh(half)
            for b in range(CHUNK_BLOCKS):
                row = pl.multiple_of(
                    tile_ref[chunk * CHUNK_BLOCKS + b] * BLOCK_WORDS, BLOCK_WORDS
                )
                pooled_ref[pl.ds(row, BLOCK_WORDS), first : first + part] += pre_ref[
                    b * BLOCK_WORDS : (b + 1) * BLOCK_WORDS, :
                ]
        return carry

    lax.fori_loop(0, scalar_ref[0], step, 0)
    pooled_ref[...] = pooled_ref[...] / len_ref[...].astype(F32)


def conv_forward(prep, char_groups, half_matrix):
    _, ids, lengths, scalars, tile, position = prep
    return pl.pallas_call(
        conv_forward_kernel,
        out_shape=jax.ShapeDtypeStruct((ids.shape[0], half_matrix.shape[1]), F32),
        in_specs=[SMEM, SMEM, SMEM, VMEM, VMEM, VMEM],
        out_specs=VMEM,
        scratch_shapes=[pltpu.VMEM((CHUNK, LANES), BF16), pltpu.VMEM((CHUNK, 512), F32)],
        compiler_params=pltpu.CompilerParams(vmem_limit_bytes=32 * MIB),
        cost_estimate=cost(16),
        name="conv_forward",
    )(scalars, tile, position, char_groups, half_matrix, lengths[:, None])


def conv_backward_kernel(
    scalar_ref, tile_ref, pos_ref, g_ref, w_ref, len_ref, gp_ref, out_ref, gg_ref, x_ref, d_ref, dw_ref
):
    filters = w_ref.shape[1]
    part = 512
    lane = lax.broadcasted_iota(jnp.int32, (BLOCK_WORDS, LANES), 1)
    dw_ref[...] = jnp.zeros_like(dw_ref)
    gg_ref[...] = jnp.zeros_like(gg_ref)

    def step(chunk, carry):
        build_windows(chunk, tile_ref, pos_ref, g_ref, len_ref, x_ref)
        for first in range(0, filters, part):
            columns = slice(first, first + part)
            half = dot(x_ref[...], w_ref[:, columns])
            tanh = jnp.tanh(half)
            slope = (1.0 + tanh) * (1.0 + (half - half * tanh))
            for b in range(CHUNK_BLOCKS):
                rows = slice(b * BLOCK_WORDS, (b + 1) * BLOCK_WORDS)
                row = pl.multiple_of(
                    tile_ref[chunk * CHUNK_BLOCKS + b] * BLOCK_WORDS, BLOCK_WORDS
                )
                d_ref[rows, columns] = (
                    gp_ref[pl.ds(row, BLOCK_WORDS), columns] * slope[rows]
                ).astype(BF16)
            dw_ref[:, columns] += dot_tn(x_ref[...], d_ref[:, columns])
        gx = dot_nt(d_ref[...], w_ref[...])
        for b in range(CHUNK_BLOCKS):
            block = chunk * CHUNK_BLOCKS + b
            row = pl.multiple_of(tile_ref[block] * BLOCK_WORDS, BLOCK_WORDS)
            position = pos_ref[block]
            group = position >> 3
            offset = (position & 7) * CHAR_DIM
            value = gx[b * BLOCK_WORDS : (b + 1) * BLOCK_WORDS, :]
            value = pltpu.roll(jnp.where(lane < BIAS_LANE, value, 0.0), offset, 1)
            gg_ref[group, pl.ds(row, BLOCK_WORDS), :] += jnp.where(lane >= offset, value, 0.0)
            gg_ref[group + 1, pl.ds(row, BLOCK_WORDS), :] += jnp.where(lane < offset, value, 0.0)
        return carry

    lax.fori_loop(0, scalar_ref[0], step, 0)
    out_ref[...] = dw_ref[...].T.astype(BF16)


def conv_backward(prep, char_groups, half_matrix, grad_scaled):
    _, ids, lengths, scalars, tile, position = prep
    filters = half_matrix.shape[1]
    return pl.pallas_call(
        conv_backward_kernel,
        out_shape=(
            jax.ShapeDtypeStruct((filters, LANES), BF16),
            jax.ShapeDtypeStruct(char_groups.shape, F32),
        ),
        in_specs=[SMEM, SMEM, SMEM, VMEM, VMEM, VMEM, VMEM],
        out_specs=(VMEM, VMEM),
        scratch_shapes=[
            pltpu.VMEM((CHUNK, LANES), BF16),
            pltpu.VMEM((CHUNK, filters), BF16),
            pltpu.VMEM((LANES, filters), F32),
        ],
        compiler_params=pltpu.CompilerParams(vmem_limit_bytes=48 * MIB),
        cost_estimate=cost(35),
        name="conv_backward",
    )(scalars, tile, position, char_groups, half_matrix, lengths[:, None], grad_scaled)


def table_kernel(scalar_ref, ids_ref, gg_ref, out_ref):
    groups = gg_ref.shape[0]
    out_ref[...] = jnp.zeros_like(out_ref)
    identity = lax.broadcasted_iota(jnp.int32, (TABLE_PAD, ROW_TILE), 0)
    for group in range(groups - 1):

        def step(index, carry, group=group):
            row = pl.multiple_of(index * ROW_TILE, ROW_TILE)
            grad = (2.0 * gg_ref[group, pl.ds(row, ROW_TILE), :]).astype(BF16)
            for k in range(GROUP):
                column = group * GROUP + k
                hot = (ids_ref[column : column + 1, pl.ds(row, ROW_TILE)] == identity).astype(F32)
                out_ref[k] += dot(hot.astype(BF16), grad)
            return carry

        lax.fori_loop(0, scalar_ref[1 + group], step, 0)


def table_gradient(prep, grad_groups, vocabulary):
    ids, scalars = prep[1], prep[3]
    total = pl.pallas_call(
        table_kernel,
        out_shape=jax.ShapeDtypeStruct((GROUP, TABLE_PAD, LANES), F32),
        in_specs=[SMEM, VMEM, VMEM],
        out_specs=VMEM,
        compiler_params=pltpu.CompilerParams(vmem_limit_bytes=32 * MIB),
        cost_estimate=cost(4),
        name="table_gradient",
    )(scalars, ids.T, grad_groups)
    parts = [total[k, :vocabulary, k * CHAR_DIM : (k + 1) * CHAR_DIM] for k in range(GROUP)]
    return sum(parts[1:], parts[0])


def table_lanes(table):
    padded = jnp.pad(table, ((0, TABLE_PAD - table.shape[0]), (0, 0)))
    return jnp.stack(
        [
            jnp.pad(padded, ((0, 0), (k * CHAR_DIM, LANES - (k + 1) * CHAR_DIM)))
            for k in range(GROUP)
        ]
    )


ANY = pl.BlockSpec(memory_space=pl.ANY)


def flat_pieces(pieces):
    return [array for half in pieces for chunk in half for array in chunk]


def piece_copies(layout, array, slot, first, own, pieces, whole_ref, sems, buffer):
    halves, chunks, arrays, rows = layout
    width = whole_ref.shape[2] // 2
    copies = []
    for half in range(halves):
        for chunk in range(chunks):
            ref = pieces[(half * chunks + chunk) * arrays + array]
            start = (own if half == 0 else 1 - own) * (chunks * rows) + chunk * rows
            start = pl.multiple_of(start, rows)
            for side in range(2):
                copies.append(
                    pltpu.make_async_copy(
                        ref.at[first if side == 0 else 1 - first, slot],
                        whole_ref.at[
                            buffer, pl.ds(start, rows), side * width : (side + 1) * width
                        ],
                        sems.at[buffer, len(copies)],
                    )
                )
    return copies


def fetch_pieces(layout, select_ref, own, pieces, whole_ref, sems):
    step = pl.program_id(0)

    def start(index):
        for array in range(layout[2]):

            @pl.when(index // 2 == array)
            def _(array=array):
                for copy in piece_copies(
                    layout, array, index % 2, select_ref[index], own, pieces, whole_ref, sems, index % 2
                ):
                    copy.start()

    @pl.when(step == 0)
    def _():
        start(0)

    @pl.when(step + 1 < pl.num_programs(0))
    def _():
        start(step + 1)

    buffer = step % 2
    for copy in piece_copies(layout, 0, 0, 0, own, pieces, whole_ref, sems, buffer):
        copy.wait()
    return buffer


def half_tanh(value):
    return 0.5 + 0.5 * jnp.tanh(0.5 * value)


def highway_forward_kernel(layout, place_ref, select_ref, core_ref, h_ref, bias_ref, *refs):
    count = layout[0] * layout[1] * layout[2]
    pieces = refs[:count]
    next_ref, transform_ref, gating_ref, low_ref, whole_ref, sems = refs[count:]
    step = pl.program_id(0)
    width = next_ref.shape[1]

    @pl.when(step == 0)
    def _():
        low_ref[...] = h_ref[...].astype(BF16)

    block = place_ref[step]
    blocks = bias_ref.shape[0] // 2
    buffer = fetch_pieces(layout, select_ref, core_ref[0], pieces, whole_ref, sems)
    mixed = dot(low_ref[...], whole_ref[buffer])
    transform = mixed[:, :width] + bias_ref[block]
    gating = half_tanh(mixed[:, width:] + bias_ref[block + blocks])
    h = h_ref[:, pl.ds(pl.multiple_of(block * width, width), width)]
    activated = transform * half_tanh(transform)
    transform_ref[...] = transform
    gating_ref[...] = gating
    next_ref[...] = activated + gating * (h - activated)


def highway_forward(h, pieces, bias_blocks, place, select, core):
    words, features = h.shape
    width = bias_blocks.shape[2]
    flat = flat_pieces(pieces)
    layout = (len(pieces), len(pieces[0]), len(pieces[0][0]), flat[0].shape[2])
    column = pl.BlockSpec((words, width), lambda j, place, *_: (0, place[j]))
    whole = lambda shape: pl.BlockSpec(shape, lambda j, *_: (0,) * len(shape))
    return pl.pallas_call(
        partial(highway_forward_kernel, layout),
        grid_spec=pltpu.PrefetchScalarGridSpec(
            num_scalar_prefetch=3,
            grid=(features // width,),
            in_specs=[whole(h.shape), whole(bias_blocks.shape)] + [ANY] * len(flat),
            out_specs=[column, column, column, whole(h.shape)],
            scratch_shapes=[
                pltpu.VMEM((2, features, 2 * width), BF16),
                pltpu.SemaphoreType.DMA((2, 2 * layout[0] * layout[1])),
            ],
        ),
        out_shape=(
            jax.ShapeDtypeStruct(h.shape, F32),
            jax.ShapeDtypeStruct(h.shape, F32),
            jax.ShapeDtypeStruct(h.shape, F32),
            jax.ShapeDtypeStruct(h.shape, BF16),
        ),
        compiler_params=pltpu.CompilerParams(vmem_limit_bytes=56 * MIB),
        cost_estimate=cost(19),
        name="highway_forward",
    )(place, select, core, h, bias_blocks, *flat)


def highway_backward_kernel(layout, place_ref, select_ref, core_ref, grad_ref, h_ref, t_ref, g_ref, *refs):
    count = layout[0] * layout[1] * layout[2]
    pieces = refs[:count]
    mixed_ref, sums_ref, out_ref, whole_ref, sems = refs[count:]
    step = pl.program_id(0)
    width = grad_ref.shape[1]
    features = out_ref.shape[1]

    @pl.when(step == 0)
    def _():
        out_ref[...] = jnp.zeros_like(out_ref)

    block = place_ref[step]
    buffer = fetch_pieces(layout, select_ref, core_ref[0], pieces, whole_ref, sems)
    grad = grad_ref[...]
    transform = t_ref[...]
    gating = g_ref[...]
    sigmoid = half_tanh(transform)
    activated = transform * sigmoid
    rest = grad * (1.0 - gating)
    low_t = (rest * (sigmoid + activated * (1.0 - sigmoid))).astype(BF16)
    low_g = (rest * gating * (h_ref[...] - activated)).astype(BF16)
    mixed_ref[0] = low_t
    mixed_ref[1] = low_g
    sums_ref[0] = jnp.sum(low_t.astype(F32), axis=0, keepdims=True)
    sums_ref[1] = jnp.sum(low_g.astype(F32), axis=0, keepdims=True)
    low = jnp.concatenate([low_t, low_g], axis=1)
    for start in range(0, features, 512):
        out_ref[:, start : start + 512] += dot_nt(
            low, whole_ref[buffer, start : start + 512, :]
        )
    out_ref[:, pl.ds(pl.multiple_of(block * width, width), width)] += grad * gating


def highway_backward(grad, h, transform, gating, pieces, place, select, core):
    words, features = h.shape
    flat = flat_pieces(pieces)
    width = flat[0].shape[3]
    layout = (len(pieces), len(pieces[0]), len(pieces[0][0]), flat[0].shape[2])
    column = pl.BlockSpec((words, width), lambda j, place, *_: (0, place[j]))
    return pl.pallas_call(
        partial(highway_backward_kernel, layout),
        grid_spec=pltpu.PrefetchScalarGridSpec(
            num_scalar_prefetch=3,
            grid=(features // width,),
            in_specs=[column] * 4 + [ANY] * len(flat),
            out_specs=[
                pl.BlockSpec((2, words, width), lambda j, place, *_: (0, 0, place[j])),
                pl.BlockSpec((2, 1, width), lambda j, place, *_: (0, 0, place[j])),
                pl.BlockSpec(h.shape, lambda j, *_: (0, 0)),
            ],
            scratch_shapes=[
                pltpu.VMEM((2, features, 2 * width), BF16),
                pltpu.SemaphoreType.DMA((2, 2 * layout[0] * layout[1])),
            ],
        ),
        out_shape=(
            jax.ShapeDtypeStruct((2, words, features), BF16),
            jax.ShapeDtypeStruct((2, 1, features), F32),
            jax.ShapeDtypeStruct(h.shape, F32),
        ),
        compiler_params=pltpu.CompilerParams(vmem_limit_bytes=56 * MIB),
        cost_estimate=cost(21),
        name="highway_backward",
    )(place, select, core, grad, h, transform, gating, *flat)


def weight_kernel(which_ref, left_ref, right_ref, *refs):
    out_ref = refs[-1]
    value = dot(left_ref[...], right_ref[0])
    width = out_ref.shape[2]
    for number in range(out_ref.shape[0]):
        block = value[:, number * width : (number + 1) * width]
        if len(refs) == 2:
            block = block + refs[0][number].astype(F32)
        out_ref[number] = block.astype(BF16)


def highway_weight_gradient(which, turned, mixed, first, rows, width, added=None, part=0):
    words, features = mixed.shape[1:]
    blocks = 8
    out = pl.BlockSpec((blocks, rows, width), lambda j, which: (j, 0, 0))
    return pl.pallas_call(
        weight_kernel,
        grid_spec=pltpu.PrefetchScalarGridSpec(
            num_scalar_prefetch=1,
            grid=(features // (blocks * width),),
            in_specs=[
                pl.BlockSpec((rows, words), lambda j, which: (first // rows, 0)),
                pl.BlockSpec((1, words, blocks * width), lambda j, which: (which[0], 0, j)),
            ]
            + (
                []
                if added is None
                else [pl.BlockSpec((blocks, rows, width), lambda j, which: (j, part, 0))]
            ),
            out_specs=out,
        ),
        out_shape=jax.ShapeDtypeStruct((features // width, rows, width), BF16),
        compiler_params=pltpu.CompilerParams(vmem_limit_bytes=32 * MIB),
        cost_estimate=cost(3),
        name="highway_weight",
    )(which, turned, mixed, *([] if added is None else [added]))


def turn_kernel(value_ref, out_ref):
    out_ref[...] = value_ref[...].T.astype(BF16)


def turn(value):
    rows, columns = value.shape
    return pl.pallas_call(
        turn_kernel,
        grid=(columns // 256,),
        in_specs=[pl.BlockSpec((rows, 256), lambda j: (0, j))],
        out_specs=pl.BlockSpec((256, rows), lambda j: (j, 0)),
        out_shape=jax.ShapeDtypeStruct((columns, rows), BF16),
        compiler_params=pltpu.CompilerParams(vmem_limit_bytes=32 * MIB),
        cost_estimate=cost(1),
        name="turn",
    )(value)


def place_rows_kernel(splits, place_ref, core_ref, *refs):
    arrays = (len(refs) - len(splits) - 1) // 2
    own_refs, other_refs = refs[:arrays], refs[arrays : 2 * arrays]
    out_refs, whole_ref = refs[2 * arrays : -1], refs[-1]
    step = pl.program_id(0)
    half_rows = own_refs[0].shape[1]
    core = core_ref[0]
    for array in range(arrays):

        @pl.when(step // 4 == array)
        def _(array=array):
            align = lambda start: pl.ds(pl.multiple_of(start, 16), half_rows)
            whole_ref[align(core * half_rows), :] = own_refs[array][0]
            whole_ref[align((1 - core) * half_rows), :] = other_refs[array][0]

    start = 0
    for rows, out_ref in zip(splits, out_refs):
        out_ref[...] = whole_ref[start : start + rows, :]
        start += rows


def place_rows(own, other, place, core, splits):
    half_rows, columns = own[0].shape[1:]

    def index(number):
        return lambda j, *_: (jnp.clip(j - 4 * number, 0, 3), 0, 0)

    specs = [pl.BlockSpec((1, half_rows, columns), index(number)) for number in range(len(own))]
    return pl.pallas_call(
        partial(place_rows_kernel, splits),
        grid_spec=pltpu.PrefetchScalarGridSpec(
            num_scalar_prefetch=2,
            grid=(4 * len(own),),
            in_specs=specs + specs,
            out_specs=[
                pl.BlockSpec((rows, columns), lambda j, place, *_: (place[j], 0)) for rows in splits
            ],
            scratch_shapes=[pltpu.VMEM((2 * half_rows, columns), BF16)],
        ),
        out_shape=[
            jax.ShapeDtypeStruct((4 * len(own) * rows, columns), BF16) for rows in splits
        ],
        compiler_params=pltpu.CompilerParams(vmem_limit_bytes=32 * MIB),
        cost_estimate=cost(7),
        name="place_rows",
    )(place, core, *own, *other)


def place_small_kernel(place_ref, *refs):
    inputs, (conv_ref, *row_refs) = refs[:4], refs[4:]
    step = pl.program_id(0)
    for number, ref in enumerate(inputs):

        @pl.when(step // 4 == number)
        def _(ref=ref):
            start = conv_ref.shape[0]
            conv_ref[...] = ref[0, :start, :]
            for row_ref in row_refs:
                row_ref[0] = ref[0, start : start + row_ref.shape[1], :]
                start += row_ref.shape[1]


def place_small(arrays, place, conv_rows, splits):
    rows, columns = arrays[0].shape[1:]

    def index(number):
        return lambda j, *_: (jnp.clip(j - 4 * number, 0, 3), 0, 0)

    return pl.pallas_call(
        place_small_kernel,
        grid_spec=pltpu.PrefetchScalarGridSpec(
            num_scalar_prefetch=1,
            grid=(16,),
            in_specs=[pl.BlockSpec((1, rows, columns), index(number)) for number in range(4)],
            out_specs=[pl.BlockSpec((conv_rows, columns), lambda j, place: (0, place[j]))]
            + [
                pl.BlockSpec((1, count, columns), lambda j, place: (place[j], 0, 0))
                for count in splits
            ],
        ),
        out_shape=[jax.ShapeDtypeStruct((conv_rows, 16 * columns), BF16)]
        + [jax.ShapeDtypeStruct((16, count, columns), BF16) for count in splits],
        compiler_params=pltpu.CompilerParams(vmem_limit_bytes=32 * MIB),
        cost_estimate=cost(2),
        name="place_small",
    )(place, *arrays)


LINKS = {
    "x": [(w, w ^ 1) for w in range(16)],
    "y": [(w, w ^ 2) for w in range(16)],
    "z": [(w, (w + 4) % 16) for w in range(16)],
    "back": [(w, (w - 4) % 16) for w in range(16)],
    "z1": [(w, w ^ 4) for w in range(16)],
    "z2": [(w, w ^ 8) for w in range(16)],
}
CORES = [(0, 1), (1, 0)]


def send(value, link):
    if link == "c":
        return lax.ppermute(value, "narrow", CORES)
    return lax.ppermute(value, "wide", LINKS[link])


def total_of(terms):
    return sum((term.astype(F32) for term in terms[1:]), terms[0].astype(F32))


class Exchange:
    windows = True

    def __init__(self):
        self.core = lax.axis_index("narrow")
        index = lax.axis_index("wide")
        self.z, self.y, self.x = index // 4, (index // 2) % 2, index % 2
        self.state, self.fresh, self.count, self.planned = {}, [], 0, []

    def put(self, key, value):
        self.state[key] = value
        self.fresh.append(key)

    def move(self, key, source, link):
        self.put(key, send(self.state[source], link))

    def plan(self, key, value, link, shape=None):
        self.planned.append((key, value, link, shape))

    def plan_move(self, source, *links):
        for link in links:
            self.plan(source + link, self.state[source], link)

    def plan_ring(self, name, step):
        self.plan(f"{name}r{step}", self.state[f"{name}r{step - 1}" if step > 1 else name], "z")

    def plan_swap(self, *names):
        for name in names:
            self.plan(name + "c", self.state[name], "c")

    def launch(self, values):
        leaves, tree = jax.tree.flatten(values)
        held = lax.optimization_barrier(
            tuple(value for _, value, _, _ in self.planned) + tuple(leaves)
        )
        for (key, _, link, shape), value in zip(self.planned, held):
            value = send(value, link)
            self.put(key, value if shape is None else value.reshape(shape))
        leaves = held[len(self.planned) :]
        self.planned = []
        return jax.tree.unflatten(tree, leaves)

    def window(self, values, hold=()):
        held_keys = [key for key in self.fresh if key in hold]
        self.fresh = [key for key in self.fresh if key not in hold]
        leaves, tree = jax.tree.flatten(values)
        held = lax.optimization_barrier(
            tuple(self.state[key] for key in self.fresh) + tuple(leaves)
        )
        for key, value in zip(self.fresh, held):
            self.state[key] = value
        leaves = held[len(self.fresh) :]
        self.fresh = held_keys
        return jax.tree.unflatten(tree, leaves)

    def swap_chain(self, *names):
        before = None
        for name in names:
            value = self.state[name]
            if before is not None:
                value, self.state[before] = lax.optimization_barrier((value, self.state[before]))
            before = name + "c"
            self.put(before, send(value, "c"))

    def stage(self, values=(), hold=()):
        return self.window(self.launch(values), hold)


    def load(self, name, value, rows=None, offset=0, whole=False):
        if not whole:
            rows = rows or value.shape[0] // 2
            value = lax.dynamic_slice_in_dim(
                value, self.core * (value.shape[0] // 2) + offset, rows, 0
            )
        self.state[name] = value

    def ring(self, name):
        received = [self.state[name]]
        for _ in range(3):
            received.append(send(received[-1], "z"))
        self.put(name + "o", jnp.stack(received))

    def ring_step(self, name, step):
        self.move(f"{name}r{step}", f"{name}r{step - 1}" if step > 1 else name, "z")

    def ring_both(self, name):
        self.put(name + "r1", send(self.state[name], "z"))
        self.put(name + "r3", send(self.state[name], "back"))
        self.put(name + "r2", send(self.state[name + "r1"], "z"))

    def ring_done(self, name):
        self.state[name + "o"] = jnp.stack(
            [self.state[name]] + [self.state[f"{name}r{step}"] for step in (1, 2, 3)]
        )

    def square(self, name):
        value = self.state[name]
        over_x = send(value, "x")
        self.put(name + "o0", jnp.stack([value, over_x, send(value, "y"), send(over_x, "y")]))

    def turn_ring(self, name, step):
        self.move(f"{name}o{step}", f"{name}o{step - 1}", "z")

    def swap(self, *names):
        for name in names:
            self.move(name + "c", name, "c")

    def near(self, name, suffix=""):
        return [self.state[name + part + suffix] for part in ("o", "ox", "oy", "oxy")]

    def layer(self, name, chunks):
        halves = []
        for suffix in ("", "c"):
            halves.append(
                [
                    [
                        array.reshape((2, 2) + array.shape[1:])
                        for array in self.near(f"{name}{chunk}", suffix)
                    ]
                    for chunk in range(chunks)
                ]
            )
        return halves

    def place(self, ring_last):
        step = jnp.arange(16)
        near, slot = (step % 4, step // 4) if ring_last else (step // 4, step % 4)
        return (
            (self.z - slot) % 4 * 4 + (self.y ^ (near >> 1)) * 2 + (self.x ^ (near & 1))
        ).astype(jnp.int32)

    def rows(self, own, other, splits, ring_last):
        core = self.core[None].astype(jnp.int32)
        return place_rows(own, other, self.place(ring_last), core, splits)


    def split(self, grads):
        blocks = [grad.astype(BF16).reshape(2, 16, -1, grad.shape[1]) for grad in grads]
        return tuple(
            jnp.concatenate(
                [lax.dynamic_index_in_dim(block, which, 0, keepdims=False) for block in blocks],
                axis=1,
            )
            for which in (self.core, 1 - self.core)
        )


class Reduction:
    def __init__(self, net, keep, sent, order):
        shape = (4, 2, 2) + keep.shape[1:]
        self.net, self.order, self.done = net, list(order), 0
        net.count += 1
        self.name = f"sum{net.count}"
        self.terms = [keep.reshape(shape)]
        self.keys, self.running, self.axes = [], None, ["z", "y", "x"]
        self.sent, self.shape = sent, shape

    def all_terms(self):
        return self.terms + [self.net.state[key] for key in self.keys]

    def pick(self, terms, index, axis):
        return [lax.dynamic_index_in_dim(term, index, axis, keepdims=False) for term in terms]

    def keep_only(self, index, axis):
        self.terms = self.pick(self.all_terms(), index, axis)
        self.keys = []

    def step(self, put=None):
        net, link = self.net, self.order[self.done]
        put = put or (lambda key, value, link, shape=None: net.put(
            key, send(value, link) if shape is None else send(value, link).reshape(shape)
        ))
        self.key = key = f"{self.name}_{self.done}"
        self.done += 1
        if link == "c":
            put(key, self.sent, "c", self.shape)
            self.keys.append(key)
        elif link in ("x", "y"):
            axis = self.axes.index(link)
            index = net.x if link == "x" else net.y
            sent = total_of(self.pick(self.all_terms(), 1 - index, axis)).astype(BF16)
            self.keep_only(index, axis)
            self.axes.remove(link)
            put(key, sent, link)
            self.keys.append(key)
        else:
            axis = self.axes.index("z")
            index = (net.z + int(link)) % 4
            terms = self.pick(self.all_terms(), index, axis)
            if self.running is not None:
                terms.append(net.state[self.running])
            put(key, total_of(terms).astype(BF16), "z")
            self.running = key
            if link == "1":
                self.keep_only(net.z, axis)
                self.axes.remove("z")
                self.keys = [key]
        return self

    def result(self):
        assert self.done == len(self.order)
        return total_of(self.all_terms())


class Ring:
    def __init__(self, net, sums, both):
        self.net, self.sums, self.both, self.done = net, sums, both, 0
        self.arrived = []
        net.count += 1
        self.name = f"ring{net.count}"

    def part(self, distance):
        index = (self.net.z + distance) % 4
        parts = [total_of(item.pick(item.all_terms(), index, 0)) for item in self.sums]
        value = parts[0] if len(parts) == 1 else jnp.concatenate(parts, axis=0)
        for key in self.arrived:
            value = value + self.net.state[key].astype(F32)
        return value

    def step(self, put):
        self.done += 1
        self.key = key = f"{self.name}_{self.done}"
        if self.both and self.done == 1:
            self.last_key = f"{self.name}_back"
            put(self.last_key, self.part(3).astype(BF16), "back")
            put(key, self.part(2).astype(BF16), "z")
        else:
            put(key, self.part((3 if self.both else 4) - self.done).astype(BF16), "z")
        self.arrived = [key]
        return self

    def result(self):
        assert self.done == (2 if self.both else 3)
        if self.both:
            self.arrived = self.arrived + [self.last_key]
        return self.part(0)


class Small:
    def __init__(self, net, value):
        self.net, self.value, self.done, self.key = net, value, 0, None
        net.count += 1
        self.name = f"small{net.count}"

    def result(self):
        return self.value if self.key is None else self.value + self.net.state[self.key]

    def step(self, put):
        self.value = self.result()
        self.key = f"{self.name}_{self.done}"
        put(self.key, self.value, ("c", "x", "y", "z1", "z2")[self.done])
        self.done += 1
        return self


class PlainReduction:
    def __init__(self, grads, axis):
        self.grads, self.axis = grads, axis

    def step(self):
        return self

    def result(self):
        return [
            lax.psum_scatter(
                grad.astype(BF16), ("narrow", "wide"), scatter_dimension=self.axis, tiled=True
            ).astype(F32)
            for grad in self.grads
        ]


def norm_rows(value, norm_gain, norm_shift):
    center = jnp.mean(value, axis=-1, keepdims=True)
    offsets = value - center
    spread = jnp.mean(offsets * offsets, axis=-1, keepdims=True)
    return offsets * lax.rsqrt(spread + EPSILON) * norm_gain + norm_shift


def norm_back(value, norm_gain, grad_rows):
    center = jnp.mean(value, axis=-1, keepdims=True)
    offsets = value - center
    spread = jnp.mean(offsets * offsets, axis=-1, keepdims=True)
    scale = lax.rsqrt(spread + EPSILON)
    normal = offsets * scale
    inner = grad_rows * norm_gain
    grad = scale * (
        inner
        - jnp.mean(inner, axis=-1, keepdims=True)
        - normal * jnp.mean(inner * normal, axis=-1, keepdims=True)
    )
    return grad, jnp.sum(grad_rows * normal, axis=0), jnp.sum(grad_rows, axis=0)


def array_copies(array, refs, held_ref, sems):
    count = len(refs)
    return [
        pltpu.make_async_copy(
            refs[index], held_ref.at[index], sems.at[index]
        )
        for index in range(array, count, count // 4)
    ]


def join_rows(slot_ref, own, refs, held_ref, up_ref, down_ref, sems):
    count = len(refs)
    arrays = count // 4
    step = pl.program_id(0)

    @pl.when(step == 0)
    def _():
        for array in range(arrays):
            for copy in array_copies(array, refs, held_ref, sems):
                copy.start()

    for array in range(arrays):

        @pl.when(step == 2 * array)
        def _(array=array):
            for copy in array_copies(array, refs, held_ref, sems):
                copy.wait()

    rows = held_ref.shape[2]
    near = step // 2
    for number in range(2):
        slot = slot_ref[step, number]
        for half in range(2):
            start = (own if half == 0 else 1 - own) * rows + number * 2 * rows
            where = pl.ds(pl.multiple_of(start, rows), rows)
            up_ref[where, :] = held_ref[half * arrays + near, slot]
            down_ref[where, :] = held_ref[(2 + half) * arrays + near, slot]


def normal_share(value, bell):
    t = 1.0 / (1.0 + (0.3275911 * 2**-0.5) * jnp.abs(value))
    series = 1.061405429
    for term in (-1.453152027, 1.421413741, -0.284496736, 0.254829592):
        series = series * t + term
    tail = (0.5 * series) * (t * bell)
    return jnp.where(value < 0.0, tail, 1.0 - tail)


def feed_forward_kernel(
    count, slot_ref, block_ref, core_ref, first_ref, bias_ref, vectors_ref, cotangent_ref, *refs
):
    (
        act_ref,
        slope_ref,
        hidden_ref,
        grad_ref,
        sums_ref,
        held_ref,
        up_ref,
        down_ref,
        low_ref,
        total_ref,
        sems,
    ) = refs[2 * count :]
    step = pl.program_id(0)

    @pl.when(step == 0)
    def _():
        low_ref[...] = first_ref[...].astype(BF16)
        total_ref[...] = first_ref[...] + vectors_ref[0:1, :]

    join_rows(slot_ref, core_ref[0], refs[: 2 * count], held_ref, up_ref, down_ref, sems)
    inner = dot_nt(low_ref[...], up_ref[...]) + bias_ref[block_ref[step]]
    bell = jnp.exp(-0.5 * inner * inner)
    share = normal_share(inner, bell)
    act = (inner * share).astype(BF16)
    act_ref[0] = act
    slope_ref[0] = (
        share + inner * (bell * (2.0 * jnp.pi) ** -0.5)
    ).astype(BF16)
    total_ref[...] += dot(act, down_ref[...])

    @pl.when(step == pl.num_programs(0) - 1)
    def _():
        value = total_ref[...]
        gain, shift = vectors_ref[1:2, :], vectors_ref[2:3, :]
        offsets = value - jnp.mean(value, axis=-1, keepdims=True)
        scale = lax.rsqrt(jnp.mean(offsets * offsets, axis=-1, keepdims=True) + EPSILON)
        normal = offsets * scale
        hidden_ref[...] = (normal * gain + shift).astype(BF16)
        cotangent = cotangent_ref[...].astype(F32)
        pulled = cotangent * gain
        grad = scale * (
            pulled
            - jnp.mean(pulled, axis=-1, keepdims=True)
            - normal * jnp.mean(pulled * normal, axis=-1, keepdims=True)
        )
        grad_ref[...] = grad
        sums_ref[0:1, :] = jnp.sum(cotangent * normal, axis=0, keepdims=True)
        sums_ref[1:2, :] = jnp.sum(cotangent, axis=0, keepdims=True)
        sums_ref[2:3, :] = jnp.sum(grad.astype(BF16).astype(F32), axis=0, keepdims=True)
        sums_ref[3:8, :] = jnp.zeros((5, sums_ref.shape[1]), F32)


def feed_forward(first, pieces, bias_blocks, vectors, cotangent, slots, block, core):
    words, columns = first.shape
    steps, width = bias_blocks.shape[0], bias_blocks.shape[2]
    up, down = pieces
    whole = lambda shape: pl.BlockSpec(shape, lambda j, *_: (0,) * len(shape))
    tile = pl.BlockSpec((1, words, width), lambda j, *_: (j, 0, 0))
    return pl.pallas_call(
        partial(feed_forward_kernel, len(up)),
        grid_spec=pltpu.PrefetchScalarGridSpec(
            num_scalar_prefetch=3,
            grid=(steps,),
            in_specs=[
                whole(first.shape),
                whole(bias_blocks.shape),
                whole(vectors.shape),
                whole(cotangent.shape),
            ]
            + [ANY] * (len(up) + len(down)),
            out_specs=[tile, tile, whole(first.shape), whole(first.shape), whole((8, columns))],
            scratch_shapes=[
                pltpu.VMEM((len(up) + len(down),) + up[0].shape, BF16),
                pltpu.VMEM((width, columns), BF16),
                pltpu.VMEM((width, columns), BF16),
                pltpu.VMEM((words, columns), BF16),
                pltpu.VMEM((words, columns), F32),
                pltpu.SemaphoreType.DMA((len(up) + len(down),)),
            ],
        ),
        out_shape=(
            jax.ShapeDtypeStruct((steps, words, width), BF16),
            jax.ShapeDtypeStruct((steps, words, width), BF16),
            jax.ShapeDtypeStruct((words, columns), BF16),
            jax.ShapeDtypeStruct((words, columns), F32),
            jax.ShapeDtypeStruct((8, columns), F32),
        ),
        compiler_params=pltpu.CompilerParams(vmem_limit_bytes=56 * MIB),
        cost_estimate=cost(20),
        name="feed_forward",
    )(slots, block, core, first, bias_blocks, vectors, cotangent, *up, *down)


def feed_forward_back_kernel(
    count,
    slot_ref,
    block_ref,
    core_ref,
    grad_ref,
    first_ref,
    act_ref,
    slope_ref,
    value_ref,
    gain_ref,
    *refs,
):
    (
        up_keep_ref,
        up_sent_ref,
        down_keep_ref,
        down_sent_ref,
        bias_ref,
        out_ref,
        sums_ref,
        held_ref,
        up_ref,
        down_ref,
        low_ref,
        low_first_ref,
        total_ref,
        sems,
    ) = refs[2 * count :]
    step = pl.program_id(0)

    @pl.when(step == 0)
    def _():
        total_ref[...] = grad_ref[...]
        low_ref[...] = grad_ref[...].astype(BF16)
        low_first_ref[...] = first_ref[...].astype(BF16)

    join_rows(slot_ref, core_ref[0], refs[: 2 * count], held_ref, up_ref, down_ref, sems)
    low = low_ref[...]
    inner = (dot_nt(low, down_ref[...]) * slope_ref[0].astype(F32)).astype(BF16)
    bias_ref[0] = jnp.sum(inner.astype(F32), axis=0, keepdims=True)
    grad_down = dot_tn(act_ref[0], low).astype(BF16)
    grad_up = dot_tn(inner, low_first_ref[...]).astype(BF16)
    total_ref[...] += dot(inner, up_ref[...])
    rows = up_keep_ref.shape[3]

    def store(value, ref):
        for number in range(4):
            ref[number // 2, 0, number % 2] = value[number * rows : (number + 1) * rows, :]

    @pl.when(step % 2 == 0)
    def _():
        store(grad_up, up_sent_ref)
        store(grad_down, down_sent_ref)

    @pl.when(step % 2 == 1)
    def _():
        store(grad_up, up_keep_ref)
        store(grad_down, down_keep_ref)

    @pl.when(step == pl.num_programs(0) - 1)
    def _():
        value = value_ref[...]
        pulling = total_ref[...]
        offsets = value - jnp.mean(value, axis=-1, keepdims=True)
        scale = lax.rsqrt(jnp.mean(offsets * offsets, axis=-1, keepdims=True) + EPSILON)
        normal = offsets * scale
        pulled = pulling * gain_ref[...]
        grad = scale * (
            pulled
            - jnp.mean(pulled, axis=-1, keepdims=True)
            - normal * jnp.mean(pulled * normal, axis=-1, keepdims=True)
        )
        out_ref[...] = grad
        sums_ref[0:1, :] = jnp.sum(pulling * normal, axis=0, keepdims=True)
        sums_ref[1:2, :] = jnp.sum(pulling, axis=0, keepdims=True)
        sums_ref[2:3, :] = jnp.sum(grad.astype(BF16).astype(F32), axis=0, keepdims=True)
        sums_ref[3:8, :] = jnp.zeros((5, sums_ref.shape[1]), F32)


def feed_forward_back(grad, first, act, slope, value, gain, pieces, slots, block, core):
    words, columns = first.shape
    steps, _, width = act.shape
    up, down = pieces
    rows = width // 4
    whole = lambda shape: pl.BlockSpec(shape, lambda j, *_: (0,) * len(shape))
    tile = pl.BlockSpec((1, words, width), lambda j, *_: (j, 0, 0))
    out = pl.BlockSpec(
        (2, 1, 2, rows, columns), lambda j, slots, block, core: (0, block[j] % (steps // 2), 0, 0, 0)
    )
    part = jax.ShapeDtypeStruct((2, steps // 2, 2, rows, columns), BF16)
    return pl.pallas_call(
        partial(feed_forward_back_kernel, len(up)),
        grid_spec=pltpu.PrefetchScalarGridSpec(
            num_scalar_prefetch=3,
            grid=(steps,),
            in_specs=[
                whole(grad.shape),
                whole(first.shape),
                tile,
                tile,
                whole(value.shape),
                whole(gain.shape),
            ]
            + [ANY] * (len(up) + len(down)),
            out_specs=[
                out,
                out,
                out,
                out,
                pl.BlockSpec((1, 1, width), lambda j, slots, block, core: (block[j], 0, 0)),
                whole(first.shape),
                whole((8, columns)),
            ],
            scratch_shapes=[
                pltpu.VMEM((len(up) + len(down),) + up[0].shape, BF16),
                pltpu.VMEM((width, columns), BF16),
                pltpu.VMEM((width, columns), BF16),
                pltpu.VMEM((words, columns), BF16),
                pltpu.VMEM((words, columns), BF16),
                pltpu.VMEM((words, columns), F32),
                pltpu.SemaphoreType.DMA((len(up) + len(down),)),
            ],
        ),
        out_shape=(
            part,
            part,
            part,
            part,
            jax.ShapeDtypeStruct((steps, 1, width), F32),
            jax.ShapeDtypeStruct((words, columns), F32),
            jax.ShapeDtypeStruct((8, columns), F32),
        ),
        compiler_params=pltpu.CompilerParams(vmem_limit_bytes=56 * MIB),
        cost_estimate=cost(25),
        name="feed_forward_back",
    )(slots, block, core, grad, first, act, slope, value, gain, *up, *down)


def softmax_parts(query, key):
    scores = dot_nt(query, key)
    scaling = HEAD_DIM ** (-0.5) * 1.4426950408889634
    exponent = jnp.exp2((scores - jnp.max(scores, axis=-1, keepdims=True)) * scaling)
    return exponent, 1.0 / jnp.sum(exponent, axis=-1, keepdims=True)


def attend_kernel(query_ref, key_ref, value_ref, out_ref):
    for start in range(0, LANES, HEAD_DIM):
        head = slice(start, start + HEAD_DIM)
        exponent, scale = softmax_parts(query_ref[:, head], key_ref[:, head])
        attention = (exponent * scale).astype(BF16)
        out_ref[:, head] = dot(attention, value_ref[:, head]).astype(BF16)


def third(number, words, thirds):
    return pl.BlockSpec((words, LANES), lambda j: (0, number * thirds + j))


def attend(qkv):
    words = qkv.shape[0]
    pairs = qkv.shape[1] // (3 * LANES)
    return pl.pallas_call(
        attend_kernel,
        grid=(pairs,),
        in_specs=[third(number, words, pairs) for number in range(3)],
        out_specs=third(0, words, pairs),
        out_shape=jax.ShapeDtypeStruct((words, pairs * LANES), BF16),
        compiler_params=pltpu.CompilerParams(vmem_limit_bytes=32 * MIB),
        cost_estimate=cost(12),
        name="attend",
    )(qkv, qkv, qkv)


def attend_back_kernel(
    query_ref, key_ref, value_ref, grad_ref, grad_query_ref, grad_key_ref, grad_value_ref
):
    scaling = HEAD_DIM ** (-0.5)
    for start in range(0, LANES, HEAD_DIM):
        head = slice(start, start + HEAD_DIM)
        query, key = query_ref[:, head], key_ref[:, head]
        grad = grad_ref[:, head]
        exponent, scale = softmax_parts(query, key)
        attention = exponent * scale
        grad_attention = dot_nt(grad, value_ref[:, head])
        inner = jnp.sum(grad_attention * attention, axis=-1, keepdims=True)
        grad_scores = (attention * (grad_attention - inner)).astype(BF16)
        grad_value_ref[:, head] = dot_tn(attention.astype(BF16), grad).astype(BF16)
        grad_query_ref[:, head] = (dot(grad_scores, key) * scaling).astype(BF16)
        grad_key_ref[:, head] = (dot_tn(grad_scores, query) * scaling).astype(BF16)


def attend_back(qkv, grad_context):
    words = qkv.shape[0]
    pairs = qkv.shape[1] // (3 * LANES)
    out = third(0, words, pairs)
    return jnp.concatenate(
        pl.pallas_call(
            attend_back_kernel,
            grid=(pairs,),
            in_specs=[third(number, words, pairs) for number in range(3)] + [out],
            out_specs=(out, out, out),
            out_shape=(jax.ShapeDtypeStruct(grad_context.shape, BF16),) * 3,
            compiler_params=pltpu.CompilerParams(vmem_limit_bytes=32 * MIB),
            cost_estimate=cost(17),
        name="attend_back",
        )(qkv, qkv, qkv, grad_context),
        axis=1,
    )


def gather_plain(value, axis):
    return lax.all_gather(value, "wide", axis=axis, tiled=True)


def plain_pieces(weight, chunks):
    whole = gather_plain(weight, 1)
    rows = whole.shape[0] // (2 * chunks)
    width = whole.shape[1] // 16
    halves = []
    for half in range(2):
        pieces = []
        for chunk in range(chunks):
            start = (half * chunks + chunk) * rows
            arrays = []
            for near in range(4):
                slots = []
                for slot in range(4):
                    block = (-slot % 4) * 4 + near
                    slots.append(whole[start : start + rows, block * width : (block + 1) * width])
                arrays.append(jnp.stack(slots).reshape(2, 2, rows, width))
            pieces.append(arrays)
        halves.append(pieces)
    return halves


def vector_rows(vectors):
    rows, places, start = [], [], 0
    for vector in vectors:
        count = -(-vector.shape[0] // LANES)
        padded = jnp.pad(vector, (0, count * LANES - vector.shape[0]))
        rows.append(padded.reshape(count, LANES))
        places.append((start, count, vector.shape[0]))
        start += count
    return jnp.pad(jnp.concatenate(rows, axis=0), ((0, -start % 16), (0, 0))), places


def plain_rows(whole):
    rows = whole.shape[0] // 16
    arrays = []
    for half in range(2):
        for near in range(4):
            starts = [((-slot % 4) * 4 + near) * rows + half * rows // 2 for slot in range(4)]
            arrays.append(jnp.stack([whole[start : start + rows // 2] for start in starts]))
    return arrays


def body(
    permutes,
    wide,
    devices,
    char_ids,
    word_lengths,
    type_ids,
    cotangent,
    character_embedding_table,
    conv_weight,
    conv_bias,
    high_weight,
    high_bias,
    proj_weight,
    proj_bias,
    pos_table,
    type_table,
    embed_gain,
    embed_shift,
    qkv_weight,
    attn_bias,
    out_weight,
    out_bias,
    attn_gain,
    attn_shift,
    up_weight,
    up_bias,
    down_weight,
    down_bias,
    ffn_gain,
    ffn_shift,
):
    layers, features = high_weight.shape[:2]
    words, chars = char_ids.shape[1:]
    model_width = proj_weight.shape[1]
    conv_rows = conv_weight.shape[0]
    lengths = word_lengths[0]
    vectors = [high_bias[layer] for layer in range(layers)] + [
        attn_bias,
        type_table[0],
        type_table[1],
        proj_bias,
        embed_gain,
        embed_shift,
        out_bias,
        attn_gain,
        attn_shift,
        up_bias,
        down_bias,
        ffn_gain,
        ffn_shift,
    ]
    conv_block = jnp.pad(
        jnp.concatenate([conv_weight, conv_bias[None]], axis=0),
        ((0, LANES - conv_rows - 1), (0, 0)),
    )
    vector_block, places = vector_rows(vectors)

    if permutes:
        net = Exchange()
        window, launch = net.window, net.launch
        core_index, z, y, x = net.core, net.z, net.y, net.x
        net.load(
            "small",
            jnp.concatenate([conv_block, vector_block, pos_table.T.reshape(-1, LANES)], axis=0),
            whole=True,
        )
        chunk_rows = features // 4
        net.load("L00", high_weight[0], chunk_rows, 0)
        (
            net.state["L00"],
            net.state["small"],
            char_ids,
            lengths,
            high_weight,
            qkv_weight,
            up_weight,
        ) = lax.optimization_barrier(
            (
                net.state["L00"],
                net.state["small"],
                char_ids,
                lengths,
                high_weight,
                qkv_weight,
                up_weight,
            )
        )
        for layer, chunk in ((0, 1), (1, 0), (1, 1)):
            net.load(f"L{layer}{chunk}", high_weight[layer], chunk_rows, chunk * chunk_rows)
        encoder_splits = [
            qkv_weight.shape[1],
            out_weight.shape[0],
            proj_weight.shape[0],
        ]
        net.load(
            "e",
            jnp.concatenate(
                [qkv_weight.T, out_weight, proj_weight],
                axis=0,
            ),
        )
        net.load("up", up_weight.T)
        net.load("down", down_weight)
        net.ring_step("L00", 1)
        net.move("smallx", "small", "x")
        net.move("smally", "small", "y")
    else:
        window = lambda values, hold=(): values
        launch = window
        core_index = z = y = x = jnp.zeros((), jnp.int32)
    prep = sort_words(char_ids[0], lengths, chars // GROUP + 2)
    table_blocks = table_lanes(character_embedding_table)
    prep, table_blocks = window((prep, table_blocks))
    if permutes:
        net.ring_step("L00", 2)
        net.move("smallxy", "smallx", "y")
        net.move("ex", "e", "x")
        net.move("ey", "e", "y")
        window(())
        net.ring_step("L00", 3)
        net.put("smallo0", jnp.stack([net.state["small" + part] for part in ("", "x", "y", "xy")]))
        net.turn_ring("small", 1)
        net.move("exy", "ex", "y")
        window(())
        net.ring_done("L00")
        net.plan_move("L00o", "x", "y")
        net.plan("smallo2", net.state["smallo1"], "z")
        launch(())
        net.ring_both("L01")
        net.state["eo0"] = jnp.stack([net.state["e" + part] for part in ("", "x", "y", "xy")])
        prep, table_blocks = window((prep, table_blocks))
        net.ring_done("L01")
        net.plan_move("L01o", "x", "y")
        net.plan("smallo3", net.state["smallo2"], "z")
        prep, table_blocks = launch((prep, table_blocks))
        net.ring_both("L10")
        net.swap_chain("L00o", "L00ox", "L00oy")
    char_groups = embed_characters(prep, table_blocks)
    char_groups = window(char_groups)

    if permutes:
        net.ring_done("L10")
        conv_all, whole_vectors, pos_all = place_small(
            [net.state[f"smallo{step}"] for step in range(4)],
            net.place(True),
            LANES,
            [vector_block.shape[0], pos_table.size // LANES],
        )
    else:
        conv_all = gather_plain(conv_block, 1)
        whole_vectors = lax.all_gather(vector_block, "wide", axis=0, tiled=False)
        pos_all = gather_plain(pos_table.T, 0)
    filters = conv_all.shape[1]
    row = jnp.arange(LANES)[:, None]
    usable = row // CHAR_DIM < filter_widths(filters)[None, :]
    half_matrix = jnp.where(usable | (row >= conv_rows), conv_all * BF16(0.5), BF16(0.0))
    if permutes:
        net.plan("L00oxy", net.state["L00ox"], "y")
        net.plan("L01oxy", net.state["L01oy"], "x")
        net.plan("eo1", net.state["eo0"], "z")
        half_matrix = launch(half_matrix)
        net.swap_chain("L01o", "L01ox", "L01oy")
    pooled = conv_forward(prep, char_groups, half_matrix)
    pooled, whole_vectors, pos_all = window((pooled, whole_vectors, pos_all))
    whole = [
        whole_vectors[:, start : start + count].reshape(wide, -1)[:, :size].reshape(-1)
        for start, count, size in places
    ]
    if permutes:
        net.plan_move("L10o", "x", "y")
        launch(())
        net.ring_both("L11")
        net.swap_chain("L00oxy", "L01oxy", "eo0")
        pooled, whole, pos_all = window((pooled, whole, pos_all))
        net.ring_done("L11")
        net.plan_move("L11o", "x", "y")
        net.plan("eo2", net.state["eo1"], "z")
        pooled = launch(pooled)
        net.swap_chain("L10o", "L10ox", "L10oy")
        pieces = [net.layer("L0", 2)]
    else:
        pieces = [plain_pieces(high_weight[layer], 2) for layer in range(layers)]
    high_bias_all, attn_bias_all = whole[:layers], whole[layers]
    (
        type_zero,
        type_one,
        proj_bias_all,
        gain_zero,
        shift_zero,
        out_bias_all,
        gain_one,
        shift_one,
        up_bias_all,
        down_bias_all,
        gain_two,
        shift_two,
    ) = (value.astype(F32) for value in whole[layers + 1 :])
    width = 2 * features // 16
    order = jnp.arange(8)
    near, low_slot = order // 2, order % 2
    slot_z = (z - low_slot) % 4
    place = ((slot_z & 1) * 4 + (y ^ (near >> 1)) * 2 + (x ^ (near & 1))).astype(jnp.int32)
    select = (slot_z // 2).astype(jnp.int32)
    core = core_index[None].astype(jnp.int32)
    bias_blocks = [bias.astype(F32).reshape(16, 1, width) for bias in high_bias_all]
    first_layer = highway_forward(pooled, pieces[0], bias_blocks[0], place, select, core)
    first_layer = window(first_layer)

    if permutes:
        net.plan("L10oxy", net.state["L10ox"], "y")
        net.plan("L11oxy", net.state["L11oy"], "x")
        net.plan("eo3", net.state["eo2"], "z")
        first_layer, pos_all = launch((first_layer, pos_all))
        net.swap_chain("L11o", "L11ox", "L11oy", "eo1", "eo2")
    turned = [turn(first_layer[3])]
    pos_rows = pos_all.reshape(model_width, words).T.astype(F32)
    turned, pos_rows = window((turned, pos_rows))
    if permutes:
        net.plan_swap("L10oxy", "L11oxy", "eo3")
        net.plan_ring("up", 1)
        net.plan_ring("down", 1)
        first_layer = net.stage(first_layer)
        net.plan_ring("up", 2)
        net.plan_ring("down", 2)
        first_layer = launch(first_layer)
        pieces.append(net.layer("L1", 2))
        qkv_all, out_all, proj_all = net.rows(
            [net.state[f"eo{step}"] for step in range(4)],
            [net.state[f"eo{step}c"] for step in range(4)],
            encoder_splits,
            True,
        )
    else:
        qkv_all, out_all, proj_all = (
            gather_plain(value, 0) for value in (qkv_weight.T, out_weight, proj_weight)
        )
    second_layer = highway_forward(first_layer[0], pieces[1], bias_blocks[1], place, select, core)
    second_layer = window(second_layer)
    if permutes:
        net.plan_ring("up", 3)
        net.plan_ring("down", 3)
        second_layer = launch(second_layer)
    states = [pooled, first_layer[0], second_layer[0]]
    transforms = [first_layer[1], second_layer[1]]
    gatings = [first_layer[2], second_layer[2]]
    perm, sorted_lengths = prep[0], prep[2]
    last = dot_tn(perm, states[2].astype(BF16)).astype(BF16)
    word_vec = dot(last, proj_all) + proj_bias_all
    type_rows = jnp.where(type_ids[0][:, None] == 1, type_one[None], type_zero[None])
    summed = word_vec + pos_rows + type_rows
    embedded = norm_rows(summed, gain_zero, shift_zero)
    turned.append(turn(second_layer[3]))
    summed, embedded, last, turned = window((summed, embedded, last, turned))

    if permutes:
        net.ring_done("up")
        net.ring_done("down")
        net.plan_move("upo", "x", "y")
        net.plan_move("downo", "x", "y")
        embedded = launch(embedded)
        net.swap_chain("upo", "downo")
    low_embedded = embedded.astype(BF16)
    bias_three = jnp.concatenate(
        [
            attn_bias_all[:model_width],
            jnp.zeros((model_width,), BF16),
            attn_bias_all[model_width:],
        ]
    ).astype(F32)
    qkv = (dot_nt(low_embedded, qkv_all) + bias_three).astype(BF16)
    context = attend(qkv)
    if permutes:
        context = window(context)
        net.plan("upoxy", net.state["upox"], "y")
        net.plan("downoxy", net.state["downoy"], "x")
        context = launch(context)
        net.swap_chain("upox", "upoy", "downox", "downoy")
    first_in = embedded + (dot(context, out_all) + out_bias_all)
    first = norm_rows(first_in, gain_one, shift_one)
    if permutes:
        first_in, first = window((first_in, first))
        net.plan_swap("upoxy", "downoxy")
        first = launch(first)
        feed_pieces = [net.near(name) + net.near(name, "c") for name in ("up", "down")]
    else:
        feed_pieces = [
            plain_rows(gather_plain(value, 0)) for value in (up_weight.T, down_weight)
        ]
    half_of = jnp.where(order % 2 == 0, 1 - core_index, core_index)
    slots = (z - (2 * half_of[:, None] + jnp.arange(2)[None, :])) % 4
    slots = slots.astype(jnp.int32)
    feed_block = (half_of * 4 + (y ^ (near >> 1)) * 2 + (x ^ (near & 1))).astype(jnp.int32)
    feed_rows = up_bias_all.shape[0] // 16
    feed_bias = jnp.moveaxis(up_bias_all.reshape(2, 2, 4, feed_rows), 1, 2).reshape(8, 1, -1)
    act, slope, hidden_out, grad_second, last_sums = feed_forward(
        first,
        feed_pieces,
        feed_bias,
        jnp.stack([down_bias_all, gain_two, shift_two]),
        cotangent[0],
        slots,
        feed_block,
        core,
    )
    grad_ffn_gain, grad_ffn_shift, grad_down_bias = last_sums[0], last_sums[1], last_sums[2]

    def sum_rows(grads, order):
        if permutes:
            return Reduction(net, *net.split(grads), order)
        return PlainReduction(grads, 0)

    def send_layer(layer, mixed, first, rows):
        sent = highway_weight_gradient(1 - core, turned[layer], mixed, first, rows, width // 2)
        key = f"layer{layer}_{first}"
        if permutes:
            net.plan(key, sent, "c")
        return layer, mixed, first, rows, (key if permutes else sent, 0)

    def keep_layer(job, order):
        layer, mixed, first, rows, (key, part) = job
        keep = highway_weight_gradient(
            core,
            turned[layer],
            mixed,
            first,
            rows,
            width // 2,
            net.state[key] if permutes else None,
            part,
        )
        if permutes:
            return Reduction(net, keep, None, order)
        other = key[:, part * rows : (part + 1) * rows]
        whole = jnp.moveaxis(jnp.concatenate([keep, other], axis=0), 1, 0).reshape(rows, -1)
        return PlainReduction([whole], 1)

    def sum_feed(keep, sent, order):
        keep, sent = (value.reshape((16,) + value.shape[3:]) for value in (keep, sent))
        if permutes:
            return Reduction(net, keep, sent, order)
        return sum_rows([jnp.concatenate([keep, sent], axis=0).reshape(-1, model_width)], "")

    def ring_of(*sums, both=False):
        return Ring(net, sums, both) if permutes else sums

    def advance(*sums):
        if permutes:
            for item in sums:
                item.step()

    def ready(*sums):
        if permutes:
            for item in sums:
                item.step(net.plan)

    def held(*sums):
        return tuple(item.key for item in sums) if permutes else ()

    def together(*sums, hold=()):
        if permutes:
            ready(*sums)
            launch(())
            window((), held(*hold))

    up_keep, up_sent, down_keep, down_sent, bias_sums, grad_resid, norm_sums = feed_forward_back(
        grad_second,
        first,
        act,
        slope,
        first_in,
        gain_one[None],
        feed_pieces,
        slots,
        feed_block,
        core,
    )
    grad_up_bias = jnp.moveaxis(bias_sums.reshape(2, 4, 2, feed_rows), 2, 1).reshape(-1)
    grad_attn_gain, grad_attn_shift, grad_out_bias = norm_sums[0], norm_sums[1], norm_sums[2]
    up_keep, up_sent, down_keep, down_sent, grad_resid = window(
        (up_keep, up_sent, down_keep, down_sent, grad_resid)
    )

    sum_up = sum_feed(up_keep, up_sent, "cxy")
    sum_down = sum_feed(down_keep, down_sent, "cyx")
    ready(sum_down, sum_up)
    grad_resid = launch(grad_resid)
    grad_branch = grad_resid.astype(BF16)
    grad_context = dot_nt(grad_branch, out_all).astype(BF16)
    grad_resid, grad_context = window((grad_resid, grad_context))
    ready(sum_down, sum_up)
    grad_context = launch(grad_context)
    grad_qkv = attend_back(qkv, grad_context)
    grad_resid, grad_qkv = window((grad_resid, grad_qkv))

    ready(sum_down, sum_up)
    grad_qkv, grad_resid = launch((grad_qkv, grad_resid))
    qkv_sums = column_sum(grad_qkv)
    grad_attn_bias = jnp.concatenate([qkv_sums[:model_width], qkv_sums[2 * model_width :]])
    grad_summed, grad_embed_gain, grad_embed_shift = norm_back(
        summed, gain_zero, grad_resid + dot(grad_qkv, qkv_all)
    )
    grad_word = grad_summed.astype(BF16)
    grad_proj_bias = column_sum(grad_word)
    running = dot_nt(dot(perm, grad_word).astype(BF16), proj_all)
    running = window(running)
    ring_feed = ring_of(sum_up, sum_down)
    ready(ring_feed)
    running = launch(running)
    mixed_one, sums_one, running = highway_backward(
        running, states[1], transforms[1], gatings[1], pieces[1], place, select, core
    )
    mixed_one, running, grad_qkv, grad_branch, grad_word, grad_summed = window(
        (mixed_one, running, grad_qkv, grad_branch, grad_word, grad_summed)
    )
    type_hot = (type_ids[0] == 1).astype(F32)[:, None]
    vector_grads = [
        grad_proj_bias,
        jnp.sum((1.0 - type_hot) * grad_summed, axis=0),
        jnp.sum(type_hot * grad_summed, axis=0),
        grad_embed_gain,
        grad_embed_shift,
        grad_attn_bias,
        grad_out_bias,
        grad_attn_gain,
        grad_attn_shift,
        grad_up_bias,
        grad_down_bias,
        grad_ffn_gain,
        grad_ffn_shift,
    ]

    half_rows, quarter = features // 2, features // 4

    def quarters(jobs, layer, mixed):
        return [
            (layer, mixed, start * quarter, quarter, (jobs[start // 2][-1][0], start % 2))
            for start in range(4)
        ]

    jobs = [send_layer(1, mixed_one, start, half_rows) for start in (0, half_rows)]
    ready(ring_feed)
    mixed_one, grad_qkv, grad_branch, grad_word, grad_summed = launch(
        (mixed_one, grad_qkv, grad_branch, grad_word, grad_summed)
    )
    grad_pos = turn(grad_summed)
    encoder_grads = [
        dot_tn(grad_qkv, low_embedded),
        dot_tn(context, grad_branch),
        dot_tn(last, grad_word),
    ]
    if permutes:
        encoder_grads.append(grad_pos.reshape(-1, model_width))
        sum_encoder = sum_rows(encoder_grads, "c321xy")
        mixed_one, running, sum_encoder.terms, sum_encoder.sent = window(
            (mixed_one, running, sum_encoder.terms, sum_encoder.sent)
        )
    else:
        sum_encoder = sum_rows(encoder_grads, "")
        sum_pos = sum_rows([grad_pos], "")

    jobs = quarters(jobs, 1, mixed_one)
    one = [None] * 4
    one[0], one[2] = keep_layer(jobs[0], "yx"), keep_layer(jobs[2], "xy")
    ready(one[0], one[2], sum_encoder, ring_feed)
    running = launch(running)
    mixed_zero, sums_zero, running = highway_backward(
        running, states[0], transforms[0], gatings[0], pieces[0], place, select, core
    )
    mixed_zero, running = window((mixed_zero, running))

    one[1], one[3] = keep_layer(jobs[1], "yx"), keep_layer(jobs[3], "xy")
    jobs = [send_layer(0, mixed_zero, start, half_rows) for start in (0, half_rows)]
    grad_scaled = running * (0.5 / sorted_lengths.astype(F32))[:, None]
    ready(one[1], one[3], sum_encoder)
    grad_scaled = launch(grad_scaled)
    matrix_turned, grad_groups = conv_backward(prep, char_groups, half_matrix, grad_scaled)
    mixed_zero, matrix_turned, grad_groups = window((mixed_zero, matrix_turned, grad_groups))

    ready(*one, sum_encoder)
    mixed_zero, grad_groups = launch((mixed_zero, grad_groups))
    jobs = quarters(jobs, 0, mixed_zero)
    zero = [keep_layer(job, order_) for job, order_ in zip(jobs, ("yx", "yx", "xy", "xy"))]
    first_two = (zero[0], zero[2])
    terms = [item.terms for item in zero] if permutes else ()
    grad_table = table_gradient(prep, grad_groups, character_embedding_table.shape[0])
    first_sum, vector_places = vector_rows(vector_grads)
    last_sum, high_places = vector_rows(
        [sums_zero.reshape(-1), sums_one.reshape(-1), grad_table.reshape(-1)]
    )
    high_places = [(first_sum.shape[0] + start, *rest) for start, *rest in high_places]
    last_sum = jnp.concatenate([first_sum, last_sum], axis=0)
    terms, last_sum = window((terms, last_sum))
    last_sum = Small(net, last_sum) if permutes else lax.psum(last_sum, ("narrow", "wide"))
    for item, value in zip(zero, terms):
        item.terms = value

    if permutes:
        conv_keep, conv_sent = net.split([matrix_turned])
        net.plan("conv", conv_sent, "c")
    else:
        sum_conv = sum_rows([matrix_turned], "")
    ready(*first_two, sum_encoder, last_sum)
    launch(())
    window(())
    if permutes:
        conv_total = total_of([conv_keep, net.state["conv"]]).astype(BF16)
        conv_total = conv_total.reshape((4, 2, 2) + conv_total.shape[1:])
        zero[3].terms = [jnp.concatenate([zero[3].terms[0], conv_total], axis=3)]

    ring_one = ring_of(*one)
    together(zero[1], zero[3], *first_two, ring_one)
    together(zero[1], zero[3], ring_one, last_sum)
    ring_first = ring_of(*first_two, both=True)
    together(ring_first, ring_one, sum_encoder, last_sum)
    ring_last = ring_of(zero[1], zero[3], both=True)
    together(ring_first, ring_last, sum_encoder, last_sum)
    together(ring_last, last_sum)
    total = last_sum.result() if permutes else last_sum

    device = lax.axis_index("narrow") * wide + lax.axis_index("wide")

    def whole_vector(total, where):
        start, count, size = where
        return total[start : start + count].reshape(-1)[:size]

    def own_part(total, where):
        piece = where[2] // devices
        return lax.dynamic_slice_in_dim(whole_vector(total, where), device * piece, piece, 0)

    results = [own_part(total, where) for where in vector_places]
    (
        sum_proj_bias,
        sum_type_zero,
        sum_type_one,
        sum_embed_gain,
        sum_embed_shift,
        sum_attn_bias,
        sum_out_bias,
        sum_attn_gain,
        sum_attn_shift,
        sum_up_bias,
        sum_down_bias,
        sum_ffn_gain,
        sum_ffn_shift,
    ) = results
    sum_high_bias = jnp.stack([own_part(total, where) for where in high_places[:layers]])
    sum_table = whole_vector(total, high_places[layers]).reshape(
        character_embedding_table.shape
    )

    def rows_of(item, sizes):
        total = item.result()
        if not permutes:
            return total
        pieces, start = [], 0
        for size in sizes:
            pieces.append(total[start : start + size])
            start += size
        return pieces

    qkv_rows, sum_out, sum_proj, *rest = rows_of(
        sum_encoder,
        [
            qkv_all.shape[0] // devices,
            out_all.shape[0] // devices,
            proj_all.shape[0] // devices,
            words * model_width // devices // model_width,
        ],
    )
    if permutes:
        pos_rows = rest[0].reshape(-1, words)
    else:
        (pos_rows,) = sum_pos.result()
    if permutes:
        up_rows, down_rows = jnp.split(ring_feed.result(), 2)
    else:
        (up_rows,), (down_rows,) = sum_up.result(), sum_down.result()
    if permutes:
        first_rows, last_rows = ring_first.result(), ring_last.result()
        conv_turned = last_rows[2 * quarter :]
    else:
        (conv_turned,) = sum_conv.result()
    own_filters = lax.dynamic_slice_in_dim(
        filter_widths(filters), device * (filters // devices), filters // devices
    )
    taps = jnp.arange(conv_rows)[:, None] // CHAR_DIM
    sum_conv_weight = jnp.where(taps < own_filters[None, :], conv_turned[:, :conv_rows].T, 0.0)

    if permutes:
        parts = [first_rows[:quarter], last_rows[:quarter], first_rows[quarter:], last_rows[quarter : 2 * quarter]]
        high_rows = [jnp.concatenate(parts, axis=0), ring_one.result()]
    else:
        high_rows = [
            jnp.concatenate([part for item in sums for part in item.result()], axis=0)
            for sums in (zero, one)
        ]

    return (
        hidden_out[None],
        sum_table,
        sum_conv_weight,
        conv_turned[:, conv_rows],
        jnp.stack(high_rows),
        sum_high_bias,
        sum_proj,
        sum_proj_bias,
        pos_rows.T,
        jnp.stack([sum_type_zero, sum_type_one]),
        sum_embed_gain,
        sum_embed_shift,
        qkv_rows.T,
        sum_attn_bias,
        sum_out,
        sum_out_bias,
        sum_attn_gain,
        sum_attn_shift,
        up_rows.T,
        sum_up_bias,
        down_rows,
        sum_down_bias,
        sum_ffn_gain,
        sum_ffn_shift,
    )


def solution(mesh):
    narrow, wide = mesh.shape["narrow"], mesh.shape["wide"]
    both = ("narrow", "wide")
    placed = (
        P(both, None, None),
        P(both, None),
        P(both, None),
        P(both, None, None),
        P(),
        P(None, "wide"),
        P("wide"),
        P(None, None, "wide"),
        P(None, "wide"),
        P("wide", None),
        P("wide"),
        P(None, "wide"),
        P(None, "wide"),
        P("wide"),
        P("wide"),
        P(None, "wide"),
        P("wide"),
        P("wide", None),
        P("wide"),
        P("wide"),
        P("wide"),
        P(None, "wide"),
        P("wide"),
        P("wide", None),
        P("wide"),
        P("wide"),
        P("wide"),
    )
    return jax.shard_map(
        partial(body, (narrow, wide) == (2, 16), wide, narrow * wide),
        mesh=mesh,
        in_specs=placed,
        out_specs=(
            P(both, None, None),
            P(),
            P(None, both),
            P(both),
            P(None, None, both),
            P(None, both),
            P(both, None),
            P(both),
            P(None, both),
            P(None, both),
            P(both),
            P(both),
            P(None, both),
            P(both),
            P(both, None),
            P(both),
            P(both),
            P(both),
            P(None, both),
            P(both),
            P(both, None),
            P(both),
            P(both),
            P(both),
        ),
        check_vma=False,
    )
```

```python
from functools import partial

import jax
import jax.numpy as jnp
from jax import lax
from jax.experimental import pallas as pl
from jax.experimental.pallas import tpu as pltpu
from jax.sharding import PartitionSpec as P

HEADS = 12
HEAD_DIM = 64
CHAR_DIM = 16
TAPS = 7
EPSILON = 1e-12

LANES = 128
GROUP = LANES // CHAR_DIM
BLOCK_WORDS = 32
CHUNK_BLOCKS = 16
CHUNK = BLOCK_WORDS * CHUNK_BLOCKS
TABLE_PAD = 384
ROW_TILE = 128
BIAS_LANE = TAPS * CHAR_DIM

F32 = jnp.float32
BF16 = jnp.bfloat16
VMEM = pl.BlockSpec(memory_space=pltpu.VMEM)
SMEM = pl.BlockSpec(memory_space=pltpu.SMEM)
MIB = 1024 * 1024


def cost(microseconds):
    return pl.CostEstimate(
        flops=int(microseconds * 1.1e9), bytes_accessed=int(microseconds * 3e6), transcendentals=0
    )


def dot(left, right):
    return lax.dot_general(left, right, (((1,), (0,)), ((), ())), preferred_element_type=F32)


def dot_nt(left, right):
    return lax.dot_general(left, right, (((1,), (1,)), ((), ())), preferred_element_type=F32)


def dot_tn(left, right):
    return lax.dot_general(left, right, (((0,), (0,)), ((), ())), preferred_element_type=F32)


def column_sum(values):
    return jnp.sum(values.astype(F32), axis=0)


def filter_widths(filter_count):
    column = jnp.arange(filter_count)
    widths = jnp.ones((filter_count,), jnp.int32)
    for exponent in range(6):
        widths = widths + (column >= filter_count * 2**exponent // 64).astype(jnp.int32)
    return widths


def sort_words(char_ids, lengths, groups):
    words, chars = char_ids.shape
    index = jnp.arange(words)
    longer = lengths[None, :] > lengths[:, None]
    tie = (lengths[None, :] == lengths[:, None]) & (index[None, :] < index[:, None])
    rank = jnp.sum((longer | tie).astype(jnp.int32), axis=1)
    perm = (rank[None, :] == index[:, None]).astype(BF16)
    live = jnp.arange(chars)[None, :] < lengths[:, None]
    shifted = jnp.where(live, char_ids + 1, 0)
    packed = jnp.concatenate(
        [shifted >> 4, shifted & 15, lengths[:, None]], axis=1
    ).astype(BF16)
    sorted_packed = dot(perm, packed).astype(jnp.int32)
    ids = (sorted_packed[:, :chars] << 4) + sorted_packed[:, chars : 2 * chars] - 1
    ids = jnp.pad(ids, ((0, 0), (0, GROUP * groups - chars)), constant_values=-1)
    sorted_lengths = sorted_packed[:, 2 * chars]
    tile_count = words // BLOCK_WORDS
    tile_max = jnp.max(sorted_lengths.reshape(tile_count, BLOCK_WORDS), axis=1)
    cum = jnp.cumsum(tile_max)
    total = cum[-1]
    block = jnp.arange(tile_count * chars + CHUNK_BLOCKS)
    tile = jnp.sum((block[:, None] >= cum[None, :]).astype(jnp.int32), axis=1)
    start = jnp.sum(
        jnp.where(tile[:, None] == jnp.arange(tile_count)[None, :], (cum - tile_max)[None, :], 0),
        axis=1,
    )
    valid = block < total
    position = jnp.where(valid, block - start, chars).astype(jnp.int32)
    tile = jnp.where(valid, tile, 0).astype(jnp.int32)
    chunks = (total + CHUNK_BLOCKS - 1) // CHUNK_BLOCKS
    reach = jnp.sum(
        (sorted_lengths[None, :] > GROUP * jnp.arange(groups - 1)[:, None]).astype(jnp.int32), axis=1
    )
    scalars = jnp.concatenate([chunks[None], (reach + ROW_TILE - 1) // ROW_TILE]).astype(jnp.int32)
    return perm, ids, sorted_lengths, scalars, tile, position


def build_windows(chunk, tile_ref, pos_ref, g_ref, len_ref, x_ref):
    lane = lax.broadcasted_iota(jnp.int32, (BLOCK_WORDS, LANES), 1)
    for b in range(CHUNK_BLOCKS):
        block = chunk * CHUNK_BLOCKS + b
        row = pl.multiple_of(tile_ref[block] * BLOCK_WORDS, BLOCK_WORDS)
        position = pos_ref[block]
        group = position >> 3
        offset = (position & 7) * CHAR_DIM
        shift = lax.rem(LANES - offset, LANES)
        here = pltpu.roll(g_ref[group, pl.ds(row, BLOCK_WORDS), :].astype(F32), shift, 1)
        after = pltpu.roll(g_ref[group + 1, pl.ds(row, BLOCK_WORDS), :].astype(F32), shift, 1)
        live = (len_ref[pl.ds(row, BLOCK_WORDS), :] > position).astype(F32)
        value = jnp.where(lane < LANES - offset, here, after)
        value = jnp.where(lane < BIAS_LANE, value, jnp.where(lane == BIAS_LANE, live, 0.0))
        x_ref[b * BLOCK_WORDS : (b + 1) * BLOCK_WORDS, :] = value.astype(BF16)


def embed_kernel(scalar_ref, ids_ref, table_ref, g_ref):
    groups = g_ref.shape[0]
    g_ref[...] = jnp.zeros_like(g_ref)
    identity = lax.broadcasted_iota(jnp.int32, (ROW_TILE, TABLE_PAD), 1)
    for group in range(groups - 1):

        def embed(step, carry, group=group):
            row = pl.multiple_of(step * ROW_TILE, ROW_TILE)
            total = jnp.zeros((ROW_TILE, LANES), F32)
            for k in range(GROUP):
                column = group * GROUP + k
                hot = (ids_ref[pl.ds(row, ROW_TILE), column : column + 1] == identity).astype(F32)
                total = total + dot(hot.astype(BF16), table_ref[k])
            g_ref[group, pl.ds(row, ROW_TILE), :] = total.astype(BF16)
            return carry

        lax.fori_loop(0, scalar_ref[1 + group], embed, 0)


def embed_characters(prep, table_blocks):
    _, ids, _, scalars, _, _ = prep
    return pl.pallas_call(
        embed_kernel,
        out_shape=jax.ShapeDtypeStruct((ids.shape[1] // GROUP, ids.shape[0], LANES), BF16),
        in_specs=[SMEM, VMEM, VMEM],
        out_specs=VMEM,
        compiler_params=pltpu.CompilerParams(vmem_limit_bytes=32 * MIB),
        cost_estimate=cost(5),
        name="embed_characters",
    )(scalars, ids, table_blocks)


def conv_forward_kernel(
    scalar_ref, tile_ref, pos_ref, g_ref, w_ref, len_ref, pooled_ref, x_ref, pre_ref
):
    filters = w_ref.shape[1]
    part = pre_ref.shape[1]
    pooled_ref[...] = jnp.zeros_like(pooled_ref)

    def step(chunk, carry):
        build_windows(chunk, tile_ref, pos_ref, g_ref, len_ref, x_ref)
        for first in range(0, filters, part):
            half = dot(x_ref[...], w_ref[:, first : first + part])
            pre_ref[...] = half + half * jnp.tanh(half)
            for b in range(CHUNK_BLOCKS):
                row = pl.multiple_of(
                    tile_ref[chunk * CHUNK_BLOCKS + b] * BLOCK_WORDS, BLOCK_WORDS
                )
                pooled_ref[pl.ds(row, BLOCK_WORDS), first : first + part] += pre_ref[
                    b * BLOCK_WORDS : (b + 1) * BLOCK_WORDS, :
                ]
        return carry

    lax.fori_loop(0, scalar_ref[0], step, 0)
    pooled_ref[...] = pooled_ref[...] / len_ref[...].astype(F32)


def conv_forward(prep, char_groups, half_matrix):
    _, ids, lengths, scalars, tile, position = prep
    return pl.pallas_call(
        conv_forward_kernel,
        out_shape=jax.ShapeDtypeStruct((ids.shape[0], half_matrix.shape[1]), F32),
        in_specs=[SMEM, SMEM, SMEM, VMEM, VMEM, VMEM],
        out_specs=VMEM,
        scratch_shapes=[pltpu.VMEM((CHUNK, LANES), BF16), pltpu.VMEM((CHUNK, 512), F32)],
        compiler_params=pltpu.CompilerParams(vmem_limit_bytes=32 * MIB),
        cost_estimate=cost(16),
        name="conv_forward",
    )(scalars, tile, position, char_groups, half_matrix, lengths[:, None])


def conv_backward_kernel(
    scalar_ref, tile_ref, pos_ref, g_ref, w_ref, len_ref, gp_ref, out_ref, gg_ref, x_ref, d_ref, dw_ref
):
    filters = w_ref.shape[1]
    part = 512
    lane = lax.broadcasted_iota(jnp.int32, (BLOCK_WORDS, LANES), 1)
    dw_ref[...] = jnp.zeros_like(dw_ref)
    gg_ref[...] = jnp.zeros_like(gg_ref)

    def step(chunk, carry):
        build_windows(chunk, tile_ref, pos_ref, g_ref, len_ref, x_ref)
        for first in range(0, filters, part):
            columns = slice(first, first + part)
            half = dot(x_ref[...], w_ref[:, columns])
            tanh = jnp.tanh(half)
            slope = (1.0 + tanh) * (1.0 + (half - half * tanh))
            for b in range(CHUNK_BLOCKS):
                rows = slice(b * BLOCK_WORDS, (b + 1) * BLOCK_WORDS)
                row = pl.multiple_of(
                    tile_ref[chunk * CHUNK_BLOCKS + b] * BLOCK_WORDS, BLOCK_WORDS
                )
                d_ref[rows, columns] = (
                    gp_ref[pl.ds(row, BLOCK_WORDS), columns] * slope[rows]
                ).astype(BF16)
            dw_ref[:, columns] += dot_tn(x_ref[...], d_ref[:, columns])
        gx = dot_nt(d_ref[...], w_ref[...])
        for b in range(CHUNK_BLOCKS):
            block = chunk * CHUNK_BLOCKS + b
            row = pl.multiple_of(tile_ref[block] * BLOCK_WORDS, BLOCK_WORDS)
            position = pos_ref[block]
            group = position >> 3
            offset = (position & 7) * CHAR_DIM
            value = gx[b * BLOCK_WORDS : (b + 1) * BLOCK_WORDS, :]
            value = pltpu.roll(jnp.where(lane < BIAS_LANE, value, 0.0), offset, 1)
            gg_ref[group, pl.ds(row, BLOCK_WORDS), :] += jnp.where(lane >= offset, value, 0.0)
            gg_ref[group + 1, pl.ds(row, BLOCK_WORDS), :] += jnp.where(lane < offset, value, 0.0)
        return carry

    lax.fori_loop(0, scalar_ref[0], step, 0)
    out_ref[...] = dw_ref[...].T.astype(BF16)


def conv_backward(prep, char_groups, half_matrix, grad_scaled):
    _, ids, lengths, scalars, tile, position = prep
    filters = half_matrix.shape[1]
    return pl.pallas_call(
        conv_backward_kernel,
        out_shape=(
            jax.ShapeDtypeStruct((filters, LANES), BF16),
            jax.ShapeDtypeStruct(char_groups.shape, F32),
        ),
        in_specs=[SMEM, SMEM, SMEM, VMEM, VMEM, VMEM, VMEM],
        out_specs=(VMEM, VMEM),
        scratch_shapes=[
            pltpu.VMEM((CHUNK, LANES), BF16),
            pltpu.VMEM((CHUNK, filters), BF16),
            pltpu.VMEM((LANES, filters), F32),
        ],
        compiler_params=pltpu.CompilerParams(vmem_limit_bytes=48 * MIB),
        cost_estimate=cost(35),
        name="conv_backward",
    )(scalars, tile, position, char_groups, half_matrix, lengths[:, None], grad_scaled)


def table_kernel(scalar_ref, ids_ref, gg_ref, out_ref):
    groups = gg_ref.shape[0]
    out_ref[...] = jnp.zeros_like(out_ref)
    identity = lax.broadcasted_iota(jnp.int32, (TABLE_PAD, ROW_TILE), 0)
    for group in range(groups - 1):

        def step(index, carry, group=group):
            row = pl.multiple_of(index * ROW_TILE, ROW_TILE)
            grad = (2.0 * gg_ref[group, pl.ds(row, ROW_TILE), :]).astype(BF16)
            for k in range(GROUP):
                column = group * GROUP + k
                hot = (ids_ref[column : column + 1, pl.ds(row, ROW_TILE)] == identity).astype(F32)
                out_ref[k] += dot(hot.astype(BF16), grad)
            return carry

        lax.fori_loop(0, scalar_ref[1 + group], step, 0)


def table_gradient(prep, grad_groups, vocabulary):
    ids, scalars = prep[1], prep[3]
    total = pl.pallas_call(
        table_kernel,
        out_shape=jax.ShapeDtypeStruct((GROUP, TABLE_PAD, LANES), F32),
        in_specs=[SMEM, VMEM, VMEM],
        out_specs=VMEM,
        compiler_params=pltpu.CompilerParams(vmem_limit_bytes=32 * MIB),
        cost_estimate=cost(4),
        name="table_gradient",
    )(scalars, ids.T, grad_groups)
    parts = [total[k, :vocabulary, k * CHAR_DIM : (k + 1) * CHAR_DIM] for k in range(GROUP)]
    return sum(parts[1:], parts[0])


def table_lanes(table):
    padded = jnp.pad(table, ((0, TABLE_PAD - table.shape[0]), (0, 0)))
    return jnp.stack(
        [
            jnp.pad(padded, ((0, 0), (k * CHAR_DIM, LANES - (k + 1) * CHAR_DIM)))
            for k in range(GROUP)
        ]
    )


ANY = pl.BlockSpec(memory_space=pl.ANY)


def flat_pieces(pieces):
    return [array for half in pieces for chunk in half for array in chunk]


def piece_copies(layout, array, slot, first, own, pieces, whole_ref, sems, buffer):
    halves, chunks, arrays, rows = layout
    width = whole_ref.shape[2] // 2
    copies = []
    for half in range(halves):
        for chunk in range(chunks):
            ref = pieces[(half * chunks + chunk) * arrays + array]
            start = (own if half == 0 else 1 - own) * (chunks * rows) + chunk * rows
            start = pl.multiple_of(start, rows)
            for side in range(2):
                copies.append(
                    pltpu.make_async_copy(
                        ref.at[first if side == 0 else 1 - first, slot],
                        whole_ref.at[
                            buffer, pl.ds(start, rows), side * width : (side + 1) * width
                        ],
                        sems.at[buffer, len(copies)],
                    )
                )
    return copies


def fetch_pieces(layout, select_ref, own, pieces, whole_ref, sems):
    step = pl.program_id(0)

    def start(index):
        for array in range(layout[2]):

            @pl.when(index // 2 == array)
            def _(array=array):
                for copy in piece_copies(
                    layout, array, index % 2, select_ref[index], own, pieces, whole_ref, sems, index % 2
                ):
                    copy.start()

    @pl.when(step == 0)
    def _():
        start(0)

    @pl.when(step + 1 < pl.num_programs(0))
    def _():
        start(step + 1)

    buffer = step % 2
    for copy in piece_copies(layout, 0, 0, 0, own, pieces, whole_ref, sems, buffer):
        copy.wait()
    return buffer


def half_tanh(value):
    return 0.5 + 0.5 * jnp.tanh(0.5 * value)


def highway_forward_kernel(layout, place_ref, select_ref, core_ref, h_ref, bias_ref, *refs):
    count = layout[0] * layout[1] * layout[2]
    pieces = refs[:count]
    next_ref, transform_ref, gating_ref, low_ref, whole_ref, sems = refs[count:]
    step = pl.program_id(0)
    width = next_ref.shape[1]

    @pl.when(step == 0)
    def _():
        low_ref[...] = h_ref[...].astype(BF16)

    block = place_ref[step]
    blocks = bias_ref.shape[0] // 2
    buffer = fetch_pieces(layout, select_ref, core_ref[0], pieces, whole_ref, sems)
    mixed = dot(low_ref[...], whole_ref[buffer])
    transform = mixed[:, :width] + bias_ref[block]
    gating = half_tanh(mixed[:, width:] + bias_ref[block + blocks])
    h = h_ref[:, pl.ds(pl.multiple_of(block * width, width), width)]
    activated = transform * half_tanh(transform)
    transform_ref[...] = transform
    gating_ref[...] = gating
    next_ref[...] = activated + gating * (h - activated)


def highway_forward(h, pieces, bias_blocks, place, select, core):
    words, features = h.shape
    width = bias_blocks.shape[2]
    flat = flat_pieces(pieces)
    layout = (len(pieces), len(pieces[0]), len(pieces[0][0]), flat[0].shape[2])
    column = pl.BlockSpec((words, width), lambda j, place, *_: (0, place[j]))
    whole = lambda shape: pl.BlockSpec(shape, lambda j, *_: (0,) * len(shape))
    return pl.pallas_call(
        partial(highway_forward_kernel, layout),
        grid_spec=pltpu.PrefetchScalarGridSpec(
            num_scalar_prefetch=3,
            grid=(features // width,),
            in_specs=[whole(h.shape), whole(bias_blocks.shape)] + [ANY] * len(flat),
            out_specs=[column, column, column, whole(h.shape)],
            scratch_shapes=[
                pltpu.VMEM((2, features, 2 * width), BF16),
                pltpu.SemaphoreType.DMA((2, 2 * layout[0] * layout[1])),
            ],
        ),
        out_shape=(
            jax.ShapeDtypeStruct(h.shape, F32),
            jax.ShapeDtypeStruct(h.shape, F32),
            jax.ShapeDtypeStruct(h.shape, F32),
            jax.ShapeDtypeStruct(h.shape, BF16),
        ),
        compiler_params=pltpu.CompilerParams(vmem_limit_bytes=56 * MIB),
        cost_estimate=cost(19),
        name="highway_forward",
    )(place, select, core, h, bias_blocks, *flat)


def highway_backward_kernel(layout, place_ref, select_ref, core_ref, grad_ref, h_ref, t_ref, g_ref, *refs):
    count = layout[0] * layout[1] * layout[2]
    pieces = refs[:count]
    mixed_ref, sums_ref, out_ref, whole_ref, sems = refs[count:]
    step = pl.program_id(0)
    width = grad_ref.shape[1]
    features = out_ref.shape[1]

    @pl.when(step == 0)
    def _():
        out_ref[...] = jnp.zeros_like(out_ref)

    block = place_ref[step]
    buffer = fetch_pieces(layout, select_ref, core_ref[0], pieces, whole_ref, sems)
    grad = grad_ref[...]
    transform = t_ref[...]
    gating = g_ref[...]
    sigmoid = half_tanh(transform)
    activated = transform * sigmoid
    rest = grad * (1.0 - gating)
    low_t = (rest * (sigmoid + activated * (1.0 - sigmoid))).astype(BF16)
    low_g = (rest * gating * (h_ref[...] - activated)).astype(BF16)
    mixed_ref[0] = low_t
    mixed_ref[1] = low_g
    sums_ref[0] = jnp.sum(low_t.astype(F32), axis=0, keepdims=True)
    sums_ref[1] = jnp.sum(low_g.astype(F32), axis=0, keepdims=True)
    low = jnp.concatenate([low_t, low_g], axis=1)
    for start in range(0, features, 512):
        out_ref[:, start : start + 512] += dot_nt(
            low, whole_ref[buffer, start : start + 512, :]
        )
    out_ref[:, pl.ds(pl.multiple_of(block * width, width), width)] += grad * gating


def highway_backward(grad, h, transform, gating, pieces, place, select, core):
    words, features = h.shape
    flat = flat_pieces(pieces)
    width = flat[0].shape[3]
    layout = (len(pieces), len(pieces[0]), len(pieces[0][0]), flat[0].shape[2])
    column = pl.BlockSpec((words, width), lambda j, place, *_: (0, place[j]))
    return pl.pallas_call(
        partial(highway_backward_kernel, layout),
        grid_spec=pltpu.PrefetchScalarGridSpec(
            num_scalar_prefetch=3,
            grid=(features // width,),
            in_specs=[column] * 4 + [ANY] * len(flat),
            out_specs=[
                pl.BlockSpec((2, words, width), lambda j, place, *_: (0, 0, place[j])),
                pl.BlockSpec((2, 1, width), lambda j, place, *_: (0, 0, place[j])),
                pl.BlockSpec(h.shape, lambda j, *_: (0, 0)),
            ],
            scratch_shapes=[
                pltpu.VMEM((2, features, 2 * width), BF16),
                pltpu.SemaphoreType.DMA((2, 2 * layout[0] * layout[1])),
            ],
        ),
        out_shape=(
            jax.ShapeDtypeStruct((2, words, features), BF16),
            jax.ShapeDtypeStruct((2, 1, features), F32),
            jax.ShapeDtypeStruct(h.shape, F32),
        ),
        compiler_params=pltpu.CompilerParams(vmem_limit_bytes=56 * MIB),
        cost_estimate=cost(21),
        name="highway_backward",
    )(place, select, core, grad, h, transform, gating, *flat)


def weight_kernel(which_ref, left_ref, right_ref, *refs):
    out_ref = refs[-1]
    value = dot(left_ref[...], right_ref[0])
    width = out_ref.shape[2]
    for number in range(out_ref.shape[0]):
        block = value[:, number * width : (number + 1) * width]
        if len(refs) == 2:
            block = block + refs[0][number].astype(F32)
        out_ref[number] = block.astype(BF16)


def highway_weight_gradient(which, turned, mixed, first, rows, width, added=None, part=0):
    words, features = mixed.shape[1:]
    blocks = 8
    out = pl.BlockSpec((blocks, rows, width), lambda j, which: (j, 0, 0))
    return pl.pallas_call(
        weight_kernel,
        grid_spec=pltpu.PrefetchScalarGridSpec(
            num_scalar_prefetch=1,
            grid=(features // (blocks * width),),
            in_specs=[
                pl.BlockSpec((rows, words), lambda j, which: (first // rows, 0)),
                pl.BlockSpec((1, words, blocks * width), lambda j, which: (which[0], 0, j)),
            ]
            + (
                []
                if added is None
                else [pl.BlockSpec((blocks, rows, width), lambda j, which: (j, part, 0))]
            ),
            out_specs=out,
        ),
        out_shape=jax.ShapeDtypeStruct((features // width, rows, width), BF16),
        compiler_params=pltpu.CompilerParams(vmem_limit_bytes=32 * MIB),
        cost_estimate=cost(3),
        name="highway_weight",
    )(which, turned, mixed, *([] if added is None else [added]))


def turn_kernel(value_ref, out_ref):
    out_ref[...] = value_ref[...].T.astype(BF16)


def turn(value):
    rows, columns = value.shape
    return pl.pallas_call(
        turn_kernel,
        grid=(columns // 256,),
        in_specs=[pl.BlockSpec((rows, 256), lambda j: (0, j))],
        out_specs=pl.BlockSpec((256, rows), lambda j: (j, 0)),
        out_shape=jax.ShapeDtypeStruct((columns, rows), BF16),
        compiler_params=pltpu.CompilerParams(vmem_limit_bytes=32 * MIB),
        cost_estimate=cost(1),
        name="turn",
    )(value)


def place_rows_kernel(splits, place_ref, core_ref, *refs):
    arrays = (len(refs) - len(splits) - 1) // 2
    own_refs, other_refs = refs[:arrays], refs[arrays : 2 * arrays]
    out_refs, whole_ref = refs[2 * arrays : -1], refs[-1]
    step = pl.program_id(0)
    half_rows = own_refs[0].shape[1]
    core = core_ref[0]
    for array in range(arrays):

        @pl.when(step // 4 == array)
        def _(array=array):
            align = lambda start: pl.ds(pl.multiple_of(start, 16), half_rows)
            whole_ref[align(core * half_rows), :] = own_refs[array][0]
            whole_ref[align((1 - core) * half_rows), :] = other_refs[array][0]

    start = 0
    for rows, out_ref in zip(splits, out_refs):
        out_ref[...] = whole_ref[start : start + rows, :]
        start += rows


def place_rows(own, other, place, core, splits):
    half_rows, columns = own[0].shape[1:]

    def index(number):
        return lambda j, *_: (jnp.clip(j - 4 * number, 0, 3), 0, 0)

    specs = [pl.BlockSpec((1, half_rows, columns), index(number)) for number in range(len(own))]
    return pl.pallas_call(
        partial(place_rows_kernel, splits),
        grid_spec=pltpu.PrefetchScalarGridSpec(
            num_scalar_prefetch=2,
            grid=(4 * len(own),),
            in_specs=specs + specs,
            out_specs=[
                pl.BlockSpec((rows, columns), lambda j, place, *_: (place[j], 0)) for rows in splits
            ],
            scratch_shapes=[pltpu.VMEM((2 * half_rows, columns), BF16)],
        ),
        out_shape=[
            jax.ShapeDtypeStruct((4 * len(own) * rows, columns), BF16) for rows in splits
        ],
        compiler_params=pltpu.CompilerParams(vmem_limit_bytes=32 * MIB),
        cost_estimate=cost(7),
        name="place_rows",
    )(place, core, *own, *other)


def place_small_kernel(place_ref, *refs):
    inputs, (conv_ref, *row_refs) = refs[:4], refs[4:]
    step = pl.program_id(0)
    for number, ref in enumerate(inputs):

        @pl.when(step // 4 == number)
        def _(ref=ref):
            start = conv_ref.shape[0]
            conv_ref[...] = ref[0, :start, :]
            for row_ref in row_refs:
                row_ref[0] = ref[0, start : start + row_ref.shape[1], :]
                start += row_ref.shape[1]


def place_small(arrays, place, conv_rows, splits):
    rows, columns = arrays[0].shape[1:]

    def index(number):
        return lambda j, *_: (jnp.clip(j - 4 * number, 0, 3), 0, 0)

    return pl.pallas_call(
        place_small_kernel,
        grid_spec=pltpu.PrefetchScalarGridSpec(
            num_scalar_prefetch=1,
            grid=(16,),
            in_specs=[pl.BlockSpec((1, rows, columns), index(number)) for number in range(4)],
            out_specs=[pl.BlockSpec((conv_rows, columns), lambda j, place: (0, place[j]))]
            + [
                pl.BlockSpec((1, count, columns), lambda j, place: (place[j], 0, 0))
                for count in splits
            ],
        ),
        out_shape=[jax.ShapeDtypeStruct((conv_rows, 16 * columns), BF16)]
        + [jax.ShapeDtypeStruct((16, count, columns), BF16) for count in splits],
        compiler_params=pltpu.CompilerParams(vmem_limit_bytes=32 * MIB),
        cost_estimate=cost(2),
        name="place_small",
    )(place, *arrays)


LINKS = {
    "x": [(w, w ^ 1) for w in range(16)],
    "y": [(w, w ^ 2) for w in range(16)],
    "z": [(w, (w + 4) % 16) for w in range(16)],
    "back": [(w, (w - 4) % 16) for w in range(16)],
    "z1": [(w, w ^ 4) for w in range(16)],
    "z2": [(w, w ^ 8) for w in range(16)],
}
CORES = [(0, 1), (1, 0)]


def send(value, link):
    if link == "c":
        return lax.ppermute(value, "narrow", CORES)
    return lax.ppermute(value, "wide", LINKS[link])


def total_of(terms):
    return sum((term.astype(F32) for term in terms[1:]), terms[0].astype(F32))


class Exchange:
    windows = True

    def __init__(self):
        self.core = lax.axis_index("narrow")
        index = lax.axis_index("wide")
        self.z, self.y, self.x = index // 4, (index // 2) % 2, index % 2
        self.state, self.fresh, self.count, self.planned = {}, [], 0, []

    def put(self, key, value):
        self.state[key] = value
        self.fresh.append(key)

    def move(self, key, source, link):
        self.put(key, send(self.state[source], link))

    def plan(self, key, value, link, shape=None):
        self.planned.append((key, value, link, shape))

    def plan_move(self, source, *links):
        for link in links:
            self.plan(source + link, self.state[source], link)

    def plan_ring(self, name, step):
        self.plan(f"{name}r{step}", self.state[f"{name}r{step - 1}" if step > 1 else name], "z")

    def plan_swap(self, *names):
        for name in names:
            self.plan(name + "c", self.state[name], "c")

    def launch(self, values):
        leaves, tree = jax.tree.flatten(values)
        held = lax.optimization_barrier(
            tuple(value for _, value, _, _ in self.planned) + tuple(leaves)
        )
        for (key, _, link, shape), value in zip(self.planned, held):
            value = send(value, link)
            self.put(key, value if shape is None else value.reshape(shape))
        leaves = held[len(self.planned) :]
        self.planned = []
        return jax.tree.unflatten(tree, leaves)

    def window(self, values, hold=()):
        held_keys = [key for key in self.fresh if key in hold]
        self.fresh = [key for key in self.fresh if key not in hold]
        leaves, tree = jax.tree.flatten(values)
        held = lax.optimization_barrier(
            tuple(self.state[key] for key in self.fresh) + tuple(leaves)
        )
        for key, value in zip(self.fresh, held):
            self.state[key] = value
        leaves = held[len(self.fresh) :]
        self.fresh = held_keys
        return jax.tree.unflatten(tree, leaves)

    def swap_chain(self, *names):
        before = None
        for name in names:
            value = self.state[name]
            if before is not None:
                value, self.state[before] = lax.optimization_barrier((value, self.state[before]))
            before = name + "c"
            self.put(before, send(value, "c"))

    def stage(self, values=(), hold=()):
        return self.window(self.launch(values), hold)


    def load(self, name, value, rows=None, offset=0, whole=False):
        if not whole:
            rows = rows or value.shape[0] // 2
            value = lax.dynamic_slice_in_dim(
                value, self.core * (value.shape[0] // 2) + offset, rows, 0
            )
        self.state[name] = value

    def ring(self, name):
        received = [self.state[name]]
        for _ in range(3):
            received.append(send(received[-1], "z"))
        self.put(name + "o", jnp.stack(received))

    def ring_step(self, name, step):
        self.move(f"{name}r{step}", f"{name}r{step - 1}" if step > 1 else name, "z")

    def ring_both(self, name):
        self.put(name + "r1", send(self.state[name], "z"))
        self.put(name + "r3", send(self.state[name], "back"))
        self.put(name + "r2", send(self.state[name + "r1"], "z"))

    def ring_done(self, name):
        self.state[name + "o"] = jnp.stack(
            [self.state[name]] + [self.state[f"{name}r{step}"] for step in (1, 2, 3)]
        )

    def square(self, name):
        value = self.state[name]
        over_x = send(value, "x")
        self.put(name + "o0", jnp.stack([value, over_x, send(value, "y"), send(over_x, "y")]))

    def turn_ring(self, name, step):
        self.move(f"{name}o{step}", f"{name}o{step - 1}", "z")

    def swap(self, *names):
        for name in names:
            self.move(name + "c", name, "c")

    def near(self, name, suffix=""):
        return [self.state[name + part + suffix] for part in ("o", "ox", "oy", "oxy")]

    def layer(self, name, chunks):
        halves = []
        for suffix in ("", "c"):
            halves.append(
                [
                    [
                        array.reshape((2, 2) + array.shape[1:])
                        for array in self.near(f"{name}{chunk}", suffix)
                    ]
                    for chunk in range(chunks)
                ]
            )
        return halves

    def place(self, ring_last):
        step = jnp.arange(16)
        near, slot = (step % 4, step // 4) if ring_last else (step // 4, step % 4)
        return (
            (self.z - slot) % 4 * 4 + (self.y ^ (near >> 1)) * 2 + (self.x ^ (near & 1))
        ).astype(jnp.int32)

    def rows(self, own, other, splits, ring_last):
        core = self.core[None].astype(jnp.int32)
        return place_rows(own, other, self.place(ring_last), core, splits)


    def split(self, grads):
        blocks = [grad.astype(BF16).reshape(2, 16, -1, grad.shape[1]) for grad in grads]
        return tuple(
            jnp.concatenate(
                [lax.dynamic_index_in_dim(block, which, 0, keepdims=False) for block in blocks],
                axis=1,
            )
            for which in (self.core, 1 - self.core)
        )


class Reduction:
    def __init__(self, net, keep, sent, order):
        shape = (4, 2, 2) + keep.shape[1:]
        self.net, self.order, self.done = net, list(order), 0
        net.count += 1
        self.name = f"sum{net.count}"
        self.terms = [keep.reshape(shape)]
        self.keys, self.running, self.axes = [], None, ["z", "y", "x"]
        self.sent, self.shape = sent, shape

    def all_terms(self):
        return self.terms + [self.net.state[key] for key in self.keys]

    def pick(self, terms, index, axis):
        return [lax.dynamic_index_in_dim(term, index, axis, keepdims=False) for term in terms]

    def keep_only(self, index, axis):
        self.terms = self.pick(self.all_terms(), index, axis)
        self.keys = []

    def step(self, put=None):
        net, link = self.net, self.order[self.done]
        put = put or (lambda key, value, link, shape=None: net.put(
            key, send(value, link) if shape is None else send(value, link).reshape(shape)
        ))
        self.key = key = f"{self.name}_{self.done}"
        self.done += 1
        if link == "c":
            put(key, self.sent, "c", self.shape)
            self.keys.append(key)
        elif link in ("x", "y"):
            axis = self.axes.index(link)
            index = net.x if link == "x" else net.y
            sent = total_of(self.pick(self.all_terms(), 1 - index, axis)).astype(BF16)
            self.keep_only(index, axis)
            self.axes.remove(link)
            put(key, sent, link)
            self.keys.append(key)
        else:
            axis = self.axes.index("z")
            index = (net.z + int(link)) % 4
            terms = self.pick(self.all_terms(), index, axis)
            if self.running is not None:
                terms.append(net.state[self.running])
            put(key, total_of(terms).astype(BF16), "z")
            self.running = key
            if link == "1":
                self.keep_only(net.z, axis)
                self.axes.remove("z")
                self.keys = [key]
        return self

    def result(self):
        assert self.done == len(self.order)
        return total_of(self.all_terms())


class Ring:
    def __init__(self, net, sums, both):
        self.net, self.sums, self.both, self.done = net, sums, both, 0
        self.arrived = []
        net.count += 1
        self.name = f"ring{net.count}"

    def part(self, distance):
        index = (self.net.z + distance) % 4
        parts = [total_of(item.pick(item.all_terms(), index, 0)) for item in self.sums]
        value = parts[0] if len(parts) == 1 else jnp.concatenate(parts, axis=0)
        for key in self.arrived:
            value = value + self.net.state[key].astype(F32)
        return value

    def step(self, put):
        self.done += 1
        self.key = key = f"{self.name}_{self.done}"
        if self.both and self.done == 1:
            self.last_key = f"{self.name}_back"
            put(self.last_key, self.part(3).astype(BF16), "back")
            put(key, self.part(2).astype(BF16), "z")
        else:
            put(key, self.part((3 if self.both else 4) - self.done).astype(BF16), "z")
        self.arrived = [key]
        return self

    def result(self):
        assert self.done == (2 if self.both else 3)
        if self.both:
            self.arrived = self.arrived + [self.last_key]
        return self.part(0)


class Small:
    def __init__(self, net, value):
        self.net, self.value, self.done, self.key = net, value, 0, None
        net.count += 1
        self.name = f"small{net.count}"

    def result(self):
        return self.value if self.key is None else self.value + self.net.state[self.key]

    def step(self, put):
        self.value = self.result()
        self.key = f"{self.name}_{self.done}"
        put(self.key, self.value, ("c", "x", "y", "z1", "z2")[self.done])
        self.done += 1
        return self


class PlainReduction:
    def __init__(self, grads, axis):
        self.grads, self.axis = grads, axis

    def step(self):
        return self

    def result(self):
        return [
            lax.psum_scatter(
                grad.astype(BF16), ("narrow", "wide"), scatter_dimension=self.axis, tiled=True
            ).astype(F32)
            for grad in self.grads
        ]


def norm_rows(value, norm_gain, norm_shift):
    center = jnp.mean(value, axis=-1, keepdims=True)
    offsets = value - center
    spread = jnp.mean(offsets * offsets, axis=-1, keepdims=True)
    return offsets * lax.rsqrt(spread + EPSILON) * norm_gain + norm_shift


def norm_back(value, norm_gain, grad_rows):
    center = jnp.mean(value, axis=-1, keepdims=True)
    offsets = value - center
    spread = jnp.mean(offsets * offsets, axis=-1, keepdims=True)
    scale = lax.rsqrt(spread + EPSILON)
    normal = offsets * scale
    inner = grad_rows * norm_gain
    grad = scale * (
        inner
        - jnp.mean(inner, axis=-1, keepdims=True)
        - normal * jnp.mean(inner * normal, axis=-1, keepdims=True)
    )
    return grad, jnp.sum(grad_rows * normal, axis=0), jnp.sum(grad_rows, axis=0)


def array_copies(array, refs, held_ref, sems):
    count = len(refs)
    return [
        pltpu.make_async_copy(
            refs[index], held_ref.at[index], sems.at[index]
        )
        for index in range(array, count, count // 4)
    ]


def join_rows(slot_ref, own, refs, held_ref, up_ref, down_ref, sems):
    count = len(refs)
    arrays = count // 4
    step = pl.program_id(0)

    @pl.when(step == 0)
    def _():
        for array in range(arrays):
            for copy in array_copies(array, refs, held_ref, sems):
                copy.start()

    for array in range(arrays):

        @pl.when(step == 2 * array)
        def _(array=array):
            for copy in array_copies(array, refs, held_ref, sems):
                copy.wait()

    rows = held_ref.shape[2]
    near = step // 2
    for number in range(2):
        slot = slot_ref[step, number]
        for half in range(2):
            start = (own if half == 0 else 1 - own) * rows + number * 2 * rows
            where = pl.ds(pl.multiple_of(start, rows), rows)
            up_ref[where, :] = held_ref[half * arrays + near, slot]
            down_ref[where, :] = held_ref[(2 + half) * arrays + near, slot]


def normal_share(value, bell):
    t = 1.0 / (1.0 + (0.3275911 * 2**-0.5) * jnp.abs(value))
    series = 1.061405429
    for term in (-1.453152027, 1.421413741, -0.284496736, 0.254829592):
        series = series * t + term
    tail = (0.5 * series) * (t * bell)
    return jnp.where(value < 0.0, tail, 1.0 - tail)


def feed_forward_kernel(
    count, slot_ref, block_ref, core_ref, first_ref, bias_ref, vectors_ref, cotangent_ref, *refs
):
    (
        act_ref,
        slope_ref,
        hidden_ref,
        grad_ref,
        sums_ref,
        held_ref,
        up_ref,
        down_ref,
        low_ref,
        total_ref,
        sems,
    ) = refs[2 * count :]
    step = pl.program_id(0)

    @pl.when(step == 0)
    def _():
        low_ref[...] = first_ref[...].astype(BF16)
        total_ref[...] = first_ref[...] + vectors_ref[0:1, :]

    join_rows(slot_ref, core_ref[0], refs[: 2 * count], held_ref, up_ref, down_ref, sems)
    inner = dot_nt(low_ref[...], up_ref[...]) + bias_ref[block_ref[step]]
    bell = jnp.exp(-0.5 * inner * inner)
    share = normal_share(inner, bell)
    act = (inner * share).astype(BF16)
    act_ref[0] = act
    slope_ref[0] = (
        share + inner * (bell * (2.0 * jnp.pi) ** -0.5)
    ).astype(BF16)
    total_ref[...] += dot(act, down_ref[...])

    @pl.when(step == pl.num_programs(0) - 1)
    def _():
        value = total_ref[...]
        gain, shift = vectors_ref[1:2, :], vectors_ref[2:3, :]
        offsets = value - jnp.mean(value, axis=-1, keepdims=True)
        scale = lax.rsqrt(jnp.mean(offsets * offsets, axis=-1, keepdims=True) + EPSILON)
        normal = offsets * scale
        hidden_ref[...] = (normal * gain + shift).astype(BF16)
        cotangent = cotangent_ref[...].astype(F32)
        pulled = cotangent * gain
        grad = scale * (
            pulled
            - jnp.mean(pulled, axis=-1, keepdims=True)
            - normal * jnp.mean(pulled * normal, axis=-1, keepdims=True)
        )
        grad_ref[...] = grad
        sums_ref[0:1, :] = jnp.sum(cotangent * normal, axis=0, keepdims=True)
        sums_ref[1:2, :] = jnp.sum(cotangent, axis=0, keepdims=True)
        sums_ref[2:3, :] = jnp.sum(grad.astype(BF16).astype(F32), axis=0, keepdims=True)
        sums_ref[3:8, :] = jnp.zeros((5, sums_ref.shape[1]), F32)


def feed_forward(first, pieces, bias_blocks, vectors, cotangent, slots, block, core):
    words, columns = first.shape
    steps, width = bias_blocks.shape[0], bias_blocks.shape[2]
    up, down = pieces
    whole = lambda shape: pl.BlockSpec(shape, lambda j, *_: (0,) * len(shape))
    tile = pl.BlockSpec((1, words, width), lambda j, *_: (j, 0, 0))
    return pl.pallas_call(
        partial(feed_forward_kernel, len(up)),
        grid_spec=pltpu.PrefetchScalarGridSpec(
            num_scalar_prefetch=3,
            grid=(steps,),
            in_specs=[
                whole(first.shape),
                whole(bias_blocks.shape),
                whole(vectors.shape),
                whole(cotangent.shape),
            ]
            + [ANY] * (len(up) + len(down)),
            out_specs=[tile, tile, whole(first.shape), whole(first.shape), whole((8, columns))],
            scratch_shapes=[
                pltpu.VMEM((len(up) + len(down),) + up[0].shape, BF16),
                pltpu.VMEM((width, columns), BF16),
                pltpu.VMEM((width, columns), BF16),
                pltpu.VMEM((words, columns), BF16),
                pltpu.VMEM((words, columns), F32),
                pltpu.SemaphoreType.DMA((len(up) + len(down),)),
            ],
        ),
        out_shape=(
            jax.ShapeDtypeStruct((steps, words, width), BF16),
            jax.ShapeDtypeStruct((steps, words, width), BF16),
            jax.ShapeDtypeStruct((words, columns), BF16),
            jax.ShapeDtypeStruct((words, columns), F32),
            jax.ShapeDtypeStruct((8, columns), F32),
        ),
        compiler_params=pltpu.CompilerParams(vmem_limit_bytes=56 * MIB),
        cost_estimate=cost(20),
        name="feed_forward",
    )(slots, block, core, first, bias_blocks, vectors, cotangent, *up, *down)


def feed_forward_back_kernel(
    count,
    slot_ref,
    block_ref,
    core_ref,
    grad_ref,
    first_ref,
    act_ref,
    slope_ref,
    value_ref,
    gain_ref,
    *refs,
):
    (
        up_keep_ref,
        up_sent_ref,
        down_keep_ref,
        down_sent_ref,
        bias_ref,
        out_ref,
        sums_ref,
        held_ref,
        up_ref,
        down_ref,
        low_ref,
        low_first_ref,
        total_ref,
        sems,
    ) = refs[2 * count :]
    step = pl.program_id(0)

    @pl.when(step == 0)
    def _():
        total_ref[...] = grad_ref[...]
        low_ref[...] = grad_ref[...].astype(BF16)
        low_first_ref[...] = first_ref[...].astype(BF16)

    join_rows(slot_ref, core_ref[0], refs[: 2 * count], held_ref, up_ref, down_ref, sems)
    low = low_ref[...]
    inner = (dot_nt(low, down_ref[...]) * slope_ref[0].astype(F32)).astype(BF16)
    bias_ref[0] = jnp.sum(inner.astype(F32), axis=0, keepdims=True)
    grad_down = dot_tn(act_ref[0], low).astype(BF16)
    grad_up = dot_tn(inner, low_first_ref[...]).astype(BF16)
    total_ref[...] += dot(inner, up_ref[...])
    rows = up_keep_ref.shape[3]

    def store(value, ref):
        for number in range(4):
            ref[number // 2, 0, number % 2] = value[number * rows : (number + 1) * rows, :]

    @pl.when(step % 2 == 0)
    def _():
        store(grad_up, up_sent_ref)
        store(grad_down, down_sent_ref)

    @pl.when(step % 2 == 1)
    def _():
        store(grad_up, up_keep_ref)
        store(grad_down, down_keep_ref)

    @pl.when(step == pl.num_programs(0) - 1)
    def _():
        value = value_ref[...]
        pulling = total_ref[...]
        offsets = value - jnp.mean(value, axis=-1, keepdims=True)
        scale = lax.rsqrt(jnp.mean(offsets * offsets, axis=-1, keepdims=True) + EPSILON)
        normal = offsets * scale
        pulled = pulling * gain_ref[...]
        grad = scale * (
            pulled
            - jnp.mean(pulled, axis=-1, keepdims=True)
            - normal * jnp.mean(pulled * normal, axis=-1, keepdims=True)
        )
        out_ref[...] = grad
        sums_ref[0:1, :] = jnp.sum(pulling * normal, axis=0, keepdims=True)
        sums_ref[1:2, :] = jnp.sum(pulling, axis=0, keepdims=True)
        sums_ref[2:3, :] = jnp.sum(grad.astype(BF16).astype(F32), axis=0, keepdims=True)
        sums_ref[3:8, :] = jnp.zeros((5, sums_ref.shape[1]), F32)


def feed_forward_back(grad, first, act, slope, value, gain, pieces, slots, block, core):
    words, columns = first.shape
    steps, _, width = act.shape
    up, down = pieces
    rows = width // 4
    whole = lambda shape: pl.BlockSpec(shape, lambda j, *_: (0,) * len(shape))
    tile = pl.BlockSpec((1, words, width), lambda j, *_: (j, 0, 0))
    out = pl.BlockSpec(
        (2, 1, 2, rows, columns), lambda j, slots, block, core: (0, block[j] % (steps // 2), 0, 0, 0)
    )
    part = jax.ShapeDtypeStruct((2, steps // 2, 2, rows, columns), BF16)
    return pl.pallas_call(
        partial(feed_forward_back_kernel, len(up)),
        grid_spec=pltpu.PrefetchScalarGridSpec(
            num_scalar_prefetch=3,
            grid=(steps,),
            in_specs=[
                whole(grad.shape),
                whole(first.shape),
                tile,
                tile,
                whole(value.shape),
                whole(gain.shape),
            ]
            + [ANY] * (len(up) + len(down)),
            out_specs=[
                out,
                out,
                out,
                out,
                pl.BlockSpec((1, 1, width), lambda j, slots, block, core: (block[j], 0, 0)),
                whole(first.shape),
                whole((8, columns)),
            ],
            scratch_shapes=[
                pltpu.VMEM((len(up) + len(down),) + up[0].shape, BF16),
                pltpu.VMEM((width, columns), BF16),
                pltpu.VMEM((width, columns), BF16),
                pltpu.VMEM((words, columns), BF16),
                pltpu.VMEM((words, columns), BF16),
                pltpu.VMEM((words, columns), F32),
                pltpu.SemaphoreType.DMA((len(up) + len(down),)),
            ],
        ),
        out_shape=(
            part,
            part,
            part,
            part,
            jax.ShapeDtypeStruct((steps, 1, width), F32),
            jax.ShapeDtypeStruct((words, columns), F32),
            jax.ShapeDtypeStruct((8, columns), F32),
        ),
        compiler_params=pltpu.CompilerParams(vmem_limit_bytes=56 * MIB),
        cost_estimate=cost(25),
        name="feed_forward_back",
    )(slots, block, core, grad, first, act, slope, value, gain, *up, *down)


def softmax_parts(query, key):
    scores = dot_nt(query, key)
    scaling = HEAD_DIM ** (-0.5) * 1.4426950408889634
    exponent = jnp.exp2((scores - jnp.max(scores, axis=-1, keepdims=True)) * scaling)
    return exponent, 1.0 / jnp.sum(exponent, axis=-1, keepdims=True)


def attend_kernel(query_ref, key_ref, value_ref, out_ref):
    for start in range(0, LANES, HEAD_DIM):
        head = slice(start, start + HEAD_DIM)
        exponent, scale = softmax_parts(query_ref[:, head], key_ref[:, head])
        attention = (exponent * scale).astype(BF16)
        out_ref[:, head] = dot(attention, value_ref[:, head]).astype(BF16)


def third(number, words, thirds):
    return pl.BlockSpec((words, LANES), lambda j: (0, number * thirds + j))


def attend(qkv):
    words = qkv.shape[0]
    pairs = qkv.shape[1] // (3 * LANES)
    return pl.pallas_call(
        attend_kernel,
        grid=(pairs,),
        in_specs=[third(number, words, pairs) for number in range(3)],
        out_specs=third(0, words, pairs),
        out_shape=jax.ShapeDtypeStruct((words, pairs * LANES), BF16),
        compiler_params=pltpu.CompilerParams(vmem_limit_bytes=32 * MIB),
        cost_estimate=cost(12),
        name="attend",
    )(qkv, qkv, qkv)


def attend_back_kernel(
    query_ref, key_ref, value_ref, grad_ref, grad_query_ref, grad_key_ref, grad_value_ref
):
    scaling = HEAD_DIM ** (-0.5)
    for start in range(0, LANES, HEAD_DIM):
        head = slice(start, start + HEAD_DIM)
        query, key = query_ref[:, head], key_ref[:, head]
        grad = grad_ref[:, head]
        exponent, scale = softmax_parts(query, key)
        attention = exponent * scale
        grad_attention = dot_nt(grad, value_ref[:, head])
        inner = jnp.sum(grad_attention * attention, axis=-1, keepdims=True)
        grad_scores = (attention * (grad_attention - inner)).astype(BF16)
        grad_value_ref[:, head] = dot_tn(attention.astype(BF16), grad).astype(BF16)
        grad_query_ref[:, head] = (dot(grad_scores, key) * scaling).astype(BF16)
        grad_key_ref[:, head] = (dot_tn(grad_scores, query) * scaling).astype(BF16)


def attend_back(qkv, grad_context):
    words = qkv.shape[0]
    pairs = qkv.shape[1] // (3 * LANES)
    out = third(0, words, pairs)
    return jnp.concatenate(
        pl.pallas_call(
            attend_back_kernel,
            grid=(pairs,),
            in_specs=[third(number, words, pairs) for number in range(3)] + [out],
            out_specs=(out, out, out),
            out_shape=(jax.ShapeDtypeStruct(grad_context.shape, BF16),) * 3,
            compiler_params=pltpu.CompilerParams(vmem_limit_bytes=32 * MIB),
            cost_estimate=cost(17),
        name="attend_back",
        )(qkv, qkv, qkv, grad_context),
        axis=1,
    )


def gather_plain(value, axis):
    return lax.all_gather(value, "wide", axis=axis, tiled=True)


def plain_pieces(weight, chunks):
    whole = gather_plain(weight, 1)
    rows = whole.shape[0] // (2 * chunks)
    width = whole.shape[1] // 16
    halves = []
    for half in range(2):
        pieces = []
        for chunk in range(chunks):
            start = (half * chunks + chunk) * rows
            arrays = []
            for near in range(4):
                slots = []
                for slot in range(4):
                    block = (-slot % 4) * 4 + near
                    slots.append(whole[start : start + rows, block * width : (block + 1) * width])
                arrays.append(jnp.stack(slots).reshape(2, 2, rows, width))
            pieces.append(arrays)
        halves.append(pieces)
    return halves


def vector_rows(vectors):
    rows, places, start = [], [], 0
    for vector in vectors:
        count = -(-vector.shape[0] // LANES)
        padded = jnp.pad(vector, (0, count * LANES - vector.shape[0]))
        rows.append(padded.reshape(count, LANES))
        places.append((start, count, vector.shape[0]))
        start += count
    return jnp.pad(jnp.concatenate(rows, axis=0), ((0, -start % 16), (0, 0))), places


def plain_rows(whole):
    rows = whole.shape[0] // 16
    arrays = []
    for half in range(2):
        for near in range(4):
            starts = [((-slot % 4) * 4 + near) * rows + half * rows // 2 for slot in range(4)]
            arrays.append(jnp.stack([whole[start : start + rows // 2] for start in starts]))
    return arrays


def body(
    permutes,
    wide,
    devices,
    char_ids,
    word_lengths,
    type_ids,
    cotangent,
    character_embedding_table,
    conv_weight,
    conv_bias,
    high_weight,
    high_bias,
    proj_weight,
    proj_bias,
    pos_table,
    type_table,
    embed_gain,
    embed_shift,
    qkv_weight,
    attn_bias,
    out_weight,
    out_bias,
    attn_gain,
    attn_shift,
    up_weight,
    up_bias,
    down_weight,
    down_bias,
    ffn_gain,
    ffn_shift,
):
    layers, features = high_weight.shape[:2]
    words, chars = char_ids.shape[1:]
    model_width = proj_weight.shape[1]
    conv_rows = conv_weight.shape[0]
    lengths = word_lengths[0]
    vectors = [high_bias[layer] for layer in range(layers)] + [
        attn_bias,
        type_table[0],
        type_table[1],
        proj_bias,
        embed_gain,
        embed_shift,
        out_bias,
        attn_gain,
        attn_shift,
        up_bias,
        down_bias,
        ffn_gain,
        ffn_shift,
    ]
    conv_block = jnp.pad(
        jnp.concatenate([conv_weight, conv_bias[None]], axis=0),
        ((0, LANES - conv_rows - 1), (0, 0)),
    )
    vector_block, places = vector_rows(vectors)

    if permutes:
        net = Exchange()
        window, launch = net.window, net.launch
        core_index, z, y, x = net.core, net.z, net.y, net.x
        net.load(
            "small",
            jnp.concatenate([conv_block, vector_block, pos_table.T.reshape(-1, LANES)], axis=0),
            whole=True,
        )
        chunk_rows = features // 4
        net.load("L00", high_weight[0], chunk_rows, 0)
        (
            net.state["L00"],
            net.state["small"],
            char_ids,
            lengths,
            high_weight,
            qkv_weight,
            up_weight,
        ) = lax.optimization_barrier(
            (
                net.state["L00"],
                net.state["small"],
                char_ids,
                lengths,
                high_weight,
                qkv_weight,
                up_weight,
            )
        )
        for layer, chunk in ((0, 1), (1, 0), (1, 1)):
            net.load(f"L{layer}{chunk}", high_weight[layer], chunk_rows, chunk * chunk_rows)
        encoder_splits = [
            qkv_weight.shape[1],
            out_weight.shape[0],
            proj_weight.shape[0],
        ]
        net.load(
            "e",
            jnp.concatenate(
                [qkv_weight.T, out_weight, proj_weight],
                axis=0,
            ),
        )
        net.load("up", up_weight.T)
        net.load("down", down_weight)
        net.put("L00r1", send(net.state["L00"], "z"))
        net.put("L00r3", send(net.state["L00"], "back"))
        net.move("smallx", "small", "x")
        net.move("smally", "small", "y")
    else:
        window = lambda values, hold=(): values
        launch = window
        core_index = z = y = x = jnp.zeros((), jnp.int32)
    prep = sort_words(char_ids[0], lengths, chars // GROUP + 2)
    table_blocks = table_lanes(character_embedding_table)
    prep, table_blocks = window((prep, table_blocks))
    if permutes:
        net.ring_step("L00", 2)
        net.move("smallxy", "smallx", "y")
        net.move("ex", "e", "x")
        net.move("ey", "e", "y")
        window(())
        net.ring_done("L00")
        net.state["smallo0"] = jnp.stack(
            [net.state["small" + part] for part in ("", "x", "y", "xy")]
        )
        net.plan_move("L00o", "x", "y")
        net.plan("smallo1", net.state["smallo0"], "z")
        launch(())
        net.turn_ring("small", 2)
        net.move("exy", "ex", "y")
        net.ring_both("L01")
        net.state["eo0"] = jnp.stack([net.state["e" + part] for part in ("", "x", "y", "xy")])
        prep, table_blocks = window((prep, table_blocks))
        net.ring_done("L01")
        net.plan_move("L01o", "x", "y")
        net.plan("smallo3", net.state["smallo2"], "z")
        prep, table_blocks = launch((prep, table_blocks))
        net.ring_both("L10")
        net.swap_chain("L00o", "L00ox", "L00oy")
    char_groups = embed_characters(prep, table_blocks)
    char_groups = window(char_groups)

    if permutes:
        net.ring_done("L10")
        conv_all, whole_vectors, pos_all = place_small(
            [net.state[f"smallo{step}"] for step in range(4)],
            net.place(True),
            LANES,
            [vector_block.shape[0], pos_table.size // LANES],
        )
    else:
        conv_all = gather_plain(conv_block, 1)
        whole_vectors = lax.all_gather(vector_block, "wide", axis=0, tiled=False)
        pos_all = gather_plain(pos_table.T, 0)
    filters = conv_all.shape[1]
    row = jnp.arange(LANES)[:, None]
    usable = row // CHAR_DIM < filter_widths(filters)[None, :]
    half_matrix = jnp.where(usable | (row >= conv_rows), conv_all * BF16(0.5), BF16(0.0))
    if permutes:
        net.plan("L00oxy", net.state["L00ox"], "y")
        net.plan("L01oxy", net.state["L01oy"], "x")
        net.state["eo0"] = jnp.stack([net.state["e" + part] for part in ("", "x", "y", "xy")])
        net.plan("eo1", net.state["eo0"], "z")
        half_matrix = launch(half_matrix)
        net.swap_chain("L01o", "L01ox", "L01oy")
    pooled = conv_forward(prep, char_groups, half_matrix)
    pooled, whole_vectors, pos_all = window((pooled, whole_vectors, pos_all))
    whole = [
        whole_vectors[:, start : start + count].reshape(wide, -1)[:, :size].reshape(-1)
        for start, count, size in places
    ]
    if permutes:
        net.plan_move("L10o", "x", "y")
        launch(())
        net.ring_both("L11")
        net.swap_chain("L00oxy", "L01oxy", "eo0")
        pooled, whole, pos_all = window((pooled, whole, pos_all))
        net.ring_done("L11")
        net.plan_move("L11o", "x", "y")
        net.plan("eo2", net.state["eo1"], "z")
        net.plan_swap("L10o")
        pooled = launch(pooled)
        pieces = [net.layer("L0", 2)]
    else:
        pieces = [plain_pieces(high_weight[layer], 2) for layer in range(layers)]
    high_bias_all, attn_bias_all = whole[:layers], whole[layers]
    (
        type_zero,
        type_one,
        proj_bias_all,
        gain_zero,
        shift_zero,
        out_bias_all,
        gain_one,
        shift_one,
        up_bias_all,
        down_bias_all,
        gain_two,
        shift_two,
    ) = (value.astype(F32) for value in whole[layers + 1 :])
    width = 2 * features // 16
    order = jnp.arange(8)
    near, low_slot = order // 2, order % 2
    slot_z = (z - low_slot) % 4
    place = ((slot_z & 1) * 4 + (y ^ (near >> 1)) * 2 + (x ^ (near & 1))).astype(jnp.int32)
    select = (slot_z // 2).astype(jnp.int32)
    core = core_index[None].astype(jnp.int32)
    bias_blocks = [bias.astype(F32).reshape(16, 1, width) for bias in high_bias_all]
    first_layer = highway_forward(pooled, pieces[0], bias_blocks[0], place, select, core)
    first_layer = window(first_layer)

    if permutes:
        net.plan("L10oxy", net.state["L10ox"], "y")
        net.plan("L11oxy", net.state["L11oy"], "x")
        net.plan("eo3", net.state["eo2"], "z")
        first_layer, pos_all = launch((first_layer, pos_all))
        net.swap_chain("L10ox", "L10oy", "L11o", "L11ox", "L11oy", "eo1", "eo2")
    turned = [turn(first_layer[3])]
    pos_rows = pos_all.reshape(model_width, words).T.astype(F32)
    turned, pos_rows = window((turned, pos_rows))
    if permutes:
        net.plan_swap("L10oxy", "L11oxy")
        for name in ("up", "down"):
            net.plan(name + "r1", net.state[name], "z")
            net.plan(name + "r3", net.state[name], "back")
        first_layer = net.stage(first_layer)
        for name in ("up", "down"):
            net.plan(name + "r2", net.state[name + "r1"], "z")
        net.plan_swap("eo3")
        first_layer = launch(first_layer)
        pieces.append(net.layer("L1", 2))
        qkv_all, out_all, proj_all = net.rows(
            [net.state[f"eo{step}"] for step in range(4)],
            [net.state[f"eo{step}c"] for step in range(4)],
            encoder_splits,
            True,
        )
    else:
        qkv_all, out_all, proj_all = (
            gather_plain(value, 0) for value in (qkv_weight.T, out_weight, proj_weight)
        )
    second_layer = highway_forward(first_layer[0], pieces[1], bias_blocks[1], place, select, core)
    second_layer = window(second_layer)
    if permutes:
        net.ring_done("up")
        net.ring_done("down")
        net.plan_move("upo", "x", "y")
        net.plan_move("downo", "x", "y")
        second_layer = launch(second_layer)
    states = [pooled, first_layer[0], second_layer[0]]
    transforms = [first_layer[1], second_layer[1]]
    gatings = [first_layer[2], second_layer[2]]
    perm, sorted_lengths = prep[0], prep[2]
    last = dot_tn(perm, states[2].astype(BF16)).astype(BF16)
    word_vec = dot(last, proj_all) + proj_bias_all
    type_rows = jnp.where(type_ids[0][:, None] == 1, type_one[None], type_zero[None])
    summed = word_vec + pos_rows + type_rows
    embedded = norm_rows(summed, gain_zero, shift_zero)
    turned.append(turn(second_layer[3]))
    summed, embedded, last, turned = window((summed, embedded, last, turned))

    if permutes:
        net.plan("upoxy", net.state["upox"], "y")
        net.plan("downoxy", net.state["downoy"], "x")
        embedded = launch(embedded)
        net.swap_chain("upo", "upox", "upoy", "downo")
    low_embedded = embedded.astype(BF16)
    bias_three = jnp.concatenate(
        [
            attn_bias_all[:model_width],
            jnp.zeros((model_width,), BF16),
            attn_bias_all[model_width:],
        ]
    ).astype(F32)
    qkv = (dot_nt(low_embedded, qkv_all) + bias_three).astype(BF16)
    context = attend(qkv)
    if permutes:
        context = window(context)
        net.plan_swap("downox", "downoy", "upoxy", "downoxy")
        context = launch(context)
    first_in = embedded + (dot(context, out_all) + out_bias_all)
    first = norm_rows(first_in, gain_one, shift_one)
    if permutes:
        first_in, first = window((first_in, first))
        feed_pieces = [net.near(name) + net.near(name, "c") for name in ("up", "down")]
    else:
        feed_pieces = [
            plain_rows(gather_plain(value, 0)) for value in (up_weight.T, down_weight)
        ]
    half_of = jnp.where(order % 2 == 0, 1 - core_index, core_index)
    slots = (z - (2 * half_of[:, None] + jnp.arange(2)[None, :])) % 4
    slots = slots.astype(jnp.int32)
    feed_block = (half_of * 4 + (y ^ (near >> 1)) * 2 + (x ^ (near & 1))).astype(jnp.int32)
    feed_rows = up_bias_all.shape[0] // 16
    feed_bias = jnp.moveaxis(up_bias_all.reshape(2, 2, 4, feed_rows), 1, 2).reshape(8, 1, -1)
    act, slope, hidden_out, grad_second, last_sums = feed_forward(
        first,
        feed_pieces,
        feed_bias,
        jnp.stack([down_bias_all, gain_two, shift_two]),
        cotangent[0],
        slots,
        feed_block,
        core,
    )
    grad_ffn_gain, grad_ffn_shift, grad_down_bias = last_sums[0], last_sums[1], last_sums[2]

    def sum_rows(grads, order):
        if permutes:
            return Reduction(net, *net.split(grads), order)
        return PlainReduction(grads, 0)

    def send_layer(layer, mixed, first, rows):
        sent = highway_weight_gradient(1 - core, turned[layer], mixed, first, rows, width // 2)
        key = f"layer{layer}_{first}"
        if permutes:
            net.plan(key, sent, "c")
        return layer, mixed, first, rows, (key if permutes else sent, 0)

    def keep_layer(job, order):
        layer, mixed, first, rows, (key, part) = job
        keep = highway_weight_gradient(
            core,
            turned[layer],
            mixed,
            first,
            rows,
            width // 2,
            net.state[key] if permutes else None,
            part,
        )
        if permutes:
            return Reduction(net, keep, None, order)
        other = key[:, part * rows : (part + 1) * rows]
        whole = jnp.moveaxis(jnp.concatenate([keep, other], axis=0), 1, 0).reshape(rows, -1)
        return PlainReduction([whole], 1)

    def sum_feed(keep, sent, order):
        keep, sent = (value.reshape((16,) + value.shape[3:]) for value in (keep, sent))
        if permutes:
            return Reduction(net, keep, sent, order)
        return sum_rows([jnp.concatenate([keep, sent], axis=0).reshape(-1, model_width)], "")

    def ring_of(*sums, both=False):
        return Ring(net, sums, both) if permutes else sums

    def advance(*sums):
        if permutes:
            for item in sums:
                item.step()

    def ready(*sums):
        if permutes:
            for item in sums:
                item.step(net.plan)

    def held(*sums):
        return tuple(item.key for item in sums) if permutes else ()

    def together(*sums, hold=()):
        if permutes:
            ready(*sums)
            launch(())
            window((), held(*hold))

    up_keep, up_sent, down_keep, down_sent, bias_sums, grad_resid, norm_sums = feed_forward_back(
        grad_second,
        first,
        act,
        slope,
        first_in,
        gain_one[None],
        feed_pieces,
        slots,
        feed_block,
        core,
    )
    grad_up_bias = jnp.moveaxis(bias_sums.reshape(2, 4, 2, feed_rows), 2, 1).reshape(-1)
    grad_attn_gain, grad_attn_shift, grad_out_bias = norm_sums[0], norm_sums[1], norm_sums[2]
    up_keep, up_sent, down_keep, down_sent, grad_resid = window(
        (up_keep, up_sent, down_keep, down_sent, grad_resid)
    )

    sum_up = sum_feed(up_keep, up_sent, "cxy")
    sum_down = sum_feed(down_keep, down_sent, "cyx")
    ready(sum_down, sum_up)
    grad_resid = launch(grad_resid)
    grad_branch = grad_resid.astype(BF16)
    grad_context = dot_nt(grad_branch, out_all).astype(BF16)
    grad_resid, grad_context = window((grad_resid, grad_context))
    ready(sum_down, sum_up)
    grad_context, grad_branch = launch((grad_context, grad_branch))
    grad_qkv = attend_back(qkv, grad_context)
    grad_out = dot_tn(context, grad_branch).astype(BF16)
    grad_resid, grad_qkv, grad_out = window((grad_resid, grad_qkv, grad_out))

    ready(sum_down, sum_up)
    grad_qkv, grad_resid = launch((grad_qkv, grad_resid))
    qkv_sums = column_sum(grad_qkv)
    grad_attn_bias = jnp.concatenate([qkv_sums[:model_width], qkv_sums[2 * model_width :]])
    grad_summed, grad_embed_gain, grad_embed_shift = norm_back(
        summed, gain_zero, grad_resid + dot(grad_qkv, qkv_all)
    )
    grad_word = grad_summed.astype(BF16)
    grad_proj_bias = column_sum(grad_word)
    running = dot_nt(dot(perm, grad_word).astype(BF16), proj_all)
    running = window(running)
    ring_feed = ring_of(sum_up, sum_down)
    ready(ring_feed)
    running = launch(running)
    mixed_one, sums_one, running = highway_backward(
        running, states[1], transforms[1], gatings[1], pieces[1], place, select, core
    )
    mixed_one, running, grad_qkv, grad_out, grad_word, grad_summed = window(
        (mixed_one, running, grad_qkv, grad_out, grad_word, grad_summed)
    )
    type_hot = (type_ids[0] == 1).astype(F32)[:, None]
    vector_grads = [
        grad_proj_bias,
        jnp.sum((1.0 - type_hot) * grad_summed, axis=0),
        jnp.sum(type_hot * grad_summed, axis=0),
        grad_embed_gain,
        grad_embed_shift,
        grad_attn_bias,
        grad_out_bias,
        grad_attn_gain,
        grad_attn_shift,
        grad_up_bias,
        grad_down_bias,
        grad_ffn_gain,
        grad_ffn_shift,
    ]

    half_rows, quarter = features // 2, features // 4

    def quarters(jobs, layer, mixed):
        return [
            (layer, mixed, start * quarter, quarter, (jobs[start // 2][-1][0], start % 2))
            for start in range(4)
        ]

    jobs = [send_layer(1, mixed_one, start, half_rows) for start in (0, half_rows)]
    ready(ring_feed)
    mixed_one, grad_qkv, grad_word, grad_summed = launch(
        (mixed_one, grad_qkv, grad_word, grad_summed)
    )
    grad_pos = turn(grad_summed)
    encoder_grads = [
        dot_tn(grad_qkv, low_embedded),
        grad_out,
        dot_tn(last, grad_word),
    ]
    if permutes:
        encoder_grads.append(grad_pos.reshape(-1, model_width))
        sum_encoder = sum_rows(encoder_grads, "c321xy")
        mixed_one, running, sum_encoder.terms, sum_encoder.sent = window(
            (mixed_one, running, sum_encoder.terms, sum_encoder.sent)
        )
    else:
        sum_encoder = sum_rows(encoder_grads, "")
        sum_pos = sum_rows([grad_pos], "")

    jobs = quarters(jobs, 1, mixed_one)
    one = [None] * 4
    one[0], one[2] = keep_layer(jobs[0], "yx"), keep_layer(jobs[2], "xy")
    ready(one[0], one[2], sum_encoder, ring_feed)
    running = launch(running)
    mixed_zero, sums_zero, running = highway_backward(
        running, states[0], transforms[0], gatings[0], pieces[0], place, select, core
    )
    mixed_zero, running = window((mixed_zero, running))

    one[1], one[3] = keep_layer(jobs[1], "yx"), keep_layer(jobs[3], "xy")
    jobs = [send_layer(0, mixed_zero, start, half_rows) for start in (0, half_rows)]
    grad_scaled = running * (0.5 / sorted_lengths.astype(F32))[:, None]
    ready(one[1], one[3], sum_encoder)
    grad_scaled = launch(grad_scaled)
    matrix_turned, grad_groups = conv_backward(prep, char_groups, half_matrix, grad_scaled)
    mixed_zero, matrix_turned, grad_groups = window((mixed_zero, matrix_turned, grad_groups))

    ready(*one, sum_encoder)
    mixed_zero, grad_groups = launch((mixed_zero, grad_groups))
    jobs = quarters(jobs, 0, mixed_zero)
    zero = [keep_layer(job, order_) for job, order_ in zip(jobs, ("yx", "yx", "xy", "xy"))]
    first_two = (zero[0], zero[2])
    terms = [item.terms for item in zero] if permutes else ()
    grad_table = table_gradient(prep, grad_groups, character_embedding_table.shape[0])
    first_sum, vector_places = vector_rows(vector_grads)
    last_sum, high_places = vector_rows(
        [sums_zero.reshape(-1), sums_one.reshape(-1), grad_table.reshape(-1)]
    )
    high_places = [(first_sum.shape[0] + start, *rest) for start, *rest in high_places]
    last_sum = jnp.concatenate([first_sum, last_sum], axis=0)
    terms, last_sum = window((terms, last_sum))
    last_sum = Small(net, last_sum) if permutes else lax.psum(last_sum, ("narrow", "wide"))
    for item, value in zip(zero, terms):
        item.terms = value

    if permutes:
        conv_keep, conv_sent = net.split([matrix_turned])
        net.plan("conv", conv_sent, "c")
    else:
        sum_conv = sum_rows([matrix_turned], "")
    ready(*first_two, sum_encoder, last_sum)
    launch(())
    window(())
    if permutes:
        conv_total = total_of([conv_keep, net.state["conv"]]).astype(BF16)
        conv_total = conv_total.reshape((4, 2, 2) + conv_total.shape[1:])
        zero[3].terms = [jnp.concatenate([zero[3].terms[0], conv_total], axis=3)]

    ring_one = ring_of(*one)
    together(zero[1], zero[3], *first_two, ring_one)
    together(zero[1], zero[3], ring_one, last_sum)
    ring_first = ring_of(*first_two, both=True)
    together(ring_first, ring_one, sum_encoder, last_sum)
    ring_last = ring_of(zero[1], zero[3], both=True)
    together(ring_first, ring_last, sum_encoder, last_sum)
    together(ring_last, last_sum)
    total = last_sum.result() if permutes else last_sum

    device = lax.axis_index("narrow") * wide + lax.axis_index("wide")

    def whole_vector(total, where):
        start, count, size = where
        return total[start : start + count].reshape(-1)[:size]

    def own_part(total, where):
        piece = where[2] // devices
        return lax.dynamic_slice_in_dim(whole_vector(total, where), device * piece, piece, 0)

    results = [own_part(total, where) for where in vector_places]
    (
        sum_proj_bias,
        sum_type_zero,
        sum_type_one,
        sum_embed_gain,
        sum_embed_shift,
        sum_attn_bias,
        sum_out_bias,
        sum_attn_gain,
        sum_attn_shift,
        sum_up_bias,
        sum_down_bias,
        sum_ffn_gain,
        sum_ffn_shift,
    ) = results
    sum_high_bias = jnp.stack([own_part(total, where) for where in high_places[:layers]])
    sum_table = whole_vector(total, high_places[layers]).reshape(
        character_embedding_table.shape
    )

    def rows_of(item, sizes):
        total = item.result()
        if not permutes:
            return total
        pieces, start = [], 0
        for size in sizes:
            pieces.append(total[start : start + size])
            start += size
        return pieces

    qkv_rows, sum_out, sum_proj, *rest = rows_of(
        sum_encoder,
        [
            qkv_all.shape[0] // devices,
            out_all.shape[0] // devices,
            proj_all.shape[0] // devices,
            words * model_width // devices // model_width,
        ],
    )
    if permutes:
        pos_rows = rest[0].reshape(-1, words)
    else:
        (pos_rows,) = sum_pos.result()
    if permutes:
        up_rows, down_rows = jnp.split(ring_feed.result(), 2)
    else:
        (up_rows,), (down_rows,) = sum_up.result(), sum_down.result()
    if permutes:
        first_rows, last_rows = ring_first.result(), ring_last.result()
        conv_turned = last_rows[2 * quarter :]
    else:
        (conv_turned,) = sum_conv.result()
    own_filters = lax.dynamic_slice_in_dim(
        filter_widths(filters), device * (filters // devices), filters // devices
    )
    taps = jnp.arange(conv_rows)[:, None] // CHAR_DIM
    sum_conv_weight = jnp.where(taps < own_filters[None, :], conv_turned[:, :conv_rows].T, 0.0)

    if permutes:
        parts = [first_rows[:quarter], last_rows[:quarter], first_rows[quarter:], last_rows[quarter : 2 * quarter]]
        high_rows = [jnp.concatenate(parts, axis=0), ring_one.result()]
    else:
        high_rows = [
            jnp.concatenate([part for item in sums for part in item.result()], axis=0)
            for sums in (zero, one)
        ]

    return (
        hidden_out[None],
        sum_table,
        sum_conv_weight,
        conv_turned[:, conv_rows],
        jnp.stack(high_rows),
        sum_high_bias,
        sum_proj,
        sum_proj_bias,
        pos_rows.T,
        jnp.stack([sum_type_zero, sum_type_one]),
        sum_embed_gain,
        sum_embed_shift,
        qkv_rows.T,
        sum_attn_bias,
        sum_out,
        sum_out_bias,
        sum_attn_gain,
        sum_attn_shift,
        up_rows.T,
        sum_up_bias,
        down_rows,
        sum_down_bias,
        sum_ffn_gain,
        sum_ffn_shift,
    )


def solution(mesh):
    narrow, wide = mesh.shape["narrow"], mesh.shape["wide"]
    both = ("narrow", "wide")
    placed = (
        P(both, None, None),
        P(both, None),
        P(both, None),
        P(both, None, None),
        P(),
        P(None, "wide"),
        P("wide"),
        P(None, None, "wide"),
        P(None, "wide"),
        P("wide", None),
        P("wide"),
        P(None, "wide"),
        P(None, "wide"),
        P("wide"),
        P("wide"),
        P(None, "wide"),
        P("wide"),
        P("wide", None),
        P("wide"),
        P("wide"),
        P("wide"),
        P(None, "wide"),
        P("wide"),
        P("wide", None),
        P("wide"),
        P("wide"),
        P("wide"),
    )
    return jax.shard_map(
        partial(body, (narrow, wide) == (2, 16), wide, narrow * wide),
        mesh=mesh,
        in_specs=placed,
        out_specs=(
            P(both, None, None),
            P(),
            P(None, both),
            P(both),
            P(None, None, both),
            P(None, both),
            P(both, None),
            P(both),
            P(None, both),
            P(None, both),
            P(both),
            P(both),
            P(None, both),
            P(both),
            P(both, None),
            P(both),
            P(both),
            P(both),
            P(None, both),
            P(both),
            P(both, None),
            P(both),
            P(both),
            P(both),
        ),
        check_vma=False,
    )
```

```python
from functools import partial

import jax
import jax.numpy as jnp
from jax import lax
from jax.experimental import pallas as pl
from jax.experimental.pallas import tpu as pltpu
from jax.sharding import PartitionSpec as P

HEADS = 12
HEAD_DIM = 64
CHAR_DIM = 16
TAPS = 7
EPSILON = 1e-12

LANES = 128
GROUP = LANES // CHAR_DIM
BLOCK_WORDS = 32
CHUNK_BLOCKS = 16
CHUNK = BLOCK_WORDS * CHUNK_BLOCKS
TABLE_PAD = 384
ROW_TILE = 128
BIAS_LANE = TAPS * CHAR_DIM

F32 = jnp.float32
BF16 = jnp.bfloat16
VMEM = pl.BlockSpec(memory_space=pltpu.VMEM)
SMEM = pl.BlockSpec(memory_space=pltpu.SMEM)
MIB = 1024 * 1024


def cost(microseconds):
    return pl.CostEstimate(
        flops=int(microseconds * 1.1e9), bytes_accessed=int(microseconds * 3e6), transcendentals=0
    )


def dot(left, right):
    return lax.dot_general(left, right, (((1,), (0,)), ((), ())), preferred_element_type=F32)


def dot_nt(left, right):
    return lax.dot_general(left, right, (((1,), (1,)), ((), ())), preferred_element_type=F32)


def dot_tn(left, right):
    return lax.dot_general(left, right, (((0,), (0,)), ((), ())), preferred_element_type=F32)


def column_sum(values):
    return jnp.sum(values.astype(F32), axis=0)


def filter_widths(filter_count):
    column = jnp.arange(filter_count)
    widths = jnp.ones((filter_count,), jnp.int32)
    for exponent in range(6):
        widths = widths + (column >= filter_count * 2**exponent // 64).astype(jnp.int32)
    return widths


def sort_words(char_ids, lengths, groups):
    words, chars = char_ids.shape
    index = jnp.arange(words)
    longer = lengths[None, :] > lengths[:, None]
    tie = (lengths[None, :] == lengths[:, None]) & (index[None, :] < index[:, None])
    rank = jnp.sum((longer | tie).astype(jnp.int32), axis=1)
    perm = (rank[None, :] == index[:, None]).astype(BF16)
    live = jnp.arange(chars)[None, :] < lengths[:, None]
    shifted = jnp.where(live, char_ids + 1, 0)
    packed = jnp.concatenate(
        [shifted >> 4, shifted & 15, lengths[:, None]], axis=1
    ).astype(BF16)
    sorted_packed = dot(perm, packed).astype(jnp.int32)
    ids = (sorted_packed[:, :chars] << 4) + sorted_packed[:, chars : 2 * chars] - 1
    ids = jnp.pad(ids, ((0, 0), (0, GROUP * groups - chars)), constant_values=-1)
    sorted_lengths = sorted_packed[:, 2 * chars]
    tile_count = words // BLOCK_WORDS
    tile_max = jnp.max(sorted_lengths.reshape(tile_count, BLOCK_WORDS), axis=1)
    cum = jnp.cumsum(tile_max)
    total = cum[-1]
    block = jnp.arange(tile_count * chars + CHUNK_BLOCKS)
    tile = jnp.sum((block[:, None] >= cum[None, :]).astype(jnp.int32), axis=1)
    start = jnp.sum(
        jnp.where(tile[:, None] == jnp.arange(tile_count)[None, :], (cum - tile_max)[None, :], 0),
        axis=1,
    )
    valid = block < total
    position = jnp.where(valid, block - start, chars).astype(jnp.int32)
    tile = jnp.where(valid, tile, 0).astype(jnp.int32)
    chunks = (total + CHUNK_BLOCKS - 1) // CHUNK_BLOCKS
    reach = jnp.sum(
        (sorted_lengths[None, :] > GROUP * jnp.arange(groups - 1)[:, None]).astype(jnp.int32), axis=1
    )
    scalars = jnp.concatenate([chunks[None], (reach + ROW_TILE - 1) // ROW_TILE]).astype(jnp.int32)
    return perm, ids, sorted_lengths, scalars, tile, position


def build_windows(chunk, tile_ref, pos_ref, g_ref, len_ref, x_ref):
    lane = lax.broadcasted_iota(jnp.int32, (BLOCK_WORDS, LANES), 1)
    for b in range(CHUNK_BLOCKS):
        block = chunk * CHUNK_BLOCKS + b
        row = pl.multiple_of(tile_ref[block] * BLOCK_WORDS, BLOCK_WORDS)
        position = pos_ref[block]
        group = position >> 3
        offset = (position & 7) * CHAR_DIM
        shift = lax.rem(LANES - offset, LANES)
        here = pltpu.roll(g_ref[group, pl.ds(row, BLOCK_WORDS), :].astype(F32), shift, 1)
        after = pltpu.roll(g_ref[group + 1, pl.ds(row, BLOCK_WORDS), :].astype(F32), shift, 1)
        live = (len_ref[pl.ds(row, BLOCK_WORDS), :] > position).astype(F32)
        value = jnp.where(lane < LANES - offset, here, after)
        value = jnp.where(lane < BIAS_LANE, value, jnp.where(lane == BIAS_LANE, live, 0.0))
        x_ref[b * BLOCK_WORDS : (b + 1) * BLOCK_WORDS, :] = value.astype(BF16)


def embed_kernel(scalar_ref, ids_ref, table_ref, g_ref):
    groups = g_ref.shape[0]
    g_ref[...] = jnp.zeros_like(g_ref)
    identity = lax.broadcasted_iota(jnp.int32, (ROW_TILE, TABLE_PAD), 1)
    for group in range(groups - 1):

        def embed(step, carry, group=group):
            row = pl.multiple_of(step * ROW_TILE, ROW_TILE)
            total = jnp.zeros((ROW_TILE, LANES), F32)
            for k in range(GROUP):
                column = group * GROUP + k
                hot = (ids_ref[pl.ds(row, ROW_TILE), column : column + 1] == identity).astype(F32)
                total = total + dot(hot.astype(BF16), table_ref[k])
            g_ref[group, pl.ds(row, ROW_TILE), :] = total.astype(BF16)
            return carry

        lax.fori_loop(0, scalar_ref[1 + group], embed, 0)


def embed_characters(prep, table_blocks):
    _, ids, _, scalars, _, _ = prep
    return pl.pallas_call(
        embed_kernel,
        out_shape=jax.ShapeDtypeStruct((ids.shape[1] // GROUP, ids.shape[0], LANES), BF16),
        in_specs=[SMEM, VMEM, VMEM],
        out_specs=VMEM,
        compiler_params=pltpu.CompilerParams(vmem_limit_bytes=32 * MIB),
        cost_estimate=cost(5),
        name="embed",
    )(scalars, ids, table_blocks)


def conv_forward_kernel(
    scalar_ref, tile_ref, pos_ref, g_ref, w_ref, len_ref, pooled_ref, x_ref, pre_ref
):
    filters = w_ref.shape[1]
    part = pre_ref.shape[1]
    pooled_ref[...] = jnp.zeros_like(pooled_ref)

    def step(chunk, carry):
        build_windows(chunk, tile_ref, pos_ref, g_ref, len_ref, x_ref)
        for first in range(0, filters, part):
            half = dot(x_ref[...], w_ref[:, first : first + part])
            pre_ref[...] = half + half * jnp.tanh(half)
            for b in range(CHUNK_BLOCKS):
                row = pl.multiple_of(
                    tile_ref[chunk * CHUNK_BLOCKS + b] * BLOCK_WORDS, BLOCK_WORDS
                )
                pooled_ref[pl.ds(row, BLOCK_WORDS), first : first + part] += pre_ref[
                    b * BLOCK_WORDS : (b + 1) * BLOCK_WORDS, :
                ]
        return carry

    lax.fori_loop(0, scalar_ref[0], step, 0)
    pooled_ref[...] = pooled_ref[...] / len_ref[...].astype(F32)


def conv_forward(prep, char_groups, half_matrix):
    _, ids, lengths, scalars, tile, position = prep
    return pl.pallas_call(
        conv_forward_kernel,
        out_shape=jax.ShapeDtypeStruct((ids.shape[0], half_matrix.shape[1]), F32),
        in_specs=[SMEM, SMEM, SMEM, VMEM, VMEM, VMEM],
        out_specs=VMEM,
        scratch_shapes=[pltpu.VMEM((CHUNK, LANES), BF16), pltpu.VMEM((CHUNK, 512), F32)],
        compiler_params=pltpu.CompilerParams(vmem_limit_bytes=32 * MIB),
        cost_estimate=cost(16),
        name="conv_forward",
    )(scalars, tile, position, char_groups, half_matrix, lengths[:, None])


def conv_backward_kernel(
    scalar_ref, tile_ref, pos_ref, g_ref, w_ref, len_ref, gp_ref, out_ref, gg_ref, x_ref, d_ref, dw_ref
):
    filters = w_ref.shape[1]
    part = 512
    lane = lax.broadcasted_iota(jnp.int32, (BLOCK_WORDS, LANES), 1)
    dw_ref[...] = jnp.zeros_like(dw_ref)
    gg_ref[...] = jnp.zeros_like(gg_ref)

    def step(chunk, carry):
        build_windows(chunk, tile_ref, pos_ref, g_ref, len_ref, x_ref)
        for first in range(0, filters, part):
            columns = slice(first, first + part)
            half = dot(x_ref[...], w_ref[:, columns])
            tanh = jnp.tanh(half)
            slope = (1.0 + tanh) * (1.0 + (half - half * tanh))
            for b in range(CHUNK_BLOCKS):
                rows = slice(b * BLOCK_WORDS, (b + 1) * BLOCK_WORDS)
                row = pl.multiple_of(
                    tile_ref[chunk * CHUNK_BLOCKS + b] * BLOCK_WORDS, BLOCK_WORDS
                )
                d_ref[rows, columns] = (
                    gp_ref[pl.ds(row, BLOCK_WORDS), columns] * slope[rows]
                ).astype(BF16)
            dw_ref[:, columns] += dot_tn(x_ref[...], d_ref[:, columns])
        gx = dot_nt(d_ref[...], w_ref[...])
        for b in range(CHUNK_BLOCKS):
            block = chunk * CHUNK_BLOCKS + b
            row = pl.multiple_of(tile_ref[block] * BLOCK_WORDS, BLOCK_WORDS)
            position = pos_ref[block]
            group = position >> 3
            offset = (position & 7) * CHAR_DIM
            value = gx[b * BLOCK_WORDS : (b + 1) * BLOCK_WORDS, :]
            value = pltpu.roll(jnp.where(lane < BIAS_LANE, value, 0.0), offset, 1)
            gg_ref[group, pl.ds(row, BLOCK_WORDS), :] += jnp.where(lane >= offset, value, 0.0)
            gg_ref[group + 1, pl.ds(row, BLOCK_WORDS), :] += jnp.where(lane < offset, value, 0.0)
        return carry

    lax.fori_loop(0, scalar_ref[0], step, 0)
    out_ref[...] = dw_ref[...].T.astype(BF16)


def conv_backward(prep, char_groups, half_matrix, grad_scaled):
    _, ids, lengths, scalars, tile, position = prep
    filters = half_matrix.shape[1]
    return pl.pallas_call(
        conv_backward_kernel,
        out_shape=(
            jax.ShapeDtypeStruct((filters, LANES), BF16),
            jax.ShapeDtypeStruct(char_groups.shape, F32),
        ),
        in_specs=[SMEM, SMEM, SMEM, VMEM, VMEM, VMEM, VMEM],
        out_specs=(VMEM, VMEM),
        scratch_shapes=[
            pltpu.VMEM((CHUNK, LANES), BF16),
            pltpu.VMEM((CHUNK, filters), BF16),
            pltpu.VMEM((LANES, filters), F32),
        ],
        compiler_params=pltpu.CompilerParams(vmem_limit_bytes=48 * MIB),
        cost_estimate=cost(35),
        name="conv_backward",
    )(scalars, tile, position, char_groups, half_matrix, lengths[:, None], grad_scaled)


def table_kernel(scalar_ref, ids_ref, gg_ref, out_ref):
    groups = gg_ref.shape[0]
    out_ref[...] = jnp.zeros_like(out_ref)
    identity = lax.broadcasted_iota(jnp.int32, (TABLE_PAD, ROW_TILE), 0)
    for group in range(groups - 1):

        def step(index, carry, group=group):
            row = pl.multiple_of(index * ROW_TILE, ROW_TILE)
            grad = (2.0 * gg_ref[group, pl.ds(row, ROW_TILE), :]).astype(BF16)
            for k in range(GROUP):
                column = group * GROUP + k
                hot = (ids_ref[column : column + 1, pl.ds(row, ROW_TILE)] == identity).astype(F32)
                out_ref[k] += dot(hot.astype(BF16), grad)
            return carry

        lax.fori_loop(0, scalar_ref[1 + group], step, 0)


def table_gradient(prep, grad_groups, vocabulary):
    ids, scalars = prep[1], prep[3]
    total = pl.pallas_call(
        table_kernel,
        out_shape=jax.ShapeDtypeStruct((GROUP, TABLE_PAD, LANES), F32),
        in_specs=[SMEM, VMEM, VMEM],
        out_specs=VMEM,
        compiler_params=pltpu.CompilerParams(vmem_limit_bytes=32 * MIB),
        cost_estimate=cost(4),
        name="table",
    )(scalars, ids.T, grad_groups)
    parts = [total[k, :vocabulary, k * CHAR_DIM : (k + 1) * CHAR_DIM] for k in range(GROUP)]
    return sum(parts[1:], parts[0])


def table_lanes(table):
    padded = jnp.pad(table, ((0, TABLE_PAD - table.shape[0]), (0, 0)))
    return jnp.stack(
        [
            jnp.pad(padded, ((0, 0), (k * CHAR_DIM, LANES - (k + 1) * CHAR_DIM)))
            for k in range(GROUP)
        ]
    )


ANY = pl.BlockSpec(memory_space=pl.ANY)


def flat_pieces(pieces):
    return [array for half in pieces for chunk in half for array in chunk]


def piece_copies(layout, array, slot, first, own, pieces, whole_ref, sems, buffer):
    halves, chunks, arrays, rows = layout
    width = whole_ref.shape[2] // 2
    copies = []
    for half in range(halves):
        for chunk in range(chunks):
            ref = pieces[(half * chunks + chunk) * arrays + array]
            start = (own if half == 0 else 1 - own) * (chunks * rows) + chunk * rows
            start = pl.multiple_of(start, rows)
            for side in range(2):
                copies.append(
                    pltpu.make_async_copy(
                        ref.at[first if side == 0 else 1 - first, slot],
                        whole_ref.at[
                            buffer, pl.ds(start, rows), side * width : (side + 1) * width
                        ],
                        sems.at[buffer, len(copies)],
                    )
                )
    return copies


def fetch_pieces(layout, select_ref, own, pieces, whole_ref, sems):
    step = pl.program_id(0)

    def start(index):
        for array in range(layout[2]):

            @pl.when(index // 2 == array)
            def _(array=array):
                for copy in piece_copies(
                    layout, array, index % 2, select_ref[index], own, pieces, whole_ref, sems, index % 2
                ):
                    copy.start()

    @pl.when(step == 0)
    def _():
        start(0)

    @pl.when(step + 1 < pl.num_programs(0))
    def _():
        start(step + 1)

    buffer = step % 2
    for copy in piece_copies(layout, 0, 0, 0, own, pieces, whole_ref, sems, buffer):
        copy.wait()
    return buffer


def half_tanh(value):
    return 0.5 + 0.5 * jnp.tanh(0.5 * value)


def highway_forward_kernel(layout, place_ref, select_ref, core_ref, h_ref, bias_ref, *refs):
    count = layout[0] * layout[1] * layout[2]
    pieces = refs[:count]
    next_ref, transform_ref, gating_ref, low_ref, whole_ref, sems = refs[count:]
    step = pl.program_id(0)
    width = next_ref.shape[1]

    @pl.when(step == 0)
    def _():
        low_ref[...] = h_ref[...].astype(BF16)

    block = place_ref[step]
    blocks = bias_ref.shape[0] // 2
    buffer = fetch_pieces(layout, select_ref, core_ref[0], pieces, whole_ref, sems)
    mixed = dot(low_ref[...], whole_ref[buffer])
    transform = mixed[:, :width] + bias_ref[block]
    gating = half_tanh(mixed[:, width:] + bias_ref[block + blocks])
    h = h_ref[:, pl.ds(pl.multiple_of(block * width, width), width)]
    activated = transform * half_tanh(transform)
    transform_ref[...] = transform
    gating_ref[...] = gating
    next_ref[...] = activated + gating * (h - activated)


def highway_forward(h, pieces, bias_blocks, place, select, core):
    words, features = h.shape
    width = bias_blocks.shape[2]
    flat = flat_pieces(pieces)
    layout = (len(pieces), len(pieces[0]), len(pieces[0][0]), flat[0].shape[2])
    column = pl.BlockSpec((words, width), lambda j, place, *_: (0, place[j]))
    whole = lambda shape: pl.BlockSpec(shape, lambda j, *_: (0,) * len(shape))
    return pl.pallas_call(
        partial(highway_forward_kernel, layout),
        grid_spec=pltpu.PrefetchScalarGridSpec(
            num_scalar_prefetch=3,
            grid=(features // width,),
            in_specs=[whole(h.shape), whole(bias_blocks.shape)] + [ANY] * len(flat),
            out_specs=[column, column, column, whole(h.shape)],
            scratch_shapes=[
                pltpu.VMEM((2, features, 2 * width), BF16),
                pltpu.SemaphoreType.DMA((2, 2 * layout[0] * layout[1])),
            ],
        ),
        out_shape=(
            jax.ShapeDtypeStruct(h.shape, F32),
            jax.ShapeDtypeStruct(h.shape, F32),
            jax.ShapeDtypeStruct(h.shape, F32),
            jax.ShapeDtypeStruct(h.shape, BF16),
        ),
        compiler_params=pltpu.CompilerParams(vmem_limit_bytes=56 * MIB),
        cost_estimate=cost(19),
        name="highway_forward",
    )(place, select, core, h, bias_blocks, *flat)


def highway_backward_kernel(layout, place_ref, select_ref, core_ref, grad_ref, h_ref, t_ref, g_ref, *refs):
    count = layout[0] * layout[1] * layout[2]
    pieces = refs[:count]
    mixed_ref, sums_ref, out_ref, whole_ref, sems = refs[count:]
    step = pl.program_id(0)
    width = grad_ref.shape[1]
    features = out_ref.shape[1]

    @pl.when(step == 0)
    def _():
        out_ref[...] = jnp.zeros_like(out_ref)

    block = place_ref[step]
    buffer = fetch_pieces(layout, select_ref, core_ref[0], pieces, whole_ref, sems)
    grad = grad_ref[...]
    transform = t_ref[...]
    gating = g_ref[...]
    sigmoid = half_tanh(transform)
    activated = transform * sigmoid
    rest = grad * (1.0 - gating)
    low_t = (rest * (sigmoid + activated * (1.0 - sigmoid))).astype(BF16)
    low_g = (rest * gating * (h_ref[...] - activated)).astype(BF16)
    mixed_ref[0] = low_t
    mixed_ref[1] = low_g
    sums_ref[0] = jnp.sum(low_t.astype(F32), axis=0, keepdims=True)
    sums_ref[1] = jnp.sum(low_g.astype(F32), axis=0, keepdims=True)
    low = jnp.concatenate([low_t, low_g], axis=1)
    for start in range(0, features, 512):
        out_ref[:, start : start + 512] += dot_nt(
            low, whole_ref[buffer, start : start + 512, :]
        )
    out_ref[:, pl.ds(pl.multiple_of(block * width, width), width)] += grad * gating


def highway_backward(grad, h, transform, gating, pieces, place, select, core):
    words, features = h.shape
    flat = flat_pieces(pieces)
    width = flat[0].shape[3]
    layout = (len(pieces), len(pieces[0]), len(pieces[0][0]), flat[0].shape[2])
    column = pl.BlockSpec((words, width), lambda j, place, *_: (0, place[j]))
    return pl.pallas_call(
        partial(highway_backward_kernel, layout),
        grid_spec=pltpu.PrefetchScalarGridSpec(
            num_scalar_prefetch=3,
            grid=(features // width,),
            in_specs=[column] * 4 + [ANY] * len(flat),
            out_specs=[
                pl.BlockSpec((2, words, width), lambda j, place, *_: (0, 0, place[j])),
                pl.BlockSpec((2, 1, width), lambda j, place, *_: (0, 0, place[j])),
                pl.BlockSpec(h.shape, lambda j, *_: (0, 0)),
            ],
            scratch_shapes=[
                pltpu.VMEM((2, features, 2 * width), BF16),
                pltpu.SemaphoreType.DMA((2, 2 * layout[0] * layout[1])),
            ],
        ),
        out_shape=(
            jax.ShapeDtypeStruct((2, words, features), BF16),
            jax.ShapeDtypeStruct((2, 1, features), F32),
            jax.ShapeDtypeStruct(h.shape, F32),
        ),
        compiler_params=pltpu.CompilerParams(vmem_limit_bytes=56 * MIB),
        cost_estimate=cost(21),
        name="highway_backward",
    )(place, select, core, grad, h, transform, gating, *flat)


def weight_kernel(which_ref, left_ref, right_ref, *refs):
    out_ref = refs[-1]
    value = dot(left_ref[...], right_ref[0])
    width = out_ref.shape[2]
    for number in range(out_ref.shape[0]):
        block = value[:, number * width : (number + 1) * width]
        if len(refs) == 2:
            block = block + refs[0][number].astype(F32)
        out_ref[number] = block.astype(BF16)


def highway_weight_gradient(which, turned, mixed, first, rows, width, added=None, part=0):
    words, features = mixed.shape[1:]
    blocks = 8
    out = pl.BlockSpec((blocks, rows, width), lambda j, which: (j, 0, 0))
    return pl.pallas_call(
        weight_kernel,
        grid_spec=pltpu.PrefetchScalarGridSpec(
            num_scalar_prefetch=1,
            grid=(features // (blocks * width),),
            in_specs=[
                pl.BlockSpec((rows, words), lambda j, which: (first // rows, 0)),
                pl.BlockSpec((1, words, blocks * width), lambda j, which: (which[0], 0, j)),
            ]
            + (
                []
                if added is None
                else [pl.BlockSpec((blocks, rows, width), lambda j, which: (j, part, 0))]
            ),
            out_specs=out,
        ),
        out_shape=jax.ShapeDtypeStruct((features // width, rows, width), BF16),
        compiler_params=pltpu.CompilerParams(vmem_limit_bytes=32 * MIB),
        cost_estimate=cost(3),
        name="highway_weight",
    )(which, turned, mixed, *([] if added is None else [added]))


def turn_kernel(value_ref, out_ref):
    out_ref[...] = value_ref[...].T.astype(BF16)


def turn(value):
    rows, columns = value.shape
    return pl.pallas_call(
        turn_kernel,
        grid=(columns // 256,),
        in_specs=[pl.BlockSpec((rows, 256), lambda j: (0, j))],
        out_specs=pl.BlockSpec((256, rows), lambda j: (j, 0)),
        out_shape=jax.ShapeDtypeStruct((columns, rows), BF16),
        compiler_params=pltpu.CompilerParams(vmem_limit_bytes=32 * MIB),
        cost_estimate=cost(1),
        name="turn",
    )(value)


def place_rows_kernel(splits, place_ref, core_ref, *refs):
    arrays = (len(refs) - len(splits) - 1) // 2
    own_refs, other_refs = refs[:arrays], refs[arrays : 2 * arrays]
    out_refs, whole_ref = refs[2 * arrays : -1], refs[-1]
    step = pl.program_id(0)
    half_rows = own_refs[0].shape[1]
    core = core_ref[0]
    for array in range(arrays):

        @pl.when(step // 4 == array)
        def _(array=array):
            align = lambda start: pl.ds(pl.multiple_of(start, 16), half_rows)
            whole_ref[align(core * half_rows), :] = own_refs[array][0]
            whole_ref[align((1 - core) * half_rows), :] = other_refs[array][0]

    start = 0
    for rows, out_ref in zip(splits, out_refs):
        out_ref[...] = whole_ref[start : start + rows, :]
        start += rows


def place_rows(own, other, place, core, splits):
    half_rows, columns = own[0].shape[1:]

    def index(number):
        return lambda j, *_: (jnp.clip(j - 4 * number, 0, 3), 0, 0)

    specs = [pl.BlockSpec((1, half_rows, columns), index(number)) for number in range(len(own))]
    return pl.pallas_call(
        partial(place_rows_kernel, splits),
        grid_spec=pltpu.PrefetchScalarGridSpec(
            num_scalar_prefetch=2,
            grid=(4 * len(own),),
            in_specs=specs + specs,
            out_specs=[
                pl.BlockSpec((rows, columns), lambda j, place, *_: (place[j], 0)) for rows in splits
            ],
            scratch_shapes=[pltpu.VMEM((2 * half_rows, columns), BF16)],
        ),
        out_shape=[
            jax.ShapeDtypeStruct((4 * len(own) * rows, columns), BF16) for rows in splits
        ],
        compiler_params=pltpu.CompilerParams(vmem_limit_bytes=32 * MIB),
        cost_estimate=cost(7),
        name="place_rows",
    )(place, core, *own, *other)


def place_small_kernel(place_ref, *refs):
    inputs, (conv_ref, *row_refs) = refs[:4], refs[4:]
    step = pl.program_id(0)
    for number, ref in enumerate(inputs):

        @pl.when(step // 4 == number)
        def _(ref=ref):
            start = conv_ref.shape[0]
            conv_ref[...] = ref[0, :start, :]
            for row_ref in row_refs:
                row_ref[0] = ref[0, start : start + row_ref.shape[1], :]
                start += row_ref.shape[1]


def place_small(arrays, place, conv_rows, splits):
    rows, columns = arrays[0].shape[1:]

    def index(number):
        return lambda j, *_: (jnp.clip(j - 4 * number, 0, 3), 0, 0)

    return pl.pallas_call(
        place_small_kernel,
        grid_spec=pltpu.PrefetchScalarGridSpec(
            num_scalar_prefetch=1,
            grid=(16,),
            in_specs=[pl.BlockSpec((1, rows, columns), index(number)) for number in range(4)],
            out_specs=[pl.BlockSpec((conv_rows, columns), lambda j, place: (0, place[j]))]
            + [
                pl.BlockSpec((1, count, columns), lambda j, place: (place[j], 0, 0))
                for count in splits
            ],
        ),
        out_shape=[jax.ShapeDtypeStruct((conv_rows, 16 * columns), BF16)]
        + [jax.ShapeDtypeStruct((16, count, columns), BF16) for count in splits],
        compiler_params=pltpu.CompilerParams(vmem_limit_bytes=32 * MIB),
        cost_estimate=cost(2),
        name="place_small",
    )(place, *arrays)


LINKS = {
    "x": [(w, w ^ 1) for w in range(16)],
    "y": [(w, w ^ 2) for w in range(16)],
    "z": [(w, (w + 4) % 16) for w in range(16)],
    "back": [(w, (w - 4) % 16) for w in range(16)],
    "z1": [(w, w ^ 4) for w in range(16)],
    "z2": [(w, w ^ 8) for w in range(16)],
}
CORES = [(0, 1), (1, 0)]


def send(value, link):
    if link == "c":
        return lax.ppermute(value, "narrow", CORES)
    return lax.ppermute(value, "wide", LINKS[link])


def total_of(terms):
    return sum((term.astype(F32) for term in terms[1:]), terms[0].astype(F32))


class Exchange:
    windows = True

    def __init__(self):
        self.core = lax.axis_index("narrow")
        index = lax.axis_index("wide")
        self.z, self.y, self.x = index // 4, (index // 2) % 2, index % 2
        self.state, self.fresh, self.count, self.planned = {}, [], 0, []

    def put(self, key, value):
        self.state[key] = value
        self.fresh.append(key)

    def move(self, key, source, link):
        self.put(key, send(self.state[source], link))

    def plan(self, key, value, link, shape=None):
        self.planned.append((key, value, link, shape))

    def plan_move(self, source, *links):
        for link in links:
            self.plan(source + link, self.state[source], link)

    def plan_ring(self, name, step):
        self.plan(f"{name}r{step}", self.state[f"{name}r{step - 1}" if step > 1 else name], "z")

    def plan_swap(self, *names):
        for name in names:
            self.plan(name + "c", self.state[name], "c")

    def launch(self, values):
        leaves, tree = jax.tree.flatten(values)
        held = lax.optimization_barrier(
            tuple(value for _, value, _, _ in self.planned) + tuple(leaves)
        )
        for (key, _, link, shape), value in zip(self.planned, held):
            value = send(value, link)
            self.put(key, value if shape is None else value.reshape(shape))
        leaves = held[len(self.planned) :]
        self.planned = []
        return jax.tree.unflatten(tree, leaves)

    def window(self, values, hold=()):
        held_keys = [key for key in self.fresh if key in hold]
        self.fresh = [key for key in self.fresh if key not in hold]
        leaves, tree = jax.tree.flatten(values)
        held = lax.optimization_barrier(
            tuple(self.state[key] for key in self.fresh) + tuple(leaves)
        )
        for key, value in zip(self.fresh, held):
            self.state[key] = value
        leaves = held[len(self.fresh) :]
        self.fresh = held_keys
        return jax.tree.unflatten(tree, leaves)

    def swap_chain(self, *names):
        before = None
        for name in names:
            value = self.state[name]
            if before is not None:
                value, self.state[before] = lax.optimization_barrier((value, self.state[before]))
            before = name + "c"
            self.put(before, send(value, "c"))

    def stage(self, values=(), hold=()):
        return self.window(self.launch(values), hold)


    def load(self, name, value, rows=None, offset=0, whole=False):
        if not whole:
            rows = rows or value.shape[0] // 2
            value = lax.dynamic_slice_in_dim(
                value, self.core * (value.shape[0] // 2) + offset, rows, 0
            )
        self.state[name] = value

    def ring(self, name):
        received = [self.state[name]]
        for _ in range(3):
            received.append(send(received[-1], "z"))
        self.put(name + "o", jnp.stack(received))

    def ring_step(self, name, step):
        self.move(f"{name}r{step}", f"{name}r{step - 1}" if step > 1 else name, "z")

    def ring_both(self, name):
        self.put(name + "r1", send(self.state[name], "z"))
        self.put(name + "r3", send(self.state[name], "back"))
        self.put(name + "r2", send(self.state[name + "r1"], "z"))

    def ring_done(self, name):
        self.state[name + "o"] = jnp.stack(
            [self.state[name]] + [self.state[f"{name}r{step}"] for step in (1, 2, 3)]
        )

    def square(self, name):
        value = self.state[name]
        over_x = send(value, "x")
        self.put(name + "o0", jnp.stack([value, over_x, send(value, "y"), send(over_x, "y")]))

    def turn_ring(self, name, step):
        self.move(f"{name}o{step}", f"{name}o{step - 1}", "z")

    def swap(self, *names):
        for name in names:
            self.move(name + "c", name, "c")

    def near(self, name, suffix=""):
        return [self.state[name + part + suffix] for part in ("o", "ox", "oy", "oxy")]

    def layer(self, name, chunks):
        halves = []
        for suffix in ("", "c"):
            halves.append(
                [
                    [
                        array.reshape((2, 2) + array.shape[1:])
                        for array in self.near(f"{name}{chunk}", suffix)
                    ]
                    for chunk in range(chunks)
                ]
            )
        return halves

    def place(self, ring_last):
        step = jnp.arange(16)
        near, slot = (step % 4, step // 4) if ring_last else (step // 4, step % 4)
        return (
            (self.z - slot) % 4 * 4 + (self.y ^ (near >> 1)) * 2 + (self.x ^ (near & 1))
        ).astype(jnp.int32)

    def rows(self, own, other, splits, ring_last):
        core = self.core[None].astype(jnp.int32)
        return place_rows(own, other, self.place(ring_last), core, splits)


    def split(self, grads):
        blocks = [grad.astype(BF16).reshape(2, 16, -1, grad.shape[1]) for grad in grads]
        return tuple(
            jnp.concatenate(
                [lax.dynamic_index_in_dim(block, which, 0, keepdims=False) for block in blocks],
                axis=1,
            )
            for which in (self.core, 1 - self.core)
        )


class Reduction:
    def __init__(self, net, keep, sent, order):
        shape = (4, 2, 2) + keep.shape[1:]
        self.net, self.order, self.done = net, list(order), 0
        net.count += 1
        self.name = f"sum{net.count}"
        self.terms = [keep.reshape(shape)]
        self.keys, self.running, self.axes = [], None, ["z", "y", "x"]
        self.sent, self.shape = sent, shape

    def all_terms(self):
        return self.terms + [self.net.state[key] for key in self.keys]

    def pick(self, terms, index, axis):
        return [lax.dynamic_index_in_dim(term, index, axis, keepdims=False) for term in terms]

    def keep_only(self, index, axis):
        self.terms = self.pick(self.all_terms(), index, axis)
        self.keys = []

    def step(self, put=None):
        net, link = self.net, self.order[self.done]
        put = put or (lambda key, value, link, shape=None: net.put(
            key, send(value, link) if shape is None else send(value, link).reshape(shape)
        ))
        self.key = key = f"{self.name}_{self.done}"
        self.done += 1
        if link == "c":
            put(key, self.sent, "c", self.shape)
            self.keys.append(key)
        elif link in ("x", "y"):
            axis = self.axes.index(link)
            index = net.x if link == "x" else net.y
            sent = total_of(self.pick(self.all_terms(), 1 - index, axis)).astype(BF16)
            self.keep_only(index, axis)
            self.axes.remove(link)
            put(key, sent, link)
            self.keys.append(key)
        else:
            axis = self.axes.index("z")
            index = (net.z + int(link)) % 4
            terms = self.pick(self.all_terms(), index, axis)
            if self.running is not None:
                terms.append(net.state[self.running])
            put(key, total_of(terms).astype(BF16), "z")
            self.running = key
            if link == "1":
                self.keep_only(net.z, axis)
                self.axes.remove("z")
                self.keys = [key]
        return self

    def result(self):
        assert self.done == len(self.order)
        return total_of(self.all_terms())


class Ring:
    def __init__(self, net, sums, both):
        self.net, self.sums, self.both, self.done = net, sums, both, 0
        self.arrived = []
        net.count += 1
        self.name = f"ring{net.count}"

    def part(self, distance):
        index = (self.net.z + distance) % 4
        parts = [total_of(item.pick(item.all_terms(), index, 0)) for item in self.sums]
        value = parts[0] if len(parts) == 1 else jnp.concatenate(parts, axis=0)
        for key in self.arrived:
            value = value + self.net.state[key].astype(F32)
        return value

    def step(self, put):
        self.done += 1
        self.key = key = f"{self.name}_{self.done}"
        if self.both and self.done == 1:
            self.last_key = f"{self.name}_back"
            put(self.last_key, self.part(3).astype(BF16), "back")
            put(key, self.part(2).astype(BF16), "z")
        else:
            put(key, self.part((3 if self.both else 4) - self.done).astype(BF16), "z")
        self.arrived = [key]
        return self

    def result(self):
        assert self.done == (2 if self.both else 3)
        if self.both:
            self.arrived = self.arrived + [self.last_key]
        return self.part(0)


class Small:
    def __init__(self, net, value):
        self.net, self.value, self.done, self.key = net, value, 0, None
        net.count += 1
        self.name = f"t{net.count}"

    def result(self):
        return self.value if self.key is None else self.value + self.net.state[self.key]

    def step(self, put):
        self.value = self.result()
        self.key = f"{self.name}_{self.done}"
        put(self.key, self.value, ("c", "z1", "x", "y", "z2")[self.done])
        self.done += 1
        return self


class PlainReduction:
    def __init__(self, grads, axis):
        self.grads, self.axis = grads, axis

    def step(self):
        return self

    def result(self):
        return [
            lax.psum_scatter(
                grad.astype(BF16), ("narrow", "wide"), scatter_dimension=self.axis, tiled=True
            ).astype(F32)
            for grad in self.grads
        ]


def norm_rows(value, norm_gain, norm_shift):
    center = jnp.mean(value, axis=-1, keepdims=True)
    offsets = value - center
    spread = jnp.mean(offsets * offsets, axis=-1, keepdims=True)
    return offsets * lax.rsqrt(spread + EPSILON) * norm_gain + norm_shift


def norm_back(value, norm_gain, grad_rows):
    center = jnp.mean(value, axis=-1, keepdims=True)
    offsets = value - center
    spread = jnp.mean(offsets * offsets, axis=-1, keepdims=True)
    scale = lax.rsqrt(spread + EPSILON)
    normal = offsets * scale
    inner = grad_rows * norm_gain
    grad = scale * (
        inner
        - jnp.mean(inner, axis=-1, keepdims=True)
        - normal * jnp.mean(inner * normal, axis=-1, keepdims=True)
    )
    return grad, jnp.sum(grad_rows * normal, axis=0), jnp.sum(grad_rows, axis=0)


def array_copies(array, refs, held_ref, sems):
    count = len(refs)
    return [
        pltpu.make_async_copy(
            refs[index], held_ref.at[index], sems.at[index]
        )
        for index in range(array, count, count // 4)
    ]


def join_rows(slot_ref, own, refs, held_ref, up_ref, down_ref, sems):
    count = len(refs)
    arrays = count // 4
    step = pl.program_id(0)

    @pl.when(step == 0)
    def _():
        for array in range(arrays):
            for copy in array_copies(array, refs, held_ref, sems):
                copy.start()

    for array in range(arrays):

        @pl.when(step == 2 * array)
        def _(array=array):
            for copy in array_copies(array, refs, held_ref, sems):
                copy.wait()

    rows = held_ref.shape[2]
    near = step // 2
    for number in range(2):
        slot = slot_ref[step, number]
        for half in range(2):
            start = (own if half == 0 else 1 - own) * rows + number * 2 * rows
            where = pl.ds(pl.multiple_of(start, rows), rows)
            up_ref[where, :] = held_ref[half * arrays + near, slot]
            down_ref[where, :] = held_ref[(2 + half) * arrays + near, slot]


def normal_share(value, bell):
    t = 1.0 / (1.0 + (0.3275911 * 2**-0.5) * jnp.abs(value))
    series = 1.061405429
    for term in (-1.453152027, 1.421413741, -0.284496736, 0.254829592):
        series = series * t + term
    tail = (0.5 * series) * (t * bell)
    return jnp.where(value < 0.0, tail, 1.0 - tail)


def feed_forward_kernel(
    count, slot_ref, block_ref, core_ref, first_ref, bias_ref, vectors_ref, cotangent_ref, *refs
):
    (
        act_ref,
        slope_ref,
        hidden_ref,
        grad_ref,
        sums_ref,
        held_ref,
        up_ref,
        down_ref,
        low_ref,
        total_ref,
        sems,
    ) = refs[2 * count :]
    step = pl.program_id(0)

    @pl.when(step == 0)
    def _():
        low_ref[...] = first_ref[...].astype(BF16)
        total_ref[...] = first_ref[...] + vectors_ref[0:1, :]

    join_rows(slot_ref, core_ref[0], refs[: 2 * count], held_ref, up_ref, down_ref, sems)
    inner = dot_nt(low_ref[...], up_ref[...]) + bias_ref[block_ref[step]]
    bell = jnp.exp(-0.5 * inner * inner)
    share = normal_share(inner, bell)
    act = (inner * share).astype(BF16)
    act_ref[0] = act
    slope_ref[0] = (
        share + inner * (bell * (2.0 * jnp.pi) ** -0.5)
    ).astype(BF16)
    total_ref[...] += dot(act, down_ref[...])

    @pl.when(step == pl.num_programs(0) - 1)
    def _():
        value = total_ref[...]
        gain, shift = vectors_ref[1:2, :], vectors_ref[2:3, :]
        offsets = value - jnp.mean(value, axis=-1, keepdims=True)
        scale = lax.rsqrt(jnp.mean(offsets * offsets, axis=-1, keepdims=True) + EPSILON)
        normal = offsets * scale
        hidden_ref[...] = (normal * gain + shift).astype(BF16)
        cotangent = cotangent_ref[...].astype(F32)
        pulled = cotangent * gain
        grad = scale * (
            pulled
            - jnp.mean(pulled, axis=-1, keepdims=True)
            - normal * jnp.mean(pulled * normal, axis=-1, keepdims=True)
        )
        grad_ref[...] = grad
        sums_ref[0:1, :] = jnp.sum(cotangent * normal, axis=0, keepdims=True)
        sums_ref[1:2, :] = jnp.sum(cotangent, axis=0, keepdims=True)
        sums_ref[2:3, :] = jnp.sum(grad.astype(BF16).astype(F32), axis=0, keepdims=True)
        sums_ref[3:8, :] = jnp.zeros((5, sums_ref.shape[1]), F32)


def feed_forward(first, pieces, bias_blocks, vectors, cotangent, slots, block, core):
    words, columns = first.shape
    steps, width = bias_blocks.shape[0], bias_blocks.shape[2]
    up, down = pieces
    whole = lambda shape: pl.BlockSpec(shape, lambda j, *_: (0,) * len(shape))
    tile = pl.BlockSpec((1, words, width), lambda j, *_: (j, 0, 0))
    return pl.pallas_call(
        partial(feed_forward_kernel, len(up)),
        grid_spec=pltpu.PrefetchScalarGridSpec(
            num_scalar_prefetch=3,
            grid=(steps,),
            in_specs=[
                whole(first.shape),
                whole(bias_blocks.shape),
                whole(vectors.shape),
                whole(cotangent.shape),
            ]
            + [ANY] * (len(up) + len(down)),
            out_specs=[tile, tile, whole(first.shape), whole(first.shape), whole((8, columns))],
            scratch_shapes=[
                pltpu.VMEM((len(up) + len(down),) + up[0].shape, BF16),
                pltpu.VMEM((width, columns), BF16),
                pltpu.VMEM((width, columns), BF16),
                pltpu.VMEM((words, columns), BF16),
                pltpu.VMEM((words, columns), F32),
                pltpu.SemaphoreType.DMA((len(up) + len(down),)),
            ],
        ),
        out_shape=(
            jax.ShapeDtypeStruct((steps, words, width), BF16),
            jax.ShapeDtypeStruct((steps, words, width), BF16),
            jax.ShapeDtypeStruct((words, columns), BF16),
            jax.ShapeDtypeStruct((words, columns), F32),
            jax.ShapeDtypeStruct((8, columns), F32),
        ),
        compiler_params=pltpu.CompilerParams(vmem_limit_bytes=56 * MIB),
        cost_estimate=cost(20),
        name="feed_forward",
    )(slots, block, core, first, bias_blocks, vectors, cotangent, *up, *down)


def feed_forward_back_kernel(
    count,
    slot_ref,
    block_ref,
    core_ref,
    grad_ref,
    first_ref,
    act_ref,
    slope_ref,
    value_ref,
    gain_ref,
    *refs,
):
    (
        up_keep_ref,
        up_sent_ref,
        down_keep_ref,
        down_sent_ref,
        bias_ref,
        out_ref,
        sums_ref,
        held_ref,
        up_ref,
        down_ref,
        low_ref,
        low_first_ref,
        total_ref,
        sems,
    ) = refs[2 * count :]
    step = pl.program_id(0)

    @pl.when(step == 0)
    def _():
        total_ref[...] = grad_ref[...]
        low_ref[...] = grad_ref[...].astype(BF16)
        low_first_ref[...] = first_ref[...].astype(BF16)

    join_rows(slot_ref, core_ref[0], refs[: 2 * count], held_ref, up_ref, down_ref, sems)
    low = low_ref[...]
    inner = (dot_nt(low, down_ref[...]) * slope_ref[0].astype(F32)).astype(BF16)
    bias_ref[0] = jnp.sum(inner.astype(F32), axis=0, keepdims=True)
    grad_down = dot_tn(act_ref[0], low).astype(BF16)
    grad_up = dot_tn(inner, low_first_ref[...]).astype(BF16)
    total_ref[...] += dot(inner, up_ref[...])
    rows = up_keep_ref.shape[3]

    def store(value, ref):
        for number in range(4):
            ref[number // 2, 0, number % 2] = value[number * rows : (number + 1) * rows, :]

    @pl.when(step % 2 == 0)
    def _():
        store(grad_up, up_sent_ref)
        store(grad_down, down_sent_ref)

    @pl.when(step % 2 == 1)
    def _():
        store(grad_up, up_keep_ref)
        store(grad_down, down_keep_ref)

    @pl.when(step == pl.num_programs(0) - 1)
    def _():
        value = value_ref[...]
        pulling = total_ref[...]
        offsets = value - jnp.mean(value, axis=-1, keepdims=True)
        scale = lax.rsqrt(jnp.mean(offsets * offsets, axis=-1, keepdims=True) + EPSILON)
        normal = offsets * scale
        pulled = pulling * gain_ref[...]
        grad = scale * (
            pulled
            - jnp.mean(pulled, axis=-1, keepdims=True)
            - normal * jnp.mean(pulled * normal, axis=-1, keepdims=True)
        )
        out_ref[...] = grad
        sums_ref[0:1, :] = jnp.sum(pulling * normal, axis=0, keepdims=True)
        sums_ref[1:2, :] = jnp.sum(pulling, axis=0, keepdims=True)
        sums_ref[2:3, :] = jnp.sum(grad.astype(BF16).astype(F32), axis=0, keepdims=True)
        sums_ref[3:8, :] = jnp.zeros((5, sums_ref.shape[1]), F32)


def feed_forward_back(grad, first, act, slope, value, gain, pieces, slots, block, core):
    words, columns = first.shape
    steps, _, width = act.shape
    up, down = pieces
    rows = width // 4
    whole = lambda shape: pl.BlockSpec(shape, lambda j, *_: (0,) * len(shape))
    tile = pl.BlockSpec((1, words, width), lambda j, *_: (j, 0, 0))
    out = pl.BlockSpec(
        (2, 1, 2, rows, columns), lambda j, slots, block, core: (0, block[j] % (steps // 2), 0, 0, 0)
    )
    part = jax.ShapeDtypeStruct((2, steps // 2, 2, rows, columns), BF16)
    return pl.pallas_call(
        partial(feed_forward_back_kernel, len(up)),
        grid_spec=pltpu.PrefetchScalarGridSpec(
            num_scalar_prefetch=3,
            grid=(steps,),
            in_specs=[
                whole(grad.shape),
                whole(first.shape),
                tile,
                tile,
                whole(value.shape),
                whole(gain.shape),
            ]
            + [ANY] * (len(up) + len(down)),
            out_specs=[
                out,
                out,
                out,
                out,
                pl.BlockSpec((1, 1, width), lambda j, slots, block, core: (block[j], 0, 0)),
                whole(first.shape),
                whole((8, columns)),
            ],
            scratch_shapes=[
                pltpu.VMEM((len(up) + len(down),) + up[0].shape, BF16),
                pltpu.VMEM((width, columns), BF16),
                pltpu.VMEM((width, columns), BF16),
                pltpu.VMEM((words, columns), BF16),
                pltpu.VMEM((words, columns), BF16),
                pltpu.VMEM((words, columns), F32),
                pltpu.SemaphoreType.DMA((len(up) + len(down),)),
            ],
        ),
        out_shape=(
            part,
            part,
            part,
            part,
            jax.ShapeDtypeStruct((steps, 1, width), F32),
            jax.ShapeDtypeStruct((words, columns), F32),
            jax.ShapeDtypeStruct((8, columns), F32),
        ),
        compiler_params=pltpu.CompilerParams(vmem_limit_bytes=56 * MIB),
        cost_estimate=cost(25),
        name="feed_back",
    )(slots, block, core, grad, first, act, slope, value, gain, *up, *down)


def softmax_parts(query, key):
    scores = dot_nt(query, key)
    scaling = HEAD_DIM ** (-0.5) * 1.4426950408889634
    exponent = jnp.exp2((scores - jnp.max(scores, axis=-1, keepdims=True)) * scaling)
    return exponent, 1.0 / jnp.sum(exponent, axis=-1, keepdims=True)


def attend_kernel(query_ref, key_ref, value_ref, out_ref):
    for start in range(0, LANES, HEAD_DIM):
        head = slice(start, start + HEAD_DIM)
        exponent, scale = softmax_parts(query_ref[:, head], key_ref[:, head])
        attention = (exponent * scale).astype(BF16)
        out_ref[:, head] = dot(attention, value_ref[:, head]).astype(BF16)


def third(number, words, thirds):
    return pl.BlockSpec((words, LANES), lambda j: (0, number * thirds + j))


def attend(qkv):
    words = qkv.shape[0]
    pairs = qkv.shape[1] // (3 * LANES)
    return pl.pallas_call(
        attend_kernel,
        grid=(pairs,),
        in_specs=[third(number, words, pairs) for number in range(3)],
        out_specs=third(0, words, pairs),
        out_shape=jax.ShapeDtypeStruct((words, pairs * LANES), BF16),
        compiler_params=pltpu.CompilerParams(vmem_limit_bytes=32 * MIB),
        cost_estimate=cost(12),
        name="attend",
    )(qkv, qkv, qkv)


def attend_back_kernel(
    query_ref, key_ref, value_ref, grad_ref, grad_query_ref, grad_key_ref, grad_value_ref
):
    scaling = HEAD_DIM ** (-0.5)
    for start in range(0, LANES, HEAD_DIM):
        head = slice(start, start + HEAD_DIM)
        query, key = query_ref[:, head], key_ref[:, head]
        grad = grad_ref[:, head]
        exponent, scale = softmax_parts(query, key)
        attention = exponent * scale
        grad_attention = dot_nt(grad, value_ref[:, head])
        inner = jnp.sum(grad_attention * attention, axis=-1, keepdims=True)
        grad_scores = (attention * (grad_attention - inner)).astype(BF16)
        grad_value_ref[:, head] = dot_tn(attention.astype(BF16), grad).astype(BF16)
        grad_query_ref[:, head] = (dot(grad_scores, key) * scaling).astype(BF16)
        grad_key_ref[:, head] = (dot_tn(grad_scores, query) * scaling).astype(BF16)


def attend_back(qkv, grad_context):
    words = qkv.shape[0]
    pairs = qkv.shape[1] // (3 * LANES)
    out = third(0, words, pairs)
    return jnp.concatenate(
        pl.pallas_call(
            attend_back_kernel,
            grid=(pairs,),
            in_specs=[third(number, words, pairs) for number in range(3)] + [out],
            out_specs=(out, out, out),
            out_shape=(jax.ShapeDtypeStruct(grad_context.shape, BF16),) * 3,
            compiler_params=pltpu.CompilerParams(vmem_limit_bytes=32 * MIB),
            cost_estimate=cost(17),
        name="attend_back",
        )(qkv, qkv, qkv, grad_context),
        axis=1,
    )


def gather_plain(value, axis):
    return lax.all_gather(value, "wide", axis=axis, tiled=True)


def plain_pieces(weight, chunks):
    whole = gather_plain(weight, 1)
    rows = whole.shape[0] // (2 * chunks)
    width = whole.shape[1] // 16
    halves = []
    for half in range(2):
        pieces = []
        for chunk in range(chunks):
            start = (half * chunks + chunk) * rows
            arrays = []
            for near in range(4):
                slots = []
                for slot in range(4):
                    block = (-slot % 4) * 4 + near
                    slots.append(whole[start : start + rows, block * width : (block + 1) * width])
                arrays.append(jnp.stack(slots).reshape(2, 2, rows, width))
            pieces.append(arrays)
        halves.append(pieces)
    return halves


def vector_rows(vectors):
    rows, places, start = [], [], 0
    for vector in vectors:
        count = -(-vector.shape[0] // LANES)
        padded = jnp.pad(vector, (0, count * LANES - vector.shape[0]))
        rows.append(padded.reshape(count, LANES))
        places.append((start, count, vector.shape[0]))
        start += count
    return jnp.pad(jnp.concatenate(rows, axis=0), ((0, -start % 16), (0, 0))), places


def plain_rows(whole):
    rows = whole.shape[0] // 16
    arrays = []
    for half in range(2):
        for near in range(4):
            starts = [((-slot % 4) * 4 + near) * rows + half * rows // 2 for slot in range(4)]
            arrays.append(jnp.stack([whole[start : start + rows // 2] for start in starts]))
    return arrays


def body(
    permutes,
    wide,
    devices,
    char_ids,
    word_lengths,
    type_ids,
    cotangent,
    character_embedding_table,
    conv_weight,
    conv_bias,
    high_weight,
    high_bias,
    proj_weight,
    proj_bias,
    pos_table,
    type_table,
    embed_gain,
    embed_shift,
    qkv_weight,
    attn_bias,
    out_weight,
    out_bias,
    attn_gain,
    attn_shift,
    up_weight,
    up_bias,
    down_weight,
    down_bias,
    ffn_gain,
    ffn_shift,
):
    layers, features = high_weight.shape[:2]
    words, chars = char_ids.shape[1:]
    model_width = proj_weight.shape[1]
    conv_rows = conv_weight.shape[0]
    lengths = word_lengths[0]
    vectors = [high_bias[layer] for layer in range(layers)] + [
        attn_bias,
        type_table[0],
        type_table[1],
        proj_bias,
        embed_gain,
        embed_shift,
        out_bias,
        attn_gain,
        attn_shift,
        up_bias,
        down_bias,
        ffn_gain,
        ffn_shift,
    ]
    conv_block = jnp.pad(
        jnp.concatenate([conv_weight, conv_bias[None]], axis=0),
        ((0, LANES - conv_rows - 1), (0, 0)),
    )
    vector_block, places = vector_rows(vectors)

    if permutes:
        net = Exchange()
        window, launch = net.window, net.launch
        core_index, z, y, x = net.core, net.z, net.y, net.x
        net.load(
            "t",
            jnp.concatenate([conv_block, vector_block, pos_table.T.reshape(-1, LANES)], axis=0),
            whole=True,
        )
        chunk_rows = features // 4
        net.load("L00", high_weight[0], chunk_rows, 0)
        (
            net.state["L00"],
            net.state["t"],
            char_ids,
            lengths,
            high_weight,
            qkv_weight,
            up_weight,
        ) = lax.optimization_barrier(
            (
                net.state["L00"],
                net.state["t"],
                char_ids,
                lengths,
                high_weight,
                qkv_weight,
                up_weight,
            )
        )
        for layer, chunk in ((0, 1), (1, 0), (1, 1)):
            net.load(f"L{layer}{chunk}", high_weight[layer], chunk_rows, chunk * chunk_rows)
        encoder_splits = [
            qkv_weight.shape[1],
            out_weight.shape[0],
            proj_weight.shape[0],
        ]
        net.load(
            "e",
            jnp.concatenate(
                [qkv_weight.T, out_weight, proj_weight],
                axis=0,
            ),
        )
        net.load("up", up_weight.T)
        net.load("down", down_weight)
        net.put("L00r1", send(net.state["L00"], "z"))
        net.put("L00r3", send(net.state["L00"], "back"))
        net.move("tx", "t", "x")
        net.move("ty", "t", "y")
    else:
        window = lambda values, hold=(): values
        launch = window
        core_index = z = y = x = jnp.zeros((), jnp.int32)
    prep = sort_words(char_ids[0], lengths, chars // GROUP + 2)
    table_blocks = table_lanes(character_embedding_table)
    prep, table_blocks = window((prep, table_blocks))
    if permutes:
        net.ring_step("L00", 2)
        net.move("txy", "tx", "y")
        net.move("ex", "e", "x")
        net.move("ey", "e", "y")
        window(())
        net.ring_done("L00")
        net.state["to0"] = jnp.stack(
            [net.state["t" + part] for part in ("", "x", "y", "xy")]
        )
        net.plan_move("L00o", "x", "y")
        net.plan("to1", net.state["to0"], "z")
        launch(())
        net.turn_ring("t", 2)
        net.move("exy", "ex", "y")
        net.ring_both("L01")
        net.state["eo0"] = jnp.stack([net.state["e" + part] for part in ("", "x", "y", "xy")])
        prep, table_blocks = window((prep, table_blocks))
        net.ring_done("L01")
        net.plan_move("L01o", "x", "y")
        net.plan("to3", net.state["to2"], "z")
        prep, table_blocks = launch((prep, table_blocks))
        net.ring_both("L10")
        net.swap_chain("L00o", "L00ox", "L00oy")
    char_groups = embed_characters(prep, table_blocks)
    char_groups = window(char_groups)

    if permutes:
        net.ring_done("L10")
        conv_all, whole_vectors, pos_all = place_small(
            [net.state[f"to{step}"] for step in range(4)],
            net.place(True),
            LANES,
            [vector_block.shape[0], pos_table.size // LANES],
        )
    else:
        conv_all = gather_plain(conv_block, 1)
        whole_vectors = lax.all_gather(vector_block, "wide", axis=0, tiled=False)
        pos_all = gather_plain(pos_table.T, 0)
    filters = conv_all.shape[1]
    row = jnp.arange(LANES)[:, None]
    usable = row // CHAR_DIM < filter_widths(filters)[None, :]
    half_matrix = jnp.where(usable | (row >= conv_rows), conv_all * BF16(0.5), BF16(0.0))
    if permutes:
        net.plan("L00oxy", net.state["L00ox"], "y")
        net.plan("L01oxy", net.state["L01oy"], "x")
        net.state["eo0"] = jnp.stack([net.state["e" + part] for part in ("", "x", "y", "xy")])
        net.plan("eo1", net.state["eo0"], "z")
        half_matrix = launch(half_matrix)
        net.swap_chain("L01o", "L01ox", "L01oy")
    pooled = conv_forward(prep, char_groups, half_matrix)
    pooled, whole_vectors, pos_all = window((pooled, whole_vectors, pos_all))
    whole = [
        whole_vectors[:, start : start + count].reshape(wide, -1)[:, :size].reshape(-1)
        for start, count, size in places
    ]
    if permutes:
        net.plan_move("L10o", "x", "y")
        launch(())
        net.ring_both("L11")
        net.swap_chain("L00oxy", "L01oxy", "eo0")
        pooled, whole, pos_all = window((pooled, whole, pos_all))
        net.ring_done("L11")
        net.plan_move("L11o", "x", "y")
        net.plan("eo2", net.state["eo1"], "z")
        net.plan_swap("L10o")
        pooled = launch(pooled)
        pieces = [net.layer("L0", 2)]
    else:
        pieces = [plain_pieces(high_weight[layer], 2) for layer in range(layers)]
    high_bias_all, attn_bias_all = whole[:layers], whole[layers]
    (
        type_zero,
        type_one,
        proj_bias_all,
        gain_zero,
        shift_zero,
        out_bias_all,
        gain_one,
        shift_one,
        up_bias_all,
        down_bias_all,
        gain_two,
        shift_two,
    ) = (value.astype(F32) for value in whole[layers + 1 :])
    width = 2 * features // 16
    order = jnp.arange(8)
    near, low_slot = order // 2, order % 2
    slot_z = (z - low_slot) % 4
    place = ((slot_z & 1) * 4 + (y ^ (near >> 1)) * 2 + (x ^ (near & 1))).astype(jnp.int32)
    select = (slot_z // 2).astype(jnp.int32)
    core = core_index[None].astype(jnp.int32)
    bias_blocks = [bias.astype(F32).reshape(16, 1, width) for bias in high_bias_all]
    first_layer = highway_forward(pooled, pieces[0], bias_blocks[0], place, select, core)
    first_layer = window(first_layer)

    if permutes:
        net.plan("L10oxy", net.state["L10ox"], "y")
        net.plan("L11oxy", net.state["L11oy"], "x")
        net.plan("eo3", net.state["eo2"], "z")
        first_layer, pos_all = launch((first_layer, pos_all))
        net.swap_chain("L10ox", "L10oy", "L11o", "L11ox", "L11oy", "eo1", "eo2")
    turned = [turn(first_layer[3])]
    pos_rows = pos_all.reshape(model_width, words).T.astype(F32)
    turned, pos_rows = window((turned, pos_rows))
    if permutes:
        net.plan_swap("L10oxy", "L11oxy")
        for name in ("up", "down"):
            net.plan(name + "r1", net.state[name], "z")
            net.plan(name + "r3", net.state[name], "back")
        first_layer = net.stage(first_layer)
        for name in ("up", "down"):
            net.plan(name + "r2", net.state[name + "r1"], "z")
        net.plan_swap("eo3")
        first_layer = launch(first_layer)
        pieces.append(net.layer("L1", 2))
        qkv_all, out_all, proj_all = net.rows(
            [net.state[f"eo{step}"] for step in range(4)],
            [net.state[f"eo{step}c"] for step in range(4)],
            encoder_splits,
            True,
        )
    else:
        qkv_all, out_all, proj_all = (
            gather_plain(value, 0) for value in (qkv_weight.T, out_weight, proj_weight)
        )
    second_layer = highway_forward(first_layer[0], pieces[1], bias_blocks[1], place, select, core)
    second_layer = window(second_layer)
    if permutes:
        net.ring_done("up")
        net.ring_done("down")
        net.plan_move("upo", "x", "y")
        net.plan_move("downo", "x", "y")
        second_layer = launch(second_layer)
    states = [pooled, first_layer[0], second_layer[0]]
    transforms = [first_layer[1], second_layer[1]]
    gatings = [first_layer[2], second_layer[2]]
    perm, sorted_lengths = prep[0], prep[2]
    last = dot_tn(perm, states[2].astype(BF16)).astype(BF16)
    word_vec = dot(last, proj_all) + proj_bias_all
    type_rows = jnp.where(type_ids[0][:, None] == 1, type_one[None], type_zero[None])
    summed = word_vec + pos_rows + type_rows
    embedded = norm_rows(summed, gain_zero, shift_zero)
    turned.append(turn(second_layer[3]))
    summed, embedded, last, turned = window((summed, embedded, last, turned))

    if permutes:
        net.plan("upoxy", net.state["upox"], "y")
        net.plan("downoxy", net.state["downoy"], "x")
        embedded = launch(embedded)
        net.swap_chain("upo", "upox", "upoy", "downo")
    low_embedded = embedded.astype(BF16)
    bias_three = jnp.concatenate(
        [
            attn_bias_all[:model_width],
            jnp.zeros((model_width,), BF16),
            attn_bias_all[model_width:],
        ]
    ).astype(F32)
    qkv = (dot_nt(low_embedded, qkv_all) + bias_three).astype(BF16)
    context = attend(qkv)
    if permutes:
        context = window(context)
        net.plan_swap("downox", "downoy", "upoxy", "downoxy")
        context = launch(context)
    first_in = embedded + (dot(context, out_all) + out_bias_all)
    first = norm_rows(first_in, gain_one, shift_one)
    if permutes:
        first_in, first = window((first_in, first))
        feed_pieces = [net.near(name) + net.near(name, "c") for name in ("up", "down")]
    else:
        feed_pieces = [
            plain_rows(gather_plain(value, 0)) for value in (up_weight.T, down_weight)
        ]
    half_of = jnp.where(order % 2 == 0, 1 - core_index, core_index)
    slots = (z - (2 * half_of[:, None] + jnp.arange(2)[None, :])) % 4
    slots = slots.astype(jnp.int32)
    feed_block = (half_of * 4 + (y ^ (near >> 1)) * 2 + (x ^ (near & 1))).astype(jnp.int32)
    feed_rows = up_bias_all.shape[0] // 16
    feed_bias = jnp.moveaxis(up_bias_all.reshape(2, 2, 4, feed_rows), 1, 2).reshape(8, 1, -1)
    act, slope, hidden_out, grad_second, last_sums = feed_forward(
        first,
        feed_pieces,
        feed_bias,
        jnp.stack([down_bias_all, gain_two, shift_two]),
        cotangent[0],
        slots,
        feed_block,
        core,
    )
    grad_ffn_gain, grad_ffn_shift, grad_down_bias = last_sums[0], last_sums[1], last_sums[2]

    def sum_rows(grads, order):
        if permutes:
            return Reduction(net, *net.split(grads), order)
        return PlainReduction(grads, 0)

    def send_layer(layer, mixed, first, rows):
        sent = highway_weight_gradient(1 - core, turned[layer], mixed, first, rows, width // 2)
        key = f"layer{layer}_{first}"
        if permutes:
            net.plan(key, sent, "c")
        return layer, mixed, first, rows, (key if permutes else sent, 0)

    def keep_layer(job, order):
        layer, mixed, first, rows, (key, part) = job
        keep = highway_weight_gradient(
            core,
            turned[layer],
            mixed,
            first,
            rows,
            width // 2,
            net.state[key] if permutes else None,
            part,
        )
        if permutes:
            return Reduction(net, keep, None, order)
        other = key[:, part * rows : (part + 1) * rows]
        whole = jnp.moveaxis(jnp.concatenate([keep, other], axis=0), 1, 0).reshape(rows, -1)
        return PlainReduction([whole], 1)

    def sum_feed(keep, sent, order):
        keep, sent = (value.reshape((16,) + value.shape[3:]) for value in (keep, sent))
        if permutes:
            return Reduction(net, keep, sent, order)
        return sum_rows([jnp.concatenate([keep, sent], axis=0).reshape(-1, model_width)], "")

    def ring_of(*sums, both=False):
        return Ring(net, sums, both) if permutes else sums

    def advance(*sums):
        if permutes:
            for item in sums:
                item.step()

    def ready(*sums):
        if permutes:
            for item in sums:
                item.step(net.plan)

    def held(*sums):
        return tuple(item.key for item in sums) if permutes else ()

    def together(*sums, hold=()):
        if permutes:
            ready(*sums)
            launch(())
            window((), held(*hold))

    up_keep, up_sent, down_keep, down_sent, bias_sums, grad_resid, norm_sums = feed_forward_back(
        grad_second,
        first,
        act,
        slope,
        first_in,
        gain_one[None],
        feed_pieces,
        slots,
        feed_block,
        core,
    )
    grad_up_bias = jnp.moveaxis(bias_sums.reshape(2, 4, 2, feed_rows), 2, 1).reshape(-1)
    grad_attn_gain, grad_attn_shift, grad_out_bias = norm_sums[0], norm_sums[1], norm_sums[2]
    up_keep, up_sent, down_keep, down_sent, grad_resid = window(
        (up_keep, up_sent, down_keep, down_sent, grad_resid)
    )

    sum_up = sum_feed(up_keep, up_sent, "cxy")
    sum_down = sum_feed(down_keep, down_sent, "cyx")
    ready(sum_down, sum_up)
    grad_resid = launch(grad_resid)
    grad_branch = grad_resid.astype(BF16)
    grad_context = dot_nt(grad_branch, out_all).astype(BF16)
    grad_resid, grad_context = window((grad_resid, grad_context))
    ready(sum_down, sum_up)
    grad_context, grad_branch = launch((grad_context, grad_branch))
    grad_qkv = attend_back(qkv, grad_context)
    grad_out = dot_tn(context, grad_branch).astype(BF16)
    grad_resid, grad_qkv, grad_out = window((grad_resid, grad_qkv, grad_out))

    ready(sum_down, sum_up)
    grad_qkv, grad_resid = launch((grad_qkv, grad_resid))
    qkv_sums = column_sum(grad_qkv)
    grad_attn_bias = jnp.concatenate([qkv_sums[:model_width], qkv_sums[2 * model_width :]])
    grad_summed, grad_embed_gain, grad_embed_shift = norm_back(
        summed, gain_zero, grad_resid + dot(grad_qkv, qkv_all)
    )
    grad_word = grad_summed.astype(BF16)
    grad_proj_bias = column_sum(grad_word)
    running = dot_nt(dot(perm, grad_word).astype(BF16), proj_all)
    running = window(running)
    ring_feed = ring_of(sum_up, sum_down)
    ready(ring_feed)
    running = launch(running)
    mixed_one, sums_one, running = highway_backward(
        running, states[1], transforms[1], gatings[1], pieces[1], place, select, core
    )
    mixed_one, running, grad_qkv, grad_out, grad_word, grad_summed = window(
        (mixed_one, running, grad_qkv, grad_out, grad_word, grad_summed)
    )
    type_hot = (type_ids[0] == 1).astype(F32)[:, None]
    vector_grads = [
        grad_proj_bias,
        jnp.sum((1.0 - type_hot) * grad_summed, axis=0),
        jnp.sum(type_hot * grad_summed, axis=0),
        grad_embed_gain,
        grad_embed_shift,
        grad_attn_bias,
        grad_out_bias,
        grad_attn_gain,
        grad_attn_shift,
        grad_up_bias,
        grad_down_bias,
        grad_ffn_gain,
        grad_ffn_shift,
    ]

    half_rows, quarter = features // 2, features // 4

    def quarters(jobs, layer, mixed):
        return [
            (layer, mixed, start * quarter, quarter, (jobs[start // 2][-1][0], start % 2))
            for start in range(4)
        ]

    jobs = [send_layer(1, mixed_one, start, half_rows) for start in (0, half_rows)]
    ready(ring_feed)
    mixed_one, grad_qkv, grad_word, grad_summed = launch(
        (mixed_one, grad_qkv, grad_word, grad_summed)
    )
    grad_pos = turn(grad_summed)
    encoder_grads = [
        dot_tn(grad_qkv, low_embedded),
        grad_out,
        dot_tn(last, grad_word),
    ]
    if permutes:
        encoder_grads.append(grad_pos.reshape(-1, model_width))
        sum_encoder = sum_rows(encoder_grads, "c321xy")
        mixed_one, running, sum_encoder.terms, sum_encoder.sent = window(
            (mixed_one, running, sum_encoder.terms, sum_encoder.sent)
        )
    else:
        sum_encoder = sum_rows(encoder_grads, "")
        sum_pos = sum_rows([grad_pos], "")

    jobs = quarters(jobs, 1, mixed_one)
    one = [None] * 4
    one[0], one[2] = keep_layer(jobs[0], "yx"), keep_layer(jobs[2], "xy")
    ready(one[0], one[2], sum_encoder, ring_feed)
    running = launch(running)
    mixed_zero, sums_zero, running = highway_backward(
        running, states[0], transforms[0], gatings[0], pieces[0], place, select, core
    )
    mixed_zero, running = window((mixed_zero, running))

    one[1], one[3] = keep_layer(jobs[1], "yx"), keep_layer(jobs[3], "xy")
    jobs = [send_layer(0, mixed_zero, start, half_rows) for start in (0, half_rows)]
    grad_scaled = running * (0.5 / sorted_lengths.astype(F32))[:, None]
    ready(one[1], one[3], sum_encoder)
    grad_scaled = launch(grad_scaled)
    matrix_turned, grad_groups = conv_backward(prep, char_groups, half_matrix, grad_scaled)
    mixed_zero, matrix_turned, grad_groups = window((mixed_zero, matrix_turned, grad_groups))

    ready(*one, sum_encoder)
    mixed_zero, grad_groups = launch((mixed_zero, grad_groups))
    jobs = quarters(jobs, 0, mixed_zero)
    zero = [keep_layer(job, order_) for job, order_ in zip(jobs, ("yx", "yx", "xy", "xy"))]
    first_two = (zero[0], zero[2])
    terms = [item.terms for item in zero] if permutes else ()
    grad_table = table_gradient(prep, grad_groups, character_embedding_table.shape[0])
    first_sum, vector_places = vector_rows(vector_grads)
    last_sum, high_places = vector_rows(
        [sums_zero.reshape(-1), sums_one.reshape(-1), grad_table.reshape(-1)]
    )
    high_places = [(first_sum.shape[0] + start, *rest) for start, *rest in high_places]
    last_sum = jnp.concatenate([first_sum, last_sum], axis=0)
    terms, last_sum = window((terms, last_sum))
    last_sum = Small(net, last_sum) if permutes else lax.psum(last_sum, ("narrow", "wide"))
    for item, value in zip(zero, terms):
        item.terms = value

    if permutes:
        conv_keep, conv_sent = net.split([matrix_turned])
        net.plan("conv", conv_sent, "c")
    else:
        sum_conv = sum_rows([matrix_turned], "")
    ready(*first_two, sum_encoder, last_sum)
    launch(())
    window(())
    if permutes:
        conv_total = total_of([conv_keep, net.state["conv"]]).astype(BF16)
        conv_total = conv_total.reshape((4, 2, 2) + conv_total.shape[1:])
        zero[3].terms = [jnp.concatenate([zero[3].terms[0], conv_total], axis=3)]

    ring_one = ring_of(*one)
    together(zero[1], zero[3], *first_two, ring_one, last_sum)
    together(zero[1], zero[3], ring_one, last_sum)
    ring_first = ring_of(*first_two, both=True)
    together(ring_first, ring_one, sum_encoder, last_sum)
    ring_last = ring_of(zero[1], zero[3], both=True)
    together(ring_first, ring_last, sum_encoder, last_sum)
    together(ring_last)
    total = last_sum.result() if permutes else last_sum

    device = lax.axis_index("narrow") * wide + lax.axis_index("wide")

    def whole_vector(total, where):
        start, count, size = where
        return total[start : start + count].reshape(-1)[:size]

    def own_part(total, where):
        piece = where[2] // devices
        return lax.dynamic_slice_in_dim(whole_vector(total, where), device * piece, piece, 0)

    results = [own_part(total, where) for where in vector_places]
    (
        sum_proj_bias,
        sum_type_zero,
        sum_type_one,
        sum_embed_gain,
        sum_embed_shift,
        sum_attn_bias,
        sum_out_bias,
        sum_attn_gain,
        sum_attn_shift,
        sum_up_bias,
        sum_down_bias,
        sum_ffn_gain,
        sum_ffn_shift,
    ) = results
    sum_high_bias = jnp.stack([own_part(total, where) for where in high_places[:layers]])
    sum_table = whole_vector(total, high_places[layers]).reshape(
        character_embedding_table.shape
    )

    def rows_of(item, sizes):
        total = item.result()
        if not permutes:
            return total
        pieces, start = [], 0
        for size in sizes:
            pieces.append(total[start : start + size])
            start += size
        return pieces

    qkv_rows, sum_out, sum_proj, *rest = rows_of(
        sum_encoder,
        [
            qkv_all.shape[0] // devices,
            out_all.shape[0] // devices,
            proj_all.shape[0] // devices,
            words * model_width // devices // model_width,
        ],
    )
    if permutes:
        pos_rows = rest[0].reshape(-1, words)
    else:
        (pos_rows,) = sum_pos.result()
    if permutes:
        up_rows, down_rows = jnp.split(ring_feed.result(), 2)
    else:
        (up_rows,), (down_rows,) = sum_up.result(), sum_down.result()
    if permutes:
        first_rows, last_rows = ring_first.result(), ring_last.result()
        conv_turned = last_rows[2 * quarter :]
    else:
        (conv_turned,) = sum_conv.result()
    own_filters = lax.dynamic_slice_in_dim(
        filter_widths(filters), device * (filters // devices), filters // devices
    )
    taps = jnp.arange(conv_rows)[:, None] // CHAR_DIM
    sum_conv_weight = jnp.where(taps < own_filters[None, :], conv_turned[:, :conv_rows].T, 0.0)

    if permutes:
        parts = [first_rows[:quarter], last_rows[:quarter], first_rows[quarter:], last_rows[quarter : 2 * quarter]]
        high_rows = [jnp.concatenate(parts, axis=0), ring_one.result()]
    else:
        high_rows = [
            jnp.concatenate([part for item in sums for part in item.result()], axis=0)
            for sums in (zero, one)
        ]

    return (
        hidden_out[None],
        sum_table,
        sum_conv_weight,
        conv_turned[:, conv_rows],
        jnp.stack(high_rows),
        sum_high_bias,
        sum_proj,
        sum_proj_bias,
        pos_rows.T,
        jnp.stack([sum_type_zero, sum_type_one]),
        sum_embed_gain,
        sum_embed_shift,
        qkv_rows.T,
        sum_attn_bias,
        sum_out,
        sum_out_bias,
        sum_attn_gain,
        sum_attn_shift,
        up_rows.T,
        sum_up_bias,
        down_rows,
        sum_down_bias,
        sum_ffn_gain,
        sum_ffn_shift,
    )


def solution(mesh):
    narrow, wide = mesh.shape["narrow"], mesh.shape["wide"]
    both = ("narrow", "wide")
    placed = (
        P(both, None, None),
        P(both, None),
        P(both, None),
        P(both, None, None),
        P(),
        P(None, "wide"),
        P("wide"),
        P(None, None, "wide"),
        P(None, "wide"),
        P("wide", None),
        P("wide"),
        P(None, "wide"),
        P(None, "wide"),
        P("wide"),
        P("wide"),
        P(None, "wide"),
        P("wide"),
        P("wide", None),
        P("wide"),
        P("wide"),
        P("wide"),
        P(None, "wide"),
        P("wide"),
        P("wide", None),
        P("wide"),
        P("wide"),
        P("wide"),
    )
    return jax.shard_map(
        partial(body, (narrow, wide) == (2, 16), wide, narrow * wide),
        mesh=mesh,
        in_specs=placed,
        out_specs=(
            P(both, None, None),
            P(),
            P(None, both),
            P(both),
            P(None, None, both),
            P(None, both),
            P(both, None),
            P(both),
            P(None, both),
            P(None, both),
            P(both),
            P(both),
            P(None, both),
            P(both),
            P(both, None),
            P(both),
            P(both),
            P(both),
            P(None, both),
            P(both),
            P(both, None),
            P(both),
            P(both),
            P(both),
        ),
        check_vma=False,
    )
```

```python
from functools import partial

import jax
import jax.numpy as jnp
from jax import lax
from jax.experimental import pallas as pl
from jax.experimental.pallas import tpu as pltpu
from jax.sharding import PartitionSpec as P

HEADS = 12
HEAD_DIM = 64
CHAR_DIM = 16
TAPS = 7
EPSILON = 1e-12

LANES = 128
GROUP = LANES // CHAR_DIM
BLOCK_WORDS = 32
CHUNK_BLOCKS = 16
CHUNK = BLOCK_WORDS * CHUNK_BLOCKS
TABLE_PAD = 384
ROW_TILE = 128
BIAS_LANE = TAPS * CHAR_DIM

F32 = jnp.float32
BF16 = jnp.bfloat16
VMEM = pl.BlockSpec(memory_space=pltpu.VMEM)
SMEM = pl.BlockSpec(memory_space=pltpu.SMEM)
MIB = 1024 * 1024


def cost(microseconds):
    return pl.CostEstimate(
        flops=int(microseconds * 1.1e9), bytes_accessed=int(microseconds * 3e6), transcendentals=0
    )


def dot(left, right):
    return lax.dot_general(left, right, (((1,), (0,)), ((), ())), preferred_element_type=F32)


def dot_nt(left, right):
    return lax.dot_general(left, right, (((1,), (1,)), ((), ())), preferred_element_type=F32)


def dot_tn(left, right):
    return lax.dot_general(left, right, (((0,), (0,)), ((), ())), preferred_element_type=F32)


def column_sum(values):
    return jnp.sum(values.astype(F32), axis=0)


def filter_widths(filter_count):
    column = jnp.arange(filter_count)
    widths = jnp.ones((filter_count,), jnp.int32)
    for exponent in range(6):
        widths = widths + (column >= filter_count * 2**exponent // 64).astype(jnp.int32)
    return widths


def sort_words(char_ids, lengths, groups):
    words, chars = char_ids.shape
    index = jnp.arange(words)
    longer = lengths[None, :] > lengths[:, None]
    tie = (lengths[None, :] == lengths[:, None]) & (index[None, :] < index[:, None])
    rank = jnp.sum((longer | tie).astype(jnp.int32), axis=1)
    perm = (rank[None, :] == index[:, None]).astype(BF16)
    live = jnp.arange(chars)[None, :] < lengths[:, None]
    shifted = jnp.where(live, char_ids + 1, 0)
    packed = jnp.concatenate(
        [shifted >> 4, shifted & 15, lengths[:, None]], axis=1
    ).astype(BF16)
    sorted_packed = dot(perm, packed).astype(jnp.int32)
    ids = (sorted_packed[:, :chars] << 4) + sorted_packed[:, chars : 2 * chars] - 1
    ids = jnp.pad(ids, ((0, 0), (0, GROUP * groups - chars)), constant_values=-1)
    sorted_lengths = sorted_packed[:, 2 * chars]
    tile_count = words // BLOCK_WORDS
    tile_max = jnp.max(sorted_lengths.reshape(tile_count, BLOCK_WORDS), axis=1)
    cum = jnp.cumsum(tile_max)
    total = cum[-1]
    block = jnp.arange(tile_count * chars + CHUNK_BLOCKS)
    tile = jnp.sum((block[:, None] >= cum[None, :]).astype(jnp.int32), axis=1)
    start = jnp.sum(
        jnp.where(tile[:, None] == jnp.arange(tile_count)[None, :], (cum - tile_max)[None, :], 0),
        axis=1,
    )
    valid = block < total
    position = jnp.where(valid, block - start, chars).astype(jnp.int32)
    tile = jnp.where(valid, tile, 0).astype(jnp.int32)
    chunks = (total + CHUNK_BLOCKS - 1) // CHUNK_BLOCKS
    reach = jnp.sum(
        (sorted_lengths[None, :] > GROUP * jnp.arange(groups - 1)[:, None]).astype(jnp.int32), axis=1
    )
    scalars = jnp.concatenate([chunks[None], (reach + ROW_TILE - 1) // ROW_TILE]).astype(jnp.int32)
    return perm, ids, sorted_lengths, scalars, tile, position


def build_windows(chunk, tile_ref, pos_ref, g_ref, len_ref, x_ref):
    lane = lax.broadcasted_iota(jnp.int32, (BLOCK_WORDS, LANES), 1)
    for b in range(CHUNK_BLOCKS):
        block = chunk * CHUNK_BLOCKS + b
        row = pl.multiple_of(tile_ref[block] * BLOCK_WORDS, BLOCK_WORDS)
        position = pos_ref[block]
        group = position >> 3
        offset = (position & 7) * CHAR_DIM
        shift = lax.rem(LANES - offset, LANES)
        here = pltpu.roll(g_ref[group, pl.ds(row, BLOCK_WORDS), :].astype(F32), shift, 1)
        after = pltpu.roll(g_ref[group + 1, pl.ds(row, BLOCK_WORDS), :].astype(F32), shift, 1)
        live = (len_ref[pl.ds(row, BLOCK_WORDS), :] > position).astype(F32)
        value = jnp.where(lane < LANES - offset, here, after)
        value = jnp.where(lane < BIAS_LANE, value, jnp.where(lane == BIAS_LANE, live, 0.0))
        x_ref[b * BLOCK_WORDS : (b + 1) * BLOCK_WORDS, :] = value.astype(BF16)


def embed_kernel(scalar_ref, ids_ref, table_ref, g_ref):
    groups = g_ref.shape[0]
    g_ref[...] = jnp.zeros_like(g_ref)
    identity = lax.broadcasted_iota(jnp.int32, (ROW_TILE, TABLE_PAD), 1)
    for group in range(groups - 1):

        def embed(step, carry, group=group):
            row = pl.multiple_of(step * ROW_TILE, ROW_TILE)
            total = jnp.zeros((ROW_TILE, LANES), F32)
            for k in range(GROUP):
                column = group * GROUP + k
                hot = (ids_ref[pl.ds(row, ROW_TILE), column : column + 1] == identity).astype(F32)
                total = total + dot(hot.astype(BF16), table_ref[k])
            g_ref[group, pl.ds(row, ROW_TILE), :] = total.astype(BF16)
            return carry

        lax.fori_loop(0, scalar_ref[1 + group], embed, 0)


def embed_characters(prep, table_blocks):
    _, ids, _, scalars, _, _ = prep
    return pl.pallas_call(
        embed_kernel,
        out_shape=jax.ShapeDtypeStruct((ids.shape[1] // GROUP, ids.shape[0], LANES), BF16),
        in_specs=[SMEM, VMEM, VMEM],
        out_specs=VMEM,
        compiler_params=pltpu.CompilerParams(vmem_limit_bytes=32 * MIB),
        cost_estimate=cost(5),
        name="embed",
    )(scalars, ids, table_blocks)


def conv_forward_kernel(
    scalar_ref, tile_ref, pos_ref, g_ref, w_ref, len_ref, pooled_ref, x_ref, pre_ref
):
    filters = w_ref.shape[1]
    part = pre_ref.shape[1]
    pooled_ref[...] = jnp.zeros_like(pooled_ref)

    def step(chunk, carry):
        build_windows(chunk, tile_ref, pos_ref, g_ref, len_ref, x_ref)
        for first in range(0, filters, part):
            half = dot(x_ref[...], w_ref[:, first : first + part])
            pre_ref[...] = half + half * jnp.tanh(half)
            for b in range(CHUNK_BLOCKS):
                row = pl.multiple_of(
                    tile_ref[chunk * CHUNK_BLOCKS + b] * BLOCK_WORDS, BLOCK_WORDS
                )
                pooled_ref[pl.ds(row, BLOCK_WORDS), first : first + part] += pre_ref[
                    b * BLOCK_WORDS : (b + 1) * BLOCK_WORDS, :
                ]
        return carry

    lax.fori_loop(0, scalar_ref[0], step, 0)
    pooled_ref[...] = pooled_ref[...] / len_ref[...].astype(F32)


def conv_forward(prep, char_groups, half_matrix):
    _, ids, lengths, scalars, tile, position = prep
    return pl.pallas_call(
        conv_forward_kernel,
        out_shape=jax.ShapeDtypeStruct((ids.shape[0], half_matrix.shape[1]), F32),
        in_specs=[SMEM, SMEM, SMEM, VMEM, VMEM, VMEM],
        out_specs=VMEM,
        scratch_shapes=[pltpu.VMEM((CHUNK, LANES), BF16), pltpu.VMEM((CHUNK, 512), F32)],
        compiler_params=pltpu.CompilerParams(vmem_limit_bytes=32 * MIB),
        cost_estimate=cost(16),
        name="conv_forward",
    )(scalars, tile, position, char_groups, half_matrix, lengths[:, None])


def conv_backward_kernel(
    scalar_ref, tile_ref, pos_ref, g_ref, w_ref, len_ref, gp_ref, out_ref, gg_ref, x_ref, d_ref, dw_ref
):
    filters = w_ref.shape[1]
    part = 512
    lane = lax.broadcasted_iota(jnp.int32, (BLOCK_WORDS, LANES), 1)
    dw_ref[...] = jnp.zeros_like(dw_ref)
    gg_ref[...] = jnp.zeros_like(gg_ref)

    def step(chunk, carry):
        build_windows(chunk, tile_ref, pos_ref, g_ref, len_ref, x_ref)
        for first in range(0, filters, part):
            columns = slice(first, first + part)
            half = dot(x_ref[...], w_ref[:, columns])
            tanh = jnp.tanh(half)
            slope = (1.0 + tanh) * (1.0 + (half - half * tanh))
            for b in range(CHUNK_BLOCKS):
                rows = slice(b * BLOCK_WORDS, (b + 1) * BLOCK_WORDS)
                row = pl.multiple_of(
                    tile_ref[chunk * CHUNK_BLOCKS + b] * BLOCK_WORDS, BLOCK_WORDS
                )
                d_ref[rows, columns] = (
                    gp_ref[pl.ds(row, BLOCK_WORDS), columns] * slope[rows]
                ).astype(BF16)
            dw_ref[:, columns] += dot_tn(x_ref[...], d_ref[:, columns])
        gx = dot_nt(d_ref[...], w_ref[...])
        for b in range(CHUNK_BLOCKS):
            block = chunk * CHUNK_BLOCKS + b
            row = pl.multiple_of(tile_ref[block] * BLOCK_WORDS, BLOCK_WORDS)
            position = pos_ref[block]
            group = position >> 3
            offset = (position & 7) * CHAR_DIM
            value = gx[b * BLOCK_WORDS : (b + 1) * BLOCK_WORDS, :]
            value = pltpu.roll(jnp.where(lane < BIAS_LANE, value, 0.0), offset, 1)
            gg_ref[group, pl.ds(row, BLOCK_WORDS), :] += jnp.where(lane >= offset, value, 0.0)
            gg_ref[group + 1, pl.ds(row, BLOCK_WORDS), :] += jnp.where(lane < offset, value, 0.0)
        return carry

    lax.fori_loop(0, scalar_ref[0], step, 0)
    out_ref[...] = dw_ref[...].T.astype(BF16)


def conv_backward(prep, char_groups, half_matrix, grad_scaled):
    _, ids, lengths, scalars, tile, position = prep
    filters = half_matrix.shape[1]
    return pl.pallas_call(
        conv_backward_kernel,
        out_shape=(
            jax.ShapeDtypeStruct((filters, LANES), BF16),
            jax.ShapeDtypeStruct(char_groups.shape, F32),
        ),
        in_specs=[SMEM, SMEM, SMEM, VMEM, VMEM, VMEM, VMEM],
        out_specs=(VMEM, VMEM),
        scratch_shapes=[
            pltpu.VMEM((CHUNK, LANES), BF16),
            pltpu.VMEM((CHUNK, filters), BF16),
            pltpu.VMEM((LANES, filters), F32),
        ],
        compiler_params=pltpu.CompilerParams(vmem_limit_bytes=48 * MIB),
        cost_estimate=cost(35),
        name="conv_backward",
    )(scalars, tile, position, char_groups, half_matrix, lengths[:, None], grad_scaled)


def table_kernel(scalar_ref, ids_ref, gg_ref, out_ref):
    groups = gg_ref.shape[0]
    out_ref[...] = jnp.zeros_like(out_ref)
    identity = lax.broadcasted_iota(jnp.int32, (TABLE_PAD, ROW_TILE), 0)
    for group in range(groups - 1):

        def step(index, carry, group=group):
            row = pl.multiple_of(index * ROW_TILE, ROW_TILE)
            grad = (2.0 * gg_ref[group, pl.ds(row, ROW_TILE), :]).astype(BF16)
            for k in range(GROUP):
                column = group * GROUP + k
                hot = (ids_ref[column : column + 1, pl.ds(row, ROW_TILE)] == identity).astype(F32)
                out_ref[k] += dot(hot.astype(BF16), grad)
            return carry

        lax.fori_loop(0, scalar_ref[1 + group], step, 0)


def table_gradient(prep, grad_groups, vocabulary):
    ids, scalars = prep[1], prep[3]
    total = pl.pallas_call(
        table_kernel,
        out_shape=jax.ShapeDtypeStruct((GROUP, TABLE_PAD, LANES), F32),
        in_specs=[SMEM, VMEM, VMEM],
        out_specs=VMEM,
        compiler_params=pltpu.CompilerParams(vmem_limit_bytes=32 * MIB),
        cost_estimate=cost(4),
        name="table",
    )(scalars, ids.T, grad_groups)
    parts = [total[k, :vocabulary, k * CHAR_DIM : (k + 1) * CHAR_DIM] for k in range(GROUP)]
    return sum(parts[1:], parts[0])


def table_lanes(table):
    padded = jnp.pad(table, ((0, TABLE_PAD - table.shape[0]), (0, 0)))
    return jnp.stack(
        [
            jnp.pad(padded, ((0, 0), (k * CHAR_DIM, LANES - (k + 1) * CHAR_DIM)))
            for k in range(GROUP)
        ]
    )


ANY = pl.BlockSpec(memory_space=pl.ANY)


def flat_pieces(pieces):
    return [array for half in pieces for chunk in half for array in chunk]


def piece_copies(layout, array, slot, first, own, pieces, whole_ref, sems, buffer):
    halves, chunks, arrays, rows = layout
    width = whole_ref.shape[2] // 2
    copies = []
    for half in range(halves):
        for chunk in range(chunks):
            ref = pieces[(half * chunks + chunk) * arrays + array]
            start = (own if half == 0 else 1 - own) * (chunks * rows) + chunk * rows
            start = pl.multiple_of(start, rows)
            for side in range(2):
                copies.append(
                    pltpu.make_async_copy(
                        ref.at[first if side == 0 else 1 - first, slot],
                        whole_ref.at[
                            buffer, pl.ds(start, rows), side * width : (side + 1) * width
                        ],
                        sems.at[buffer, len(copies)],
                    )
                )
    return copies


def fetch_pieces(layout, select_ref, own, pieces, whole_ref, sems):
    step = pl.program_id(0)

    def start(index):
        for array in range(layout[2]):

            @pl.when(index // 2 == array)
            def _(array=array):
                for copy in piece_copies(
                    layout, array, index % 2, select_ref[index], own, pieces, whole_ref, sems, index % 2
                ):
                    copy.start()

    @pl.when(step == 0)
    def _():
        start(0)

    @pl.when(step + 1 < pl.num_programs(0))
    def _():
        start(step + 1)

    buffer = step % 2
    for copy in piece_copies(layout, 0, 0, 0, own, pieces, whole_ref, sems, buffer):
        copy.wait()
    return buffer


def half_tanh(value):
    return 0.5 + 0.5 * jnp.tanh(0.5 * value)


def highway_forward_kernel(layout, place_ref, select_ref, core_ref, h_ref, bias_ref, *refs):
    count = layout[0] * layout[1] * layout[2]
    pieces = refs[:count]
    next_ref, transform_ref, gating_ref, low_ref, whole_ref, sems = refs[count:]
    step = pl.program_id(0)
    width = next_ref.shape[1]

    @pl.when(step == 0)
    def _():
        low_ref[...] = h_ref[...].astype(BF16)

    block = place_ref[step]
    blocks = bias_ref.shape[0] // 2
    buffer = fetch_pieces(layout, select_ref, core_ref[0], pieces, whole_ref, sems)
    mixed = dot(low_ref[...], whole_ref[buffer])
    transform = mixed[:, :width] + bias_ref[block]
    gating = half_tanh(mixed[:, width:] + bias_ref[block + blocks])
    h = h_ref[:, pl.ds(pl.multiple_of(block * width, width), width)]
    activated = transform * half_tanh(transform)
    transform_ref[...] = transform
    gating_ref[...] = gating
    next_ref[...] = activated + gating * (h - activated)


def highway_forward(h, pieces, bias_blocks, place, select, core):
    words, features = h.shape
    width = bias_blocks.shape[2]
    flat = flat_pieces(pieces)
    layout = (len(pieces), len(pieces[0]), len(pieces[0][0]), flat[0].shape[2])
    column = pl.BlockSpec((words, width), lambda j, place, *_: (0, place[j]))
    whole = lambda shape: pl.BlockSpec(shape, lambda j, *_: (0,) * len(shape))
    return pl.pallas_call(
        partial(highway_forward_kernel, layout),
        grid_spec=pltpu.PrefetchScalarGridSpec(
            num_scalar_prefetch=3,
            grid=(features // width,),
            in_specs=[whole(h.shape), whole(bias_blocks.shape)] + [ANY] * len(flat),
            out_specs=[column, column, column, whole(h.shape)],
            scratch_shapes=[
                pltpu.VMEM((2, features, 2 * width), BF16),
                pltpu.SemaphoreType.DMA((2, 2 * layout[0] * layout[1])),
            ],
        ),
        out_shape=(
            jax.ShapeDtypeStruct(h.shape, F32),
            jax.ShapeDtypeStruct(h.shape, F32),
            jax.ShapeDtypeStruct(h.shape, F32),
            jax.ShapeDtypeStruct(h.shape, BF16),
        ),
        compiler_params=pltpu.CompilerParams(vmem_limit_bytes=56 * MIB),
        cost_estimate=cost(19),
        name="highway_forward",
    )(place, select, core, h, bias_blocks, *flat)


def highway_backward_kernel(layout, place_ref, select_ref, core_ref, grad_ref, h_ref, t_ref, g_ref, *refs):
    count = layout[0] * layout[1] * layout[2]
    pieces = refs[:count]
    mixed_ref, sums_ref, out_ref, whole_ref, sems = refs[count:]
    step = pl.program_id(0)
    width = grad_ref.shape[1]
    features = out_ref.shape[1]

    @pl.when(step == 0)
    def _():
        out_ref[...] = jnp.zeros_like(out_ref)

    block = place_ref[step]
    buffer = fetch_pieces(layout, select_ref, core_ref[0], pieces, whole_ref, sems)
    grad = grad_ref[...]
    transform = t_ref[...]
    gating = g_ref[...]
    sigmoid = half_tanh(transform)
    activated = transform * sigmoid
    rest = grad * (1.0 - gating)
    low_t = (rest * (sigmoid + activated * (1.0 - sigmoid))).astype(BF16)
    low_g = (rest * gating * (h_ref[...] - activated)).astype(BF16)
    mixed_ref[0] = low_t
    mixed_ref[1] = low_g
    sums_ref[0] = jnp.sum(low_t.astype(F32), axis=0, keepdims=True)
    sums_ref[1] = jnp.sum(low_g.astype(F32), axis=0, keepdims=True)
    low = jnp.concatenate([low_t, low_g], axis=1)
    for start in range(0, features, 512):
        out_ref[:, start : start + 512] += dot_nt(
            low, whole_ref[buffer, start : start + 512, :]
        )
    out_ref[:, pl.ds(pl.multiple_of(block * width, width), width)] += grad * gating


def highway_backward(grad, h, transform, gating, pieces, place, select, core):
    words, features = h.shape
    flat = flat_pieces(pieces)
    width = flat[0].shape[3]
    layout = (len(pieces), len(pieces[0]), len(pieces[0][0]), flat[0].shape[2])
    column = pl.BlockSpec((words, width), lambda j, place, *_: (0, place[j]))
    return pl.pallas_call(
        partial(highway_backward_kernel, layout),
        grid_spec=pltpu.PrefetchScalarGridSpec(
            num_scalar_prefetch=3,
            grid=(features // width,),
            in_specs=[column] * 4 + [ANY] * len(flat),
            out_specs=[
                pl.BlockSpec((2, words, width), lambda j, place, *_: (0, 0, place[j])),
                pl.BlockSpec((2, 1, width), lambda j, place, *_: (0, 0, place[j])),
                pl.BlockSpec(h.shape, lambda j, *_: (0, 0)),
            ],
            scratch_shapes=[
                pltpu.VMEM((2, features, 2 * width), BF16),
                pltpu.SemaphoreType.DMA((2, 2 * layout[0] * layout[1])),
            ],
        ),
        out_shape=(
            jax.ShapeDtypeStruct((2, words, features), BF16),
            jax.ShapeDtypeStruct((2, 1, features), F32),
            jax.ShapeDtypeStruct(h.shape, F32),
        ),
        compiler_params=pltpu.CompilerParams(vmem_limit_bytes=56 * MIB),
        cost_estimate=cost(21),
        name="highway_backward",
    )(place, select, core, grad, h, transform, gating, *flat)


def weight_kernel(which_ref, left_ref, right_ref, *refs):
    out_ref = refs[-1]
    value = dot(left_ref[...], right_ref[0])
    width = out_ref.shape[2]
    for number in range(out_ref.shape[0]):
        block = value[:, number * width : (number + 1) * width]
        if len(refs) == 2:
            block = block + refs[0][number].astype(F32)
        out_ref[number] = block.astype(BF16)


def highway_weight_gradient(which, turned, mixed, first, rows, width, added=None, part=0):
    words, features = mixed.shape[1:]
    blocks = 8
    out = pl.BlockSpec((blocks, rows, width), lambda j, which: (j, 0, 0))
    return pl.pallas_call(
        weight_kernel,
        grid_spec=pltpu.PrefetchScalarGridSpec(
            num_scalar_prefetch=1,
            grid=(features // (blocks * width),),
            in_specs=[
                pl.BlockSpec((rows, words), lambda j, which: (first // rows, 0)),
                pl.BlockSpec((1, words, blocks * width), lambda j, which: (which[0], 0, j)),
            ]
            + (
                []
                if added is None
                else [pl.BlockSpec((blocks, rows, width), lambda j, which: (j, part, 0))]
            ),
            out_specs=out,
        ),
        out_shape=jax.ShapeDtypeStruct((features // width, rows, width), BF16),
        compiler_params=pltpu.CompilerParams(vmem_limit_bytes=32 * MIB),
        cost_estimate=cost(3),
        name="highway_weight",
    )(which, turned, mixed, *([] if added is None else [added]))


def turn_kernel(value_ref, out_ref):
    out_ref[...] = value_ref[...].T.astype(BF16)


def turn(value):
    rows, columns = value.shape
    return pl.pallas_call(
        turn_kernel,
        grid=(columns // 256,),
        in_specs=[pl.BlockSpec((rows, 256), lambda j: (0, j))],
        out_specs=pl.BlockSpec((256, rows), lambda j: (j, 0)),
        out_shape=jax.ShapeDtypeStruct((columns, rows), BF16),
        compiler_params=pltpu.CompilerParams(vmem_limit_bytes=32 * MIB),
        cost_estimate=cost(1),
        name="turn",
    )(value)


def place_rows_kernel(splits, place_ref, core_ref, *refs):
    arrays = (len(refs) - len(splits) - 1) // 2
    own_refs, other_refs = refs[:arrays], refs[arrays : 2 * arrays]
    out_refs, whole_ref = refs[2 * arrays : -1], refs[-1]
    step = pl.program_id(0)
    half_rows = own_refs[0].shape[1]
    core = core_ref[0]
    for array in range(arrays):

        @pl.when(step // 4 == array)
        def _(array=array):
            align = lambda start: pl.ds(pl.multiple_of(start, 16), half_rows)
            whole_ref[align(core * half_rows), :] = own_refs[array][0]
            whole_ref[align((1 - core) * half_rows), :] = other_refs[array][0]

    start = 0
    for rows, out_ref in zip(splits, out_refs):
        out_ref[...] = whole_ref[start : start + rows, :]
        start += rows


def place_rows(own, other, place, core, splits):
    half_rows, columns = own[0].shape[1:]

    def index(number):
        return lambda j, *_: (jnp.clip(j - 4 * number, 0, 3), 0, 0)

    specs = [pl.BlockSpec((1, half_rows, columns), index(number)) for number in range(len(own))]
    return pl.pallas_call(
        partial(place_rows_kernel, splits),
        grid_spec=pltpu.PrefetchScalarGridSpec(
            num_scalar_prefetch=2,
            grid=(4 * len(own),),
            in_specs=specs + specs,
            out_specs=[
                pl.BlockSpec((rows, columns), lambda j, place, *_: (place[j], 0)) for rows in splits
            ],
            scratch_shapes=[pltpu.VMEM((2 * half_rows, columns), BF16)],
        ),
        out_shape=[
            jax.ShapeDtypeStruct((4 * len(own) * rows, columns), BF16) for rows in splits
        ],
        compiler_params=pltpu.CompilerParams(vmem_limit_bytes=32 * MIB),
        cost_estimate=cost(7),
        name="place_rows",
    )(place, core, *own, *other)


def place_small_kernel(place_ref, *refs):
    inputs, (conv_ref, *row_refs) = refs[:4], refs[4:]
    step = pl.program_id(0)
    for number, ref in enumerate(inputs):

        @pl.when(step // 4 == number)
        def _(ref=ref):
            start = conv_ref.shape[0]
            conv_ref[...] = ref[0, :start, :]
            for row_ref in row_refs:
                row_ref[0] = ref[0, start : start + row_ref.shape[1], :]
                start += row_ref.shape[1]


def place_small(arrays, place, conv_rows, splits):
    rows, columns = arrays[0].shape[1:]

    def index(number):
        return lambda j, *_: (jnp.clip(j - 4 * number, 0, 3), 0, 0)

    return pl.pallas_call(
        place_small_kernel,
        grid_spec=pltpu.PrefetchScalarGridSpec(
            num_scalar_prefetch=1,
            grid=(16,),
            in_specs=[pl.BlockSpec((1, rows, columns), index(number)) for number in range(4)],
            out_specs=[pl.BlockSpec((conv_rows, columns), lambda j, place: (0, place[j]))]
            + [
                pl.BlockSpec((1, count, columns), lambda j, place: (place[j], 0, 0))
                for count in splits
            ],
        ),
        out_shape=[jax.ShapeDtypeStruct((conv_rows, 16 * columns), BF16)]
        + [jax.ShapeDtypeStruct((16, count, columns), BF16) for count in splits],
        compiler_params=pltpu.CompilerParams(vmem_limit_bytes=32 * MIB),
        cost_estimate=cost(2),
        name="place_small",
    )(place, *arrays)


LINKS = {
    "x": [(w, w ^ 1) for w in range(16)],
    "y": [(w, w ^ 2) for w in range(16)],
    "z": [(w, (w + 4) % 16) for w in range(16)],
    "back": [(w, (w - 4) % 16) for w in range(16)],
    "z1": [(w, w ^ 4) for w in range(16)],
    "z2": [(w, w ^ 8) for w in range(16)],
}
CORES = [(0, 1), (1, 0)]


def send(value, link):
    if link == "c":
        return lax.ppermute(value, "narrow", CORES)
    return lax.ppermute(value, "wide", LINKS[link])


def total_of(terms):
    return sum((term.astype(F32) for term in terms[1:]), terms[0].astype(F32))


class Exchange:
    windows = True

    def __init__(self):
        self.core = lax.axis_index("narrow")
        index = lax.axis_index("wide")
        self.z, self.y, self.x = index // 4, (index // 2) % 2, index % 2
        self.state, self.fresh, self.count, self.planned = {}, [], 0, []

    def put(self, key, value):
        self.state[key] = value
        self.fresh.append(key)

    def move(self, key, source, link):
        self.put(key, send(self.state[source], link))

    def plan(self, key, value, link, shape=None):
        self.planned.append((key, value, link, shape))

    def plan_move(self, source, *links):
        for link in links:
            self.plan(source + link, self.state[source], link)

    def plan_ring(self, name, step):
        self.plan(f"{name}r{step}", self.state[f"{name}r{step - 1}" if step > 1 else name], "z")

    def plan_swap(self, *names):
        for name in names:
            self.plan(name + "c", self.state[name], "c")

    def launch(self, values):
        leaves, tree = jax.tree.flatten(values)
        held = lax.optimization_barrier(
            tuple(value for _, value, _, _ in self.planned) + tuple(leaves)
        )
        for (key, _, link, shape), value in zip(self.planned, held):
            value = send(value, link)
            self.put(key, value if shape is None else value.reshape(shape))
        leaves = held[len(self.planned) :]
        self.planned = []
        return jax.tree.unflatten(tree, leaves)

    def window(self, values, hold=()):
        held_keys = [key for key in self.fresh if key in hold]
        self.fresh = [key for key in self.fresh if key not in hold]
        leaves, tree = jax.tree.flatten(values)
        held = lax.optimization_barrier(
            tuple(self.state[key] for key in self.fresh) + tuple(leaves)
        )
        for key, value in zip(self.fresh, held):
            self.state[key] = value
        leaves = held[len(self.fresh) :]
        self.fresh = held_keys
        return jax.tree.unflatten(tree, leaves)

    def swap_chain(self, *names):
        before = None
        for name in names:
            value = self.state[name]
            if before is not None:
                value, self.state[before] = lax.optimization_barrier((value, self.state[before]))
            before = name + "c"
            self.put(before, send(value, "c"))

    def stage(self, values=(), hold=()):
        return self.window(self.launch(values), hold)


    def load(self, name, value, rows=None, offset=0, whole=False):
        if not whole:
            rows = rows or value.shape[0] // 2
            value = lax.dynamic_slice_in_dim(
                value, self.core * (value.shape[0] // 2) + offset, rows, 0
            )
        self.state[name] = value

    def ring(self, name):
        received = [self.state[name]]
        for _ in range(3):
            received.append(send(received[-1], "z"))
        self.put(name + "o", jnp.stack(received))

    def ring_step(self, name, step):
        self.move(f"{name}r{step}", f"{name}r{step - 1}" if step > 1 else name, "z")

    def ring_both(self, name):
        self.put(name + "r1", send(self.state[name], "z"))
        self.put(name + "r3", send(self.state[name], "back"))
        self.put(name + "r2", send(self.state[name + "r1"], "z"))

    def ring_done(self, name):
        self.state[name + "o"] = jnp.stack(
            [self.state[name]] + [self.state[f"{name}r{step}"] for step in (1, 2, 3)]
        )

    def square(self, name):
        value = self.state[name]
        over_x = send(value, "x")
        self.put(name + "o0", jnp.stack([value, over_x, send(value, "y"), send(over_x, "y")]))

    def turn_ring(self, name, step):
        self.move(f"{name}o{step}", f"{name}o{step - 1}", "z")

    def swap(self, *names):
        for name in names:
            self.move(name + "c", name, "c")

    def near(self, name, suffix=""):
        return [self.state[name + part + suffix] for part in ("o", "ox", "oy", "oxy")]

    def layer(self, name, chunks):
        halves = []
        for suffix in ("", "c"):
            halves.append(
                [
                    [
                        array.reshape((2, 2) + array.shape[1:])
                        for array in self.near(f"{name}{chunk}", suffix)
                    ]
                    for chunk in range(chunks)
                ]
            )
        return halves

    def place(self, ring_last):
        step = jnp.arange(16)
        near, slot = (step % 4, step // 4) if ring_last else (step // 4, step % 4)
        return (
            (self.z - slot) % 4 * 4 + (self.y ^ (near >> 1)) * 2 + (self.x ^ (near & 1))
        ).astype(jnp.int32)

    def rows(self, own, other, splits, ring_last):
        core = self.core[None].astype(jnp.int32)
        return place_rows(own, other, self.place(ring_last), core, splits)


    def split(self, grads):
        blocks = [grad.astype(BF16).reshape(2, 16, -1, grad.shape[1]) for grad in grads]
        return tuple(
            jnp.concatenate(
                [lax.dynamic_index_in_dim(block, which, 0, keepdims=False) for block in blocks],
                axis=1,
            )
            for which in (self.core, 1 - self.core)
        )


class Reduction:
    def __init__(self, net, keep, sent, order):
        shape = (4, 2, 2) + keep.shape[1:]
        self.net, self.order, self.done = net, list(order), 0
        net.count += 1
        self.name = f"sum{net.count}"
        self.terms = [keep.reshape(shape)]
        self.keys, self.running, self.axes = [], None, ["z", "y", "x"]
        self.sent, self.shape = sent, shape

    def all_terms(self):
        return self.terms + [self.net.state[key] for key in self.keys]

    def pick(self, terms, index, axis):
        return [lax.dynamic_index_in_dim(term, index, axis, keepdims=False) for term in terms]

    def keep_only(self, index, axis):
        self.terms = self.pick(self.all_terms(), index, axis)
        self.keys = []

    def step(self, put=None):
        net, link = self.net, self.order[self.done]
        put = put or (lambda key, value, link, shape=None: net.put(
            key, send(value, link) if shape is None else send(value, link).reshape(shape)
        ))
        self.key = key = f"{self.name}_{self.done}"
        self.done += 1
        if link == "c":
            put(key, self.sent, "c", self.shape)
            self.keys.append(key)
        elif link in ("x", "y"):
            axis = self.axes.index(link)
            index = net.x if link == "x" else net.y
            sent = total_of(self.pick(self.all_terms(), 1 - index, axis)).astype(BF16)
            self.keep_only(index, axis)
            self.axes.remove(link)
            put(key, sent, link)
            self.keys.append(key)
        else:
            axis = self.axes.index("z")
            index = (net.z + int(link)) % 4
            terms = self.pick(self.all_terms(), index, axis)
            if self.running is not None:
                terms.append(net.state[self.running])
            put(key, total_of(terms).astype(BF16), "z")
            self.running = key
            if link == "1":
                self.keep_only(net.z, axis)
                self.axes.remove("z")
                self.keys = [key]
        return self

    def result(self):
        assert self.done == len(self.order)
        return total_of(self.all_terms())


class Ring:
    def __init__(self, net, sums, both):
        self.net, self.sums, self.both, self.done = net, sums, both, 0
        self.arrived = []
        net.count += 1
        self.name = f"ring{net.count}"

    def part(self, distance):
        index = (self.net.z + distance) % 4
        parts = [total_of(item.pick(item.all_terms(), index, 0)) for item in self.sums]
        value = parts[0] if len(parts) == 1 else jnp.concatenate(parts, axis=0)
        for key in self.arrived:
            value = value + self.net.state[key].astype(F32)
        return value

    def step(self, put):
        self.done += 1
        self.key = key = f"{self.name}_{self.done}"
        if self.both and self.done == 1:
            self.last_key = f"{self.name}_back"
            put(self.last_key, self.part(3).astype(BF16), "back")
            put(key, self.part(2).astype(BF16), "z")
        else:
            put(key, self.part((3 if self.both else 4) - self.done).astype(BF16), "z")
        self.arrived = [key]
        return self

    def result(self):
        assert self.done == (2 if self.both else 3)
        if self.both:
            self.arrived = self.arrived + [self.last_key]
        return self.part(0)


class Small:
    def __init__(self, net, value):
        self.net, self.value, self.done, self.key = net, value, 0, None
        net.count += 1
        self.name = f"t{net.count}"

    def result(self):
        return self.value if self.key is None else self.value + self.net.state[self.key]

    def step(self, put):
        self.value = self.result()
        self.key = f"{self.name}_{self.done}"
        put(self.key, self.value, ("c", "z1", "x", "y", "z2")[self.done])
        self.done += 1
        return self


class PlainReduction:
    def __init__(self, grads, axis):
        self.grads, self.axis = grads, axis

    def step(self):
        return self

    def result(self):
        return [
            lax.psum_scatter(
                grad.astype(BF16), ("narrow", "wide"), scatter_dimension=self.axis, tiled=True
            ).astype(F32)
            for grad in self.grads
        ]


def norm_rows(value, norm_gain, norm_shift):
    center = jnp.mean(value, axis=-1, keepdims=True)
    offsets = value - center
    spread = jnp.mean(offsets * offsets, axis=-1, keepdims=True)
    return offsets * lax.rsqrt(spread + EPSILON) * norm_gain + norm_shift


def norm_back(value, norm_gain, grad_rows):
    center = jnp.mean(value, axis=-1, keepdims=True)
    offsets = value - center
    spread = jnp.mean(offsets * offsets, axis=-1, keepdims=True)
    scale = lax.rsqrt(spread + EPSILON)
    normal = offsets * scale
    inner = grad_rows * norm_gain
    grad = scale * (
        inner
        - jnp.mean(inner, axis=-1, keepdims=True)
        - normal * jnp.mean(inner * normal, axis=-1, keepdims=True)
    )
    return grad, jnp.sum(grad_rows * normal, axis=0), jnp.sum(grad_rows, axis=0)


def array_copies(array, refs, held_ref, sems):
    count = len(refs)
    return [
        pltpu.make_async_copy(
            refs[index], held_ref.at[index], sems.at[index]
        )
        for index in range(array, count, count // 4)
    ]


def join_rows(slot_ref, own, refs, held_ref, up_ref, down_ref, sems):
    count = len(refs)
    arrays = count // 4
    step = pl.program_id(0)

    @pl.when(step == 0)
    def _():
        for array in range(arrays):
            for copy in array_copies(array, refs, held_ref, sems):
                copy.start()

    for array in range(arrays):

        @pl.when(step == 2 * array)
        def _(array=array):
            for copy in array_copies(array, refs, held_ref, sems):
                copy.wait()

    rows = held_ref.shape[2]
    near = step // 2
    for number in range(2):
        slot = slot_ref[step, number]
        for half in range(2):
            start = (own if half == 0 else 1 - own) * rows + number * 2 * rows
            where = pl.ds(pl.multiple_of(start, rows), rows)
            up_ref[where, :] = held_ref[half * arrays + near, slot]
            down_ref[where, :] = held_ref[(2 + half) * arrays + near, slot]


def normal_share(value, bell):
    t = 1.0 / (1.0 + (0.3275911 * 2**-0.5) * jnp.abs(value))
    series = 1.061405429
    for term in (-1.453152027, 1.421413741, -0.284496736, 0.254829592):
        series = series * t + term
    tail = (0.5 * series) * (t * bell)
    return jnp.where(value < 0.0, tail, 1.0 - tail)


def feed_forward_kernel(
    count, slot_ref, block_ref, core_ref, first_ref, bias_ref, vectors_ref, cotangent_ref, *refs
):
    (
        act_ref,
        slope_ref,
        hidden_ref,
        grad_ref,
        sums_ref,
        held_ref,
        up_ref,
        down_ref,
        low_ref,
        total_ref,
        sems,
    ) = refs[2 * count :]
    step = pl.program_id(0)

    @pl.when(step == 0)
    def _():
        low_ref[...] = first_ref[...].astype(BF16)
        total_ref[...] = first_ref[...] + vectors_ref[0:1, :]

    join_rows(slot_ref, core_ref[0], refs[: 2 * count], held_ref, up_ref, down_ref, sems)
    inner = dot_nt(low_ref[...], up_ref[...]) + bias_ref[block_ref[step]]
    bell = jnp.exp2(inner * inner * (-0.5 * 1.4426950408889634))
    share = normal_share(inner, bell)
    act = (inner * share).astype(BF16)
    act_ref[0] = act
    slope_ref[0] = (
        share + inner * (bell * (2.0 * jnp.pi) ** -0.5)
    ).astype(BF16)
    total_ref[...] += dot(act, down_ref[...])

    @pl.when(step == pl.num_programs(0) - 1)
    def _():
        value = total_ref[...]
        gain, shift = vectors_ref[1:2, :], vectors_ref[2:3, :]
        offsets = value - jnp.mean(value, axis=-1, keepdims=True)
        scale = lax.rsqrt(jnp.mean(offsets * offsets, axis=-1, keepdims=True) + EPSILON)
        normal = offsets * scale
        hidden_ref[...] = (normal * gain + shift).astype(BF16)
        cotangent = cotangent_ref[...].astype(F32)
        pulled = cotangent * gain
        grad = scale * (
            pulled
            - jnp.mean(pulled, axis=-1, keepdims=True)
            - normal * jnp.mean(pulled * normal, axis=-1, keepdims=True)
        )
        grad_ref[...] = grad
        sums_ref[0:1, :] = jnp.sum(cotangent * normal, axis=0, keepdims=True)
        sums_ref[1:2, :] = jnp.sum(cotangent, axis=0, keepdims=True)
        sums_ref[2:3, :] = jnp.sum(grad.astype(BF16).astype(F32), axis=0, keepdims=True)
        sums_ref[3:8, :] = jnp.zeros((5, sums_ref.shape[1]), F32)


def feed_forward(first, pieces, bias_blocks, vectors, cotangent, slots, block, core):
    words, columns = first.shape
    steps, width = bias_blocks.shape[0], bias_blocks.shape[2]
    up, down = pieces
    whole = lambda shape: pl.BlockSpec(shape, lambda j, *_: (0,) * len(shape))
    tile = pl.BlockSpec((1, words, width), lambda j, *_: (j, 0, 0))
    return pl.pallas_call(
        partial(feed_forward_kernel, len(up)),
        grid_spec=pltpu.PrefetchScalarGridSpec(
            num_scalar_prefetch=3,
            grid=(steps,),
            in_specs=[
                whole(first.shape),
                whole(bias_blocks.shape),
                whole(vectors.shape),
                whole(cotangent.shape),
            ]
            + [ANY] * (len(up) + len(down)),
            out_specs=[tile, tile, whole(first.shape), whole(first.shape), whole((8, columns))],
            scratch_shapes=[
                pltpu.VMEM((len(up) + len(down),) + up[0].shape, BF16),
                pltpu.VMEM((width, columns), BF16),
                pltpu.VMEM((width, columns), BF16),
                pltpu.VMEM((words, columns), BF16),
                pltpu.VMEM((words, columns), F32),
                pltpu.SemaphoreType.DMA((len(up) + len(down),)),
            ],
        ),
        out_shape=(
            jax.ShapeDtypeStruct((steps, words, width), BF16),
            jax.ShapeDtypeStruct((steps, words, width), BF16),
            jax.ShapeDtypeStruct((words, columns), BF16),
            jax.ShapeDtypeStruct((words, columns), F32),
            jax.ShapeDtypeStruct((8, columns), F32),
        ),
        compiler_params=pltpu.CompilerParams(vmem_limit_bytes=56 * MIB),
        cost_estimate=cost(20),
        name="feed_forward",
    )(slots, block, core, first, bias_blocks, vectors, cotangent, *up, *down)


def feed_forward_back_kernel(
    count,
    slot_ref,
    block_ref,
    core_ref,
    grad_ref,
    first_ref,
    act_ref,
    slope_ref,
    value_ref,
    gain_ref,
    *refs,
):
    (
        up_keep_ref,
        up_sent_ref,
        down_keep_ref,
        down_sent_ref,
        bias_ref,
        out_ref,
        sums_ref,
        held_ref,
        up_ref,
        down_ref,
        low_ref,
        low_first_ref,
        total_ref,
        sems,
    ) = refs[2 * count :]
    step = pl.program_id(0)

    @pl.when(step == 0)
    def _():
        total_ref[...] = grad_ref[...]
        low_ref[...] = grad_ref[...].astype(BF16)
        low_first_ref[...] = first_ref[...].astype(BF16)

    join_rows(slot_ref, core_ref[0], refs[: 2 * count], held_ref, up_ref, down_ref, sems)
    low = low_ref[...]
    inner = (dot_nt(low, down_ref[...]) * slope_ref[0].astype(F32)).astype(BF16)
    bias_ref[0] = jnp.sum(inner.astype(F32), axis=0, keepdims=True)
    grad_down = dot_tn(act_ref[0], low).astype(BF16)
    grad_up = dot_tn(inner, low_first_ref[...]).astype(BF16)
    total_ref[...] += dot(inner, up_ref[...])
    rows = up_keep_ref.shape[3]

    def store(value, ref):
        for number in range(4):
            ref[number // 2, 0, number % 2] = value[number * rows : (number + 1) * rows, :]

    @pl.when(step % 2 == 0)
    def _():
        store(grad_up, up_sent_ref)
        store(grad_down, down_sent_ref)

    @pl.when(step % 2 == 1)
    def _():
        store(grad_up, up_keep_ref)
        store(grad_down, down_keep_ref)

    @pl.when(step == pl.num_programs(0) - 1)
    def _():
        value = value_ref[...]
        pulling = total_ref[...]
        offsets = value - jnp.mean(value, axis=-1, keepdims=True)
        scale = lax.rsqrt(jnp.mean(offsets * offsets, axis=-1, keepdims=True) + EPSILON)
        normal = offsets * scale
        pulled = pulling * gain_ref[...]
        grad = scale * (
            pulled
            - jnp.mean(pulled, axis=-1, keepdims=True)
            - normal * jnp.mean(pulled * normal, axis=-1, keepdims=True)
        )
        out_ref[...] = grad
        sums_ref[0:1, :] = jnp.sum(pulling * normal, axis=0, keepdims=True)
        sums_ref[1:2, :] = jnp.sum(pulling, axis=0, keepdims=True)
        sums_ref[2:3, :] = jnp.sum(grad.astype(BF16).astype(F32), axis=0, keepdims=True)
        sums_ref[3:8, :] = jnp.zeros((5, sums_ref.shape[1]), F32)


def feed_forward_back(grad, first, act, slope, value, gain, pieces, slots, block, core):
    words, columns = first.shape
    steps, _, width = act.shape
    up, down = pieces
    rows = width // 4
    whole = lambda shape: pl.BlockSpec(shape, lambda j, *_: (0,) * len(shape))
    tile = pl.BlockSpec((1, words, width), lambda j, *_: (j, 0, 0))
    out = pl.BlockSpec(
        (2, 1, 2, rows, columns), lambda j, slots, block, core: (0, block[j] % (steps // 2), 0, 0, 0)
    )
    part = jax.ShapeDtypeStruct((2, steps // 2, 2, rows, columns), BF16)
    return pl.pallas_call(
        partial(feed_forward_back_kernel, len(up)),
        grid_spec=pltpu.PrefetchScalarGridSpec(
            num_scalar_prefetch=3,
            grid=(steps,),
            in_specs=[
                whole(grad.shape),
                whole(first.shape),
                tile,
                tile,
                whole(value.shape),
                whole(gain.shape),
            ]
            + [ANY] * (len(up) + len(down)),
            out_specs=[
                out,
                out,
                out,
                out,
                pl.BlockSpec((1, 1, width), lambda j, slots, block, core: (block[j], 0, 0)),
                whole(first.shape),
                whole((8, columns)),
            ],
            scratch_shapes=[
                pltpu.VMEM((len(up) + len(down),) + up[0].shape, BF16),
                pltpu.VMEM((width, columns), BF16),
                pltpu.VMEM((width, columns), BF16),
                pltpu.VMEM((words, columns), BF16),
                pltpu.VMEM((words, columns), BF16),
                pltpu.VMEM((words, columns), F32),
                pltpu.SemaphoreType.DMA((len(up) + len(down),)),
            ],
        ),
        out_shape=(
            part,
            part,
            part,
            part,
            jax.ShapeDtypeStruct((steps, 1, width), F32),
            jax.ShapeDtypeStruct((words, columns), F32),
            jax.ShapeDtypeStruct((8, columns), F32),
        ),
        compiler_params=pltpu.CompilerParams(vmem_limit_bytes=56 * MIB),
        cost_estimate=cost(25),
        name="feed_back",
    )(slots, block, core, grad, first, act, slope, value, gain, *up, *down)


def softmax_parts(query, key):
    scores = dot_nt(query, key)
    scaling = HEAD_DIM ** (-0.5) * 1.4426950408889634
    exponent = jnp.exp2((scores - jnp.max(scores, axis=-1, keepdims=True)) * scaling)
    return exponent, 1.0 / jnp.sum(exponent, axis=-1, keepdims=True)


def attend_kernel(query_ref, key_ref, value_ref, out_ref):
    for start in range(0, LANES, HEAD_DIM):
        head = slice(start, start + HEAD_DIM)
        exponent, scale = softmax_parts(query_ref[:, head], key_ref[:, head])
        attention = (exponent * scale).astype(BF16)
        out_ref[:, head] = dot(attention, value_ref[:, head]).astype(BF16)


def third(number, words, thirds):
    return pl.BlockSpec((words, LANES), lambda j: (0, number * thirds + j))


def attend(qkv):
    words = qkv.shape[0]
    pairs = qkv.shape[1] // (3 * LANES)
    return pl.pallas_call(
        attend_kernel,
        grid=(pairs,),
        in_specs=[third(number, words, pairs) for number in range(3)],
        out_specs=third(0, words, pairs),
        out_shape=jax.ShapeDtypeStruct((words, pairs * LANES), BF16),
        compiler_params=pltpu.CompilerParams(vmem_limit_bytes=32 * MIB),
        cost_estimate=cost(12),
        name="attend",
    )(qkv, qkv, qkv)


def attend_back_kernel(
    query_ref, key_ref, value_ref, grad_ref, grad_query_ref, grad_key_ref, grad_value_ref
):
    scaling = HEAD_DIM ** (-0.5)
    for start in range(0, LANES, HEAD_DIM):
        head = slice(start, start + HEAD_DIM)
        query, key = query_ref[:, head], key_ref[:, head]
        grad = grad_ref[:, head]
        exponent, scale = softmax_parts(query, key)
        attention = exponent * scale
        grad_attention = dot_nt(grad, value_ref[:, head])
        inner = jnp.sum(grad_attention * attention, axis=-1, keepdims=True)
        grad_scores = (attention * (grad_attention - inner)).astype(BF16)
        grad_value_ref[:, head] = dot_tn(attention.astype(BF16), grad).astype(BF16)
        grad_query_ref[:, head] = (dot(grad_scores, key) * scaling).astype(BF16)
        grad_key_ref[:, head] = (dot_tn(grad_scores, query) * scaling).astype(BF16)


def attend_back(qkv, grad_context):
    words = qkv.shape[0]
    pairs = qkv.shape[1] // (3 * LANES)
    out = third(0, words, pairs)
    return jnp.concatenate(
        pl.pallas_call(
            attend_back_kernel,
            grid=(pairs,),
            in_specs=[third(number, words, pairs) for number in range(3)] + [out],
            out_specs=(out, out, out),
            out_shape=(jax.ShapeDtypeStruct(grad_context.shape, BF16),) * 3,
            compiler_params=pltpu.CompilerParams(vmem_limit_bytes=32 * MIB),
            cost_estimate=cost(17),
        name="attend_back",
        )(qkv, qkv, qkv, grad_context),
        axis=1,
    )


def gather_plain(value, axis):
    return lax.all_gather(value, "wide", axis=axis, tiled=True)


def plain_pieces(weight, chunks):
    whole = gather_plain(weight, 1)
    rows = whole.shape[0] // (2 * chunks)
    width = whole.shape[1] // 16
    halves = []
    for half in range(2):
        pieces = []
        for chunk in range(chunks):
            start = (half * chunks + chunk) * rows
            arrays = []
            for near in range(4):
                slots = []
                for slot in range(4):
                    block = (-slot % 4) * 4 + near
                    slots.append(whole[start : start + rows, block * width : (block + 1) * width])
                arrays.append(jnp.stack(slots).reshape(2, 2, rows, width))
            pieces.append(arrays)
        halves.append(pieces)
    return halves


def vector_rows(vectors):
    rows, places, start = [], [], 0
    for vector in vectors:
        count = -(-vector.shape[0] // LANES)
        padded = jnp.pad(vector, (0, count * LANES - vector.shape[0]))
        rows.append(padded.reshape(count, LANES))
        places.append((start, count, vector.shape[0]))
        start += count
    return jnp.pad(jnp.concatenate(rows, axis=0), ((0, -start % 16), (0, 0))), places


def plain_rows(whole):
    rows = whole.shape[0] // 16
    arrays = []
    for half in range(2):
        for near in range(4):
            starts = [((-slot % 4) * 4 + near) * rows + half * rows // 2 for slot in range(4)]
            arrays.append(jnp.stack([whole[start : start + rows // 2] for start in starts]))
    return arrays


def body(
    permutes,
    wide,
    devices,
    char_ids,
    word_lengths,
    type_ids,
    cotangent,
    character_embedding_table,
    conv_weight,
    conv_bias,
    high_weight,
    high_bias,
    proj_weight,
    proj_bias,
    pos_table,
    type_table,
    embed_gain,
    embed_shift,
    qkv_weight,
    attn_bias,
    out_weight,
    out_bias,
    attn_gain,
    attn_shift,
    up_weight,
    up_bias,
    down_weight,
    down_bias,
    ffn_gain,
    ffn_shift,
):
    layers, features = high_weight.shape[:2]
    words, chars = char_ids.shape[1:]
    model_width = proj_weight.shape[1]
    conv_rows = conv_weight.shape[0]
    lengths = word_lengths[0]
    vectors = [high_bias[layer] for layer in range(layers)] + [
        attn_bias,
        type_table[0],
        type_table[1],
        proj_bias,
        embed_gain,
        embed_shift,
        out_bias,
        attn_gain,
        attn_shift,
        up_bias,
        down_bias,
        ffn_gain,
        ffn_shift,
    ]
    conv_block = jnp.pad(
        jnp.concatenate([conv_weight, conv_bias[None]], axis=0),
        ((0, LANES - conv_rows - 1), (0, 0)),
    )
    vector_block, places = vector_rows(vectors)

    if permutes:
        net = Exchange()
        window, launch = net.window, net.launch
        core_index, z, y, x = net.core, net.z, net.y, net.x
        net.load(
            "t",
            jnp.concatenate([conv_block, vector_block, pos_table.T.reshape(-1, LANES)], axis=0),
            whole=True,
        )
        chunk_rows = features // 4
        net.load("L00", high_weight[0], chunk_rows, 0)
        (
            net.state["L00"],
            net.state["t"],
            char_ids,
            lengths,
            high_weight,
            qkv_weight,
            up_weight,
        ) = lax.optimization_barrier(
            (
                net.state["L00"],
                net.state["t"],
                char_ids,
                lengths,
                high_weight,
                qkv_weight,
                up_weight,
            )
        )
        for layer, chunk in ((0, 1), (1, 0), (1, 1)):
            net.load(f"L{layer}{chunk}", high_weight[layer], chunk_rows, chunk * chunk_rows)
        encoder_splits = [
            qkv_weight.shape[1],
            out_weight.shape[0],
            proj_weight.shape[0],
        ]
        net.load(
            "e",
            jnp.concatenate(
                [qkv_weight.T, out_weight, proj_weight],
                axis=0,
            ),
        )
        net.load("up", up_weight.T)
        net.load("down", down_weight)
        net.put("L00r1", send(net.state["L00"], "z"))
        net.put("L00r3", send(net.state["L00"], "back"))
        net.move("tx", "t", "x")
        net.move("ty", "t", "y")
    else:
        window = lambda values, hold=(): values
        launch = window
        core_index = z = y = x = jnp.zeros((), jnp.int32)
    prep = sort_words(char_ids[0], lengths, chars // GROUP + 2)
    table_blocks = table_lanes(character_embedding_table)
    prep, table_blocks = window((prep, table_blocks))
    if permutes:
        net.ring_step("L00", 2)
        net.move("txy", "tx", "y")
        net.move("ex", "e", "x")
        net.move("ey", "e", "y")
        window(())
        net.ring_done("L00")
        net.state["to0"] = jnp.stack(
            [net.state["t" + part] for part in ("", "x", "y", "xy")]
        )
        net.plan_move("L00o", "x", "y")
        net.plan("to1", net.state["to0"], "z")
        launch(())
        net.turn_ring("t", 2)
        net.move("exy", "ex", "y")
        net.ring_both("L01")
        net.state["eo0"] = jnp.stack([net.state["e" + part] for part in ("", "x", "y", "xy")])
        prep, table_blocks = window((prep, table_blocks))
        net.ring_done("L01")
        net.plan_move("L01o", "x", "y")
        net.plan("to3", net.state["to2"], "z")
        prep, table_blocks = launch((prep, table_blocks))
        net.ring_both("L10")
        net.swap_chain("L00o", "L00ox", "L00oy")
    char_groups = embed_characters(prep, table_blocks)
    char_groups = window(char_groups)

    if permutes:
        net.ring_done("L10")
        conv_all, whole_vectors, pos_all = place_small(
            [net.state[f"to{step}"] for step in range(4)],
            net.place(True),
            LANES,
            [vector_block.shape[0], pos_table.size // LANES],
        )
    else:
        conv_all = gather_plain(conv_block, 1)
        whole_vectors = lax.all_gather(vector_block, "wide", axis=0, tiled=False)
        pos_all = gather_plain(pos_table.T, 0)
    filters = conv_all.shape[1]
    row = jnp.arange(LANES)[:, None]
    usable = row // CHAR_DIM < filter_widths(filters)[None, :]
    half_matrix = jnp.where(usable | (row >= conv_rows), conv_all * BF16(0.5), BF16(0.0))
    if permutes:
        net.plan("L00oxy", net.state["L00ox"], "y")
        net.plan("L01oxy", net.state["L01oy"], "x")
        net.state["eo0"] = jnp.stack([net.state["e" + part] for part in ("", "x", "y", "xy")])
        net.plan("eo1", net.state["eo0"], "z")
        half_matrix = launch(half_matrix)
        net.swap_chain("L01o", "L01ox", "L01oy")
    pooled = conv_forward(prep, char_groups, half_matrix)
    pooled, whole_vectors, pos_all = window((pooled, whole_vectors, pos_all))
    whole = [
        whole_vectors[:, start : start + count].reshape(wide, -1)[:, :size].reshape(-1)
        for start, count, size in places
    ]
    if permutes:
        net.plan_move("L10o", "x", "y")
        launch(())
        net.ring_both("L11")
        net.swap_chain("L00oxy", "L01oxy", "eo0")
        pooled, whole, pos_all = window((pooled, whole, pos_all))
        net.ring_done("L11")
        net.plan_move("L11o", "x", "y")
        net.plan("eo2", net.state["eo1"], "z")
        net.plan_swap("L10o")
        pooled = launch(pooled)
        pieces = [net.layer("L0", 2)]
    else:
        pieces = [plain_pieces(high_weight[layer], 2) for layer in range(layers)]
    high_bias_all, attn_bias_all = whole[:layers], whole[layers]
    (
        type_zero,
        type_one,
        proj_bias_all,
        gain_zero,
        shift_zero,
        out_bias_all,
        gain_one,
        shift_one,
        up_bias_all,
        down_bias_all,
        gain_two,
        shift_two,
    ) = (value.astype(F32) for value in whole[layers + 1 :])
    width = 2 * features // 16
    order = jnp.arange(8)
    near, low_slot = order // 2, order % 2
    slot_z = (z - low_slot) % 4
    place = ((slot_z & 1) * 4 + (y ^ (near >> 1)) * 2 + (x ^ (near & 1))).astype(jnp.int32)
    select = (slot_z // 2).astype(jnp.int32)
    core = core_index[None].astype(jnp.int32)
    bias_blocks = [bias.astype(F32).reshape(16, 1, width) for bias in high_bias_all]
    first_layer = highway_forward(pooled, pieces[0], bias_blocks[0], place, select, core)
    first_layer = window(first_layer)

    if permutes:
        net.plan("L10oxy", net.state["L10ox"], "y")
        net.plan("L11oxy", net.state["L11oy"], "x")
        net.plan("eo3", net.state["eo2"], "z")
        first_layer, pos_all = launch((first_layer, pos_all))
        net.swap_chain("L10ox", "L10oy", "L11o", "L11ox", "L11oy", "eo1", "eo2")
    turned = [turn(first_layer[3])]
    pos_rows = pos_all.reshape(model_width, words).T.astype(F32)
    turned, pos_rows = window((turned, pos_rows))
    if permutes:
        net.plan_swap("L10oxy", "L11oxy")
        for name in ("up", "down"):
            net.plan(name + "r1", net.state[name], "z")
            net.plan(name + "r3", net.state[name], "back")
        first_layer = net.stage(first_layer)
        for name in ("up", "down"):
            net.plan(name + "r2", net.state[name + "r1"], "z")
        net.plan_swap("eo3")
        first_layer = launch(first_layer)
        pieces.append(net.layer("L1", 2))
        qkv_all, out_all, proj_all = net.rows(
            [net.state[f"eo{step}"] for step in range(4)],
            [net.state[f"eo{step}c"] for step in range(4)],
            encoder_splits,
            True,
        )
    else:
        qkv_all, out_all, proj_all = (
            gather_plain(value, 0) for value in (qkv_weight.T, out_weight, proj_weight)
        )
    second_layer = highway_forward(first_layer[0], pieces[1], bias_blocks[1], place, select, core)
    second_layer = window(second_layer)
    if permutes:
        net.ring_done("up")
        net.ring_done("down")
        net.plan_move("upo", "x", "y")
        net.plan_move("downo", "x", "y")
        second_layer = launch(second_layer)
    states = [pooled, first_layer[0], second_layer[0]]
    transforms = [first_layer[1], second_layer[1]]
    gatings = [first_layer[2], second_layer[2]]
    perm, sorted_lengths = prep[0], prep[2]
    last = dot_tn(perm, states[2].astype(BF16)).astype(BF16)
    word_vec = dot(last, proj_all) + proj_bias_all
    type_rows = jnp.where(type_ids[0][:, None] == 1, type_one[None], type_zero[None])
    summed = word_vec + pos_rows + type_rows
    embedded = norm_rows(summed, gain_zero, shift_zero)
    turned.append(turn(second_layer[3]))
    summed, embedded, last, turned = window((summed, embedded, last, turned))

    if permutes:
        net.plan("upoxy", net.state["upox"], "y")
        net.plan("downoxy", net.state["downoy"], "x")
        embedded = launch(embedded)
        net.swap_chain("upo", "upox", "upoy", "downo")
    low_embedded = embedded.astype(BF16)
    bias_three = jnp.concatenate(
        [
            attn_bias_all[:model_width],
            jnp.zeros((model_width,), BF16),
            attn_bias_all[model_width:],
        ]
    ).astype(F32)
    qkv = (dot_nt(low_embedded, qkv_all) + bias_three).astype(BF16)
    context = attend(qkv)
    if permutes:
        context = window(context)
        net.plan_swap("downox", "downoy", "upoxy", "downoxy")
        context = launch(context)
    first_in = embedded + (dot(context, out_all) + out_bias_all)
    first = norm_rows(first_in, gain_one, shift_one)
    if permutes:
        first_in, first = window((first_in, first))
        feed_pieces = [net.near(name) + net.near(name, "c") for name in ("up", "down")]
    else:
        feed_pieces = [
            plain_rows(gather_plain(value, 0)) for value in (up_weight.T, down_weight)
        ]
    half_of = jnp.where(order % 2 == 0, 1 - core_index, core_index)
    slots = (z - (2 * half_of[:, None] + jnp.arange(2)[None, :])) % 4
    slots = slots.astype(jnp.int32)
    feed_block = (half_of * 4 + (y ^ (near >> 1)) * 2 + (x ^ (near & 1))).astype(jnp.int32)
    feed_rows = up_bias_all.shape[0] // 16
    feed_bias = jnp.moveaxis(up_bias_all.reshape(2, 2, 4, feed_rows), 1, 2).reshape(8, 1, -1)
    act, slope, hidden_out, grad_second, last_sums = feed_forward(
        first,
        feed_pieces,
        feed_bias,
        jnp.stack([down_bias_all, gain_two, shift_two]),
        cotangent[0],
        slots,
        feed_block,
        core,
    )
    grad_ffn_gain, grad_ffn_shift, grad_down_bias = last_sums[0], last_sums[1], last_sums[2]

    def sum_rows(grads, order):
        if permutes:
            return Reduction(net, *net.split(grads), order)
        return PlainReduction(grads, 0)

    def send_layer(layer, mixed, first, rows):
        sent = highway_weight_gradient(1 - core, turned[layer], mixed, first, rows, width // 2)
        key = f"layer{layer}_{first}"
        if permutes:
            net.plan(key, sent, "c")
        return layer, mixed, first, rows, (key if permutes else sent, 0)

    def keep_layer(job, order):
        layer, mixed, first, rows, (key, part) = job
        keep = highway_weight_gradient(
            core,
            turned[layer],
            mixed,
            first,
            rows,
            width // 2,
            net.state[key] if permutes else None,
            part,
        )
        if permutes:
            return Reduction(net, keep, None, order)
        other = key[:, part * rows : (part + 1) * rows]
        whole = jnp.moveaxis(jnp.concatenate([keep, other], axis=0), 1, 0).reshape(rows, -1)
        return PlainReduction([whole], 1)

    def sum_feed(keep, sent, order):
        keep, sent = (value.reshape((16,) + value.shape[3:]) for value in (keep, sent))
        if permutes:
            return Reduction(net, keep, sent, order)
        return sum_rows([jnp.concatenate([keep, sent], axis=0).reshape(-1, model_width)], "")

    def ring_of(*sums, both=False):
        return Ring(net, sums, both) if permutes else sums

    def advance(*sums):
        if permutes:
            for item in sums:
                item.step()

    def ready(*sums):
        if permutes:
            for item in sums:
                item.step(net.plan)

    def held(*sums):
        return tuple(item.key for item in sums) if permutes else ()

    def together(*sums, hold=()):
        if permutes:
            ready(*sums)
            launch(())
            window((), held(*hold))

    up_keep, up_sent, down_keep, down_sent, bias_sums, grad_resid, norm_sums = feed_forward_back(
        grad_second,
        first,
        act,
        slope,
        first_in,
        gain_one[None],
        feed_pieces,
        slots,
        feed_block,
        core,
    )
    grad_up_bias = jnp.moveaxis(bias_sums.reshape(2, 4, 2, feed_rows), 2, 1).reshape(-1)
    grad_attn_gain, grad_attn_shift, grad_out_bias = norm_sums[0], norm_sums[1], norm_sums[2]
    up_keep, up_sent, down_keep, down_sent, grad_resid = window(
        (up_keep, up_sent, down_keep, down_sent, grad_resid)
    )

    sum_up = sum_feed(up_keep, up_sent, "cxy")
    sum_down = sum_feed(down_keep, down_sent, "cyx")
    ready(sum_down, sum_up)
    grad_resid = launch(grad_resid)
    grad_branch = grad_resid.astype(BF16)
    grad_context = dot_nt(grad_branch, out_all).astype(BF16)
    grad_resid, grad_context = window((grad_resid, grad_context))
    ready(sum_down, sum_up)
    grad_context, grad_branch = launch((grad_context, grad_branch))
    grad_qkv = attend_back(qkv, grad_context)
    grad_out = dot_tn(context, grad_branch).astype(BF16)
    grad_resid, grad_qkv, grad_out = window((grad_resid, grad_qkv, grad_out))

    ready(sum_down, sum_up)
    grad_qkv, grad_resid = launch((grad_qkv, grad_resid))
    qkv_sums = column_sum(grad_qkv)
    grad_attn_bias = jnp.concatenate([qkv_sums[:model_width], qkv_sums[2 * model_width :]])
    grad_summed, grad_embed_gain, grad_embed_shift = norm_back(
        summed, gain_zero, grad_resid + dot(grad_qkv, qkv_all)
    )
    grad_word = grad_summed.astype(BF16)
    grad_proj_bias = column_sum(grad_word)
    running = dot_nt(dot(perm, grad_word).astype(BF16), proj_all)
    running = window(running)
    ring_feed = ring_of(sum_up, sum_down)
    ready(ring_feed)
    running = launch(running)
    mixed_one, sums_one, running = highway_backward(
        running, states[1], transforms[1], gatings[1], pieces[1], place, select, core
    )
    mixed_one, running, grad_qkv, grad_out, grad_word, grad_summed = window(
        (mixed_one, running, grad_qkv, grad_out, grad_word, grad_summed)
    )
    type_hot = (type_ids[0] == 1).astype(F32)[:, None]
    vector_grads = [
        grad_proj_bias,
        jnp.sum((1.0 - type_hot) * grad_summed, axis=0),
        jnp.sum(type_hot * grad_summed, axis=0),
        grad_embed_gain,
        grad_embed_shift,
        grad_attn_bias,
        grad_out_bias,
        grad_attn_gain,
        grad_attn_shift,
        grad_up_bias,
        grad_down_bias,
        grad_ffn_gain,
        grad_ffn_shift,
    ]

    half_rows, quarter = features // 2, features // 4

    def quarters(jobs, layer, mixed):
        return [
            (layer, mixed, start * quarter, quarter, (jobs[start // 2][-1][0], start % 2))
            for start in range(4)
        ]

    jobs = [send_layer(1, mixed_one, start, half_rows) for start in (0, half_rows)]
    ready(ring_feed)
    mixed_one, grad_qkv, grad_word, grad_summed = launch(
        (mixed_one, grad_qkv, grad_word, grad_summed)
    )
    grad_pos = turn(grad_summed)
    encoder_grads = [
        dot_tn(grad_qkv, low_embedded),
        grad_out,
        dot_tn(last, grad_word),
    ]
    if permutes:
        encoder_grads.append(grad_pos.reshape(-1, model_width))
        sum_encoder = sum_rows(encoder_grads, "c321xy")
        mixed_one, running, sum_encoder.terms, sum_encoder.sent = window(
            (mixed_one, running, sum_encoder.terms, sum_encoder.sent)
        )
    else:
        sum_encoder = sum_rows(encoder_grads, "")
        sum_pos = sum_rows([grad_pos], "")

    jobs = quarters(jobs, 1, mixed_one)
    one = [None] * 4
    one[0], one[2] = keep_layer(jobs[0], "yx"), keep_layer(jobs[2], "xy")
    ready(one[0], one[2], sum_encoder, ring_feed)
    running = launch(running)
    mixed_zero, sums_zero, running = highway_backward(
        running, states[0], transforms[0], gatings[0], pieces[0], place, select, core
    )
    mixed_zero, running = window((mixed_zero, running))

    one[1], one[3] = keep_layer(jobs[1], "yx"), keep_layer(jobs[3], "xy")
    jobs = [send_layer(0, mixed_zero, start, half_rows) for start in (0, half_rows)]
    grad_scaled = running * (0.5 / sorted_lengths.astype(F32))[:, None]
    ready(one[1], one[3], sum_encoder)
    grad_scaled = launch(grad_scaled)
    matrix_turned, grad_groups = conv_backward(prep, char_groups, half_matrix, grad_scaled)
    mixed_zero, matrix_turned, grad_groups = window((mixed_zero, matrix_turned, grad_groups))

    ready(*one, sum_encoder)
    mixed_zero, grad_groups = launch((mixed_zero, grad_groups))
    jobs = quarters(jobs, 0, mixed_zero)
    zero = [keep_layer(job, order_) for job, order_ in zip(jobs, ("yx", "yx", "xy", "xy"))]
    first_two = (zero[0], zero[2])
    terms = [item.terms for item in zero] if permutes else ()
    grad_table = table_gradient(prep, grad_groups, character_embedding_table.shape[0])
    first_sum, vector_places = vector_rows(vector_grads)
    last_sum, high_places = vector_rows(
        [sums_zero.reshape(-1), sums_one.reshape(-1), grad_table.reshape(-1)]
    )
    high_places = [(first_sum.shape[0] + start, *rest) for start, *rest in high_places]
    last_sum = jnp.concatenate([first_sum, last_sum], axis=0)
    terms, last_sum = window((terms, last_sum))
    last_sum = Small(net, last_sum) if permutes else lax.psum(last_sum, ("narrow", "wide"))
    for item, value in zip(zero, terms):
        item.terms = value

    if permutes:
        conv_keep, conv_sent = net.split([matrix_turned])
        net.plan("conv", conv_sent, "c")
    else:
        sum_conv = sum_rows([matrix_turned], "")
    ready(*first_two, sum_encoder, last_sum)
    launch(())
    window(())
    if permutes:
        conv_total = total_of([conv_keep, net.state["conv"]]).astype(BF16)
        conv_total = conv_total.reshape((4, 2, 2) + conv_total.shape[1:])
        zero[3].terms = [jnp.concatenate([zero[3].terms[0], conv_total], axis=3)]

    ring_one = ring_of(*one)
    together(zero[1], zero[3], *first_two, ring_one, last_sum)
    together(zero[1], zero[3], ring_one, last_sum)
    ring_first = ring_of(*first_two, both=True)
    together(ring_first, ring_one, sum_encoder, last_sum)
    ring_last = ring_of(zero[1], zero[3], both=True)
    together(ring_first, ring_last, sum_encoder, last_sum)
    together(ring_last)
    total = last_sum.result() if permutes else last_sum

    device = lax.axis_index("narrow") * wide + lax.axis_index("wide")

    def whole_vector(total, where):
        start, count, size = where
        return total[start : start + count].reshape(-1)[:size]

    def own_part(total, where):
        piece = where[2] // devices
        return lax.dynamic_slice_in_dim(whole_vector(total, where), device * piece, piece, 0)

    results = [own_part(total, where) for where in vector_places]
    (
        sum_proj_bias,
        sum_type_zero,
        sum_type_one,
        sum_embed_gain,
        sum_embed_shift,
        sum_attn_bias,
        sum_out_bias,
        sum_attn_gain,
        sum_attn_shift,
        sum_up_bias,
        sum_down_bias,
        sum_ffn_gain,
        sum_ffn_shift,
    ) = results
    sum_high_bias = jnp.stack([own_part(total, where) for where in high_places[:layers]])
    sum_table = whole_vector(total, high_places[layers]).reshape(
        character_embedding_table.shape
    )

    def rows_of(item, sizes):
        total = item.result()
        if not permutes:
            return total
        pieces, start = [], 0
        for size in sizes:
            pieces.append(total[start : start + size])
            start += size
        return pieces

    qkv_rows, sum_out, sum_proj, *rest = rows_of(
        sum_encoder,
        [
            qkv_all.shape[0] // devices,
            out_all.shape[0] // devices,
            proj_all.shape[0] // devices,
            words * model_width // devices // model_width,
        ],
    )
    if permutes:
        pos_rows = rest[0].reshape(-1, words)
    else:
        (pos_rows,) = sum_pos.result()
    if permutes:
        up_rows, down_rows = jnp.split(ring_feed.result(), 2)
    else:
        (up_rows,), (down_rows,) = sum_up.result(), sum_down.result()
    if permutes:
        first_rows, last_rows = ring_first.result(), ring_last.result()
        conv_turned = last_rows[2 * quarter :]
    else:
        (conv_turned,) = sum_conv.result()
    own_filters = lax.dynamic_slice_in_dim(
        filter_widths(filters), device * (filters // devices), filters // devices
    )
    taps = jnp.arange(conv_rows)[:, None] // CHAR_DIM
    sum_conv_weight = jnp.where(taps < own_filters[None, :], conv_turned[:, :conv_rows].T, 0.0)

    if permutes:
        parts = [first_rows[:quarter], last_rows[:quarter], first_rows[quarter:], last_rows[quarter : 2 * quarter]]
        high_rows = [jnp.concatenate(parts, axis=0), ring_one.result()]
    else:
        high_rows = [
            jnp.concatenate([part for item in sums for part in item.result()], axis=0)
            for sums in (zero, one)
        ]

    return (
        hidden_out[None],
        sum_table,
        sum_conv_weight,
        conv_turned[:, conv_rows],
        jnp.stack(high_rows),
        sum_high_bias,
        sum_proj,
        sum_proj_bias,
        pos_rows.T,
        jnp.stack([sum_type_zero, sum_type_one]),
        sum_embed_gain,
        sum_embed_shift,
        qkv_rows.T,
        sum_attn_bias,
        sum_out,
        sum_out_bias,
        sum_attn_gain,
        sum_attn_shift,
        up_rows.T,
        sum_up_bias,
        down_rows,
        sum_down_bias,
        sum_ffn_gain,
        sum_ffn_shift,
    )


def solution(mesh):
    narrow, wide = mesh.shape["narrow"], mesh.shape["wide"]
    both = ("narrow", "wide")
    placed = (
        P(both, None, None),
        P(both, None),
        P(both, None),
        P(both, None, None),
        P(),
        P(None, "wide"),
        P("wide"),
        P(None, None, "wide"),
        P(None, "wide"),
        P("wide", None),
        P("wide"),
        P(None, "wide"),
        P(None, "wide"),
        P("wide"),
        P("wide"),
        P(None, "wide"),
        P("wide"),
        P("wide", None),
        P("wide"),
        P("wide"),
        P("wide"),
        P(None, "wide"),
        P("wide"),
        P("wide", None),
        P("wide"),
        P("wide"),
        P("wide"),
    )
    return jax.shard_map(
        partial(body, (narrow, wide) == (2, 16), wide, narrow * wide),
        mesh=mesh,
        in_specs=placed,
        out_specs=(
            P(both, None, None),
            P(),
            P(None, both),
            P(both),
            P(None, None, both),
            P(None, both),
            P(both, None),
            P(both),
            P(None, both),
            P(None, both),
            P(both),
            P(both),
            P(None, both),
            P(both),
            P(both, None),
            P(both),
            P(both),
            P(both),
            P(None, both),
            P(both),
            P(both, None),
            P(both),
            P(both),
            P(both),
        ),
        check_vma=False,
    )
```
